32 devices in a mesh: dp: 2 (over x), ctx: 4 (over z), exp: 4 (over y, core).
Axes of the slice: x: 2, y: 2, z: 4, core: 2. Of those that a mesh axis runs over, the one named last changes fastest.
Arguments:
- tokens: bfloat16 [16, 1024, 2048], P(('dp', 'exp'), 'ctx'), may hold values from -6 to 6
- segments: int32 [16, 1024], P(('dp', 'exp')), may hold values from 0 to 5, as said below
- routes: int32 [16, 1024, 2], P(('dp', 'exp'), 'ctx'), may hold values from 0 to 3, all different within a row; in each aligned block of 256 rows (0 to 255, 256 to 511, ..., all dimensions but the last counted through in order) at most 160 rows name the same one
- attn_norm: float32 [2048], replicated, may hold values from 0.25 to 1.75
- query_weight: bfloat16 [2048, 2048], P(('dp', 'ctx', 'exp')), may hold values from -0.125 to 0.125
- key_weight: bfloat16 [2048, 2048], P(('dp', 'ctx', 'exp')), may hold values from -0.125 to 0.125
- value_weight: bfloat16 [2048, 2048], P(('dp', 'ctx', 'exp')), may hold values from -0.125 to 0.125
- output_weight: bfloat16 [2048, 2048], P(('dp', 'ctx', 'exp')), may hold values from -1 to 1
- expert_norm: float32 [2048], replicated, may hold values from 0.25 to 1.75
- router: bfloat16 [2048, 4], replicated, may hold values from -0.079589844 to 0.079589844
- gate_weight: bfloat16 [4, 2048, 5632], P('exp', None, 'dp'), may hold values from -0.125 to 0.125
- up_weight: bfloat16 [4, 2048, 5632], P('exp', None, 'dp'), may hold values from -0.125 to 0.125
- down_weight: bfloat16 [4, 5632, 2048], P('exp', 'dp'), may hold values from -0.15625 to 0.15625
- grad_out: bfloat16 [16, 1024, 2048], P(('dp', 'exp'), 'ctx'), may hold values from -6 to 6
Outputs:
- output: bfloat16 [16, 1024, 2048], P(('dp', 'exp'), 'ctx')
- grad_tokens: float32 [16, 1024, 2048], P(('dp', 'exp'), 'ctx')
- grad_attn_norm: float32 [2048], P(('dp', 'ctx', 'exp'))
- grad_query: float32 [2048, 2048], P(('dp', 'ctx', 'exp'))
- grad_key: float32 [2048, 2048], P(('dp', 'ctx', 'exp'))
- grad_value: float32 [2048, 2048], P(('dp', 'ctx', 'exp'))
- grad_output: float32 [2048, 2048], P(('dp', 'ctx', 'exp'))
- grad_expert_norm: float32 [2048], P(('dp', 'ctx', 'exp'))
- grad_router: float32 [2048, 4], P(('dp', 'ctx', 'exp'))
- grad_gate: float32 [4, 2048, 5632], P('exp', 'ctx', 'dp')
- grad_up: float32 [4, 2048, 5632], P('exp', 'ctx', 'dp')
- grad_down: float32 [4, 5632, 2048], P('exp', 'dp', 'ctx')
The draws below stay inside these ranges and needn't reach their ends.
Inputs may be any that keep to these rules, and one draw needn't show every extreme that they name: `segments`: segment numbers start at 0 and never fall along a sequence; a document has 200 to 2000 positions, except the last of a sequence, which may be shorter; in each group of 2 consecutive sequences one, drawn from the seed, is a single document; in every draw one other sequence, drawn from the seed, is made of documents of exactly 200 positions. `routes`: A token names 2 different experts. In each aligned block of 256 rows (one sequence's positions on one device) no expert is named more than 160 times, a bound that some block reaches.
All inputs are finite; a program needn't handle non-finite values.
Results may differ from the reference program's by a relative error of at most 0.02.
Values may be sent and summed in bfloat16 or wider, within the bound.
A program may use at most 448 MiB of HBM per device.

```python
import math
import jax
import jax.numpy as jnp
import numpy as np
from jax import lax

D = 2048
HEADS = 16
HEAD = 128
FF = 5632
EXPERTS = 4
TOPK = 2
SEQS = 2
DOC_LO = 200
DOC_HI = 2000
LENGTH = 1024
SEQ_DEV = 256
CAP = 160
NSEQ = 16


def draw_segments(key, part):
    length_key, whole_key, short_key = jax.random.split(jax.random.fold_in(key, 17), 3)
    doc_count = LENGTH // DOC_LO + 1
    group_count = NSEQ // SEQS
    whole_pick = jax.random.randint(whole_key, (group_count,), 0, SEQS)
    short_group = jax.random.randint(short_key, (), 0, group_count)
    short_member = (whole_pick[short_group] + 1) % SEQS
    short_seq = short_group * SEQS + short_member
    doc_lengths = jax.random.randint(length_key, (NSEQ, doc_count), DOC_LO, DOC_HI + 1)
    seq_numbers = jnp.arange(NSEQ)[:, None]
    doc_lengths = jnp.where(seq_numbers == short_seq, DOC_LO, doc_lengths)
    doc_ends = jnp.cumsum(doc_lengths, axis=1)
    places = jnp.arange(LENGTH)
    packed = jnp.sum((doc_ends[:, None, :] <= places[None, :, None]).astype(jnp.int32), axis=2)
    member = jnp.arange(SEQS)[None, :]
    single = (member == whole_pick[:, None]).reshape(NSEQ)
    return jnp.where(single[:, None], 0, packed).astype(jnp.int32)


def steps_of(key, shape, cuts, smallest, top_value):
    def one(dim, blocks):
        heights = jax.random.uniform(jax.random.fold_in(jax.random.fold_in(key, 6), dim), (blocks,), jnp.float32, smallest / len(cuts), top_value / len(cuts))
        return jnp.repeat(jnp.exp(heights), shape[dim] // blocks).reshape((-1,) + (1,) * (len(shape) - dim - 1))

    level = one(*cuts[0])
    for cut in cuts[1:]:
        level = level * one(*cut)
    return level


def routed_block(rng, own, number, rows, count, top, reach, lean):
    ranking = jax.random.permutation(rng, count)
    crowded, usual = shares(count, rows * top, reach, lean, True), shares(count, rows * top, reach, lean, False)
    places = jnp.arange(count)

    def named(lengths, turn):
        used = int((lengths > 0).sum())
        fixed = max(1, used // 4)
        moved = fixed + (places - fixed + turn * (used - fixed)) % max(1, count - fixed)
        return jnp.zeros((count,), jnp.int32).at[ranking[jnp.where(places < fixed, places, moved)]].set(jnp.asarray(lengths, jnp.int32))

    lengths = jnp.where(number % 4 == 0, named(crowded, number // 4), named(usual, number - number // 4 - 1))
    mixed = jax.random.permutation(jax.random.fold_in(own, 3), count)
    giver, sink = mixed[0:count // 2 * 2:2], mixed[1:count // 2 * 2:2]
    room = jnp.minimum(lengths[giver] - 1, reach - lengths[sink]) // 2
    room = jnp.where((giver == ranking[0]) | (sink == ranking[0]) | (lengths[sink] == 0), 0, jnp.maximum(room, 0))
    moved = jax.random.randint(jax.random.fold_in(own, 4), (count // 2,), 0, 1 << 20) % (room + 1)
    lengths = lengths.at[giver].add(-moved).at[sink].add(moved)
    labels = jnp.searchsorted(jnp.cumsum(lengths), jnp.arange(rows * top), side="right").astype(jnp.int32)
    grid = labels.reshape(top, rows).T
    grid = grid[jax.random.permutation(jax.random.fold_in(own, 1), rows)]
    turn = jax.random.randint(jax.random.fold_in(own, 2), (rows, 1), 0, top)
    return jnp.take_along_axis(grid, (jnp.arange(top)[None, :] + turn) % top, axis=1)


def shares(count, total, reach, lean, full):
    portions = [(1 << 20) // math.isqrt(rank ** lean) + 1 for rank in range(1, count + 1)]
    largest = reach if full else min(reach, max(-(-total // count), total * portions[0] // sum(portions)))
    least = 1 if total - largest >= count - 1 else 0
    counts, spare = [largest] + [least] * (count - 1), total - largest - least * (count - 1)
    while spare > 0:
        movable = [i for i in range(1, count) if counts[i] < largest] or [i for i in range(1, count) if counts[i] < reach]
        whole, budget = sum([portions[i] for i in movable]), spare
        for i in movable:
            more = min(reach - counts[i], max(1, budget * portions[i] // whole), spare)
            counts[i] = counts[i] + more
            spare = spare - more
    return np.array(counts)


def noise(key, dims, scale, reach, cuts=(), kind=jnp.bfloat16):
    loudness = steps_of(key, dims, cuts, -0.22, 0.18) if cuts else 1.0
    values = jax.random.normal(key, dims, jnp.float32) * scale * loudness
    return jnp.minimum(jnp.maximum(values, -reach), reach).astype(kind)


def setup_inputs(seed: int = 0) -> dict:
    streams_of = jax.random.split(jax.random.key(seed), 15)
    tokens = noise(streams_of[0], (NSEQ, LENGTH, D), 1.0, 6.0, ((0, 8), (1, 4)))
    segments = draw_segments(jax.random.fold_in(streams_of[14], 71), 0)
    routes_keys = jax.random.split(jax.random.fold_in(streams_of[2], 1), NSEQ * LENGTH // SEQ_DEV)
    routes_turns = jax.random.permutation(jax.random.fold_in(streams_of[2], 3), NSEQ * LENGTH // SEQ_DEV)
    routes = jax.vmap(lambda own, number: routed_block(jax.random.fold_in(streams_of[2], 2), own, number, SEQ_DEV, EXPERTS, TOPK, CAP, 1))(routes_keys, routes_turns).reshape((NSEQ, LENGTH, TOPK))
    attn_norm = jnp.clip(1.0 + 0.15 * jax.random.normal(streams_of[3], (D,), jnp.float32), 0.25, 1.75)
    query_weight = noise(streams_of[4], (D, D), D ** -0.5, 0.125, ((0, 32),))
    key_weight = noise(streams_of[5], (D, D), D ** -0.5, 0.125, ((0, 32),))
    value_weight = noise(streams_of[6], (D, D), D ** -0.5, 0.125, ((0, 32),))
    output_weight = noise(streams_of[7], (D, D), (D // 64) ** -0.5, 1.0, ((0, 32),))
    expert_norm = jnp.clip(1.0 + 0.15 * jax.random.normal(streams_of[8], (D,), jnp.float32), 0.25, 1.75)
    router = noise(streams_of[9], (D, EXPERTS), 0.0155, 0.079589844)
    gate_weight = noise(streams_of[10], (EXPERTS, D, FF), D ** -0.5, 0.125, ((0, 4), (2, 2)))
    up_weight = noise(streams_of[11], (EXPERTS, D, FF), D ** -0.5, 0.125, ((0, 4), (2, 2)))
    down_weight = noise(streams_of[12], (EXPERTS, FF, D), (FF // 4) ** -0.5, 0.15625, ((0, 4), (1, 2)))
    grad_out = noise(streams_of[13], (NSEQ, LENGTH, D), 1.0, 6.0, ((0, 8), (1, 4)))
    return {"tokens": tokens, "segments": segments, "routes": routes, "attn_norm": attn_norm, "query_weight": query_weight, "key_weight": key_weight, "value_weight": value_weight, "output_weight": output_weight, "expert_norm": expert_norm, "router": router, "gate_weight": gate_weight, "up_weight": up_weight, "down_weight": down_weight, "grad_out": grad_out}


@jax.custom_vjp
def low(v):
    return lax.optimization_barrier(v.astype(jnp.bfloat16)).astype(jnp.float32)

@jax.custom_vjp
def low_back(v):
    return v

def low_keep(v):
    return (low(v), None)

def low_pass(kept, grad):
    return (grad,)

def back_keep(v):
    return (v, None)

def back_low(kept, grad):
    return (low(grad),)
low.defvjp(low_keep, low_pass)
low_back.defvjp(back_keep, back_low)
highest = lax.Precision.HIGHEST
epsilon = 1e-05
theta_base = 10000.0
masked_score = -1e+30

def matmul(matrix_one, matrix_two):
    return jnp.dot(matrix_one, matrix_two, precision=highest, preferred_element_type=jnp.float32)

def rms_normed(values):
    return values * lax.rsqrt(lax.optimization_barrier(jnp.mean(values * values, axis=-1, keepdims=True)) + epsilon)

def rotary_tables(positions):
    half_size = HEAD // 2
    frequency = theta_base ** (-jnp.arange(half_size, dtype=jnp.float32) / half_size)
    angles = positions[:, None] * frequency[None, :]
    return (jnp.cos(angles)[:, None, :], jnp.sin(angles)[:, None, :])

def rotate(values, cosine_table, sine_table):
    half_size = values.shape[-1] // 2
    front_half = values[..., :half_size]
    back_half = values[..., half_size:]
    return jnp.concatenate([front_half * cosine_table - back_half * sine_table, back_half * cosine_table + front_half * sine_table], axis=-1)

def attend_sequence(hidden, segment, query_weight, key_weight, value_weight, output_weight):
    length = hidden.shape[0]
    places = jnp.arange(length)
    cosine_table, sine_table = rotary_tables(places.astype(jnp.float32))
    query_rows = low(rotate(low_back(matmul(hidden, query_weight)).reshape(length, HEADS, HEAD), cosine_table, sine_table))
    key_rows = low(rotate(low_back(matmul(hidden, key_weight)).reshape(length, HEADS, HEAD), cosine_table, sine_table))
    value_rows = low(low_back(matmul(hidden, value_weight))).reshape(length, HEADS, HEAD)
    scores = low_back(jnp.einsum('qhd,khd->hqk', query_rows, key_rows, precision=highest) * HEAD ** (-0.5))
    visible = (segment[:, None] == segment[None, :]) & (places[None, :] <= places[:, None])
    scores = jnp.where(visible[None], scores, masked_score)
    row_top = lax.optimization_barrier(jnp.max(scores, axis=-1, keepdims=True))
    weights = jnp.exp(scores - row_top)
    row_total = lax.optimization_barrier(jnp.sum(weights, axis=-1))
    summed = low_back(jnp.einsum('hqk,khd->qhd', low(weights), value_rows, precision=highest))
    attended = summed / jnp.transpose(row_total)[:, :, None]
    mixed_heads = low(low_back(attended)).reshape(length, HEADS * HEAD)
    return low_back(matmul(mixed_heads, output_weight))

def reference(tokens, segments, routes, attn_norm, query_weight, key_weight, value_weight, output_weight, expert_norm, router, gate_weight, up_weight, down_weight, grad_out):
    token_count = NSEQ * LENGTH
    blocks = token_count // SEQ_DEV
    pair_routes = routes.reshape(blocks, SEQ_DEV * TOPK).astype(jnp.int32)
    onehot = (pair_routes[:, :, None] == jnp.arange(EXPERTS, dtype=jnp.int32)[None, None, :]).astype(jnp.int32)
    earlier = jnp.cumsum(onehot, axis=1) - onehot
    slot_rank = lax.optimization_barrier(jnp.sum(earlier * onehot, axis=2)).astype(jnp.int32)
    block_ids = jnp.arange(blocks, dtype=jnp.int32)[:, None]
    pair_ids = (block_ids * (SEQ_DEV * TOPK) + jnp.arange(SEQ_DEV * TOPK, dtype=jnp.int32)[None, :]).astype(jnp.int32)
    slot_table = jnp.full((blocks, EXPERTS, CAP), token_count * TOPK, jnp.int32)
    slot_table = slot_table.at[jnp.broadcast_to(block_ids, slot_rank.shape), pair_routes, slot_rank].set(pair_ids)
    source_rows = (jnp.transpose(slot_table, (1, 0, 2)).reshape(EXPERTS, blocks * CAP) // TOPK).astype(jnp.int32)
    where_index = (pair_routes * (blocks * CAP) + block_ids * CAP + slot_rank).reshape(-1).astype(jnp.int32)
    flat_routes = routes.reshape(token_count, TOPK).astype(jnp.int32)

    def forward(token_float, attn_gain, query_full, key_full, value_full, output_full, expert_gain, router_full, gate_full, up_full, down_full):
        hidden_one = low(rms_normed(token_float) * attn_gain)

        def attend_one(sequence_item):
            return attend_sequence(sequence_item[0], sequence_item[1], query_full, key_full, value_full, output_full)
        branch = lax.map(jax.checkpoint(attend_one), (hidden_one, segments))
        residual = token_float + branch
        hidden_two = low(rms_normed(residual) * expert_gain)
        flat_hidden = hidden_two.reshape(token_count, D)
        logits = low_back(matmul(flat_hidden, router_full))
        chosen = jnp.take_along_axis(logits, flat_routes, axis=1)
        gate_values = jax.nn.softmax(chosen, axis=-1)
        padded = jnp.concatenate([flat_hidden, jnp.zeros((1, D), flat_hidden.dtype)], axis=0)

        def expert_apply(expert_item):
            gate_one, up_one, down_one, row_index = expert_item
            inputs = low_back(padded[row_index])
            gate_pre = low_back(matmul(inputs, gate_one))
            up_pre = low_back(matmul(inputs, up_one))
            hidden_units = low(jax.nn.silu(gate_pre) * up_pre)
            return low(low_back(matmul(hidden_units, down_one)))
        expert_rows = lax.map(jax.checkpoint(expert_apply), (gate_full, up_full, down_full, source_rows))
        pair_outputs = expert_rows.reshape(EXPERTS * blocks * CAP, D)[where_index].reshape(token_count, TOPK, D)
        mixture = lax.optimization_barrier(jnp.sum(gate_values[:, :, None] * pair_outputs, axis=1))
        return residual + mixture.reshape(NSEQ, LENGTH, D)
    floats = tuple((array.astype(jnp.float32) for array in (tokens, attn_norm, query_weight, key_weight, value_weight, output_weight, expert_norm, router, gate_weight, up_weight, down_weight)))
    result, pullback = jax.vjp(forward, floats[0], floats[1], floats[2], floats[3], floats[4], floats[5], floats[6], floats[7], floats[8], floats[9], floats[10])
    gradients = pullback(grad_out.astype(jnp.float32))
    return (result.astype(jnp.bfloat16), gradients[0], gradients[1], gradients[2], gradients[3], gradients[4], gradients[5], gradients[6], gradients[7], gradients[8], gradients[9], gradients[10])
```

```python
import functools

import jax
import jax.numpy as jnp
from jax import lax
from jax.experimental import pallas as pl
from jax.experimental.pallas import tpu as pltpu
from jax.sharding import Mesh, PartitionSpec as P

HEADS = 16
CORES = 2

epsilon = 1e-05
theta_base = 10000.0
masked_score = -1e30
bf16 = jnp.bfloat16
f32 = jnp.float32

PLANE = ("dp", "y", "core")
CHIP = ("r", "core")
SPREAD = ("dp", "seq", "y")
CTX = ("seq", "r")
EVERY = ("dp", "seq", "r", "y", "core")


def product(a, b):
    return jnp.dot(a, b, preferred_element_type=f32)


def product_t(a, b):
    return lax.dot_general(a, b, (((1,), (1,)), ((), ())), preferred_element_type=f32)


def t_product(a, b):
    return lax.dot_general(a, b, (((0,), (0,)), ((), ())), preferred_element_type=f32)


def swap(a, axis):
    return lax.ppermute(a, axis, [(0, 1), (1, 0)])


def halves(a, axis):
    size = a.shape[axis] // 2
    me = lax.axis_index("core")
    mine = lax.dynamic_slice_in_dim(a, me * size, size, axis)
    other = lax.dynamic_slice_in_dim(a, (1 - me) * size, size, axis)
    return mine, other


def by_core(mine, other, axis):
    first = lax.axis_index("core") == 0
    return jnp.concatenate([jnp.where(first, mine, other), jnp.where(first, other, mine)], axis=axis)


def chip_gather(a, axis, parts):
    if parts == 2:
        return by_core(a, swap(a, "core"), axis)
    return lax.all_gather(a, CHIP, axis=axis, tiled=True)


def chip_scatter(a, axis, parts):
    if parts == 2:
        mine, other = halves(a, axis)
        return mine.astype(f32) + swap(other, "core").astype(f32)
    return lax.psum_scatter(a, CHIP, scatter_dimension=axis, tiled=True).astype(f32)


def chip_exchange(a, split, concat, parts):
    if parts == 2:
        mine, other = halves(a, split)
        return by_core(mine, swap(other, "core"), concat)
    return lax.all_to_all(a, CHIP, split_axis=split, concat_axis=concat, tiled=True)


def core_exchange(a, split, concat):
    mine, other = halves(a, split)
    return by_core(mine, swap(other, "core"), concat)


def to_sequences(a):
    a = core_exchange(a, 1, 0)
    return lax.all_to_all(a, "seq", split_axis=0, concat_axis=0, tiled=True)


def from_sequences(a):
    a = lax.all_to_all(a, "seq", split_axis=0, concat_axis=0, tiled=True)
    return core_exchange(a, 0, 1)


def plane_scatter(rows, width):
    count = rows.shape[0] // 8
    blocks = rows.reshape(2, 2, 2, count, width)
    got = swap(blocks[:, :, 1], "core")
    held = (blocks[:, :, 0].astype(f32) + got.astype(f32)).astype(bf16)
    half = count // 2
    by_x = swap(held[1, 1, :half], "dp")
    by_y = swap(held[1, 1, half:], "y")
    to_x = jnp.concatenate(
        [held[1, 0, :half], (held[1, 0, half:].astype(f32) + by_y.astype(f32)).astype(bf16)], axis=0
    )
    to_y = jnp.concatenate(
        [(held[0, 1, :half].astype(f32) + by_x.astype(f32)).astype(bf16), held[0, 1, half:]], axis=0
    )
    from_x = swap(to_x, "dp")
    from_y = swap(to_y, "y")
    return held[0, 0].astype(f32) + from_x.astype(f32) + from_y.astype(f32)


def visible_block(seg_row, seg_col, start, rows, cols):
    row_place = start + lax.broadcasted_iota(jnp.int32, (rows, cols), 0)
    col_place = lax.broadcasted_iota(jnp.int32, (rows, cols), 1)
    return (seg_col == seg_row) & (col_place <= row_place)


def turned(u, cosine, sine):
    return u * cosine + pltpu.roll(u, u.shape[1] // 2, 1) * sine


def attend_kernel(scale, block, qp, kp, vp, cosine, sine, seg_row, seg_col, q_out, k_out, v_out, mixed):
    length = qp.shape[0]
    q_out[...] = turned(qp[...], cosine[...], sine[...]).astype(bf16)
    k_out[...] = turned(kp[...], cosine[...], sine[...]).astype(bf16)
    v_out[...] = vp[...].astype(bf16)
    for start in range(0, length, block):
        stop = start + block
        scores = product_t(q_out[start:stop, :], k_out[:stop, :]) * scale
        seen = visible_block(seg_row[:, :stop], seg_col[start:stop, :], start, block, stop)
        scores = jnp.where(seen, scores, masked_score)
        top = jnp.max(scores, axis=1, keepdims=True)
        weights = jnp.exp(scores - top)
        total = jnp.sum(weights, axis=1, keepdims=True)
        summed = product(weights.astype(bf16), v_out[:stop, :])
        mixed[start:stop, :] = (summed / total).astype(bf16)


def attend(qkv, cosine, sine, seg_row, seg_col, heads):
    length, head = qkv.shape[0], cosine.shape[1]
    block = min(256, length)

    def column(offset):
        return pl.BlockSpec((length, head), lambda h: (0, offset + h))

    def whole(shape):
        return pl.BlockSpec(shape, lambda h: (0, 0))

    out = jax.ShapeDtypeStruct((length, heads * head), bf16)
    pairs = length * (length + block) // 2 * heads
    return pl.pallas_call(
        functools.partial(attend_kernel, head**-0.5, block),
        grid=(heads,),
        in_specs=[
            column(0),
            column(heads),
            column(2 * heads),
            whole((length, head)),
            whole((length, head)),
            whole((1, length)),
            whole((length, 1)),
        ],
        out_specs=[column(0)] * 4,
        out_shape=[out] * 4,
        compiler_params=pltpu.CompilerParams(vmem_limit_bytes=48 * 2**20),
        cost_estimate=pl.CostEstimate(
            flops=4 * pairs * head, bytes_accessed=20 * length * heads * head, transcendentals=pairs
        ),
        name="attend",
    )(qkv, qkv, qkv, cosine, sine, seg_row, seg_col)


def attend_back_kernel(
    scale, block, q, k, v, mixed, dmixed, cosine, sine, seg_row, seg_col, dq_out, dk_out, dv_out, dk_sum, dv_sum
):
    length = q.shape[0]
    dk_sum[...] = jnp.zeros_like(dk_sum)
    dv_sum[...] = jnp.zeros_like(dv_sum)
    for start in range(0, length, block):
        stop = start + block
        scores = product_t(q[start:stop, :], k[:stop, :]) * scale
        seen = visible_block(seg_row[:, :stop], seg_col[start:stop, :], start, block, stop)
        scores = jnp.where(seen, scores, masked_score)
        top = jnp.max(scores, axis=1, keepdims=True)
        weights = jnp.exp(scores - top)
        inverse = 1.0 / jnp.sum(weights, axis=1, keepdims=True)
        grad = dmixed[start:stop, :].astype(f32)
        delta = jnp.sum(grad * mixed[start:stop, :].astype(f32), axis=1, keepdims=True) * inverse
        unit = (grad * inverse).astype(bf16)
        dweights = product_t(unit, v[:stop, :])
        dscores = (weights * (dweights - delta)).astype(bf16)
        dq = product(dscores, k[:stop, :]) * scale
        dq_out[start:stop, :] = turned(dq, cosine[start:stop, :], -sine[start:stop, :]).astype(bf16)
        dk_sum[:stop, :] += t_product(dscores, q[start:stop, :])
        dv_sum[:stop, :] += t_product(weights.astype(bf16), unit)
    dk_out[...] = turned(dk_sum[...] * scale, cosine[...], -sine[...]).astype(bf16)
    dv_out[...] = dv_sum[...].astype(bf16)


def attend_back(q, k, v, mixed, dmixed, cosine, sine, seg_row, seg_col, heads):
    length, head = q.shape[0], cosine.shape[1]
    block = min(256, length)
    column = pl.BlockSpec((length, head), lambda h: (0, h))

    def whole(shape):
        return pl.BlockSpec(shape, lambda h: (0, 0))

    out = jax.ShapeDtypeStruct((length, heads * head), bf16)
    pairs = length * (length + block) // 2 * heads
    return pl.pallas_call(
        functools.partial(attend_back_kernel, head**-0.5, block),
        grid=(heads,),
        in_specs=[column] * 5
        + [whole((length, head)), whole((length, head)), whole((1, length)), whole((length, 1))],
        out_specs=[column] * 3,
        out_shape=[out] * 3,
        scratch_shapes=[pltpu.VMEM((length, head), f32)] * 2,
        compiler_params=pltpu.CompilerParams(vmem_limit_bytes=48 * 2**20),
        cost_estimate=pl.CostEstimate(
            flops=10 * pairs * head, bytes_accessed=16 * length * heads * head, transcendentals=pairs
        ),
        name="attend_back",
    )(q, k, v, mixed, dmixed, cosine, sine, seg_row, seg_col)


def units_kernel(chunk, x, dy, gate, up, down, units, dgate, dup):
    gate_w, up_w, down_w = gate[...], up[...], down[...]

    def step(i, carry):
        rows = pl.ds(pl.multiple_of(i * chunk, chunk), chunk)
        gpre = product(x[rows, :], gate_w)
        upre = product(x[rows, :], up_w)
        dunits = product_t(dy[rows, :], down_w)
        s = jax.nn.sigmoid(gpre)
        silu = gpre * s
        units[rows, :] = (silu * upre).astype(bf16)
        dgate[rows, :] = (dunits * upre * (s * (1.0 + gpre * (1.0 - s)))).astype(bf16)
        dup[rows, :] = (dunits * silu).astype(bf16)
        return carry

    lax.fori_loop(0, x.shape[0] // chunk, step, 0)


def expert_units(x, dy, gate, up, down):
    rows, width = x.shape
    units = gate.shape[1]
    chunk = max(c for c in range(16, 513, 16) if rows % c == 0)
    tile = 256 if units % 256 == 0 else units
    once = pl.BlockSpec((rows, width), lambda j: (0, 0), pipeline_mode=pl.Buffered(1))
    out = jax.ShapeDtypeStruct((rows, units), bf16)
    return pl.pallas_call(
        functools.partial(units_kernel, chunk),
        grid=(units // tile,),
        in_specs=[
            once,
            once,
            pl.BlockSpec((width, tile), lambda j: (0, j)),
            pl.BlockSpec((width, tile), lambda j: (0, j)),
            pl.BlockSpec((tile, width), lambda j: (j, 0)),
        ],
        out_specs=[pl.BlockSpec((rows, tile), lambda j: (0, j))] * 3,
        out_shape=[out] * 3,
        compiler_params=pltpu.CompilerParams(vmem_limit_bytes=56 * 2**20),
        cost_estimate=pl.CostEstimate(
            flops=6 * rows * width * units,
            bytes_accessed=4 * rows * width + 6 * width * units + 6 * rows * units,
            transcendentals=rows * units,
        ),
        name="expert_units",
    )(x, dy, gate, up, down)


def counts_before(flags):
    rows = flags.reshape(-1, 128).astype(bf16)
    lanes = jnp.arange(128)
    inside = product(rows, (lanes[:, None] < lanes[None, :]).astype(bf16))
    lines = jnp.arange(rows.shape[0])
    earlier = (lines[None, :] < lines[:, None]).astype(f32)
    ahead = jnp.sum(earlier * jnp.sum(rows.astype(f32), axis=1)[None, :], axis=1)
    return (inside + ahead[:, None]).astype(jnp.int32).reshape(-1)


def norm_backward(grad_rows, normed, inverse, gain):
    weighted = grad_rows * gain
    mean_term = jnp.mean(weighted * normed, axis=-1, keepdims=True)
    return inverse * (weighted - normed * mean_term), jnp.sum(grad_rows * normed, axis=0)


def pick(a, index, axis):
    return lax.dynamic_index_in_dim(a, index, axis, keepdims=False)


def on_device(
    sizes,
    tokens,
    segments,
    routes,
    attn_norm,
    query_weight,
    key_weight,
    value_weight,
    output_weight,
    expert_norm,
    router,
    gate_weight,
    up_weight,
    down_weight,
    grad_out,
):
    dp_n, seq_n, r_n, y_n, core_n = sizes
    parts = r_n * core_n
    seq_count, seq_dev, width = tokens.shape
    piece = seq_dev // core_n
    length = segments.shape[1]
    home = seq_n * piece
    head = width // HEADS
    heads = HEADS // parts
    columns = width // parts
    experts = router.shape[1]
    topk = routes.shape[2]
    plane = 8 * home
    capacity = (5 * seq_dev * topk // (4 * experts)) * (plane // seq_dev)
    dp_i, seq_i, r_i, y_i, core_i = (lax.axis_index(a) for a in EVERY)
    group, member = seq_i // seq_count, seq_i % seq_count

    own_segments = lax.dynamic_slice_in_dim(segments, (seq_i * r_n + r_i) * seq_dev, seq_dev, 1)
    small = jnp.concatenate(
        [jnp.transpose(routes, (2, 0, 1)), own_segments[None]], axis=0
    ).reshape((topk + 1) * seq_count, seq_dev)
    small = lax.all_gather(small, EVERY, axis=0, tiled=True).reshape(
        dp_n, seq_n, r_n, y_n, core_n, topk + 1, seq_count, seq_dev
    )
    small = pick(pick(small, group, 4), member, 5)
    segment = pick(pick(small, dp_i, 0), y_i, 2)[:, :, topk].reshape(length)
    plane_routes = (
        pick(small, r_i, 2)[:, :, :, :topk]
        .reshape(dp_n, seq_n, y_n, topk, core_n, piece)
        .transpose(3, 0, 2, 4, 1, 5)
        .reshape(topk, dp_n, y_n, core_n, home)
    )

    local = jnp.concatenate([query_weight, key_weight, value_weight, output_weight], axis=1)
    rows_here = local.shape[0]
    local = local.reshape(rows_here, 4, parts, columns)
    local = chip_exchange(local, 2, 0, parts).reshape(parts, rows_here, 4 * columns)

    def gathered(block):
        whole = lax.all_gather(block.reshape(parts * rows_here, -1), SPREAD, axis=0, tiled=True)
        if r_n > 1:
            whole = (
                whole.reshape(dp_n * seq_n, y_n, r_n, core_n * rows_here, -1)
                .transpose(0, 2, 1, 3, 4)
                .reshape(width, -1)
            )
        return whole

    weight_in = gathered(local[:, :, : 3 * columns])
    weight_out = gathered(local[:, :, 3 * columns :])

    token_float = to_sequences(tokens).astype(f32)
    grad_home = to_sequences(grad_out)
    inverse_one = lax.rsqrt(jnp.mean(token_float * token_float, axis=-1, keepdims=True) + epsilon)
    hidden_one = (token_float * inverse_one * attn_norm).astype(bf16)
    hidden_full = chip_gather(hidden_one, 1, parts).reshape(length, width)

    grad_plane = lax.all_gather(grad_home.reshape(home, width), PLANE, axis=0, tiled=True)

    half = head // 2
    frequency = theta_base ** (-jnp.arange(half, dtype=f32) / half)
    angles = jnp.arange(length, dtype=f32)[:, None] * frequency[None, :]
    cosine = jnp.concatenate([jnp.cos(angles)] * 2, axis=1)
    sine = jnp.concatenate([-jnp.sin(angles), jnp.sin(angles)], axis=1)
    seg_row, seg_col = segment[None, :], segment[:, None]

    qkv = product(hidden_full, weight_in)
    query, keys, values, mixed = attend(qkv, cosine, sine, seg_row, seg_col, heads)
    mixed_full = chip_gather(mixed, 1, parts)
    branch = product(mixed_full, weight_out).reshape(seq_n, parts, piece, columns)
    branch = chip_exchange(branch, 1, 3, parts).reshape(seq_n, piece, width)
    residual = token_float + branch
    inverse_two = lax.rsqrt(jnp.mean(residual * residual, axis=-1, keepdims=True) + epsilon)
    normed_two = residual * inverse_two
    hidden_two = (normed_two * expert_norm).astype(bf16).reshape(home, width)

    hidden_plane = lax.all_gather(hidden_two, PLANE, axis=0, tiled=True)
    all_routes = plane_routes.reshape(topk, plane)
    mine = y_i * core_n + core_i
    to_me = all_routes == mine
    chosen_here = jnp.any(to_me, axis=0)
    rank = counts_before(chosen_here)
    ends = rank + chosen_here.astype(jnp.int32)
    slots = jnp.arange(capacity, dtype=jnp.int32)
    source = jnp.sum((ends[None, :] <= slots[:, None]).astype(jnp.int32), axis=1)
    filled = source < plane
    source = jnp.minimum(source, plane - 1)

    def gates_of(rows, where):
        logits = product(rows, router)
        hot = where[:, :, None] == jnp.arange(experts, dtype=jnp.int32)[None, None, :]
        picked = jnp.sum(jnp.where(hot, logits[None], 0.0), axis=2)
        return jax.nn.softmax(picked, axis=0), hot

    plane_gates, _ = gates_of(hidden_plane, all_routes)
    my_gate = jnp.sum(jnp.where(to_me, plane_gates, 0.0), axis=0)
    row_gate = jnp.where(filled, my_gate[source], 0.0)[:, None]
    expert_in = hidden_plane[source]
    dout_rows = grad_plane[source]
    dy_rows = (row_gate * dout_rows.astype(f32)).astype(bf16)

    gate_one, up_one, down_one = gate_weight[0], up_weight[0], down_weight[0]
    units, dgpre, dupre = expert_units(expert_in, dy_rows, gate_one, up_one, down_one)

    def over_ctx(part):
        return lax.psum_scatter(part.astype(bf16), CTX, scatter_dimension=0, tiled=True).astype(f32)

    grad_down = jnp.transpose(over_ctx(t_product(dy_rows, units)))[None]
    grad_gate = over_ctx(t_product(expert_in, dgpre))[None]
    grad_up = over_ctx(t_product(expert_in, dupre))[None]

    ypair = product(units, down_one).astype(bf16)
    dgate_rows = jnp.sum(dout_rows.astype(f32) * ypair.astype(f32), axis=1)
    weighted = (row_gate * ypair.astype(f32)).astype(bf16)
    dinput = (product_t(dgpre, gate_one) + product_t(dupre, up_one)).astype(bf16)

    def relative(a):
        a = a.reshape(dp_n, y_n, core_n, home)
        for axis, index in ((0, dp_i), (1, y_i), (2, core_i)):
            a = jnp.where(index == 0, a, jnp.flip(a, axis))
        return a.reshape(plane)

    place = relative(jnp.where(chosen_here, rank, -1))
    has = (place >= 0)[:, None]
    place = jnp.maximum(place, 0)

    def returned(rows):
        return plane_scatter(jnp.where(has, rows[place], jnp.zeros((), bf16)), width)

    dgate_plane = jnp.where(chosen_here, dgate_rows[jnp.minimum(rank, capacity - 1)], 0.0)
    dgate_home = lax.all_to_all(
        dgate_plane.reshape(8, home), PLANE, split_axis=0, concat_axis=0, tiled=True
    ).reshape(dp_n, experts, home).sum(axis=0)

    mixture = returned(weighted).reshape(seq_n, piece, width)
    output = from_sequences((residual + mixture).astype(bf16))

    my_routes = pick(pick(pick(plane_routes, dp_i, 1), y_i, 1), core_i, 1)
    gates, hot = gates_of(hidden_two, my_routes)
    dgate = jnp.sum(jnp.where(hot, jnp.transpose(dgate_home)[None], 0.0), axis=2)
    dsel = gates * (dgate - jnp.sum(gates * dgate, axis=0, keepdims=True))
    dlogits = jnp.sum(jnp.where(hot, dsel[:, :, None], 0.0), axis=0).astype(bf16)
    router_grad = t_product(hidden_two, dlogits)
    dhidden_two = returned(dinput) + product_t(dlogits, router)

    flat_two = normed_two.reshape(home, width)
    dresid, expert_norm_grad = norm_backward(
        dhidden_two, flat_two, inverse_two.reshape(home, 1), expert_norm
    )
    dresid = dresid + grad_home.reshape(home, width).astype(f32)
    dbranch = chip_gather(dresid.astype(bf16).reshape(seq_n, piece, width), 1, parts).reshape(length, width)
    column_start = (r_i * core_n + core_i) * columns
    dbranch_here = lax.dynamic_slice_in_dim(dbranch, column_start, columns, 1)
    out_grad = t_product(mixed_full, dbranch_here)
    dmixed = chip_scatter(product_t(dbranch_here, weight_out).astype(bf16), 1, parts).astype(bf16)
    dqpre, dkpre, dvpre = attend_back(
        query, keys, values, mixed, dmixed, cosine, sine, seg_row, seg_col, heads
    )
    dqkv = jnp.concatenate([dqpre, dkpre, dvpre], axis=1)
    in_grad = t_product(hidden_full, dqkv)
    dhidden_one = chip_scatter(
        product_t(dqkv, weight_in).astype(bf16).reshape(seq_n, parts * piece, width), 1, parts
    )
    normed_one = token_float * inverse_one
    dtokens, attn_norm_grad = norm_backward(
        dhidden_one.reshape(home, width),
        normed_one.reshape(home, width),
        inverse_one.reshape(home, 1),
        attn_norm,
    )
    grad_tokens = from_sequences((dtokens + dresid).astype(bf16).reshape(seq_n, piece, width)).astype(f32)

    def spread_sum(part):
        if r_n > 1:
            part = (
                part.reshape(dp_n * seq_n, r_n, y_n, core_n * rows_here, -1)
                .transpose(0, 2, 1, 3, 4)
                .reshape(width, -1)
            )
        part = lax.psum_scatter(part.astype(bf16), SPREAD, scatter_dimension=0, tiled=True)
        part = part.reshape(parts, rows_here, -1, 1, columns)
        return chip_exchange(part, 0, 3, parts).reshape(rows_here, -1, width).astype(f32)

    [grad_output] = jnp.moveaxis(spread_sum(out_grad), 1, 0)
    grad_query, grad_key, grad_value = jnp.moveaxis(spread_sum(in_grad), 1, 0)

    gains = jnp.concatenate(
        [attn_norm_grad[:, None], expert_norm_grad[:, None], router_grad], axis=1
    )
    gains = lax.psum_scatter(gains, EVERY, scatter_dimension=0, tiled=True)
    return (
        output,
        grad_tokens,
        gains[:, 0],
        grad_query,
        grad_key,
        grad_value,
        grad_output,
        gains[:, 1],
        gains[:, 2:],
        grad_gate,
        grad_up,
        grad_down,
    )


def solution(mesh):
    dp_n, ctx_n, exp_n = mesh.shape["dp"], mesh.shape["ctx"], mesh.shape["exp"]

    def block(*arrays):
        tokens = arrays[0]
        seq_count = tokens.shape[0] // (dp_n * exp_n)
        seq_n = seq_count * CORES
        sizes = (dp_n, seq_n, ctx_n // seq_n, exp_n // CORES, CORES)
        fine = Mesh(mesh.devices.reshape(sizes), EVERY)
        group = ("dp", "y", "core")
        exp = ("y", "core")
        return jax.shard_map(
            functools.partial(on_device, sizes),
            mesh=fine,
            in_specs=(
                P(group, CTX, None),
                P(group, None),
                P(group, CTX, None),
                P(),
                P(EVERY, None),
                P(EVERY, None),
                P(EVERY, None),
                P(EVERY, None),
                P(),
                P(),
                P(exp, None, "dp"),
                P(exp, None, "dp"),
                P(exp, "dp", None),
                P(group, CTX, None),
            ),
            out_specs=(
                P(group, CTX, None),
                P(group, CTX, None),
                P(EVERY),
                P(EVERY, None),
                P(EVERY, None),
                P(EVERY, None),
                P(EVERY, None),
                P(EVERY),
                P(EVERY, None),
                P(exp, CTX, "dp"),
                P(exp, CTX, "dp"),
                P(exp, "dp", CTX),
            ),
            check_vma=False,
        )(*arrays)

    return block
```

```python
import functools

import jax
import jax.numpy as jnp
from jax import lax
from jax.experimental import pallas as pl
from jax.experimental.pallas import tpu as pltpu
from jax.sharding import Mesh, PartitionSpec as P

HEADS = 16
CORES = 2

epsilon = 1e-05
theta_base = 10000.0
masked_score = -1e30
bf16 = jnp.bfloat16
f32 = jnp.float32

PLANE = ("dp", "y", "core")
CHIP = ("r", "core")
SPREAD = ("dp", "seq", "y")
CTX = ("seq", "r")
EVERY = ("dp", "seq", "r", "y", "core")


def product(a, b):
    return jnp.dot(a, b, preferred_element_type=f32)


def product_t(a, b):
    return lax.dot_general(a, b, (((1,), (1,)), ((), ())), preferred_element_type=f32)


def t_product(a, b):
    return lax.dot_general(a, b, (((0,), (0,)), ((), ())), preferred_element_type=f32)


def swap(a, axis):
    return lax.ppermute(a, axis, [(0, 1), (1, 0)])


def halves(a, axis):
    size = a.shape[axis] // 2
    me = lax.axis_index("core")
    mine = lax.dynamic_slice_in_dim(a, me * size, size, axis)
    other = lax.dynamic_slice_in_dim(a, (1 - me) * size, size, axis)
    return mine, other


def by_core(mine, other, axis):
    first = lax.axis_index("core") == 0
    return jnp.concatenate([jnp.where(first, mine, other), jnp.where(first, other, mine)], axis=axis)


def chip_gather(a, axis, parts):
    if parts == 2:
        return by_core(a, swap(a, "core"), axis)
    return lax.all_gather(a, CHIP, axis=axis, tiled=True)


def chip_scatter(a, axis, parts):
    if parts == 2:
        mine, other = halves(a, axis)
        return mine.astype(f32) + swap(other, "core").astype(f32)
    return lax.psum_scatter(a, CHIP, scatter_dimension=axis, tiled=True).astype(f32)


def chip_exchange(a, split, concat, parts):
    if parts == 2:
        mine, other = halves(a, split)
        return by_core(mine, swap(other, "core"), concat)
    return lax.all_to_all(a, CHIP, split_axis=split, concat_axis=concat, tiled=True)


def core_exchange(a, split, concat):
    mine, other = halves(a, split)
    return by_core(mine, swap(other, "core"), concat)


def to_sequences(a):
    a = core_exchange(a, 1, 0)
    return lax.all_to_all(a, "seq", split_axis=0, concat_axis=0, tiled=True)


def from_sequences(a):
    a = lax.all_to_all(a, "seq", split_axis=0, concat_axis=0, tiled=True)
    return core_exchange(a, 0, 1)


def plane_scatter(blocks):
    got = swap(blocks[:, :, 1], "core")
    held = (blocks[:, :, 0].astype(f32) + got.astype(f32)).astype(bf16)
    half = blocks.shape[3] // 2
    by_x = swap(held[1, 1, :half], "dp")
    by_y = swap(held[1, 1, half:], "y")
    to_x = jnp.concatenate(
        [held[1, 0, :half], (held[1, 0, half:].astype(f32) + by_y.astype(f32)).astype(bf16)], axis=0
    )
    to_y = jnp.concatenate(
        [(held[0, 1, :half].astype(f32) + by_x.astype(f32)).astype(bf16), held[0, 1, half:]], axis=0
    )
    from_x = swap(to_x, "dp")
    from_y = swap(to_y, "y")
    return held[0, 0].astype(f32) + from_x.astype(f32) + from_y.astype(f32)


def visible_block(seg_row, seg_col, start, rows, cols):
    row_place = start + lax.broadcasted_iota(jnp.int32, (rows, cols), 0)
    col_place = lax.broadcasted_iota(jnp.int32, (rows, cols), 1)
    return (seg_col == seg_row) & (col_place <= row_place)


def turned(u, cosine, sine):
    return u * cosine + pltpu.roll(u, u.shape[1] // 2, 1) * sine


def attend_kernel(scale, block, qp, kp, vp, cosine, sine, seg_row, seg_col, q_out, k_out, v_out, mixed):
    length = qp.shape[0]
    q_out[...] = turned(qp[...], cosine[...], sine[...]).astype(bf16)
    k_out[...] = turned(kp[...], cosine[...], sine[...]).astype(bf16)
    v_out[...] = vp[...].astype(bf16)
    for start in range(0, length, block):
        stop = start + block
        scores = product_t(q_out[start:stop, :], k_out[:stop, :]) * scale
        seen = visible_block(seg_row[:, :stop], seg_col[start:stop, :], start, block, stop)
        scores = jnp.where(seen, scores, masked_score)
        top = jnp.max(scores, axis=1, keepdims=True)
        weights = jnp.exp(scores - top)
        total = jnp.sum(weights, axis=1, keepdims=True)
        summed = product(weights.astype(bf16), v_out[:stop, :])
        mixed[start:stop, :] = (summed / total).astype(bf16)


def attend(qkv, cosine, sine, seg_row, seg_col, heads):
    length, head = qkv.shape[0], cosine.shape[1]
    block = min(256, length)

    def column(offset):
        return pl.BlockSpec((length, head), lambda h: (0, offset + h))

    def whole(shape):
        return pl.BlockSpec(shape, lambda h: (0, 0))

    out = jax.ShapeDtypeStruct((length, heads * head), bf16)
    pairs = length * (length + block) // 2 * heads
    return pl.pallas_call(
        functools.partial(attend_kernel, head**-0.5, block),
        grid=(heads,),
        in_specs=[
            column(0),
            column(heads),
            column(2 * heads),
            whole((length, head)),
            whole((length, head)),
            whole((1, length)),
            whole((length, 1)),
        ],
        out_specs=[column(0)] * 4,
        out_shape=[out] * 4,
        compiler_params=pltpu.CompilerParams(vmem_limit_bytes=48 * 2**20),
        cost_estimate=pl.CostEstimate(
            flops=4 * pairs * head, bytes_accessed=20 * length * heads * head, transcendentals=pairs
        ),
        name="attend",
    )(qkv, qkv, qkv, cosine, sine, seg_row, seg_col)


def attend_back_kernel(
    scale, block, q, k, v, mixed, dmixed, cosine, sine, seg_row, seg_col, *rest
):
    dq_out, dk_out, dv_out, dk_sum, dv_sum = rest[-5:]
    length = q.shape[0]
    dk_sum[...] = jnp.zeros_like(dk_sum)
    dv_sum[...] = jnp.zeros_like(dv_sum)
    for start in range(0, length, block):
        stop = start + block
        scores = product_t(q[start:stop, :], k[:stop, :]) * scale
        seen = visible_block(seg_row[:, :stop], seg_col[start:stop, :], start, block, stop)
        scores = jnp.where(seen, scores, masked_score)
        top = jnp.max(scores, axis=1, keepdims=True)
        weights = jnp.exp(scores - top)
        inverse = 1.0 / jnp.sum(weights, axis=1, keepdims=True)
        grad = dmixed[start:stop, :].astype(f32)
        delta = jnp.sum(grad * mixed[start:stop, :].astype(f32), axis=1, keepdims=True) * inverse
        unit = (grad * inverse).astype(bf16)
        dweights = product_t(unit, v[:stop, :])
        dscores = (weights * (dweights - delta)).astype(bf16)
        dq = product(dscores, k[:stop, :]) * scale
        dq_out[start:stop, :] = turned(dq, cosine[start:stop, :], -sine[start:stop, :]).astype(bf16)
        dk_sum[:stop, :] += t_product(dscores, q[start:stop, :])
        dv_sum[:stop, :] += t_product(weights.astype(bf16), unit)
    dk_out[...] = turned(dk_sum[...] * scale, cosine[...], -sine[...]).astype(bf16)
    dv_out[...] = dv_sum[...].astype(bf16)


def attend_back(q, k, v, mixed, dmixed, cosine, sine, seg_row, seg_col, heads, *before):
    length, head = q.shape[0], cosine.shape[1]
    block = min(256, length)
    column = pl.BlockSpec((length, head), lambda h: (0, h))

    def whole(shape):
        return pl.BlockSpec(shape, lambda h: (0, 0))

    out = jax.ShapeDtypeStruct((length, heads * head), bf16)
    pairs = length * (length + block) // 2 * heads
    return pl.pallas_call(
        functools.partial(attend_back_kernel, head**-0.5, block),
        grid=(heads,),
        in_specs=[column] * 5
        + [whole((length, head)), whole((length, head)), whole((1, length)), whole((length, 1))]
        + [pl.BlockSpec(memory_space=pl.ANY)] * len(before),
        out_specs=[column] * 3,
        out_shape=[out] * 3,
        scratch_shapes=[pltpu.VMEM((length, head), f32)] * 2,
        compiler_params=pltpu.CompilerParams(vmem_limit_bytes=48 * 2**20),
        cost_estimate=pl.CostEstimate(
            flops=10 * pairs * head, bytes_accessed=16 * length * heads * head, transcendentals=pairs
        ),
        name="attend_back",
    )(q, k, v, mixed, dmixed, cosine, sine, seg_row, seg_col, *before)


def units_kernel(chunk, x, dy, gate, up, down, units, dgate, dup):
    gate_w, up_w, down_w = gate[...], up[...], down[...]

    def step(i, carry):
        rows = pl.ds(pl.multiple_of(i * chunk, chunk), chunk)
        gpre = product(x[rows, :], gate_w)
        upre = product(x[rows, :], up_w)
        dunits = product_t(dy[rows, :], down_w)
        s = jax.nn.sigmoid(gpre)
        silu = gpre * s
        units[rows, :] = (silu * upre).astype(bf16)
        dgate[rows, :] = (dunits * upre * (s * (1.0 + gpre * (1.0 - s)))).astype(bf16)
        dup[rows, :] = (dunits * silu).astype(bf16)
        return carry

    lax.fori_loop(0, x.shape[0] // chunk, step, 0)


def expert_units(x, dy, gate, up, down):
    rows, width = x.shape
    units = gate.shape[1]
    chunk = max(c for c in range(16, 513, 16) if rows % c == 0)
    tile = 256 if units % 256 == 0 else units
    once = pl.BlockSpec((rows, width), lambda j: (0, 0), pipeline_mode=pl.Buffered(1))
    out = jax.ShapeDtypeStruct((rows, units), bf16)
    return pl.pallas_call(
        functools.partial(units_kernel, chunk),
        grid=(units // tile,),
        in_specs=[
            once,
            once,
            pl.BlockSpec((width, tile), lambda j: (0, j)),
            pl.BlockSpec((width, tile), lambda j: (0, j)),
            pl.BlockSpec((tile, width), lambda j: (j, 0)),
        ],
        out_specs=[pl.BlockSpec((rows, tile), lambda j: (0, j))] * 3,
        out_shape=[out] * 3,
        compiler_params=pltpu.CompilerParams(vmem_limit_bytes=56 * 2**20),
        cost_estimate=pl.CostEstimate(
            flops=6 * rows * width * units,
            bytes_accessed=4 * rows * width + 6 * width * units + 6 * rows * units,
            transcendentals=rows * units,
        ),
        name="expert_units",
    )(x, dy, gate, up, down)


def dispatch_kernel(me, hidden, dout, slot, routes, router, rows, dy_rows, gate):
    size = hidden.shape[1] * hidden.shape[3]
    width = hidden.shape[4]
    mine = me[3]
    tokens = hidden[...].reshape(size, width)
    logits = product(tokens, router[...])
    lanes = lax.broadcasted_iota(jnp.int32, logits.shape, 1)
    first, second = routes[0, :, 0:1], routes[0, :, 1:2]
    one = jnp.sum(jnp.where(lanes == first, logits, 0.0), axis=1, keepdims=True)
    two = jnp.sum(jnp.where(lanes == second, logits, 0.0), axis=1, keepdims=True)
    top = jnp.maximum(one, two)
    one, two = jnp.exp(one - top), jnp.exp(two - top)
    share = jnp.where(first == mine, one, jnp.where(second == mine, two, 0.0)) / (one + two)
    gate[0] = share
    chosen = (
        lax.broadcasted_iota(jnp.int32, (rows.shape[1], size), 0) == slot[0]
    ).astype(bf16)
    rows[0] = product(chosen, tokens).astype(bf16)
    dy = (share * dout[...].reshape(size, width).astype(f32)).astype(bf16)
    dy_rows[0] = product(chosen, dy).astype(bf16)


def plane_block(seq_n, piece, width):
    return pl.BlockSpec((1, 2, 1, piece, width), lambda b, me: (b // seq_n, 0, b % seq_n, 0, 0))


def relative_block(seq_n, piece, width):
    return pl.BlockSpec(
        (1, 1, 2, 1, piece, width),
        lambda b, me: (
            lax.rem(b // (2 * seq_n) + me[0], 2),
            lax.rem(b // seq_n + me[1], 2),
            0,
            b % seq_n,
            0,
            0,
        ),
    )


def dispatch(me, hidden, dout, slot, routes, router, seq_n, piece, cap):
    blocks, size = slot.shape[0], slot.shape[2]
    width = hidden.shape[1]
    seen = (4, 2, seq_n, piece, width)
    each = pl.BlockSpec((1, cap, width), lambda b, me: (b, 0, 0))
    out = jax.ShapeDtypeStruct((blocks, cap, width), bf16)
    spare = jnp.zeros((width, 128 - router.shape[1]), router.dtype)
    return pl.pallas_call(
        dispatch_kernel,
        grid_spec=pltpu.PrefetchScalarGridSpec(
            num_scalar_prefetch=1,
            grid=(blocks,),
            in_specs=[
                plane_block(seq_n, piece, width),
                plane_block(seq_n, piece, width),
                pl.BlockSpec((1, 1, size), lambda b, me: (b, 0, 0)),
                pl.BlockSpec((1, size, routes.shape[2]), lambda b, me: (b, 0, 0)),
                pl.BlockSpec((width, 128), lambda b, me: (0, 0)),
            ],
            out_specs=[each, each, pl.BlockSpec((1, size, 1), lambda b, me: (b, 0, 0))],
        ),
        out_shape=[out, out, jax.ShapeDtypeStruct((blocks, size, 1), f32)],
        compiler_params=pltpu.CompilerParams(vmem_limit_bytes=40 * 2**20),
        cost_estimate=pl.CostEstimate(
            flops=4 * blocks * size * width * (cap + 64),
            bytes_accessed=4 * blocks * (size + cap) * width,
            transcendentals=2 * blocks * size,
        ),
        name="dispatch",
    )(
        me,
        hidden.reshape(seen),
        dout.reshape(seen),
        slot,
        routes,
        jnp.concatenate([router, spare], axis=1),
    )


def spread_rows(slot, rows):
    size, cap = slot.shape[0], rows.shape[0]
    chosen = (lax.broadcasted_iota(jnp.int32, (size, cap), 1) == slot).astype(bf16)
    return product(chosen, rows)


def place_cores(me, out, dense):
    piece = out.shape[4]
    for core in range(2):
        out[0, 0, lax.rem(me[2] + core, 2), 0] = dense[core * piece : (core + 1) * piece, :].astype(bf16)


def combine_kernel(me, rows, slot, gate, dout, out, dgate):
    dense = spread_rows(slot[0], rows[0])
    grads = dout[...].reshape(dense.shape).astype(f32)
    dgate[0] = jnp.sum(grads * dense, axis=1, keepdims=True)
    place_cores(me, out, gate[0] * dense)


def collect_kernel(me, rows, slot, out):
    place_cores(me, out, spread_rows(slot[0], rows[0]))


def combine(me, rows, slot, seq_n, piece, gate=None, dout=None):
    blocks, cap, width = rows.shape
    size = slot.shape[1]
    column = pl.BlockSpec((1, size, 1), lambda b, me: (b, 0, 0))
    weigh = gate is not None
    operands = [rows, slot]
    in_specs = [pl.BlockSpec((1, cap, width), lambda b, me: (b, 0, 0)), column]
    out_specs = [relative_block(seq_n, piece, width)]
    out_shape = [jax.ShapeDtypeStruct((2, 2, 2, seq_n, piece, width), bf16)]
    if weigh:
        operands += [gate, dout.reshape(4, 2, seq_n, piece, width)]
        in_specs += [column, plane_block(seq_n, piece, width)]
        out_specs += [column]
        out_shape += [jax.ShapeDtypeStruct((blocks, size, 1), f32)]
    return pl.pallas_call(
        combine_kernel if weigh else collect_kernel,
        grid_spec=pltpu.PrefetchScalarGridSpec(
            num_scalar_prefetch=1, grid=(blocks,), in_specs=in_specs, out_specs=out_specs
        ),
        out_shape=out_shape,
        compiler_params=pltpu.CompilerParams(vmem_limit_bytes=40 * 2**20),
        cost_estimate=pl.CostEstimate(
            flops=2 * blocks * size * width * cap,
            bytes_accessed=2 * blocks * (2 * size + cap) * width,
            transcendentals=0,
        ),
        name="combine" if weigh else "collect",
    )(me, *operands)


def down_kernel(units, down, *rest):
    rest[-1][...] = product(units[...], down[...]).astype(bf16)


def expert_down(units, down, *before):
    rows, inner = units.shape
    width = down.shape[1]
    m, n = tile_of(rows), tile_of(width)
    return pl.pallas_call(
        down_kernel,
        grid=(width // n, rows // m),
        in_specs=[
            pl.BlockSpec((m, inner), lambda j, i: (i, 0)),
            pl.BlockSpec((inner, n), lambda j, i: (0, j)),
        ]
        + [pl.BlockSpec(memory_space=pl.ANY)] * len(before),
        out_specs=pl.BlockSpec((m, n), lambda j, i: (i, j)),
        out_shape=jax.ShapeDtypeStruct((rows, width), bf16),
        compiler_params=pltpu.CompilerParams(vmem_limit_bytes=48 * 2**20),
        cost_estimate=pl.CostEstimate(
            flops=2 * rows * inner * width,
            bytes_accessed=2 * (rows * inner + inner * width + rows * width),
            transcendentals=0,
        ),
        name="expert_down",
    )(units, down, *before)


def input_kernel(dgate, dup, gate, up, *rest):
    total = product_t(dgate[...], gate[...]) + product_t(dup[...], up[...])
    rest[-1][...] = total.astype(bf16)


def expert_input_grad(dgate, dup, gate, up, *before):
    rows, inner = dgate.shape
    width = gate.shape[0]
    m, n = tile_of(rows), tile_of(width)
    left = pl.BlockSpec((m, inner), lambda j, i: (i, 0))
    right = pl.BlockSpec((n, inner), lambda j, i: (j, 0))
    return pl.pallas_call(
        input_kernel,
        grid=(width // n, rows // m),
        in_specs=[left, left, right, right] + [pl.BlockSpec(memory_space=pl.ANY)] * len(before),
        out_specs=pl.BlockSpec((m, n), lambda j, i: (i, j)),
        out_shape=jax.ShapeDtypeStruct((rows, width), bf16),
        compiler_params=pltpu.CompilerParams(vmem_limit_bytes=52 * 2**20),
        cost_estimate=pl.CostEstimate(
            flops=4 * rows * inner * width,
            bytes_accessed=2 * (2 * rows * inner + 2 * inner * width + rows * width),
            transcendentals=0,
        ),
        name="expert_input_grad",
    )(dgate, dup, gate, up, *before)


def tile_of(size):
    return max(c for c in range(16, 513, 16) if size % c == 0)


def anchor_kernel(*refs):
    pass


def after(a, *before):
    return pl.pallas_call(
        anchor_kernel,
        in_specs=[pl.BlockSpec(memory_space=pl.ANY)] * (1 + len(before)),
        out_specs=pl.BlockSpec(memory_space=pl.ANY),
        out_shape=jax.ShapeDtypeStruct(a.shape, a.dtype),
        input_output_aliases={0: 0},
        cost_estimate=pl.CostEstimate(flops=0, bytes_accessed=0, transcendentals=0),
        name="after",
    )(a, *before)


def norm_backward(grad_rows, normed, inverse, gain):
    weighted = grad_rows * gain
    mean_term = jnp.mean(weighted * normed, axis=-1, keepdims=True)
    return inverse * (weighted - normed * mean_term), jnp.sum(grad_rows * normed, axis=0)


def pick(a, index, axis):
    return lax.dynamic_index_in_dim(a, index, axis, keepdims=False)


def on_device(
    sizes,
    tokens,
    segments,
    routes,
    attn_norm,
    query_weight,
    key_weight,
    value_weight,
    output_weight,
    expert_norm,
    router,
    gate_weight,
    up_weight,
    down_weight,
    grad_out,
):
    dp_n, seq_n, r_n, y_n, core_n = sizes
    parts = r_n * core_n
    seq_count, seq_dev, width = tokens.shape
    piece = seq_dev // core_n
    length = segments.shape[1]
    home = seq_n * piece
    head = width // HEADS
    heads = HEADS // parts
    columns = width // parts
    experts = router.shape[1]
    topk = routes.shape[2]
    plane = 8 * home
    blocks = plane // seq_dev
    cap = 5 * seq_dev * topk // (4 * experts)
    dp_i, seq_i, r_i, y_i, core_i = (lax.axis_index(a) for a in EVERY)
    group, member = seq_i // seq_count, seq_i % seq_count

    own_segments = lax.dynamic_slice_in_dim(segments, (seq_i * r_n + r_i) * seq_dev, seq_dev, 1)
    small = jnp.concatenate(
        [jnp.transpose(routes, (2, 0, 1)), own_segments[None]], axis=0
    ).reshape((topk + 1) * seq_count, seq_dev)
    small = lax.all_gather(small, EVERY, axis=0, tiled=True).reshape(
        dp_n, seq_n, r_n, y_n, core_n, topk + 1, seq_count, seq_dev
    )
    small = pick(pick(small, group, 4), member, 5)
    segment = pick(pick(small, dp_i, 0), y_i, 2)[:, :, topk].reshape(length)
    plane_routes = pick(small, r_i, 2)[:, :, :, :topk].transpose(0, 2, 1, 3, 4)
    block_routes = plane_routes.reshape(blocks, topk, seq_dev)
    home_routes = (
        pick(pick(plane_routes, dp_i, 0), y_i, 0)
        .reshape(seq_n, topk, core_n, piece)
        .transpose(1, 2, 0, 3)
    )
    home_routes = pick(home_routes, core_i, 1).reshape(topk, home)

    local = jnp.concatenate([query_weight, key_weight, value_weight, output_weight], axis=1)
    rows_here = local.shape[0]
    local = local.reshape(rows_here, 4, parts, columns)
    local = chip_exchange(local, 2, 0, parts).reshape(parts, rows_here, 4 * columns)

    def gathered(block):
        whole = lax.all_gather(block.reshape(parts * rows_here, -1), SPREAD, axis=0, tiled=True)
        if r_n > 1:
            whole = (
                whole.reshape(dp_n * seq_n, y_n, r_n, core_n * rows_here, -1)
                .transpose(0, 2, 1, 3, 4)
                .reshape(width, -1)
            )
        return whole

    weights = gathered(local)
    weight_in, weight_out = weights[:, : 3 * columns], weights[:, 3 * columns :]

    token_float = to_sequences(tokens).astype(f32)
    grad_home = to_sequences(grad_out)
    inverse_one = lax.rsqrt(jnp.mean(token_float * token_float, axis=-1, keepdims=True) + epsilon)
    hidden_one = (token_float * inverse_one * attn_norm).astype(bf16)
    hidden_full = chip_gather(hidden_one, 1, parts).reshape(length, width)

    grad_plane = lax.all_gather(grad_home.reshape(home, width), PLANE, axis=0, tiled=True)

    half = head // 2
    frequency = theta_base ** (-jnp.arange(half, dtype=f32) / half)
    angles = jnp.arange(length, dtype=f32)[:, None] * frequency[None, :]
    cosine = jnp.concatenate([jnp.cos(angles)] * 2, axis=1)
    sine = jnp.concatenate([-jnp.sin(angles), jnp.sin(angles)], axis=1)
    seg_row, seg_col = segment[None, :], segment[:, None]

    qkv = product(hidden_full, weight_in)
    query, keys, values, mixed = attend(qkv, cosine, sine, seg_row, seg_col, heads)
    mixed_full = chip_gather(mixed, 1, parts)
    branch = product(mixed_full, weight_out).reshape(seq_n, parts, piece, columns)
    branch = chip_exchange(branch, 1, 3, parts).reshape(seq_n, piece, width)
    residual = token_float + branch
    inverse_two = lax.rsqrt(jnp.mean(residual * residual, axis=-1, keepdims=True) + epsilon)
    normed_two = residual * inverse_two
    hidden_two = (normed_two * expert_norm).astype(bf16).reshape(home, width)

    hidden_plane = lax.all_gather(hidden_two, PLANE, axis=0, tiled=True)
    mine = y_i * core_n + core_i
    chosen = jnp.any(block_routes == mine, axis=1)
    places = jnp.arange(seq_dev)
    rank = product(chosen.astype(bf16), (places[:, None] < places[None, :]).astype(bf16))
    slot = jnp.where(chosen, rank.astype(jnp.int32), -1)
    slot_row, slot_col = slot[:, None, :], slot[:, :, None]
    me = jnp.stack([dp_i, y_i, core_i, mine]).astype(jnp.int32)
    expert_rows, dy_rows, row_gate = dispatch(
        me,
        hidden_plane,
        grad_plane,
        slot_row,
        jnp.transpose(block_routes, (0, 2, 1)),
        router,
        seq_n,
        piece,
        cap,
    )
    expert_in = expert_rows.reshape(blocks * cap, width)
    dy_rows = dy_rows.reshape(blocks * cap, width)

    gate_one, up_one, down_one = gate_weight[0], up_weight[0], down_weight[0]
    units, dgpre, dupre = expert_units(expert_in, dy_rows, gate_one, up_one, down_one)

    def over_ctx(part):
        return lax.psum_scatter(part, CTX, scatter_dimension=0, tiled=True)

    down_part = t_product(dy_rows, units).astype(bf16)
    gate_part = t_product(expert_in, dgpre).astype(bf16)
    up_part = t_product(expert_in, dupre).astype(bf16)
    down_sum, gate_sum, up_sum = over_ctx(down_part), over_ctx(gate_part), over_ctx(up_part)
    grad_down = jnp.transpose(down_sum.astype(f32))[None]
    grad_gate = gate_sum.astype(f32)[None]
    grad_up = up_sum.astype(f32)[None]

    dinput = expert_input_grad(dgpre, dupre, gate_one, up_one, down_part, gate_part, up_part)
    [back] = combine(me, dinput.reshape(blocks, cap, width), slot_col, seq_n, piece)
    ypair = expert_down(units, down_one, dinput)
    mixed_rows, dgate_plane = combine(
        me, ypair.reshape(blocks, cap, width), slot_col, seq_n, piece, row_gate, grad_plane
    )

    dgate_plane = dgate_plane.reshape(dp_n * y_n, seq_n, core_n, piece).transpose(0, 2, 1, 3)
    dgate_home = lax.all_to_all(
        dgate_plane.reshape(8, home), PLANE, split_axis=0, concat_axis=0, tiled=True
    ).reshape(dp_n, experts, home).sum(axis=0)

    mixture = plane_scatter(mixed_rows)
    output = from_sequences((residual + mixture).astype(bf16))

    logits = product(hidden_two, router)
    hot = home_routes[:, :, None] == jnp.arange(experts, dtype=jnp.int32)[None, None, :]
    gates = jax.nn.softmax(jnp.sum(jnp.where(hot, logits[None], 0.0), axis=2), axis=0)
    dgate = jnp.sum(jnp.where(hot, jnp.transpose(dgate_home)[None], 0.0), axis=2)
    dsel = gates * (dgate - jnp.sum(gates * dgate, axis=0, keepdims=True))
    dlogits = jnp.sum(jnp.where(hot, dsel[:, :, None], 0.0), axis=0).astype(bf16)
    router_grad = t_product(hidden_two, dlogits)
    dhidden_two = plane_scatter(back).reshape(home, width) + product_t(dlogits, router)

    flat_two = normed_two.reshape(home, width)
    dresid, expert_norm_grad = norm_backward(
        dhidden_two, flat_two, inverse_two.reshape(home, 1), expert_norm
    )
    dresid = dresid + grad_home.reshape(home, width).astype(f32)
    dbranch = chip_gather(dresid.astype(bf16).reshape(seq_n, piece, width), 1, parts).reshape(length, width)
    column_start = (r_i * core_n + core_i) * columns
    dbranch_here = lax.dynamic_slice_in_dim(dbranch, column_start, columns, 1)
    out_grad = t_product(mixed_full, dbranch_here)
    dmixed = chip_scatter(product_t(dbranch_here, weight_out).astype(bf16), 1, parts).astype(bf16)
    dqpre, dkpre, dvpre = attend_back(
        query, keys, values, mixed, dmixed, cosine, sine, seg_row, seg_col, heads, down_sum
    )
    dqkv = jnp.concatenate([dqpre, dkpre, dvpre], axis=1)
    in_grad = t_product(hidden_full, dqkv)
    dhidden_one = chip_scatter(
        product_t(dqkv, weight_in).astype(bf16).reshape(seq_n, parts * piece, width), 1, parts
    )
    normed_one = token_float * inverse_one
    dtokens, attn_norm_grad = norm_backward(
        dhidden_one.reshape(home, width),
        normed_one.reshape(home, width),
        inverse_one.reshape(home, 1),
        attn_norm,
    )
    grad_tokens = from_sequences((dtokens + dresid).astype(bf16).reshape(seq_n, piece, width)).astype(f32)

    def spread_sum(part):
        part = part.astype(bf16).reshape(dp_n, seq_n, r_n, y_n, core_n * rows_here, -1)
        count = part.shape[-1] // 2

        def half(a, axis, index, name):
            keep, give = pick(a, index, axis), pick(a, 1 - index, axis)
            return (keep.astype(f32) + swap(give, name).astype(f32)).astype(bf16)

        one = half(part[..., :count], 0, dp_i, "dp")
        two = half(part[..., count:], 3, y_i, "y")
        one = half(one, 2, y_i, "y")
        two = half(two, 0, dp_i, "dp")
        part = jnp.concatenate([one, two], axis=-1)
        part = lax.all_to_all(part, "seq", split_axis=0, concat_axis=0, tiled=True)
        part = jnp.sum(part.astype(f32), axis=0).astype(bf16)
        part = part.reshape(parts, rows_here, -1, 1, columns)
        return chip_exchange(part, 0, 3, parts).reshape(rows_here, -1, width).astype(f32)

    [grad_output] = jnp.moveaxis(spread_sum(out_grad), 1, 0)
    grad_query, grad_key, grad_value = jnp.moveaxis(spread_sum(in_grad), 1, 0)

    gains = jnp.concatenate(
        [attn_norm_grad[:, None], expert_norm_grad[:, None], router_grad], axis=1
    )
    gains = lax.psum_scatter(gains, EVERY, scatter_dimension=0, tiled=True)
    return (
        output,
        grad_tokens,
        gains[:, 0],
        grad_query,
        grad_key,
        grad_value,
        grad_output,
        gains[:, 1],
        gains[:, 2:],
        grad_gate,
        grad_up,
        grad_down,
    )


def solution(mesh):
    dp_n, ctx_n, exp_n = mesh.shape["dp"], mesh.shape["ctx"], mesh.shape["exp"]

    def block(*arrays):
        tokens = arrays[0]
        seq_count = tokens.shape[0] // (dp_n * exp_n)
        seq_n = seq_count * CORES
        sizes = (dp_n, seq_n, ctx_n // seq_n, exp_n // CORES, CORES)
        fine = Mesh(mesh.devices.reshape(sizes), EVERY)
        group = ("dp", "y", "core")
        exp = ("y", "core")
        return jax.shard_map(
            functools.partial(on_device, sizes),
            mesh=fine,
            in_specs=(
                P(group, CTX, None),
                P(group, None),
                P(group, CTX, None),
                P(),
                P(EVERY, None),
                P(EVERY, None),
                P(EVERY, None),
                P(EVERY, None),
                P(),
                P(),
                P(exp, None, "dp"),
                P(exp, None, "dp"),
                P(exp, "dp", None),
                P(group, CTX, None),
            ),
            out_specs=(
                P(group, CTX, None),
                P(group, CTX, None),
                P(EVERY),
                P(EVERY, None),
                P(EVERY, None),
                P(EVERY, None),
                P(EVERY, None),
                P(EVERY),
                P(EVERY, None),
                P(exp, CTX, "dp"),
                P(exp, CTX, "dp"),
                P(exp, "dp", CTX),
            ),
            check_vma=False,
        )(*arrays)

    return block
```

```python
import functools

import jax
import jax.numpy as jnp
from jax import lax
from jax.experimental import pallas as pl
from jax.experimental.pallas import tpu as pltpu
from jax.sharding import Mesh, PartitionSpec as P

HEADS = 16
CORES = 2

epsilon = 1e-05
theta_base = 10000.0
masked_score = -1e30
bf16 = jnp.bfloat16
f32 = jnp.float32

PLANE = ("dp", "y", "core")
CHIP = ("r", "core")
SPREAD = ("dp", "seq", "y")
CTX = ("seq", "r")
EVERY = ("dp", "seq", "r", "y", "core")


def product(a, b):
    return jnp.dot(a, b, preferred_element_type=f32)


def product_t(a, b):
    return lax.dot_general(a, b, (((1,), (1,)), ((), ())), preferred_element_type=f32)


def t_product(a, b):
    return lax.dot_general(a, b, (((0,), (0,)), ((), ())), preferred_element_type=f32)


def swap(a, axis):
    return lax.ppermute(a, axis, [(0, 1), (1, 0)])


def halves(a, axis):
    size = a.shape[axis] // 2
    me = lax.axis_index("core")
    mine = lax.dynamic_slice_in_dim(a, me * size, size, axis)
    other = lax.dynamic_slice_in_dim(a, (1 - me) * size, size, axis)
    return mine, other


def by_core(mine, other, axis):
    first = lax.axis_index("core") == 0
    return jnp.concatenate([jnp.where(first, mine, other), jnp.where(first, other, mine)], axis=axis)


def chip_gather(a, axis, parts):
    if parts == 2:
        return by_core(a, swap(a, "core"), axis)
    return lax.all_gather(a, CHIP, axis=axis, tiled=True)


def chip_scatter(a, axis, parts):
    if parts == 2:
        mine, other = halves(a, axis)
        return mine.astype(f32) + swap(other, "core").astype(f32)
    return lax.psum_scatter(a, CHIP, scatter_dimension=axis, tiled=True).astype(f32)


def chip_exchange(a, split, concat, parts):
    if parts == 2:
        mine, other = halves(a, split)
        return by_core(mine, swap(other, "core"), concat)
    return lax.all_to_all(a, CHIP, split_axis=split, concat_axis=concat, tiled=True)


def core_exchange(a, split, concat):
    mine, other = halves(a, split)
    return by_core(mine, swap(other, "core"), concat)


def to_sequences(a):
    a = core_exchange(a, 1, 0)
    return lax.all_to_all(a, "seq", split_axis=0, concat_axis=0, tiled=True)


def from_sequences(a):
    a = lax.all_to_all(a, "seq", split_axis=0, concat_axis=0, tiled=True)
    return core_exchange(a, 0, 1)


def plane_scatter(blocks):
    got = swap(blocks[:, :, 1], "core")
    held = (blocks[:, :, 0].astype(f32) + got.astype(f32)).astype(bf16)
    half = blocks.shape[3] // 2
    by_x = swap(held[1, 1, :half], "dp")
    by_y = swap(held[1, 1, half:], "y")
    to_x = jnp.concatenate(
        [held[1, 0, :half], (held[1, 0, half:].astype(f32) + by_y.astype(f32)).astype(bf16)], axis=0
    )
    to_y = jnp.concatenate(
        [(held[0, 1, :half].astype(f32) + by_x.astype(f32)).astype(bf16), held[0, 1, half:]], axis=0
    )
    from_x = swap(to_x, "dp")
    from_y = swap(to_y, "y")
    return held[0, 0].astype(f32) + from_x.astype(f32) + from_y.astype(f32)


def visible_block(seg_row, seg_col, start, rows, cols):
    row_place = start + lax.broadcasted_iota(jnp.int32, (rows, cols), 0)
    col_place = lax.broadcasted_iota(jnp.int32, (rows, cols), 1)
    return (seg_col == seg_row) & (col_place <= row_place)


def turned(u, cosine, sine):
    return u * cosine + pltpu.roll(u, u.shape[1] // 2, 1) * sine


def attend_kernel(scale, block, qp, kp, vp, cosine, sine, seg_row, seg_col, q_out, k_out, v_out, mixed):
    length = qp.shape[0]
    q_out[...] = turned(qp[...], cosine[...], sine[...]).astype(bf16)
    k_out[...] = turned(kp[...], cosine[...], sine[...]).astype(bf16)
    v_out[...] = vp[...].astype(bf16)
    for start in range(0, length, block):
        stop = start + block
        scores = product_t(q_out[start:stop, :], k_out[:stop, :]) * scale
        seen = visible_block(seg_row[:, :stop], seg_col[start:stop, :], start, block, stop)
        scores = jnp.where(seen, scores, masked_score)
        top = jnp.max(scores, axis=1, keepdims=True)
        weights = jnp.exp(scores - top)
        total = jnp.sum(weights, axis=1, keepdims=True)
        summed = product(weights.astype(bf16), v_out[:stop, :])
        mixed[start:stop, :] = (summed / total).astype(bf16)


def attend(qkv, cosine, sine, seg_row, seg_col, heads):
    length, head = qkv.shape[0], cosine.shape[1]
    block = min(256, length)

    def column(offset):
        return pl.BlockSpec((length, head), lambda h: (0, offset + h))

    def whole(shape):
        return pl.BlockSpec(shape, lambda h: (0, 0))

    out = jax.ShapeDtypeStruct((length, heads * head), bf16)
    pairs = length * (length + block) // 2 * heads
    return pl.pallas_call(
        functools.partial(attend_kernel, head**-0.5, block),
        grid=(heads,),
        in_specs=[
            column(0),
            column(heads),
            column(2 * heads),
            whole((length, head)),
            whole((length, head)),
            whole((1, length)),
            whole((length, 1)),
        ],
        out_specs=[column(0)] * 4,
        out_shape=[out] * 4,
        compiler_params=pltpu.CompilerParams(vmem_limit_bytes=48 * 2**20),
        cost_estimate=pl.CostEstimate(
            flops=4 * pairs * head, bytes_accessed=20 * length * heads * head, transcendentals=pairs
        ),
        name="attend",
    )(qkv, qkv, qkv, cosine, sine, seg_row, seg_col)


def attend_back_kernel(
    scale, block, q, k, v, mixed, dmixed, cosine, sine, seg_row, seg_col, *rest
):
    dq_out, dk_out, dv_out, dk_sum, dv_sum = rest[-5:]
    length = q.shape[0]
    dk_sum[...] = jnp.zeros_like(dk_sum)
    dv_sum[...] = jnp.zeros_like(dv_sum)
    for start in range(0, length, block):
        stop = start + block
        scores = product_t(q[start:stop, :], k[:stop, :]) * scale
        seen = visible_block(seg_row[:, :stop], seg_col[start:stop, :], start, block, stop)
        scores = jnp.where(seen, scores, masked_score)
        top = jnp.max(scores, axis=1, keepdims=True)
        weights = jnp.exp(scores - top)
        inverse = 1.0 / jnp.sum(weights, axis=1, keepdims=True)
        grad = dmixed[start:stop, :].astype(f32)
        delta = jnp.sum(grad * mixed[start:stop, :].astype(f32), axis=1, keepdims=True) * inverse
        unit = (grad * inverse).astype(bf16)
        dweights = product_t(unit, v[:stop, :])
        dscores = (weights * (dweights - delta)).astype(bf16)
        dq = product(dscores, k[:stop, :]) * scale
        dq_out[start:stop, :] = turned(dq, cosine[start:stop, :], -sine[start:stop, :]).astype(bf16)
        dk_sum[:stop, :] += t_product(dscores, q[start:stop, :])
        dv_sum[:stop, :] += t_product(weights.astype(bf16), unit)
    dk_out[...] = turned(dk_sum[...] * scale, cosine[...], -sine[...]).astype(bf16)
    dv_out[...] = dv_sum[...].astype(bf16)


def attend_back(q, k, v, mixed, dmixed, cosine, sine, seg_row, seg_col, heads, *before):
    length, head = q.shape[0], cosine.shape[1]
    block = min(256, length)
    column = pl.BlockSpec((length, head), lambda h: (0, h))

    def whole(shape):
        return pl.BlockSpec(shape, lambda h: (0, 0))

    out = jax.ShapeDtypeStruct((length, heads * head), bf16)
    pairs = length * (length + block) // 2 * heads
    return pl.pallas_call(
        functools.partial(attend_back_kernel, head**-0.5, block),
        grid=(heads,),
        in_specs=[column] * 5
        + [whole((length, head)), whole((length, head)), whole((1, length)), whole((length, 1))]
        + [pl.BlockSpec(memory_space=pl.ANY)] * len(before),
        out_specs=[column] * 3,
        out_shape=[out] * 3,
        scratch_shapes=[pltpu.VMEM((length, head), f32)] * 2,
        compiler_params=pltpu.CompilerParams(vmem_limit_bytes=48 * 2**20),
        cost_estimate=pl.CostEstimate(
            flops=10 * pairs * head, bytes_accessed=16 * length * heads * head, transcendentals=pairs
        ),
        name="attend_back",
    )(q, k, v, mixed, dmixed, cosine, sine, seg_row, seg_col, *before)


def units_kernel(chunk, x, dy, gate, up, down, *rest):
    units, dgate, dup = rest[-3:]
    gate_w, up_w, down_w = gate[...], up[...], down[...]

    def step(i, carry):
        rows = pl.ds(pl.multiple_of(i * chunk, chunk), chunk)
        gpre = product(x[rows, :], gate_w)
        upre = product(x[rows, :], up_w)
        dunits = product_t(dy[rows, :], down_w)
        s = jax.nn.sigmoid(gpre)
        silu = gpre * s
        units[rows, :] = (silu * upre).astype(bf16)
        dgate[rows, :] = (dunits * upre * (s * (1.0 + gpre * (1.0 - s)))).astype(bf16)
        dup[rows, :] = (dunits * silu).astype(bf16)
        return carry

    lax.fori_loop(0, x.shape[0] // chunk, step, 0)


def expert_units(x, dy, gate, up, down, start, stop, *before):
    rows, width = x.shape
    units = stop - start
    chunk = tile_of(rows)
    tile = unit_tile(gate.shape[1])
    first = start // tile
    once = pl.BlockSpec((rows, width), lambda j: (0, 0), pipeline_mode=pl.Buffered(1))
    out = jax.ShapeDtypeStruct((rows, units), bf16)
    return pl.pallas_call(
        functools.partial(units_kernel, chunk),
        grid=(units // tile,),
        in_specs=[
            once,
            once,
            pl.BlockSpec((width, tile), lambda j: (0, first + j)),
            pl.BlockSpec((width, tile), lambda j: (0, first + j)),
            pl.BlockSpec((tile, width), lambda j: (first + j, 0)),
        ]
        + [pl.BlockSpec(memory_space=pl.ANY)] * len(before),
        out_specs=[pl.BlockSpec((rows, tile), lambda j: (0, j))] * 3,
        out_shape=[out] * 3,
        compiler_params=pltpu.CompilerParams(vmem_limit_bytes=56 * 2**20),
        cost_estimate=pl.CostEstimate(
            flops=6 * rows * width * units,
            bytes_accessed=4 * rows * width + 6 * width * units + 6 * rows * units,
            transcendentals=rows * units,
        ),
        name="expert_units",
    )(x, dy, gate, up, down, *before)


def unit_tile(units):
    return 256 if units % 256 == 0 else units


def unit_cut(units):
    tile = unit_tile(units)
    return units // tile // 2 * tile


def dispatch_kernel(me, hidden, dout, slot, routes, router, rows, dy_rows, gate):
    size = hidden.shape[1] * hidden.shape[3]
    width = hidden.shape[4]
    mine = me[3]
    tokens = hidden[...].reshape(size, width)
    logits = product(tokens, router[...])
    lanes = lax.broadcasted_iota(jnp.int32, logits.shape, 1)
    first, second = routes[0, :, 0:1], routes[0, :, 1:2]
    one = jnp.sum(jnp.where(lanes == first, logits, 0.0), axis=1, keepdims=True)
    two = jnp.sum(jnp.where(lanes == second, logits, 0.0), axis=1, keepdims=True)
    top = jnp.maximum(one, two)
    one, two = jnp.exp(one - top), jnp.exp(two - top)
    share = jnp.where(first == mine, one, jnp.where(second == mine, two, 0.0)) / (one + two)
    gate[0] = share
    chosen = (
        lax.broadcasted_iota(jnp.int32, (rows.shape[1], size), 0) == slot[0]
    ).astype(bf16)
    rows[0] = product(chosen, tokens).astype(bf16)
    dy = (share * dout[...].reshape(size, width).astype(f32)).astype(bf16)
    dy_rows[0] = product(chosen, dy).astype(bf16)


def plane_block(seq_n, piece, width):
    return pl.BlockSpec((1, 2, 1, piece, width), lambda b, me: (b // seq_n, 0, b % seq_n, 0, 0))


def relative_block(seq_n, piece, width):
    return pl.BlockSpec(
        (1, 1, 2, 1, piece, width),
        lambda b, me: (
            lax.rem(b // (2 * seq_n) + me[0], 2),
            lax.rem(b // seq_n + me[1], 2),
            0,
            b % seq_n,
            0,
            0,
        ),
    )


def dispatch(me, hidden, dout, slot, routes, router, seq_n, piece, cap):
    blocks, size = slot.shape[0], slot.shape[2]
    width = hidden.shape[1]
    seen = (4, 2, seq_n, piece, width)
    each = pl.BlockSpec((1, cap, width), lambda b, me: (b, 0, 0))
    out = jax.ShapeDtypeStruct((blocks, cap, width), bf16)
    spare = jnp.zeros((width, 128 - router.shape[1]), router.dtype)
    return pl.pallas_call(
        dispatch_kernel,
        grid_spec=pltpu.PrefetchScalarGridSpec(
            num_scalar_prefetch=1,
            grid=(blocks,),
            in_specs=[
                plane_block(seq_n, piece, width),
                plane_block(seq_n, piece, width),
                pl.BlockSpec((1, 1, size), lambda b, me: (b, 0, 0)),
                pl.BlockSpec((1, size, routes.shape[2]), lambda b, me: (b, 0, 0)),
                pl.BlockSpec((width, 128), lambda b, me: (0, 0)),
            ],
            out_specs=[each, each, pl.BlockSpec((1, size, 1), lambda b, me: (b, 0, 0))],
        ),
        out_shape=[out, out, jax.ShapeDtypeStruct((blocks, size, 1), f32)],
        compiler_params=pltpu.CompilerParams(vmem_limit_bytes=40 * 2**20),
        cost_estimate=pl.CostEstimate(
            flops=4 * blocks * size * width * (cap + 64),
            bytes_accessed=4 * blocks * (size + cap) * width,
            transcendentals=2 * blocks * size,
        ),
        name="dispatch",
    )(
        me,
        hidden.reshape(seen),
        dout.reshape(seen),
        slot,
        routes,
        jnp.concatenate([router, spare], axis=1),
    )


def spread_rows(slot, rows):
    size, cap = slot.shape[0], rows.shape[0]
    chosen = (lax.broadcasted_iota(jnp.int32, (size, cap), 1) == slot).astype(bf16)
    return product(chosen, rows)


def place_cores(me, out, dense):
    piece = out.shape[4]
    for core in range(2):
        out[0, 0, lax.rem(me[2] + core, 2), 0] = dense[core * piece : (core + 1) * piece, :].astype(bf16)


def combine_kernel(me, rows, slot, gate, dout, out, dgate):
    dense = spread_rows(slot[0], rows[0])
    grads = dout[...].reshape(dense.shape).astype(f32)
    dgate[0] = jnp.sum(grads * dense, axis=1, keepdims=True)
    place_cores(me, out, gate[0] * dense)


def collect_kernel(me, rows, slot, out):
    place_cores(me, out, spread_rows(slot[0], rows[0]))


def combine(me, rows, slot, seq_n, piece, gate=None, dout=None):
    blocks, cap, width = rows.shape
    size = slot.shape[1]
    column = pl.BlockSpec((1, size, 1), lambda b, me: (b, 0, 0))
    weigh = gate is not None
    operands = [rows, slot]
    in_specs = [pl.BlockSpec((1, cap, width), lambda b, me: (b, 0, 0)), column]
    out_specs = [relative_block(seq_n, piece, width)]
    out_shape = [jax.ShapeDtypeStruct((2, 2, 2, seq_n, piece, width), bf16)]
    if weigh:
        operands += [gate, dout.reshape(4, 2, seq_n, piece, width)]
        in_specs += [column, plane_block(seq_n, piece, width)]
        out_specs += [column]
        out_shape += [jax.ShapeDtypeStruct((blocks, size, 1), f32)]
    return pl.pallas_call(
        combine_kernel if weigh else collect_kernel,
        grid_spec=pltpu.PrefetchScalarGridSpec(
            num_scalar_prefetch=1, grid=(blocks,), in_specs=in_specs, out_specs=out_specs
        ),
        out_shape=out_shape,
        compiler_params=pltpu.CompilerParams(vmem_limit_bytes=40 * 2**20),
        cost_estimate=pl.CostEstimate(
            flops=2 * blocks * size * width * cap,
            bytes_accessed=2 * blocks * (2 * size + cap) * width,
            transcendentals=0,
        ),
        name="combine" if weigh else "collect",
    )(me, *operands)


def down_kernel(cut, units_a, units_b, down, *rest):
    total = product(units_a[...], down[:cut, :]) + product(units_b[...], down[cut:, :])
    rest[-1][...] = total.astype(bf16)


def expert_down(units_a, units_b, down, *before):
    rows, cut = units_a.shape
    inner, width = down.shape
    m, n = tile_of(rows), tile_of(width)
    return pl.pallas_call(
        functools.partial(down_kernel, cut),
        grid=(width // n, rows // m),
        in_specs=[
            pl.BlockSpec((m, cut), lambda j, i: (i, 0)),
            pl.BlockSpec((m, inner - cut), lambda j, i: (i, 0)),
            pl.BlockSpec((inner, n), lambda j, i: (0, j)),
        ]
        + [pl.BlockSpec(memory_space=pl.ANY)] * len(before),
        out_specs=pl.BlockSpec((m, n), lambda j, i: (i, j)),
        out_shape=jax.ShapeDtypeStruct((rows, width), bf16),
        compiler_params=pltpu.CompilerParams(vmem_limit_bytes=48 * 2**20),
        cost_estimate=pl.CostEstimate(
            flops=2 * rows * inner * width,
            bytes_accessed=2 * (rows * inner + inner * width + rows * width),
            transcendentals=0,
        ),
        name="expert_down",
    )(units_a, units_b, down, *before)


def input_kernel(cut, dgate_a, dgate_b, dup_a, dup_b, gate, up, *rest):
    total = product_t(dgate_a[...], gate[:, :cut]) + product_t(dgate_b[...], gate[:, cut:])
    total += product_t(dup_a[...], up[:, :cut]) + product_t(dup_b[...], up[:, cut:])
    rest[-1][...] = total.astype(bf16)


def expert_input_grad(dgate_a, dgate_b, dup_a, dup_b, gate, up, *before):
    rows, cut = dgate_a.shape
    width, inner = gate.shape
    m, n = tile_of(rows), tile_of(width)
    left_a = pl.BlockSpec((m, cut), lambda j, i: (i, 0))
    left_b = pl.BlockSpec((m, inner - cut), lambda j, i: (i, 0))
    right = pl.BlockSpec((n, inner), lambda j, i: (j, 0))
    return pl.pallas_call(
        functools.partial(input_kernel, cut),
        grid=(width // n, rows // m),
        in_specs=[left_a, left_b, left_a, left_b, right, right]
        + [pl.BlockSpec(memory_space=pl.ANY)] * len(before),
        out_specs=pl.BlockSpec((m, n), lambda j, i: (i, j)),
        out_shape=jax.ShapeDtypeStruct((rows, width), bf16),
        compiler_params=pltpu.CompilerParams(vmem_limit_bytes=52 * 2**20),
        cost_estimate=pl.CostEstimate(
            flops=4 * rows * inner * width,
            bytes_accessed=2 * (2 * rows * inner + 2 * inner * width + rows * width),
            transcendentals=0,
        ),
        name="expert_input_grad",
    )(dgate_a, dgate_b, dup_a, dup_b, gate, up, *before)


def tile_of(size):
    return max(c for c in range(16, 513, 16) if size % c == 0)


def anchor_kernel(*refs):
    pass


def after(a, *before):
    return pl.pallas_call(
        anchor_kernel,
        in_specs=[pl.BlockSpec(memory_space=pl.ANY)] * (1 + len(before)),
        out_specs=pl.BlockSpec(memory_space=pl.ANY),
        out_shape=jax.ShapeDtypeStruct(a.shape, a.dtype),
        input_output_aliases={0: 0},
        cost_estimate=pl.CostEstimate(flops=0, bytes_accessed=0, transcendentals=0),
        name="after",
    )(a, *before)


def norm_backward(grad_rows, normed, inverse, gain):
    weighted = grad_rows * gain
    mean_term = jnp.mean(weighted * normed, axis=-1, keepdims=True)
    return inverse * (weighted - normed * mean_term), jnp.sum(grad_rows * normed, axis=0)


def pick(a, index, axis):
    return lax.dynamic_index_in_dim(a, index, axis, keepdims=False)


def on_device(
    sizes,
    tokens,
    segments,
    routes,
    attn_norm,
    query_weight,
    key_weight,
    value_weight,
    output_weight,
    expert_norm,
    router,
    gate_weight,
    up_weight,
    down_weight,
    grad_out,
):
    dp_n, seq_n, r_n, y_n, core_n = sizes
    parts = r_n * core_n
    seq_count, seq_dev, width = tokens.shape
    piece = seq_dev // core_n
    length = segments.shape[1]
    home = seq_n * piece
    head = width // HEADS
    heads = HEADS // parts
    columns = width // parts
    experts = router.shape[1]
    topk = routes.shape[2]
    plane = 8 * home
    blocks = plane // seq_dev
    cap = 5 * seq_dev * topk // (4 * experts)
    dp_i, seq_i, r_i, y_i, core_i = (lax.axis_index(a) for a in EVERY)
    group, member = seq_i // seq_count, seq_i % seq_count

    own_segments = lax.dynamic_slice_in_dim(segments, (seq_i * r_n + r_i) * seq_dev, seq_dev, 1)
    small = jnp.concatenate(
        [jnp.transpose(routes, (2, 0, 1)), own_segments[None]], axis=0
    ).reshape((topk + 1) * seq_count, seq_dev)
    small = lax.all_gather(small, EVERY, axis=0, tiled=True).reshape(
        dp_n, seq_n, r_n, y_n, core_n, topk + 1, seq_count, seq_dev
    )
    small = pick(pick(small, group, 4), member, 5)
    segment = pick(pick(small, dp_i, 0), y_i, 2)[:, :, topk].reshape(length)
    plane_routes = pick(small, r_i, 2)[:, :, :, :topk].transpose(0, 2, 1, 3, 4)
    block_routes = plane_routes.reshape(blocks, topk, seq_dev)
    home_routes = (
        pick(pick(plane_routes, dp_i, 0), y_i, 0)
        .reshape(seq_n, topk, core_n, piece)
        .transpose(1, 2, 0, 3)
    )
    home_routes = pick(home_routes, core_i, 1).reshape(topk, home)

    local = jnp.concatenate([query_weight, key_weight, value_weight, output_weight], axis=1)
    rows_here = local.shape[0]
    local = local.reshape(rows_here, 4, parts, columns)
    local = chip_exchange(local, 2, 0, parts).reshape(parts, rows_here, 4 * columns)

    def gathered(block):
        whole = lax.all_gather(block.reshape(parts * rows_here, -1), SPREAD, axis=0, tiled=True)
        if r_n > 1:
            whole = (
                whole.reshape(dp_n * seq_n, y_n, r_n, core_n * rows_here, -1)
                .transpose(0, 2, 1, 3, 4)
                .reshape(width, -1)
            )
        return whole

    weights = gathered(local)
    weight_in, weight_out = weights[:, : 3 * columns], weights[:, 3 * columns :]

    token_float = to_sequences(tokens).astype(f32)
    grad_home = to_sequences(grad_out)
    inverse_one = lax.rsqrt(jnp.mean(token_float * token_float, axis=-1, keepdims=True) + epsilon)
    hidden_one = (token_float * inverse_one * attn_norm).astype(bf16)
    hidden_full = chip_gather(hidden_one, 1, parts).reshape(length, width)

    grad_plane = lax.all_gather(grad_home.reshape(home, width), PLANE, axis=0, tiled=True)

    half = head // 2
    frequency = theta_base ** (-jnp.arange(half, dtype=f32) / half)
    angles = jnp.arange(length, dtype=f32)[:, None] * frequency[None, :]
    cosine = jnp.concatenate([jnp.cos(angles)] * 2, axis=1)
    sine = jnp.concatenate([-jnp.sin(angles), jnp.sin(angles)], axis=1)
    seg_row, seg_col = segment[None, :], segment[:, None]

    qkv = product(hidden_full, weight_in)
    query, keys, values, mixed = attend(qkv, cosine, sine, seg_row, seg_col, heads)
    mixed_full = chip_gather(mixed, 1, parts)
    branch = product(mixed_full, weight_out).reshape(seq_n, parts, piece, columns)
    branch = chip_exchange(branch, 1, 3, parts).reshape(seq_n, piece, width)
    residual = token_float + branch
    inverse_two = lax.rsqrt(jnp.mean(residual * residual, axis=-1, keepdims=True) + epsilon)
    normed_two = residual * inverse_two
    hidden_two = (normed_two * expert_norm).astype(bf16).reshape(home, width)

    hidden_plane = lax.all_gather(hidden_two, PLANE, axis=0, tiled=True)
    mine = y_i * core_n + core_i
    chosen = jnp.any(block_routes == mine, axis=1)
    places = jnp.arange(seq_dev)
    rank = product(chosen.astype(bf16), (places[:, None] < places[None, :]).astype(bf16))
    slot = jnp.where(chosen, rank.astype(jnp.int32), -1)
    slot_row, slot_col = slot[:, None, :], slot[:, :, None]
    me = jnp.stack([dp_i, y_i, core_i, mine]).astype(jnp.int32)
    expert_rows, dy_rows, row_gate = dispatch(
        me,
        hidden_plane,
        grad_plane,
        slot_row,
        jnp.transpose(block_routes, (0, 2, 1)),
        router,
        seq_n,
        piece,
        cap,
    )
    expert_in = expert_rows.reshape(blocks * cap, width)
    dy_rows = dy_rows.reshape(blocks * cap, width)

    gate_one, up_one, down_one = gate_weight[0], up_weight[0], down_weight[0]
    inner = gate_one.shape[1]
    cut = unit_cut(inner)
    full = (gate_one, up_one, down_one)

    def over_ctx(part):
        return lax.psum_scatter(part, CTX, scatter_dimension=0, tiled=True)

    def rows_product(rows, part):
        return t_product(rows, part).astype(bf16)

    units_a, dgpre_a, dupre_a = expert_units(expert_in, dy_rows, *full, 0, cut)
    down_a = rows_product(dy_rows, units_a)
    units_b, dgpre_b, dupre_b = expert_units(expert_in, dy_rows, *full, cut, inner, down_a)
    down_b = rows_product(dy_rows, units_b)
    dinput = expert_input_grad(dgpre_a, dgpre_b, dupre_a, dupre_b, gate_one, up_one, down_b)
    [back] = combine(me, dinput.reshape(blocks, cap, width), slot_col, seq_n, piece)
    gate_a = rows_product(expert_in, after(dgpre_a, back))
    gate_b = rows_product(expert_in, after(dgpre_b, back))
    ypair = expert_down(units_a, units_b, down_one, gate_a)
    mixed_rows, dgate_plane = combine(
        me, ypair.reshape(blocks, cap, width), slot_col, seq_n, piece, row_gate, grad_plane
    )

    dgate_plane = dgate_plane.reshape(dp_n * y_n, seq_n, core_n, piece).transpose(0, 2, 1, 3)
    dgate_home = lax.all_to_all(
        dgate_plane.reshape(8, home), PLANE, split_axis=0, concat_axis=0, tiled=True
    ).reshape(dp_n, experts, home).sum(axis=0)

    logits = product(hidden_two, router)
    hot = home_routes[:, :, None] == jnp.arange(experts, dtype=jnp.int32)[None, None, :]
    gates = jax.nn.softmax(jnp.sum(jnp.where(hot, logits[None], 0.0), axis=2), axis=0)
    dgate = jnp.sum(jnp.where(hot, jnp.transpose(dgate_home)[None], 0.0), axis=2)
    dsel = gates * (dgate - jnp.sum(gates * dgate, axis=0, keepdims=True))
    dlogits = jnp.sum(jnp.where(hot, dsel[:, :, None], 0.0), axis=0).astype(bf16)
    router_grad = t_product(hidden_two, dlogits)
    dhidden_two = plane_scatter(back).reshape(home, width) + product_t(dlogits, router)

    flat_two = normed_two.reshape(home, width)
    dresid, expert_norm_grad = norm_backward(
        dhidden_two, flat_two, inverse_two.reshape(home, 1), expert_norm
    )
    dresid = dresid + grad_home.reshape(home, width).astype(f32)
    dbranch = chip_gather(dresid.astype(bf16).reshape(seq_n, piece, width), 1, parts).reshape(length, width)
    column_start = (r_i * core_n + core_i) * columns
    dbranch_here = lax.dynamic_slice_in_dim(dbranch, column_start, columns, 1)
    out_grad = t_product(mixed_full, dbranch_here)
    dmixed = chip_scatter(product_t(dbranch_here, weight_out).astype(bf16), 1, parts).astype(bf16)
    dqpre, dkpre, dvpre = attend_back(
        query, keys, values, mixed, dmixed, cosine, sine, seg_row, seg_col, heads, gate_b
    )
    dqkv = jnp.concatenate([dqpre, dkpre, dvpre], axis=1)
    in_grad = t_product(hidden_full, dqkv).astype(bf16)
    up_a = rows_product(expert_in, after(dupre_a, dqpre))
    up_b = rows_product(expert_in, after(dupre_b, dqpre))

    grad_down = jnp.concatenate([over_ctx(down_a), over_ctx(down_b)], axis=1).astype(f32).T[None]
    grad_gate = jnp.concatenate([over_ctx(gate_a), over_ctx(gate_b)], axis=1).astype(f32)[None]
    grad_up = jnp.concatenate([over_ctx(up_a), over_ctx(up_b)], axis=1).astype(f32)[None]

    dhidden_one = chip_scatter(
        product_t(dqkv, weight_in).astype(bf16).reshape(seq_n, parts * piece, width), 1, parts
    )
    normed_one = token_float * inverse_one
    dtokens, attn_norm_grad = norm_backward(
        dhidden_one.reshape(home, width),
        normed_one.reshape(home, width),
        inverse_one.reshape(home, 1),
        attn_norm,
    )
    grad_tokens = from_sequences((dtokens + dresid).astype(bf16).reshape(seq_n, piece, width)).astype(f32)

    mixture = plane_scatter(after(mixed_rows, dqpre))
    output = from_sequences((residual + mixture).astype(bf16))

    gains = jnp.concatenate([attn_norm_grad[:, None], expert_norm_grad[:, None], router_grad], axis=1)
    gain_n = gains.shape[1]
    gains = jnp.pad(gains, ((0, 0), (0, 128 - gain_n))).astype(bf16)

    def seen(part):
        return part.reshape(dp_n, seq_n, r_n, y_n, core_n * rows_here, -1)

    def half(a, axis, index, name):
        keep, give = pick(a, index, axis), pick(a, 1 - index, axis)
        return (keep.astype(f32) + swap(give, name).astype(f32)).astype(bf16)

    one = seen(jnp.concatenate([out_grad.astype(bf16), in_grad[:, :columns]], axis=1))
    two = seen(jnp.concatenate([in_grad[:, columns:], gains], axis=1))
    one = half(half(one, 0, dp_i, "dp"), 2, y_i, "y")
    two = half(half(two, 3, y_i, "y"), 0, dp_i, "dp")
    part = jnp.concatenate([one, two], axis=-1)
    part = lax.all_to_all(part, "seq", split_axis=0, concat_axis=0, tiled=True)
    part = jnp.sum(part.astype(f32), axis=0).astype(bf16)
    part = part.reshape(parts, rows_here, -1)
    gains = chip_scatter(part[:, :, 4 * columns :], 0, parts)[0, :, :gain_n]
    part = part[:, :, : 4 * columns].reshape(parts, rows_here, 4, 1, columns)
    part = chip_exchange(part, 0, 3, parts).reshape(rows_here, 4, width).astype(f32)
    grad_output, grad_query, grad_key, grad_value = (part[:, i] for i in range(4))

    return (
        output,
        grad_tokens,
        gains[:, 0],
        grad_query,
        grad_key,
        grad_value,
        grad_output,
        gains[:, 1],
        gains[:, 2:],
        grad_gate,
        grad_up,
        grad_down,
    )


def solution(mesh):
    dp_n, ctx_n, exp_n = mesh.shape["dp"], mesh.shape["ctx"], mesh.shape["exp"]

    def block(*arrays):
        tokens = arrays[0]
        seq_count = tokens.shape[0] // (dp_n * exp_n)
        seq_n = seq_count * CORES
        sizes = (dp_n, seq_n, ctx_n // seq_n, exp_n // CORES, CORES)
        fine = Mesh(mesh.devices.reshape(sizes), EVERY)
        group = ("dp", "y", "core")
        exp = ("y", "core")
        return jax.shard_map(
            functools.partial(on_device, sizes),
            mesh=fine,
            in_specs=(
                P(group, CTX, None),
                P(group, None),
                P(group, CTX, None),
                P(),
                P(EVERY, None),
                P(EVERY, None),
                P(EVERY, None),
                P(EVERY, None),
                P(),
                P(),
                P(exp, None, "dp"),
                P(exp, None, "dp"),
                P(exp, "dp", None),
                P(group, CTX, None),
            ),
            out_specs=(
                P(group, CTX, None),
                P(group, CTX, None),
                P(EVERY),
                P(EVERY, None),
                P(EVERY, None),
                P(EVERY, None),
                P(EVERY, None),
                P(EVERY),
                P(EVERY, None),
                P(exp, CTX, "dp"),
                P(exp, CTX, "dp"),
                P(exp, "dp", CTX),
            ),
            check_vma=False,
        )(*arrays)

    return block
```

```python
import functools

import jax
import jax.numpy as jnp
from jax import lax
from jax.experimental import pallas as pl
from jax.experimental.pallas import tpu as pltpu
from jax.sharding import Mesh, PartitionSpec as P

HEADS = 16
CORES = 2

epsilon = 1e-05
theta_base = 10000.0
masked_score = -1e30
bf16 = jnp.bfloat16
f32 = jnp.float32

PLANE = ("dp", "y", "core")
CHIP = ("r", "core")
SPREAD = ("dp", "seq", "y")
CTX = ("seq", "r")
EVERY = ("dp", "seq", "r", "y", "core")


def product(a, b):
    return jnp.dot(a, b, preferred_element_type=f32)


def product_t(a, b):
    return lax.dot_general(a, b, (((1,), (1,)), ((), ())), preferred_element_type=f32)


def t_product(a, b):
    return lax.dot_general(a, b, (((0,), (0,)), ((), ())), preferred_element_type=f32)


def swap(a, axis):
    return lax.ppermute(a, axis, [(0, 1), (1, 0)])


def halves(a, axis):
    size = a.shape[axis] // 2
    me = lax.axis_index("core")
    mine = lax.dynamic_slice_in_dim(a, me * size, size, axis)
    other = lax.dynamic_slice_in_dim(a, (1 - me) * size, size, axis)
    return mine, other


def by_core(mine, other, axis):
    first = lax.axis_index("core") == 0
    return jnp.concatenate([jnp.where(first, mine, other), jnp.where(first, other, mine)], axis=axis)


def chip_gather(a, axis, parts):
    if parts == 2:
        return by_core(a, swap(a, "core"), axis)
    return lax.all_gather(a, CHIP, axis=axis, tiled=True)


def chip_scatter(a, axis, parts):
    if parts == 2:
        mine, other = halves(a, axis)
        return mine.astype(f32) + swap(other, "core").astype(f32)
    return lax.psum_scatter(a, CHIP, scatter_dimension=axis, tiled=True).astype(f32)


def chip_exchange(a, split, concat, parts):
    if parts == 2:
        mine, other = halves(a, split)
        return by_core(mine, swap(other, "core"), concat)
    return lax.all_to_all(a, CHIP, split_axis=split, concat_axis=concat, tiled=True)


def core_exchange(a, split, concat):
    mine, other = halves(a, split)
    return by_core(mine, swap(other, "core"), concat)


def seq_pieces(a):
    count = a.shape[0]
    me = lax.axis_index("seq")
    pieces = [pick(a, me, 0)]
    for step in range(1, count):
        give = pick(a, lax.rem(me + step, count), 0)
        pieces.append(lax.ppermute(give, "seq", [(i, (i + step) % count) for i in range(count)]))
    return pieces


def seq_exchange(a):
    count = a.shape[0]
    me = lax.axis_index("seq")
    pieces = jnp.stack(seq_pieces(a))
    return jnp.stack([pick(pieces, lax.rem(me + count - s, count), 0) for s in range(count)])


def to_sequences(a):
    return seq_exchange(core_exchange(a, 1, 0))


def from_sequences(a):
    return core_exchange(seq_exchange(a), 0, 1)


def plane_scatter(blocks):
    got = swap(blocks[:, :, 1], "core")
    held = (blocks[:, :, 0].astype(f32) + got.astype(f32)).astype(bf16)
    half = blocks.shape[3] // 2
    by_x = swap(held[1, 1, :half], "dp")
    by_y = swap(held[1, 1, half:], "y")
    to_x = jnp.concatenate(
        [held[1, 0, :half], (held[1, 0, half:].astype(f32) + by_y.astype(f32)).astype(bf16)], axis=0
    )
    to_y = jnp.concatenate(
        [(held[0, 1, :half].astype(f32) + by_x.astype(f32)).astype(bf16), held[0, 1, half:]], axis=0
    )
    from_x = swap(to_x, "dp")
    from_y = swap(to_y, "y")
    return held[0, 0].astype(f32) + from_x.astype(f32) + from_y.astype(f32)


def visible_block(seg_row, seg_col, start, rows, cols):
    row_place = start + lax.broadcasted_iota(jnp.int32, (rows, cols), 0)
    col_place = lax.broadcasted_iota(jnp.int32, (rows, cols), 1)
    return (seg_col == seg_row) & (col_place <= row_place)


def turned(u, cosine, sine):
    return u * cosine + pltpu.roll(u, u.shape[1] // 2, 1) * sine


def attend_kernel(scale, block, qp, kp, vp, cosine, sine, seg_row, seg_col, q_out, k_out, v_out, mixed):
    length = qp.shape[0]
    q_out[...] = turned(qp[...], cosine[...], sine[...]).astype(bf16)
    k_out[...] = turned(kp[...], cosine[...], sine[...]).astype(bf16)
    v_out[...] = vp[...].astype(bf16)
    for start in range(0, length, block):
        stop = start + block
        scores = product_t(q_out[start:stop, :], k_out[:stop, :]) * scale
        seen = visible_block(seg_row[:, :stop], seg_col[start:stop, :], start, block, stop)
        scores = jnp.where(seen, scores, masked_score)
        top = jnp.max(scores, axis=1, keepdims=True)
        weights = jnp.exp(scores - top)
        total = jnp.sum(weights, axis=1, keepdims=True)
        summed = product(weights.astype(bf16), v_out[:stop, :])
        mixed[start:stop, :] = (summed / total).astype(bf16)


def attend(qkv, cosine, sine, seg_row, seg_col, heads):
    length, head = qkv.shape[0], cosine.shape[1]
    block = min(256, length)

    def column(offset):
        return pl.BlockSpec((length, head), lambda h: (0, offset + h))

    def whole(shape):
        return pl.BlockSpec(shape, lambda h: (0, 0))

    out = jax.ShapeDtypeStruct((length, heads * head), bf16)
    pairs = length * (length + block) // 2 * heads
    return pl.pallas_call(
        functools.partial(attend_kernel, head**-0.5, block),
        grid=(heads,),
        in_specs=[
            column(0),
            column(heads),
            column(2 * heads),
            whole((length, head)),
            whole((length, head)),
            whole((1, length)),
            whole((length, 1)),
        ],
        out_specs=[column(0)] * 4,
        out_shape=[out] * 4,
        compiler_params=pltpu.CompilerParams(vmem_limit_bytes=48 * 2**20),
        cost_estimate=pl.CostEstimate(
            flops=4 * pairs * head, bytes_accessed=20 * length * heads * head, transcendentals=pairs
        ),
        name="attend",
    )(qkv, qkv, qkv, cosine, sine, seg_row, seg_col)


def attend_back_kernel(
    scale, block, q, k, v, mixed, dmixed, cosine, sine, seg_row, seg_col, *rest
):
    dq_out, dk_out, dv_out, dk_sum, dv_sum = rest[-5:]
    length = q.shape[0]
    dk_sum[...] = jnp.zeros_like(dk_sum)
    dv_sum[...] = jnp.zeros_like(dv_sum)
    for start in range(0, length, block):
        stop = start + block
        scores = product_t(q[start:stop, :], k[:stop, :]) * scale
        seen = visible_block(seg_row[:, :stop], seg_col[start:stop, :], start, block, stop)
        scores = jnp.where(seen, scores, masked_score)
        top = jnp.max(scores, axis=1, keepdims=True)
        weights = jnp.exp(scores - top)
        inverse = 1.0 / jnp.sum(weights, axis=1, keepdims=True)
        grad = dmixed[start:stop, :].astype(f32)
        delta = jnp.sum(grad * mixed[start:stop, :].astype(f32), axis=1, keepdims=True) * inverse
        unit = (grad * inverse).astype(bf16)
        dweights = product_t(unit, v[:stop, :])
        dscores = (weights * (dweights - delta)).astype(bf16)
        dq = product(dscores, k[:stop, :]) * scale
        dq_out[start:stop, :] = turned(dq, cosine[start:stop, :], -sine[start:stop, :]).astype(bf16)
        dk_sum[:stop, :] += t_product(dscores, q[start:stop, :])
        dv_sum[:stop, :] += t_product(weights.astype(bf16), unit)
    dk_out[...] = turned(dk_sum[...] * scale, cosine[...], -sine[...]).astype(bf16)
    dv_out[...] = dv_sum[...].astype(bf16)


def attend_back(q, k, v, mixed, dmixed, cosine, sine, seg_row, seg_col, heads, *before):
    length, head = q.shape[0], cosine.shape[1]
    block = min(256, length)
    column = pl.BlockSpec((length, head), lambda h: (0, h))

    def whole(shape):
        return pl.BlockSpec(shape, lambda h: (0, 0))

    out = jax.ShapeDtypeStruct((length, heads * head), bf16)
    pairs = length * (length + block) // 2 * heads
    return pl.pallas_call(
        functools.partial(attend_back_kernel, head**-0.5, block),
        grid=(heads,),
        in_specs=[column] * 5
        + [whole((length, head)), whole((length, head)), whole((1, length)), whole((length, 1))]
        + [pl.BlockSpec(memory_space=pl.ANY)] * len(before),
        out_specs=[column] * 3,
        out_shape=[out] * 3,
        scratch_shapes=[pltpu.VMEM((length, head), f32)] * 2,
        compiler_params=pltpu.CompilerParams(vmem_limit_bytes=48 * 2**20),
        cost_estimate=pl.CostEstimate(
            flops=10 * pairs * head, bytes_accessed=16 * length * heads * head, transcendentals=pairs
        ),
        name="attend_back",
    )(q, k, v, mixed, dmixed, cosine, sine, seg_row, seg_col, *before)


def units_kernel(chunk, x, dy, gate, up, down, *rest):
    units, dgate, dup = rest[-3:]
    gate_w, up_w, down_w = gate[...], up[...], down[...]

    def step(i, carry):
        rows = pl.ds(pl.multiple_of(i * chunk, chunk), chunk)
        gpre = product(x[rows, :], gate_w)
        upre = product(x[rows, :], up_w)
        dunits = product_t(dy[rows, :], down_w)
        s = jax.nn.sigmoid(gpre)
        silu = gpre * s
        units[rows, :] = (silu * upre).astype(bf16)
        dgate[rows, :] = (dunits * upre * (s * (1.0 + gpre * (1.0 - s)))).astype(bf16)
        dup[rows, :] = (dunits * silu).astype(bf16)
        return carry

    lax.fori_loop(0, x.shape[0] // chunk, step, 0)


def expert_units(x, dy, gate, up, down, start, stop, *before):
    rows, width = x.shape
    units = stop - start
    chunk = tile_of(rows)
    tile = unit_tile(gate.shape[1])
    first = start // tile
    once = pl.BlockSpec((rows, width), lambda j: (0, 0), pipeline_mode=pl.Buffered(1))
    out = jax.ShapeDtypeStruct((rows, units), bf16)
    return pl.pallas_call(
        functools.partial(units_kernel, chunk),
        grid=(units // tile,),
        in_specs=[
            once,
            once,
            pl.BlockSpec((width, tile), lambda j: (0, first + j)),
            pl.BlockSpec((width, tile), lambda j: (0, first + j)),
            pl.BlockSpec((tile, width), lambda j: (first + j, 0)),
        ]
        + [pl.BlockSpec(memory_space=pl.ANY)] * len(before),
        out_specs=[pl.BlockSpec((rows, tile), lambda j: (0, j))] * 3,
        out_shape=[out] * 3,
        compiler_params=pltpu.CompilerParams(vmem_limit_bytes=56 * 2**20),
        cost_estimate=pl.CostEstimate(
            flops=6 * rows * width * units,
            bytes_accessed=4 * rows * width + 6 * width * units + 6 * rows * units,
            transcendentals=rows * units,
        ),
        name="expert_units",
    )(x, dy, gate, up, down, *before)


def unit_tile(units):
    return 256 if units % 256 == 0 else units


def unit_cut(units):
    tile = unit_tile(units)
    return units // tile * 3 // 4 * tile


def dispatch_kernel(me, hidden, dout, slot, routes, router, rows, dy_rows, gate):
    size = hidden.shape[1] * hidden.shape[3]
    width = hidden.shape[4]
    mine = me[3]
    tokens = hidden[...].reshape(size, width)
    logits = product(tokens, router[...])
    lanes = lax.broadcasted_iota(jnp.int32, logits.shape, 1)
    first, second = routes[0, :, 0:1], routes[0, :, 1:2]
    one = jnp.sum(jnp.where(lanes == first, logits, 0.0), axis=1, keepdims=True)
    two = jnp.sum(jnp.where(lanes == second, logits, 0.0), axis=1, keepdims=True)
    top = jnp.maximum(one, two)
    one, two = jnp.exp(one - top), jnp.exp(two - top)
    share = jnp.where(first == mine, one, jnp.where(second == mine, two, 0.0)) / (one + two)
    gate[0] = share
    chosen = (
        lax.broadcasted_iota(jnp.int32, (rows.shape[1], size), 0) == slot[0]
    ).astype(bf16)
    rows[0] = product(chosen, tokens).astype(bf16)
    dy = (share * dout[...].reshape(size, width).astype(f32)).astype(bf16)
    dy_rows[0] = product(chosen, dy).astype(bf16)


def plane_block(seq_n, piece, width):
    return pl.BlockSpec((1, 2, 1, piece, width), lambda b, me: (b // seq_n, 0, b % seq_n, 0, 0))


def relative_block(seq_n, piece, width):
    return pl.BlockSpec(
        (1, 1, 2, 1, piece, width),
        lambda b, me: (
            lax.rem(b // (2 * seq_n) + me[0], 2),
            lax.rem(b // seq_n + me[1], 2),
            0,
            b % seq_n,
            0,
            0,
        ),
    )


def dispatch(me, hidden, dout, slot, routes, router, seq_n, piece, cap):
    blocks, size = slot.shape[0], slot.shape[2]
    width = hidden.shape[1]
    seen = (4, 2, seq_n, piece, width)
    each = pl.BlockSpec((1, cap, width), lambda b, me: (b, 0, 0))
    out = jax.ShapeDtypeStruct((blocks, cap, width), bf16)
    spare = jnp.zeros((width, 128 - router.shape[1]), router.dtype)
    return pl.pallas_call(
        dispatch_kernel,
        grid_spec=pltpu.PrefetchScalarGridSpec(
            num_scalar_prefetch=1,
            grid=(blocks,),
            in_specs=[
                plane_block(seq_n, piece, width),
                plane_block(seq_n, piece, width),
                pl.BlockSpec((1, 1, size), lambda b, me: (b, 0, 0)),
                pl.BlockSpec((1, size, routes.shape[2]), lambda b, me: (b, 0, 0)),
                pl.BlockSpec((width, 128), lambda b, me: (0, 0)),
            ],
            out_specs=[each, each, pl.BlockSpec((1, size, 1), lambda b, me: (b, 0, 0))],
        ),
        out_shape=[out, out, jax.ShapeDtypeStruct((blocks, size, 1), f32)],
        compiler_params=pltpu.CompilerParams(vmem_limit_bytes=40 * 2**20),
        cost_estimate=pl.CostEstimate(
            flops=4 * blocks * size * width * (cap + 64),
            bytes_accessed=4 * blocks * (size + cap) * width,
            transcendentals=2 * blocks * size,
        ),
        name="dispatch",
    )(
        me,
        hidden.reshape(seen),
        dout.reshape(seen),
        slot,
        routes,
        jnp.concatenate([router, spare], axis=1),
    )


def spread_rows(slot, rows):
    size, cap = slot.shape[0], rows.shape[0]
    chosen = (lax.broadcasted_iota(jnp.int32, (size, cap), 1) == slot).astype(bf16)
    return product(chosen, rows)


def place_cores(me, out, dense):
    piece = out.shape[4]
    for core in range(2):
        out[0, 0, lax.rem(me[2] + core, 2), 0] = dense[core * piece : (core + 1) * piece, :].astype(bf16)


def combine_kernel(me, rows, slot, gate, dout, out, dgate):
    dense = spread_rows(slot[0], rows[0])
    grads = dout[...].reshape(dense.shape).astype(f32)
    dgate[0] = jnp.sum(grads * dense, axis=1, keepdims=True)
    place_cores(me, out, gate[0] * dense)


def collect_kernel(me, left, slot, right, *rest):
    dense = [spread_rows(slot[0], left[0]), spread_rows(slot[0], right[0])]
    place_cores(me, rest[-1], jnp.concatenate(dense, axis=1))


def combine(me, rows, slot, seq_n, piece, gate=None, dout=None, right=None):
    blocks, cap, part = rows.shape
    size = slot.shape[1]
    width = part if right is None else 2 * part
    column = pl.BlockSpec((1, size, 1), lambda b, me: (b, 0, 0))
    weigh = gate is not None
    operands = [rows, slot]
    in_specs = [pl.BlockSpec((1, cap, part), lambda b, me: (b, 0, 0)), column]
    out_specs = [relative_block(seq_n, piece, width)]
    out_shape = [jax.ShapeDtypeStruct((2, 2, 2, seq_n, piece, width), bf16)]
    if weigh:
        operands += [gate, dout.reshape(4, 2, seq_n, piece, width)]
        in_specs += [column, plane_block(seq_n, piece, width)]
        out_specs += [column]
        out_shape += [jax.ShapeDtypeStruct((blocks, size, 1), f32)]
    else:
        operands += [right]
        in_specs += in_specs[:1]
    return pl.pallas_call(
        combine_kernel if weigh else collect_kernel,
        grid_spec=pltpu.PrefetchScalarGridSpec(
            num_scalar_prefetch=1, grid=(blocks,), in_specs=in_specs, out_specs=out_specs
        ),
        out_shape=out_shape,
        compiler_params=pltpu.CompilerParams(vmem_limit_bytes=40 * 2**20),
        cost_estimate=pl.CostEstimate(
            flops=2 * blocks * size * width * cap,
            bytes_accessed=2 * blocks * (2 * size + cap) * width,
            transcendentals=0,
        ),
        name="combine" if weigh else "collect",
    )(me, *operands)


def down_kernel(cut, units_a, units_b, down, *rest):
    total = product(units_a[...], down[:cut, :]) + product(units_b[...], down[cut:, :])
    rest[-1][...] = total.astype(bf16)


def expert_down(units_a, units_b, down, *before):
    rows, cut = units_a.shape
    inner, width = down.shape
    m, n = tile_of(rows), tile_of(width)
    return pl.pallas_call(
        functools.partial(down_kernel, cut),
        grid=(width // n, rows // m),
        in_specs=[
            pl.BlockSpec((m, cut), lambda j, i: (i, 0)),
            pl.BlockSpec((m, inner - cut), lambda j, i: (i, 0)),
            pl.BlockSpec((inner, n), lambda j, i: (0, j)),
        ]
        + [pl.BlockSpec(memory_space=pl.ANY)] * len(before),
        out_specs=pl.BlockSpec((m, n), lambda j, i: (i, j)),
        out_shape=jax.ShapeDtypeStruct((rows, width), bf16),
        compiler_params=pltpu.CompilerParams(vmem_limit_bytes=48 * 2**20),
        cost_estimate=pl.CostEstimate(
            flops=2 * rows * inner * width,
            bytes_accessed=2 * (rows * inner + inner * width + rows * width),
            transcendentals=0,
        ),
        name="expert_down",
    )(units_a, units_b, down, *before)


def input_kernel(cut, dgate_a, dgate_b, dup_a, dup_b, gate, up, *rest):
    total = product_t(dgate_a[...], gate[:, :cut]) + product_t(dgate_b[...], gate[:, cut:])
    total += product_t(dup_a[...], up[:, :cut]) + product_t(dup_b[...], up[:, cut:])
    rest[-1][...] = total.astype(bf16)


def expert_input_grad(dgate_a, dgate_b, dup_a, dup_b, gate, up, start, stop, *before):
    rows, cut = dgate_a.shape
    inner = gate.shape[1]
    width = stop - start
    m, n = tile_of(rows), tile_of(width)
    first = start // n
    left_a = pl.BlockSpec((m, cut), lambda j, i: (i, 0))
    left_b = pl.BlockSpec((m, inner - cut), lambda j, i: (i, 0))
    right = pl.BlockSpec((n, inner), lambda j, i: (first + j, 0))
    return pl.pallas_call(
        functools.partial(input_kernel, cut),
        grid=(width // n, rows // m),
        in_specs=[left_a, left_b, left_a, left_b, right, right]
        + [pl.BlockSpec(memory_space=pl.ANY)] * len(before),
        out_specs=pl.BlockSpec((m, n), lambda j, i: (i, j)),
        out_shape=jax.ShapeDtypeStruct((rows, width), bf16),
        compiler_params=pltpu.CompilerParams(vmem_limit_bytes=52 * 2**20),
        cost_estimate=pl.CostEstimate(
            flops=4 * rows * inner * width,
            bytes_accessed=2 * (2 * rows * inner + 2 * inner * width + rows * width),
            transcendentals=0,
        ),
        name="expert_input_grad",
    )(dgate_a, dgate_b, dup_a, dup_b, gate, up, *before)


def tile_of(size):
    return max(c for c in range(16, 513, 16) if size % c == 0)


def anchor_kernel(*refs):
    pass


def after(a, *before):
    return pl.pallas_call(
        anchor_kernel,
        in_specs=[pl.BlockSpec(memory_space=pl.ANY)] * (1 + len(before)),
        out_specs=pl.BlockSpec(memory_space=pl.ANY),
        out_shape=jax.ShapeDtypeStruct(a.shape, a.dtype),
        input_output_aliases={0: 0},
        cost_estimate=pl.CostEstimate(flops=0, bytes_accessed=0, transcendentals=0),
        name="after",
    )(a, *before)


def norm_backward(grad_rows, normed, inverse, gain):
    weighted = grad_rows * gain
    mean_term = jnp.mean(weighted * normed, axis=-1, keepdims=True)
    return inverse * (weighted - normed * mean_term), jnp.sum(grad_rows * normed, axis=0)


def pick(a, index, axis):
    return lax.dynamic_index_in_dim(a, index, axis, keepdims=False)


def on_device(
    sizes,
    tokens,
    segments,
    routes,
    attn_norm,
    query_weight,
    key_weight,
    value_weight,
    output_weight,
    expert_norm,
    router,
    gate_weight,
    up_weight,
    down_weight,
    grad_out,
):
    dp_n, seq_n, r_n, y_n, core_n = sizes
    parts = r_n * core_n
    seq_count, seq_dev, width = tokens.shape
    piece = seq_dev // core_n
    length = segments.shape[1]
    home = seq_n * piece
    head = width // HEADS
    heads = HEADS // parts
    columns = width // parts
    experts = router.shape[1]
    topk = routes.shape[2]
    plane = 8 * home
    blocks = plane // seq_dev
    cap = 5 * seq_dev * topk // (4 * experts)
    dp_i, seq_i, r_i, y_i, core_i = (lax.axis_index(a) for a in EVERY)
    group, member = seq_i // seq_count, seq_i % seq_count

    own_segments = lax.dynamic_slice_in_dim(segments, (seq_i * r_n + r_i) * seq_dev, seq_dev, 1)
    small = jnp.concatenate(
        [jnp.transpose(routes, (2, 0, 1)), own_segments[None]], axis=0
    ).reshape((topk + 1) * seq_count, seq_dev)
    small = lax.all_gather(small, EVERY, axis=0, tiled=True).reshape(
        dp_n, seq_n, r_n, y_n, core_n, topk + 1, seq_count, seq_dev
    )
    small = pick(pick(small, group, 4), member, 5)
    segment = pick(pick(small, dp_i, 0), y_i, 2)[:, :, topk].reshape(length)
    plane_routes = pick(small, r_i, 2)[:, :, :, :topk].transpose(0, 2, 1, 3, 4)
    block_routes = plane_routes.reshape(blocks, topk, seq_dev)
    home_routes = (
        pick(pick(plane_routes, dp_i, 0), y_i, 0)
        .reshape(seq_n, topk, core_n, piece)
        .transpose(1, 2, 0, 3)
    )
    home_routes = pick(home_routes, core_i, 1).reshape(topk, home)

    local = jnp.concatenate([query_weight, key_weight, value_weight, output_weight], axis=1)
    rows_here = local.shape[0]
    local = local.reshape(rows_here, 4, parts, columns)
    local = chip_exchange(local, 2, 0, parts).reshape(parts, rows_here, 4 * columns)

    def gathered(block):
        whole = lax.all_gather(block.reshape(parts * rows_here, -1), SPREAD, axis=0, tiled=True)
        if r_n > 1:
            whole = (
                whole.reshape(dp_n * seq_n, y_n, r_n, core_n * rows_here, -1)
                .transpose(0, 2, 1, 3, 4)
                .reshape(width, -1)
            )
        return whole

    weights = gathered(local)
    weight_in, weight_out = weights[:, : 3 * columns], weights[:, 3 * columns :]

    token_float = to_sequences(tokens).astype(f32)
    grad_home = to_sequences(grad_out)
    inverse_one = lax.rsqrt(jnp.mean(token_float * token_float, axis=-1, keepdims=True) + epsilon)
    hidden_one = (token_float * inverse_one * attn_norm).astype(bf16)
    hidden_full = chip_gather(hidden_one, 1, parts).reshape(length, width)

    grad_plane = lax.all_gather(grad_home.reshape(home, width), PLANE, axis=0, tiled=True)

    half = head // 2
    frequency = theta_base ** (-jnp.arange(half, dtype=f32) / half)
    angles = jnp.arange(length, dtype=f32)[:, None] * frequency[None, :]
    cosine = jnp.concatenate([jnp.cos(angles)] * 2, axis=1)
    sine = jnp.concatenate([-jnp.sin(angles), jnp.sin(angles)], axis=1)
    seg_row, seg_col = segment[None, :], segment[:, None]

    qkv = product(hidden_full, weight_in)
    query, keys, values, mixed = attend(qkv, cosine, sine, seg_row, seg_col, heads)
    mixed_full = chip_gather(mixed, 1, parts)
    branch = product(mixed_full, weight_out).reshape(seq_n, parts, piece, columns)
    branch = chip_exchange(branch, 1, 3, parts).reshape(seq_n, piece, width)
    residual = token_float + branch
    inverse_two = lax.rsqrt(jnp.mean(residual * residual, axis=-1, keepdims=True) + epsilon)
    normed_two = residual * inverse_two
    hidden_two = (normed_two * expert_norm).astype(bf16).reshape(home, width)

    hidden_plane = lax.all_gather(hidden_two, PLANE, axis=0, tiled=True)
    mine = y_i * core_n + core_i
    chosen = jnp.any(block_routes == mine, axis=1)
    places = jnp.arange(seq_dev)
    rank = product(chosen.astype(bf16), (places[:, None] < places[None, :]).astype(bf16))
    slot = jnp.where(chosen, rank.astype(jnp.int32), -1)
    slot_row, slot_col = slot[:, None, :], slot[:, :, None]
    me = jnp.stack([dp_i, y_i, core_i, mine]).astype(jnp.int32)
    expert_rows, dy_rows, row_gate = dispatch(
        me,
        hidden_plane,
        grad_plane,
        slot_row,
        jnp.transpose(block_routes, (0, 2, 1)),
        router,
        seq_n,
        piece,
        cap,
    )
    expert_in = expert_rows.reshape(blocks * cap, width)
    dy_rows = dy_rows.reshape(blocks * cap, width)

    gate_one, up_one, down_one = gate_weight[0], up_weight[0], down_weight[0]
    inner = gate_one.shape[1]
    cut = unit_cut(inner)
    full = (gate_one, up_one, down_one)

    def over_ctx(part):
        return lax.psum_scatter(part, CTX, scatter_dimension=0, tiled=True)

    def rows_product(rows, part):
        return t_product(rows, part).astype(bf16)

    units_a, dgpre_a, dupre_a = expert_units(expert_in, dy_rows, *full, 0, cut)
    down_a = rows_product(dy_rows, units_a)
    units_b, dgpre_b, dupre_b = expert_units(expert_in, dy_rows, *full, cut, inner, down_a)
    down_b = rows_product(dy_rows, units_b)
    down_sum_a, down_sum_b = over_ctx(down_a), over_ctx(down_b)
    grads = (dgpre_a, dgpre_b, dupre_a, dupre_b, gate_one, up_one)
    left = expert_input_grad(*grads, 0, width // 2, down_b)
    right = expert_input_grad(*grads, width // 2, width, left)
    left, right = (part.reshape(blocks, cap, width // 2) for part in (left, right))
    [back] = combine(me, left, slot_col, seq_n, piece, right=right)
    gate_a = rows_product(expert_in, after(dgpre_a, back, down_sum_a))
    gate_b = rows_product(expert_in, after(dgpre_b, back))
    ypair = expert_down(units_a, units_b, down_one, gate_a)
    mixed_rows, dgate_plane = combine(
        me, ypair.reshape(blocks, cap, width), slot_col, seq_n, piece, row_gate, grad_plane
    )

    dgate_plane = dgate_plane.reshape(dp_n * y_n, seq_n, core_n, piece).transpose(0, 2, 1, 3)
    dgate_home = lax.all_to_all(
        dgate_plane.reshape(8, home), PLANE, split_axis=0, concat_axis=0, tiled=True
    ).reshape(dp_n, experts, home).sum(axis=0)

    logits = product(hidden_two, router)
    hot = home_routes[:, :, None] == jnp.arange(experts, dtype=jnp.int32)[None, None, :]
    gates = jax.nn.softmax(jnp.sum(jnp.where(hot, logits[None], 0.0), axis=2), axis=0)
    dgate = jnp.sum(jnp.where(hot, jnp.transpose(dgate_home)[None], 0.0), axis=2)
    dsel = gates * (dgate - jnp.sum(gates * dgate, axis=0, keepdims=True))
    dlogits = jnp.sum(jnp.where(hot, dsel[:, :, None], 0.0), axis=0).astype(bf16)
    router_grad = t_product(hidden_two, dlogits)
    dhidden_two = plane_scatter(back).reshape(home, width) + product_t(dlogits, router)

    flat_two = normed_two.reshape(home, width)
    dresid, expert_norm_grad = norm_backward(
        dhidden_two, flat_two, inverse_two.reshape(home, 1), expert_norm
    )
    dresid = dresid + grad_home.reshape(home, width).astype(f32)
    dbranch = chip_gather(dresid.astype(bf16).reshape(seq_n, piece, width), 1, parts).reshape(length, width)
    column_start = (r_i * core_n + core_i) * columns
    dbranch_here = lax.dynamic_slice_in_dim(dbranch, column_start, columns, 1)
    dmixed = chip_scatter(product_t(dbranch_here, weight_out).astype(bf16), 1, parts).astype(bf16)
    dqpre, dkpre, dvpre = attend_back(
        query, keys, values, mixed, dmixed, cosine, sine, seg_row, seg_col, heads, gate_b, down_sum_b
    )
    dqkv = jnp.concatenate([dqpre, dkpre, dvpre], axis=1)
    out_grad = t_product(mixed_full, after(dbranch_here, dqpre))
    in_grad = t_product(hidden_full, dqkv).astype(bf16)
    up_a = rows_product(expert_in, after(dupre_a, dqpre))
    up_b = rows_product(expert_in, after(dupre_b, dqpre))

    grad_down = jnp.concatenate([down_sum_a, down_sum_b], axis=1).astype(f32).T[None]
    grad_gate = jnp.concatenate([over_ctx(gate_a), over_ctx(gate_b)], axis=1).astype(f32)[None]
    grad_up = jnp.concatenate([over_ctx(up_a), over_ctx(up_b)], axis=1).astype(f32)[None]

    dhidden_one = chip_scatter(
        product_t(dqkv, weight_in).astype(bf16).reshape(seq_n, parts * piece, width), 1, parts
    )
    normed_one = token_float * inverse_one
    dtokens, attn_norm_grad = norm_backward(
        dhidden_one.reshape(home, width),
        normed_one.reshape(home, width),
        inverse_one.reshape(home, 1),
        attn_norm,
    )
    grad_tokens = from_sequences((dtokens + dresid).astype(bf16).reshape(seq_n, piece, width)).astype(f32)

    mixture = plane_scatter(after(mixed_rows, dqpre))
    output = from_sequences((residual + mixture).astype(bf16))

    def seen(part):
        return part.reshape(dp_n, seq_n, r_n, y_n, core_n * rows_here, -1)

    def half(a, axis, index, name):
        keep, give = pick(a, index, axis), pick(a, 1 - index, axis)
        return (keep.astype(f32) + swap(give, name).astype(f32)).astype(bf16)

    def over_plane(a, b):
        a, b = half(seen(a), 0, dp_i, "dp"), half(seen(b), 3, y_i, "y")
        return half(a, 2, y_i, "y"), half(b, 0, dp_i, "dp")

    def over_seq(a):
        return sum(piece.astype(f32) for piece in seq_pieces(a)).astype(bf16)

    def to_rows(a):
        a = a.reshape(parts, rows_here, -1, 1, columns)
        return chip_exchange(a, 0, 3, parts).reshape(rows_here, -1, width).astype(f32)

    one, two = over_plane(in_grad[:, : 3 * columns // 2], in_grad[:, 3 * columns // 2 :])
    inward = to_rows(over_seq(jnp.concatenate([one, two], axis=-1)))
    one, two = over_plane(*jnp.split(out_grad.astype(bf16), 2, axis=1))
    outward = to_rows(over_seq(jnp.concatenate([one, two], axis=-1)))
    grad_output = outward[:, 0]
    grad_query, grad_key, grad_value = (inward[:, i] for i in range(3))

    gains = jnp.concatenate([attn_norm_grad[None], expert_norm_grad[None], router_grad.T], axis=0)
    gain_n = gains.shape[0]
    gains = gains.reshape(gain_n, -1, rows_here).transpose(1, 0, 2)
    gains = lax.all_to_all(gains, EVERY, split_axis=0, concat_axis=0, tiled=True)
    gains = jnp.sum(gains, axis=0).T

    return (
        output,
        grad_tokens,
        gains[:, 0],
        grad_query,
        grad_key,
        grad_value,
        grad_output,
        gains[:, 1],
        gains[:, 2:],
        grad_gate,
        grad_up,
        grad_down,
    )


def solution(mesh):
    dp_n, ctx_n, exp_n = mesh.shape["dp"], mesh.shape["ctx"], mesh.shape["exp"]

    def block(*arrays):
        tokens = arrays[0]
        seq_count = tokens.shape[0] // (dp_n * exp_n)
        seq_n = seq_count * CORES
        sizes = (dp_n, seq_n, ctx_n // seq_n, exp_n // CORES, CORES)
        fine = Mesh(mesh.devices.reshape(sizes), EVERY)
        group = ("dp", "y", "core")
        exp = ("y", "core")
        return jax.shard_map(
            functools.partial(on_device, sizes),
            mesh=fine,
            in_specs=(
                P(group, CTX, None),
                P(group, None),
                P(group, CTX, None),
                P(),
                P(EVERY, None),
                P(EVERY, None),
                P(EVERY, None),
                P(EVERY, None),
                P(),
                P(),
                P(exp, None, "dp"),
                P(exp, None, "dp"),
                P(exp, "dp", None),
                P(group, CTX, None),
            ),
            out_specs=(
                P(group, CTX, None),
                P(group, CTX, None),
                P(EVERY),
                P(EVERY, None),
                P(EVERY, None),
                P(EVERY, None),
                P(EVERY, None),
                P(EVERY),
                P(EVERY, None),
                P(exp, CTX, "dp"),
                P(exp, CTX, "dp"),
                P(exp, "dp", CTX),
            ),
            check_vma=False,
        )(*arrays)

    return block
```

```python
import functools

import jax
import jax.numpy as jnp
from jax import lax
from jax.experimental import pallas as pl
from jax.experimental.pallas import tpu as pltpu
from jax.sharding import Mesh, PartitionSpec as P

HEADS = 16
CORES = 2

epsilon = 1e-05
theta_base = 10000.0
masked_score = -1e30
bf16 = jnp.bfloat16
f32 = jnp.float32

PLANE = ("dp", "y", "core")
CHIP = ("r", "core")
SPREAD = ("dp", "seq", "y")
CTX = ("seq", "r")
EVERY = ("dp", "seq", "r", "y", "core")


def product(a, b):
    return jnp.dot(a, b, preferred_element_type=f32)


def product_t(a, b):
    return lax.dot_general(a, b, (((1,), (1,)), ((), ())), preferred_element_type=f32)


def t_product(a, b):
    return lax.dot_general(a, b, (((0,), (0,)), ((), ())), preferred_element_type=f32)


def swap(a, axis):
    return lax.ppermute(a, axis, [(0, 1), (1, 0)])


def halves(a, axis):
    size = a.shape[axis] // 2
    me = lax.axis_index("core")
    mine = lax.dynamic_slice_in_dim(a, me * size, size, axis)
    other = lax.dynamic_slice_in_dim(a, (1 - me) * size, size, axis)
    return mine, other


def by_core(mine, other, axis):
    first = lax.axis_index("core") == 0
    return jnp.concatenate([jnp.where(first, mine, other), jnp.where(first, other, mine)], axis=axis)


def chip_gather(a, axis, parts):
    if parts == 2:
        return by_core(a, swap(a, "core"), axis)
    return lax.all_gather(a, CHIP, axis=axis, tiled=True)


def chip_scatter(a, axis, parts):
    if parts == 2:
        mine, other = halves(a, axis)
        return mine.astype(f32) + swap(other, "core").astype(f32)
    return lax.psum_scatter(a, CHIP, scatter_dimension=axis, tiled=True).astype(f32)


def chip_exchange(a, split, concat, parts):
    if parts == 2:
        mine, other = halves(a, split)
        return by_core(mine, swap(other, "core"), concat)
    return lax.all_to_all(a, CHIP, split_axis=split, concat_axis=concat, tiled=True)


def core_exchange(a, split, concat):
    mine, other = halves(a, split)
    return by_core(mine, swap(other, "core"), concat)


def seq_pieces(a):
    count = a.shape[0]
    me = lax.axis_index("seq")
    pieces = [pick(a, me, 0)]
    for step in range(1, count):
        give = pick(a, lax.rem(me + step, count), 0)
        pieces.append(lax.ppermute(give, "seq", [(i, (i + step) % count) for i in range(count)]))
    return pieces


def seq_exchange(a):
    count = a.shape[0]
    me = lax.axis_index("seq")
    pieces = jnp.stack(seq_pieces(a))
    return jnp.stack([pick(pieces, lax.rem(me + count - s, count), 0) for s in range(count)])


def to_sequences(a):
    return seq_exchange(core_exchange(a, 1, 0))


def from_sequences(a):
    return core_exchange(seq_exchange(a), 0, 1)


def plane_scatter(blocks):
    got = swap(blocks[:, :, 1], "core")
    held = (blocks[:, :, 0].astype(f32) + got.astype(f32)).astype(bf16)
    half = blocks.shape[3] // 2
    by_x = swap(held[1, 1, :half], "dp")
    by_y = swap(held[1, 1, half:], "y")
    to_x = jnp.concatenate(
        [held[1, 0, :half], (held[1, 0, half:].astype(f32) + by_y.astype(f32)).astype(bf16)], axis=0
    )
    to_y = jnp.concatenate(
        [(held[0, 1, :half].astype(f32) + by_x.astype(f32)).astype(bf16), held[0, 1, half:]], axis=0
    )
    from_x = swap(to_x, "dp")
    from_y = swap(to_y, "y")
    return held[0, 0].astype(f32) + from_x.astype(f32) + from_y.astype(f32)


MESH = pl.DeviceIdType.MESH
Z_UP, Z_DOWN, X_A, Y_A, Y_B, X_B, Y_A2, X_B2 = range(8)


def first_kernel(
    query,
    key,
    value,
    output,
    tokens,
    grads,
    segments,
    weights,
    tokens_out,
    grads_out,
    segments_out,
    send,
    recv,
    core_send,
    core_recv,
    core_local,
    row_send,
    row_recv,
    row_local,
):
    dp, z, y, core = (lax.axis_index(a) for a in ("dp", "seq", "y", "core"))
    seq_n = weights.shape[1]
    rows, columns = query.shape[0], weights.shape[4] // 4
    half = weights.shape[4] // 2
    piece = tokens_out.shape[1]
    x_next, y_next, z_next, z_last, other = (
        {"dp": 1 - dp},
        {"y": 1 - y},
        {"seq": lax.rem(z + 1, seq_n)},
        {"seq": lax.rem(z + seq_n - 1, seq_n)},
        {"core": 1 - core},
    )

    barrier = pltpu.get_barrier_semaphore()
    partners = [x_next, y_next] + [
        {"seq": lax.rem(z + dz, seq_n), "core": lax.rem(core + dc, 2)}
        for dz in range(seq_n)
        for dc in range(2)
        if dz or dc
    ]
    for partner in partners:
        pl.semaphore_signal(barrier, inc=1, device_id=partner, device_id_type=MESH)
    pl.semaphore_wait(barrier, len(partners))

    here = pl.ds(pl.multiple_of(core * rows, rows), rows)
    locals_, remotes = [], []
    for m, matrix in enumerate((query, key, value, output)):
        place = weights.at[dp, z, y, here, pl.ds(m * columns, columns)]
        mine = matrix.at[:, pl.ds(pl.multiple_of(core * columns, columns), columns)]
        theirs = matrix.at[:, pl.ds(pl.multiple_of((1 - core) * columns, columns), columns)]
        locals_.append(pltpu.make_async_copy(mine, place, core_local.at[m]))
        remotes.append(
            pltpu.make_async_remote_copy(
                theirs, place, core_send.at[m], core_recv.at[m], device_id=other, device_id_type=MESH
            )
        )
    segment_local = pltpu.make_async_copy(segments, segments_out.at[core], core_local.at[4])
    segment_remote = pltpu.make_async_remote_copy(
        segments, segments_out.at[core], core_send.at[4], core_recv.at[4], device_id=other, device_id_type=MESH
    )
    for copy in remotes + [segment_remote] + locals_ + [segment_local]:
        copy.start()
    for copy in remotes + locals_:
        copy.wait()

    def part(kind, dp_b, z_b, y_b, device):
        if kind in (Z_UP, Z_DOWN):
            ref = weights.at[dp_b, z_b, y_b]
        else:
            start = 0 if kind in (X_A, Y_A, Y_A2) else half
            ref = weights.at[dp_b, z_b, y_b, :, pl.ds(start, half)]
        return pltpu.make_async_remote_copy(
            ref, ref, send.at[kind, z_b], recv.at[kind, z_b], device_id=device, device_id_type=MESH
        )

    def own(kind, z_b):
        device = {Z_UP: z_next, Z_DOWN: z_last, X_A: x_next, X_B: x_next, Y_A: y_next, Y_B: y_next}[kind]
        return part(kind, dp, z_b, y, device)

    def from_x(kind, z_b):
        return part(kind, 1 - dp, z_b, y, x_next)

    def from_y(kind, z_b):
        return part(kind, dp, z_b, 1 - y, y_next)

    def on_y(z_b):
        return part(Y_A2, 1 - dp, z_b, y, y_next)

    def on_x(z_b):
        return part(X_B2, dp, z_b, 1 - y, x_next)

    def spread(z_b):
        for kind in (X_A, Y_B, X_B, Y_A):
            own(kind, z_b).start()

    def relay(z_b):
        from_x(X_A, z_b).wait_recv()
        on_y(z_b).start()
        from_y(Y_B, z_b).wait_recv()
        on_x(z_b).start()

    def at_step(step, act_up, act_down):
        @pl.when(z - step >= 0)
        def _():
            act_up(z - step)

        @pl.when(z + step < seq_n)
        def _():
            act_down(z + step)

    def come_up(z_b):
        own(Z_UP, z_b).wait_recv()

        @pl.when(z < seq_n - 1)
        def _():
            own(Z_UP, z_b).start()

        spread(z_b)

    def come_down(z_b):
        own(Z_DOWN, z_b).wait_recv()

        @pl.when(z > 0)
        def _():
            own(Z_DOWN, z_b).start()

        spread(z_b)

    def rows_of(n, source, target, act):
        for s in range(tokens.shape[0]):
            z_to = tokens.shape[0] * core + s
            for d in range(2):
                core_to = lax.rem(core + d, 2)
                ref = source.at[s, pl.ds(pl.multiple_of(core_to * piece, piece), piece), :]
                copy = pltpu.make_async_remote_copy(
                    ref,
                    target.at[z],
                    row_send.at[n, s, d],
                    row_recv.at[n, z],
                    device_id={"seq": z_to, "core": core_to},
                    device_id_type=MESH,
                )
                if d:
                    act(copy)
                else:
                    keep = pltpu.make_async_copy(ref, target.at[z], row_local.at[n])

                    @pl.when(z_to != z)
                    def _(copy=copy):
                        act(copy)

                    @pl.when(z_to == z)
                    def _(keep=keep):
                        if act is begin:
                            keep.start()
                        else:
                            keep.wait()

    def begin(copy):
        copy.start()

    def sent(copy):
        copy.wait_send()

    def rows_in(n, target):
        group = z // tokens.shape[0]
        for z_from in range(seq_n):
            copy = pltpu.make_async_remote_copy(
                target.at[z_from],
                target.at[z_from],
                row_send.at[n, 0, 0],
                row_recv.at[n, z_from],
                device_id=other,
                device_id_type=MESH,
            )

            @pl.when((z_from != z) | (group != core))
            def _(copy=copy):
                copy.wait_recv()

    @pl.when(z < seq_n - 1)
    def _():
        own(Z_UP, z).start()

    @pl.when(z > 0)
    def _():
        own(Z_DOWN, z).start()

    spread(z)
    for step in range(1, seq_n):
        at_step(step, come_up, come_down)
        if step == 1:
            relay(z)
        else:
            at_step(step - 1, relay, relay)
        if step == seq_n - 2:
            rows_of(0, tokens, tokens_out, begin)
    rows_of(1, grads, grads_out, begin)
    at_step(seq_n - 1, relay, relay)

    segment_remote.wait()
    segment_local.wait()
    for z_b in range(seq_n):
        from_y(Y_A, z_b).wait_recv()
        from_x(X_B, z_b).wait_recv()
        part(Y_A2, 1 - dp, z_b, 1 - y, y_next).wait_recv()
        part(X_B2, 1 - dp, z_b, 1 - y, x_next).wait_recv()
        for kind in (X_A, Y_B, X_B, Y_A):
            own(kind, z_b).wait_send()
        on_y(z_b).wait_send()
        on_x(z_b).wait_send()

        @pl.when((z < seq_n - 1) & (z_b <= z))
        def _(z_b=z_b):
            own(Z_UP, z_b).wait_send()

        @pl.when((z > 0) & (z_b >= z))
        def _(z_b=z_b):
            own(Z_DOWN, z_b).wait_send()

    rows_of(0, tokens, tokens_out, sent)
    rows_of(1, grads, grads_out, sent)
    rows_in(0, tokens_out)
    rows_in(1, grads_out)


def first_transfers(query, key, value, output, tokens, grads, segments, sizes):
    dp_n, seq_n, r_n, y_n, core_n = sizes
    rows, width = query.shape
    piece = tokens.shape[1] // core_n
    columns = width // core_n
    held = pl.BlockSpec(memory_space=pl.ANY)
    out = jax.ShapeDtypeStruct((seq_n, piece, width), bf16)
    dma = pltpu.SemaphoreType.DMA
    weights, tokens, grads, segments = pl.pallas_call(
        first_kernel,
        in_specs=[held] * 7,
        out_specs=[held] * 4,
        out_shape=[
            jax.ShapeDtypeStruct((dp_n, seq_n, y_n, core_n * rows, 4 * columns), bf16),
            out,
            out,
            jax.ShapeDtypeStruct((core_n,) + segments.shape, segments.dtype),
        ],
        scratch_shapes=[
            dma((8, seq_n)),
            dma((8, seq_n)),
            dma((5,)),
            dma((5,)),
            dma((5,)),
            dma((2, tokens.shape[0], 2)),
            dma((2, seq_n)),
            dma((2,)),
        ],
        compiler_params=pltpu.CompilerParams(collective_id=0, has_side_effects=True),
        cost_estimate=pl.CostEstimate(flops=0, bytes_accessed=2 * 4 * columns * width, transcendentals=0),
        name="first_transfers",
    )(query, key, value, output, tokens, grads, segments)
    return weights.reshape(width, 4 * columns), tokens, grads, segments


def visible_block(seg_row, seg_col, start, rows, cols):
    row_place = start + lax.broadcasted_iota(jnp.int32, (rows, cols), 0)
    col_place = lax.broadcasted_iota(jnp.int32, (rows, cols), 1)
    return (seg_col == seg_row) & (col_place <= row_place)


def turned(u, cosine, sine):
    return u * cosine + pltpu.roll(u, u.shape[1] // 2, 1) * sine


def attend_kernel(scale, block, qp, kp, vp, cosine, sine, seg_row, seg_col, q_out, k_out, v_out, mixed):
    length = qp.shape[0]
    q_out[...] = turned(qp[...], cosine[...], sine[...]).astype(bf16)
    k_out[...] = turned(kp[...], cosine[...], sine[...]).astype(bf16)
    v_out[...] = vp[...].astype(bf16)
    for start in range(0, length, block):
        stop = start + block
        scores = product_t(q_out[start:stop, :], k_out[:stop, :]) * scale
        seen = visible_block(seg_row[:, :stop], seg_col[start:stop, :], start, block, stop)
        scores = jnp.where(seen, scores, masked_score)
        top = jnp.max(scores, axis=1, keepdims=True)
        weights = jnp.exp(scores - top)
        total = jnp.sum(weights, axis=1, keepdims=True)
        summed = product(weights.astype(bf16), v_out[:stop, :])
        mixed[start:stop, :] = (summed / total).astype(bf16)


def attend(qkv, cosine, sine, seg_row, seg_col, heads):
    length, head = qkv.shape[0], cosine.shape[1]
    block = min(256, length)

    def column(offset):
        return pl.BlockSpec((length, head), lambda h: (0, offset + h))

    def whole(shape):
        return pl.BlockSpec(shape, lambda h: (0, 0))

    out = jax.ShapeDtypeStruct((length, heads * head), bf16)
    pairs = length * (length + block) // 2 * heads
    return pl.pallas_call(
        functools.partial(attend_kernel, head**-0.5, block),
        grid=(heads,),
        in_specs=[
            column(0),
            column(heads),
            column(2 * heads),
            whole((length, head)),
            whole((length, head)),
            whole((1, length)),
            whole((length, 1)),
        ],
        out_specs=[column(0)] * 4,
        out_shape=[out] * 4,
        compiler_params=pltpu.CompilerParams(vmem_limit_bytes=48 * 2**20),
        cost_estimate=pl.CostEstimate(
            flops=4 * pairs * head, bytes_accessed=20 * length * heads * head, transcendentals=pairs
        ),
        name="attend",
    )(qkv, qkv, qkv, cosine, sine, seg_row, seg_col)


def attend_back_kernel(
    scale, block, q, k, v, mixed, dmixed, cosine, sine, seg_row, seg_col, *rest
):
    dq_out, dk_out, dv_out, dk_sum, dv_sum = rest[-5:]
    length = q.shape[0]
    dk_sum[...] = jnp.zeros_like(dk_sum)
    dv_sum[...] = jnp.zeros_like(dv_sum)
    for start in range(0, length, block):
        stop = start + block
        scores = product_t(q[start:stop, :], k[:stop, :]) * scale
        seen = visible_block(seg_row[:, :stop], seg_col[start:stop, :], start, block, stop)
        scores = jnp.where(seen, scores, masked_score)
        top = jnp.max(scores, axis=1, keepdims=True)
        weights = jnp.exp(scores - top)
        inverse = 1.0 / jnp.sum(weights, axis=1, keepdims=True)
        grad = dmixed[start:stop, :].astype(f32)
        delta = jnp.sum(grad * mixed[start:stop, :].astype(f32), axis=1, keepdims=True) * inverse
        unit = (grad * inverse).astype(bf16)
        dweights = product_t(unit, v[:stop, :])
        dscores = (weights * (dweights - delta)).astype(bf16)
        dq = product(dscores, k[:stop, :]) * scale
        dq_out[start:stop, :] = turned(dq, cosine[start:stop, :], -sine[start:stop, :]).astype(bf16)
        dk_sum[:stop, :] += t_product(dscores, q[start:stop, :])
        dv_sum[:stop, :] += t_product(weights.astype(bf16), unit)
    dk_out[...] = turned(dk_sum[...] * scale, cosine[...], -sine[...]).astype(bf16)
    dv_out[...] = dv_sum[...].astype(bf16)


def attend_back(q, k, v, mixed, dmixed, cosine, sine, seg_row, seg_col, heads, *before):
    length, head = q.shape[0], cosine.shape[1]
    block = min(256, length)
    column = pl.BlockSpec((length, head), lambda h: (0, h))

    def whole(shape):
        return pl.BlockSpec(shape, lambda h: (0, 0))

    out = jax.ShapeDtypeStruct((length, heads * head), bf16)
    pairs = length * (length + block) // 2 * heads
    return pl.pallas_call(
        functools.partial(attend_back_kernel, head**-0.5, block),
        grid=(heads,),
        in_specs=[column] * 5
        + [whole((length, head)), whole((length, head)), whole((1, length)), whole((length, 1))]
        + [pl.BlockSpec(memory_space=pl.ANY)] * len(before),
        out_specs=[column] * 3,
        out_shape=[out] * 3,
        scratch_shapes=[pltpu.VMEM((length, head), f32)] * 2,
        compiler_params=pltpu.CompilerParams(vmem_limit_bytes=48 * 2**20),
        cost_estimate=pl.CostEstimate(
            flops=10 * pairs * head, bytes_accessed=16 * length * heads * head, transcendentals=pairs
        ),
        name="attend_back",
    )(q, k, v, mixed, dmixed, cosine, sine, seg_row, seg_col, *before)


def units_kernel(chunk, x, dy, gate, up, down, *rest):
    units, dgate, dup = rest[-3:]
    gate_w, up_w, down_w = gate[...], up[...], down[...]

    def step(i, carry):
        rows = pl.ds(pl.multiple_of(i * chunk, chunk), chunk)
        gpre = product(x[rows, :], gate_w)
        upre = product(x[rows, :], up_w)
        dunits = product_t(dy[rows, :], down_w)
        s = jax.nn.sigmoid(gpre)
        silu = gpre * s
        units[rows, :] = (silu * upre).astype(bf16)
        dgate[rows, :] = (dunits * upre * (s * (1.0 + gpre * (1.0 - s)))).astype(bf16)
        dup[rows, :] = (dunits * silu).astype(bf16)
        return carry

    lax.fori_loop(0, x.shape[0] // chunk, step, 0)


def expert_units(x, dy, gate, up, down, start, stop, *before):
    rows, width = x.shape
    units = stop - start
    chunk = tile_of(rows)
    tile = unit_tile(gate.shape[1])
    first = start // tile
    once = pl.BlockSpec((rows, width), lambda j: (0, 0), pipeline_mode=pl.Buffered(1))
    out = jax.ShapeDtypeStruct((rows, units), bf16)
    return pl.pallas_call(
        functools.partial(units_kernel, chunk),
        grid=(units // tile,),
        in_specs=[
            once,
            once,
            pl.BlockSpec((width, tile), lambda j: (0, first + j)),
            pl.BlockSpec((width, tile), lambda j: (0, first + j)),
            pl.BlockSpec((tile, width), lambda j: (first + j, 0)),
        ]
        + [pl.BlockSpec(memory_space=pl.ANY)] * len(before),
        out_specs=[pl.BlockSpec((rows, tile), lambda j: (0, j))] * 3,
        out_shape=[out] * 3,
        compiler_params=pltpu.CompilerParams(vmem_limit_bytes=56 * 2**20),
        cost_estimate=pl.CostEstimate(
            flops=6 * rows * width * units,
            bytes_accessed=4 * rows * width + 6 * width * units + 6 * rows * units,
            transcendentals=rows * units,
        ),
        name="expert_units",
    )(x, dy, gate, up, down, *before)


def unit_tile(units):
    return 256 if units % 256 == 0 else units


def unit_cut(units):
    tile = unit_tile(units)
    return units // tile * 3 // 4 * tile


def dispatch_kernel(me, hidden, dout, slot, routes, router, rows, dy_rows, gate):
    size = hidden.shape[1] * hidden.shape[3]
    width = hidden.shape[4]
    mine = me[3]
    tokens = hidden[...].reshape(size, width)
    logits = product(tokens, router[...])
    lanes = lax.broadcasted_iota(jnp.int32, logits.shape, 1)
    first, second = routes[0, :, 0:1], routes[0, :, 1:2]
    one = jnp.sum(jnp.where(lanes == first, logits, 0.0), axis=1, keepdims=True)
    two = jnp.sum(jnp.where(lanes == second, logits, 0.0), axis=1, keepdims=True)
    top = jnp.maximum(one, two)
    one, two = jnp.exp(one - top), jnp.exp(two - top)
    share = jnp.where(first == mine, one, jnp.where(second == mine, two, 0.0)) / (one + two)
    gate[0] = share
    chosen = (
        lax.broadcasted_iota(jnp.int32, (rows.shape[1], size), 0) == slot[0]
    ).astype(bf16)
    rows[0] = product(chosen, tokens).astype(bf16)
    dy = (share * dout[...].reshape(size, width).astype(f32)).astype(bf16)
    dy_rows[0] = product(chosen, dy).astype(bf16)


def plane_block(seq_n, piece, width):
    return pl.BlockSpec((1, 2, 1, piece, width), lambda b, me: (b // seq_n, 0, b % seq_n, 0, 0))


def relative_block(seq_n, piece, width):
    return pl.BlockSpec(
        (1, 1, 2, 1, piece, width),
        lambda b, me: (
            lax.rem(b // (2 * seq_n) + me[0], 2),
            lax.rem(b // seq_n + me[1], 2),
            0,
            b % seq_n,
            0,
            0,
        ),
    )


def dispatch(me, hidden, dout, slot, routes, router, seq_n, piece, cap):
    blocks, size = slot.shape[0], slot.shape[2]
    width = hidden.shape[1]
    seen = (4, 2, seq_n, piece, width)
    each = pl.BlockSpec((1, cap, width), lambda b, me: (b, 0, 0))
    out = jax.ShapeDtypeStruct((blocks, cap, width), bf16)
    spare = jnp.zeros((width, 128 - router.shape[1]), router.dtype)
    return pl.pallas_call(
        dispatch_kernel,
        grid_spec=pltpu.PrefetchScalarGridSpec(
            num_scalar_prefetch=1,
            grid=(blocks,),
            in_specs=[
                plane_block(seq_n, piece, width),
                plane_block(seq_n, piece, width),
                pl.BlockSpec((1, 1, size), lambda b, me: (b, 0, 0)),
                pl.BlockSpec((1, size, routes.shape[2]), lambda b, me: (b, 0, 0)),
                pl.BlockSpec((width, 128), lambda b, me: (0, 0)),
            ],
            out_specs=[each, each, pl.BlockSpec((1, size, 1), lambda b, me: (b, 0, 0))],
        ),
        out_shape=[out, out, jax.ShapeDtypeStruct((blocks, size, 1), f32)],
        compiler_params=pltpu.CompilerParams(vmem_limit_bytes=40 * 2**20),
        cost_estimate=pl.CostEstimate(
            flops=4 * blocks * size * width * (cap + 64),
            bytes_accessed=4 * blocks * (size + cap) * width,
            transcendentals=2 * blocks * size,
        ),
        name="dispatch",
    )(
        me,
        hidden.reshape(seen),
        dout.reshape(seen),
        slot,
        routes,
        jnp.concatenate([router, spare], axis=1),
    )


def spread_rows(slot, rows):
    size, cap = slot.shape[0], rows.shape[0]
    chosen = (lax.broadcasted_iota(jnp.int32, (size, cap), 1) == slot).astype(bf16)
    return product(chosen, rows)


def place_cores(me, out, dense):
    piece = out.shape[4]
    for core in range(2):
        out[0, 0, lax.rem(me[2] + core, 2), 0] = dense[core * piece : (core + 1) * piece, :].astype(bf16)


def combine_kernel(me, rows, slot, gate, dout, out, dgate):
    dense = spread_rows(slot[0], rows[0])
    grads = dout[...].reshape(dense.shape).astype(f32)
    dgate[0] = jnp.sum(grads * dense, axis=1, keepdims=True)
    place_cores(me, out, gate[0] * dense)


def collect_kernel(me, left, slot, right, *rest):
    dense = [spread_rows(slot[0], left[0]), spread_rows(slot[0], right[0])]
    place_cores(me, rest[-1], jnp.concatenate(dense, axis=1))


def combine(me, rows, slot, seq_n, piece, gate=None, dout=None, right=None):
    blocks, cap, part = rows.shape
    size = slot.shape[1]
    width = part if right is None else 2 * part
    column = pl.BlockSpec((1, size, 1), lambda b, me: (b, 0, 0))
    weigh = gate is not None
    operands = [rows, slot]
    in_specs = [pl.BlockSpec((1, cap, part), lambda b, me: (b, 0, 0)), column]
    out_specs = [relative_block(seq_n, piece, width)]
    out_shape = [jax.ShapeDtypeStruct((2, 2, 2, seq_n, piece, width), bf16)]
    if weigh:
        operands += [gate, dout.reshape(4, 2, seq_n, piece, width)]
        in_specs += [column, plane_block(seq_n, piece, width)]
        out_specs += [column]
        out_shape += [jax.ShapeDtypeStruct((blocks, size, 1), f32)]
    else:
        operands += [right]
        in_specs += in_specs[:1]
    return pl.pallas_call(
        combine_kernel if weigh else collect_kernel,
        grid_spec=pltpu.PrefetchScalarGridSpec(
            num_scalar_prefetch=1, grid=(blocks,), in_specs=in_specs, out_specs=out_specs
        ),
        out_shape=out_shape,
        compiler_params=pltpu.CompilerParams(vmem_limit_bytes=40 * 2**20),
        cost_estimate=pl.CostEstimate(
            flops=2 * blocks * size * width * cap,
            bytes_accessed=2 * blocks * (2 * size + cap) * width,
            transcendentals=0,
        ),
        name="combine" if weigh else "collect",
    )(me, *operands)


def down_kernel(cut, units_a, units_b, down, *rest):
    total = product(units_a[...], down[:cut, :]) + product(units_b[...], down[cut:, :])
    rest[-1][...] = total.astype(bf16)


def expert_down(units_a, units_b, down, *before):
    rows, cut = units_a.shape
    inner, width = down.shape
    m, n = tile_of(rows), tile_of(width)
    return pl.pallas_call(
        functools.partial(down_kernel, cut),
        grid=(width // n, rows // m),
        in_specs=[
            pl.BlockSpec((m, cut), lambda j, i: (i, 0)),
            pl.BlockSpec((m, inner - cut), lambda j, i: (i, 0)),
            pl.BlockSpec((inner, n), lambda j, i: (0, j)),
        ]
        + [pl.BlockSpec(memory_space=pl.ANY)] * len(before),
        out_specs=pl.BlockSpec((m, n), lambda j, i: (i, j)),
        out_shape=jax.ShapeDtypeStruct((rows, width), bf16),
        compiler_params=pltpu.CompilerParams(vmem_limit_bytes=48 * 2**20),
        cost_estimate=pl.CostEstimate(
            flops=2 * rows * inner * width,
            bytes_accessed=2 * (rows * inner + inner * width + rows * width),
            transcendentals=0,
        ),
        name="expert_down",
    )(units_a, units_b, down, *before)


def input_kernel(cut, dgate_a, dgate_b, dup_a, dup_b, gate, up, *rest):
    total = product_t(dgate_a[...], gate[:, :cut]) + product_t(dgate_b[...], gate[:, cut:])
    total += product_t(dup_a[...], up[:, :cut]) + product_t(dup_b[...], up[:, cut:])
    rest[-1][...] = total.astype(bf16)


def expert_input_grad(dgate_a, dgate_b, dup_a, dup_b, gate, up, start, stop, *before):
    rows, cut = dgate_a.shape
    inner = gate.shape[1]
    width = stop - start
    m, n = tile_of(rows), tile_of(width)
    first = start // n
    left_a = pl.BlockSpec((m, cut), lambda j, i: (i, 0))
    left_b = pl.BlockSpec((m, inner - cut), lambda j, i: (i, 0))
    right = pl.BlockSpec((n, inner), lambda j, i: (first + j, 0))
    return pl.pallas_call(
        functools.partial(input_kernel, cut),
        grid=(width // n, rows // m),
        in_specs=[left_a, left_b, left_a, left_b, right, right]
        + [pl.BlockSpec(memory_space=pl.ANY)] * len(before),
        out_specs=pl.BlockSpec((m, n), lambda j, i: (i, j)),
        out_shape=jax.ShapeDtypeStruct((rows, width), bf16),
        compiler_params=pltpu.CompilerParams(vmem_limit_bytes=52 * 2**20),
        cost_estimate=pl.CostEstimate(
            flops=4 * rows * inner * width,
            bytes_accessed=2 * (2 * rows * inner + 2 * inner * width + rows * width),
            transcendentals=0,
        ),
        name="expert_input_grad",
    )(dgate_a, dgate_b, dup_a, dup_b, gate, up, *before)


def tile_of(size):
    return max(c for c in range(16, 513, 16) if size % c == 0)


def anchor_kernel(*refs):
    pass


def after(a, *before):
    return pl.pallas_call(
        anchor_kernel,
        in_specs=[pl.BlockSpec(memory_space=pl.ANY)] * (1 + len(before)),
        out_specs=pl.BlockSpec(memory_space=pl.ANY),
        out_shape=jax.ShapeDtypeStruct(a.shape, a.dtype),
        input_output_aliases={0: 0},
        cost_estimate=pl.CostEstimate(flops=0, bytes_accessed=0, transcendentals=0),
        name="after",
    )(a, *before)


def norm_backward(grad_rows, normed, inverse, gain):
    weighted = grad_rows * gain
    mean_term = jnp.mean(weighted * normed, axis=-1, keepdims=True)
    return inverse * (weighted - normed * mean_term), jnp.sum(grad_rows * normed, axis=0)


def pick(a, index, axis):
    return lax.dynamic_index_in_dim(a, index, axis, keepdims=False)


def on_device(
    sizes,
    tokens,
    segments,
    routes,
    attn_norm,
    query_weight,
    key_weight,
    value_weight,
    output_weight,
    expert_norm,
    router,
    gate_weight,
    up_weight,
    down_weight,
    grad_out,
):
    dp_n, seq_n, r_n, y_n, core_n = sizes
    parts = r_n * core_n
    seq_count, seq_dev, width = tokens.shape
    piece = seq_dev // core_n
    length = segments.shape[1]
    home = seq_n * piece
    head = width // HEADS
    heads = HEADS // parts
    columns = width // parts
    experts = router.shape[1]
    topk = routes.shape[2]
    plane = 8 * home
    blocks = plane // seq_dev
    cap = 5 * seq_dev * topk // (4 * experts)
    dp_i, seq_i, r_i, y_i, core_i = (lax.axis_index(a) for a in EVERY)
    group, member = seq_i // seq_count, seq_i % seq_count

    rows_here = query_weight.shape[0]
    if r_n == 1 and parts == 2 and dp_n == 2 and y_n == 2 and seq_n == 2 * seq_count:
        weights, token_home, grad_home, chip_segments = first_transfers(
            query_weight, key_weight, value_weight, output_weight, tokens, grad_out, segments, sizes
        )
        segment = pick(pick(chip_segments, group, 0), member, 0)
    else:
        local = jnp.concatenate([query_weight, key_weight, value_weight, output_weight], axis=1)
        local = chip_exchange(local.reshape(rows_here, 4, parts, columns), 2, 0, parts)
        weights = lax.all_gather(
            local.reshape(parts * rows_here, 4 * columns), SPREAD, axis=0, tiled=True
        )
        weights = (
            weights.reshape(dp_n * seq_n, y_n, r_n, core_n * rows_here, -1)
            .transpose(0, 2, 1, 3, 4)
            .reshape(width, -1)
        )
        token_home, grad_home = to_sequences(tokens), to_sequences(grad_out)
        chip_segments = lax.all_gather(segments, "core")
        segment = pick(pick(chip_segments, group, 0), member, 0)
    weight_in, weight_out = weights[:, : 3 * columns], weights[:, 3 * columns :]

    token_float = token_home.astype(f32)
    inverse_one = lax.rsqrt(jnp.mean(token_float * token_float, axis=-1, keepdims=True) + epsilon)
    hidden_one = (token_float * inverse_one * attn_norm).astype(bf16)
    hidden_full = chip_gather(hidden_one, 1, parts).reshape(length, width)

    grad_plane = lax.all_gather(grad_home.reshape(home, width), PLANE, axis=0, tiled=True)

    half = head // 2
    frequency = theta_base ** (-jnp.arange(half, dtype=f32) / half)
    angles = jnp.arange(length, dtype=f32)[:, None] * frequency[None, :]
    cosine = jnp.concatenate([jnp.cos(angles)] * 2, axis=1)
    sine = jnp.concatenate([-jnp.sin(angles), jnp.sin(angles)], axis=1)
    seg_row, seg_col = segment[None, :], segment[:, None]

    qkv = product(hidden_full, weight_in)
    query, keys, values, mixed = attend(qkv, cosine, sine, seg_row, seg_col, heads)
    mixed_full = chip_gather(mixed, 1, parts)
    branch = product(mixed_full, weight_out).reshape(seq_n, parts, piece, columns)
    branch = chip_exchange(branch, 1, 3, parts).reshape(seq_n, piece, width)
    residual = token_float + branch
    inverse_two = lax.rsqrt(jnp.mean(residual * residual, axis=-1, keepdims=True) + epsilon)
    normed_two = residual * inverse_two
    hidden_two = (normed_two * expert_norm).astype(bf16).reshape(home, width)

    hidden_plane = lax.all_gather(hidden_two, PLANE, axis=0, tiled=True)
    small = after(jnp.transpose(routes, (2, 0, 1)).reshape(topk * seq_count, seq_dev), hidden_two)
    small = lax.all_gather(small, EVERY, axis=0, tiled=True).reshape(
        dp_n, seq_n, r_n, y_n, core_n, topk, seq_count, seq_dev
    )
    small = pick(pick(small, group, 4), member, 5)
    plane_routes = pick(small, r_i, 2).transpose(0, 2, 1, 3, 4)
    block_routes = plane_routes.reshape(blocks, topk, seq_dev)
    home_routes = (
        pick(pick(plane_routes, dp_i, 0), y_i, 0)
        .reshape(seq_n, topk, core_n, piece)
        .transpose(1, 2, 0, 3)
    )
    home_routes = pick(home_routes, core_i, 1).reshape(topk, home)
    mine = y_i * core_n + core_i
    chosen = jnp.any(block_routes == mine, axis=1)
    places = jnp.arange(seq_dev)
    rank = product(chosen.astype(bf16), (places[:, None] < places[None, :]).astype(bf16))
    slot = jnp.where(chosen, rank.astype(jnp.int32), -1)
    slot_row, slot_col = slot[:, None, :], slot[:, :, None]
    me = jnp.stack([dp_i, y_i, core_i, mine]).astype(jnp.int32)
    expert_rows, dy_rows, row_gate = dispatch(
        me,
        hidden_plane,
        grad_plane,
        slot_row,
        jnp.transpose(block_routes, (0, 2, 1)),
        router,
        seq_n,
        piece,
        cap,
    )
    expert_in = expert_rows.reshape(blocks * cap, width)
    dy_rows = dy_rows.reshape(blocks * cap, width)

    gate_one, up_one, down_one = gate_weight[0], up_weight[0], down_weight[0]
    inner = gate_one.shape[1]
    cut = unit_cut(inner)
    full = (gate_one, up_one, down_one)

    def over_ctx(part):
        return lax.psum_scatter(part, CTX, scatter_dimension=0, tiled=True)

    def rows_product(rows, part):
        return t_product(rows, part).astype(bf16)

    units_a, dgpre_a, dupre_a = expert_units(expert_in, dy_rows, *full, 0, cut)
    down_a = rows_product(dy_rows, units_a)
    units_b, dgpre_b, dupre_b = expert_units(expert_in, dy_rows, *full, cut, inner, down_a)
    down_b = rows_product(dy_rows, units_b)
    down_sum_a, down_sum_b = over_ctx(down_a), over_ctx(down_b)
    grads = (dgpre_a, dgpre_b, dupre_a, dupre_b, gate_one, up_one)
    left = expert_input_grad(*grads, 0, width // 2, down_b)
    right = expert_input_grad(*grads, width // 2, width, left)
    left, right = (part.reshape(blocks, cap, width // 2) for part in (left, right))
    [back] = combine(me, left, slot_col, seq_n, piece, right=right)
    gate_a = rows_product(expert_in, after(dgpre_a, back, down_sum_a))
    gate_b = rows_product(expert_in, after(dgpre_b, back))
    ypair = expert_down(units_a, units_b, down_one, gate_a)
    mixed_rows, dgate_plane = combine(
        me, ypair.reshape(blocks, cap, width), slot_col, seq_n, piece, row_gate, grad_plane
    )

    dgate_plane = dgate_plane.reshape(dp_n * y_n, seq_n, core_n, piece).transpose(0, 2, 1, 3)
    dgate_home = lax.all_to_all(
        dgate_plane.reshape(8, home), PLANE, split_axis=0, concat_axis=0, tiled=True
    ).reshape(dp_n, experts, home).sum(axis=0)

    logits = product(hidden_two, router)
    hot = home_routes[:, :, None] == jnp.arange(experts, dtype=jnp.int32)[None, None, :]
    gates = jax.nn.softmax(jnp.sum(jnp.where(hot, logits[None], 0.0), axis=2), axis=0)
    dgate = jnp.sum(jnp.where(hot, jnp.transpose(dgate_home)[None], 0.0), axis=2)
    dsel = gates * (dgate - jnp.sum(gates * dgate, axis=0, keepdims=True))
    dlogits = jnp.sum(jnp.where(hot, dsel[:, :, None], 0.0), axis=0).astype(bf16)
    router_grad = t_product(hidden_two, dlogits)
    dhidden_two = plane_scatter(back).reshape(home, width) + product_t(dlogits, router)

    flat_two = normed_two.reshape(home, width)
    dresid, expert_norm_grad = norm_backward(
        dhidden_two, flat_two, inverse_two.reshape(home, 1), expert_norm
    )
    dresid = dresid + grad_home.reshape(home, width).astype(f32)
    dbranch = chip_gather(dresid.astype(bf16).reshape(seq_n, piece, width), 1, parts).reshape(length, width)
    column_start = (r_i * core_n + core_i) * columns
    dbranch_here = lax.dynamic_slice_in_dim(dbranch, column_start, columns, 1)
    dmixed = chip_scatter(product_t(dbranch_here, weight_out).astype(bf16), 1, parts).astype(bf16)
    dqpre, dkpre, dvpre = attend_back(
        query, keys, values, mixed, dmixed, cosine, sine, seg_row, seg_col, heads, gate_b, down_sum_b
    )
    dqkv = jnp.concatenate([dqpre, dkpre, dvpre], axis=1)
    out_grad = t_product(mixed_full, after(dbranch_here, dqpre))
    dhidden_part = product_t(dqkv, weight_in).astype(bf16)
    in_grad = t_product(hidden_full, after(dqkv, dhidden_part)).astype(bf16)
    up_b = rows_product(expert_in, after(dupre_b, in_grad))
    up_a = rows_product(expert_in, after(dupre_a, in_grad))

    grad_down = jnp.concatenate([down_sum_a, down_sum_b], axis=1).astype(f32).T[None]
    grad_gate = jnp.concatenate([over_ctx(gate_a), over_ctx(gate_b)], axis=1).astype(f32)[None]
    grad_up = jnp.concatenate([over_ctx(up_a), over_ctx(up_b)], axis=1).astype(f32)[None]

    dhidden_one = chip_scatter(
        dhidden_part.reshape(seq_n, parts * piece, width), 1, parts
    )
    normed_one = token_float * inverse_one
    dtokens, attn_norm_grad = norm_backward(
        dhidden_one.reshape(home, width),
        normed_one.reshape(home, width),
        inverse_one.reshape(home, 1),
        attn_norm,
    )
    grad_tokens = from_sequences((dtokens + dresid).astype(bf16).reshape(seq_n, piece, width)).astype(f32)

    mixture = plane_scatter(after(mixed_rows, dbranch))
    output = from_sequences((residual + mixture).astype(bf16))

    def seen(part):
        return part.reshape(dp_n, seq_n, r_n, y_n, core_n * rows_here, -1)

    def half(a, axis, index, name):
        keep, give = pick(a, index, axis), pick(a, 1 - index, axis)
        return (keep.astype(f32) + swap(give, name).astype(f32)).astype(bf16)

    def over_plane(a, b):
        a, b = half(seen(a), 0, dp_i, "dp"), half(seen(b), 3, y_i, "y")
        return half(a, 2, y_i, "y"), half(b, 0, dp_i, "dp")

    def over_seq(a):
        return sum(piece.astype(f32) for piece in seq_pieces(a)).astype(bf16)

    def to_rows(a):
        a = a.reshape(parts, rows_here, -1, 1, columns)
        return chip_exchange(a, 0, 3, parts).reshape(rows_here, -1, width).astype(f32)

    one, two = over_plane(in_grad[:, : 3 * columns // 2], in_grad[:, 3 * columns // 2 :])
    inward = to_rows(over_seq(jnp.concatenate([one, two], axis=-1)))
    one, two = over_plane(*jnp.split(out_grad.astype(bf16), 2, axis=1))
    outward = to_rows(over_seq(jnp.concatenate([one, two], axis=-1)))
    grad_output = outward[:, 0]
    grad_query, grad_key, grad_value = (inward[:, i] for i in range(3))

    gains = jnp.concatenate([attn_norm_grad[None], expert_norm_grad[None], router_grad.T], axis=0)
    gain_n = gains.shape[0]
    gains = gains.reshape(gain_n, -1, rows_here).transpose(1, 0, 2)
    gains = lax.all_to_all(gains, EVERY, split_axis=0, concat_axis=0, tiled=True)
    gains = jnp.sum(gains, axis=0).T

    return (
        output,
        grad_tokens,
        gains[:, 0],
        grad_query,
        grad_key,
        grad_value,
        grad_output,
        gains[:, 1],
        gains[:, 2:],
        grad_gate,
        grad_up,
        grad_down,
    )


def solution(mesh):
    dp_n, ctx_n, exp_n = mesh.shape["dp"], mesh.shape["ctx"], mesh.shape["exp"]

    def block(*arrays):
        tokens = arrays[0]
        seq_count = tokens.shape[0] // (dp_n * exp_n)
        seq_n = seq_count * CORES
        sizes = (dp_n, seq_n, ctx_n // seq_n, exp_n // CORES, CORES)
        fine = Mesh(mesh.devices.reshape(sizes), EVERY)
        group = ("dp", "y", "core")
        exp = ("y", "core")
        return jax.shard_map(
            functools.partial(on_device, sizes),
            mesh=fine,
            in_specs=(
                P(group, CTX, None),
                P(group, None),
                P(group, CTX, None),
                P(),
                P(EVERY, None),
                P(EVERY, None),
                P(EVERY, None),
                P(EVERY, None),
                P(),
                P(),
                P(exp, None, "dp"),
                P(exp, None, "dp"),
                P(exp, "dp", None),
                P(group, CTX, None),
            ),
            out_specs=(
                P(group, CTX, None),
                P(group, CTX, None),
                P(EVERY),
                P(EVERY, None),
                P(EVERY, None),
                P(EVERY, None),
                P(EVERY, None),
                P(EVERY),
                P(EVERY, None),
                P(exp, CTX, "dp"),
                P(exp, CTX, "dp"),
                P(exp, "dp", CTX),
            ),
            check_vma=False,
        )(*arrays)

    return block
```

```python
import functools

import jax
import jax.numpy as jnp
from jax import lax
from jax.experimental import pallas as pl
from jax.experimental.pallas import tpu as pltpu
from jax.sharding import Mesh, PartitionSpec as P

HEADS = 16
CORES = 2

epsilon = 1e-05
theta_base = 10000.0
masked_score = -1e30
bf16 = jnp.bfloat16
f32 = jnp.float32

PLANE = ("dp", "y", "core")
CHIP = ("r", "core")
SPREAD = ("dp", "seq", "y")
CTX = ("seq", "r")
EVERY = ("dp", "seq", "r", "y", "core")


def product(a, b):
    return jnp.dot(a, b, preferred_element_type=f32)


def product_t(a, b):
    return lax.dot_general(a, b, (((1,), (1,)), ((), ())), preferred_element_type=f32)


def t_product(a, b):
    return lax.dot_general(a, b, (((0,), (0,)), ((), ())), preferred_element_type=f32)


def swap(a, axis):
    return lax.ppermute(a, axis, [(0, 1), (1, 0)])


def halves(a, axis):
    size = a.shape[axis] // 2
    me = lax.axis_index("core")
    mine = lax.dynamic_slice_in_dim(a, me * size, size, axis)
    other = lax.dynamic_slice_in_dim(a, (1 - me) * size, size, axis)
    return mine, other


def by_core(mine, other, axis):
    first = lax.axis_index("core") == 0
    return jnp.concatenate([jnp.where(first, mine, other), jnp.where(first, other, mine)], axis=axis)


def chip_gather(a, axis, parts):
    if parts == 2:
        return by_core(a, swap(a, "core"), axis)
    return lax.all_gather(a, CHIP, axis=axis, tiled=True)


def chip_scatter(a, axis, parts):
    if parts == 2:
        mine, other = halves(a, axis)
        return mine.astype(f32) + swap(other, "core").astype(f32)
    return lax.psum_scatter(a, CHIP, scatter_dimension=axis, tiled=True).astype(f32)


def chip_exchange(a, split, concat, parts):
    if parts == 2:
        mine, other = halves(a, split)
        return by_core(mine, swap(other, "core"), concat)
    return lax.all_to_all(a, CHIP, split_axis=split, concat_axis=concat, tiled=True)


def core_exchange(a, split, concat):
    mine, other = halves(a, split)
    return by_core(mine, swap(other, "core"), concat)


def seq_pieces(a):
    count = a.shape[0]
    me = lax.axis_index("seq")
    pieces = [pick(a, me, 0)]
    for step in range(1, count):
        give = pick(a, lax.rem(me + step, count), 0)
        pieces.append(lax.ppermute(give, "seq", [(i, (i + step) % count) for i in range(count)]))
    return pieces


def seq_exchange(a):
    count = a.shape[0]
    me = lax.axis_index("seq")
    pieces = jnp.stack(seq_pieces(a))
    return jnp.stack([pick(pieces, lax.rem(me + count - s, count), 0) for s in range(count)])


def to_sequences(a):
    return seq_exchange(core_exchange(a, 1, 0))


def from_sequences(a):
    return core_exchange(seq_exchange(a), 0, 1)


def total(*parts):
    return sum(part.astype(f32) for part in parts)


def plane_scatter(blocks, check=lambda stage, *arrays: arrays):
    held = total(blocks[:, :, 0], swap(blocks[:, :, 1], "core")).astype(bf16)
    [held] = check(0, held)
    half = blocks.shape[3] // 2
    by_x = swap(held[1, 1, :half], "dp")
    by_y = swap(held[1, 1, half:], "y")
    to_x = jnp.concatenate([held[1, 0, :half], total(held[1, 0, half:], by_y).astype(bf16)], axis=0)
    to_y = jnp.concatenate([total(held[0, 1, :half], by_x).astype(bf16), held[0, 1, half:]], axis=0)
    to_x, to_y = check(1, to_x, to_y)
    return total(held[0, 0], swap(to_x, "dp"), swap(to_y, "y"))


MESH = pl.DeviceIdType.MESH
Z_UP, Z_DOWN, X_A, Y_A, Y_B, X_B, Y_A2, X_B2 = range(8)


def first_kernel(
    query,
    key,
    value,
    output,
    tokens,
    grads,
    segments,
    weights,
    tokens_out,
    grads_out,
    segments_out,
    send,
    recv,
    core_send,
    core_recv,
    core_local,
    row_send,
    row_recv,
    row_local,
):
    dp, z, y, core = (lax.axis_index(a) for a in ("dp", "seq", "y", "core"))
    seq_n = weights.shape[1]
    rows, columns = query.shape[0], weights.shape[4] // 4
    half = weights.shape[4] // 2
    piece = tokens_out.shape[1]
    x_next, y_next, z_next, z_last, other = (
        {"dp": 1 - dp},
        {"y": 1 - y},
        {"seq": lax.rem(z + 1, seq_n)},
        {"seq": lax.rem(z + seq_n - 1, seq_n)},
        {"core": 1 - core},
    )

    barrier = pltpu.get_barrier_semaphore()
    partners = [x_next, y_next] + [
        {"seq": lax.rem(z + dz, seq_n), "core": lax.rem(core + dc, 2)}
        for dz in range(seq_n)
        for dc in range(2)
        if dz or dc
    ]
    for partner in partners:
        pl.semaphore_signal(barrier, inc=1, device_id=partner, device_id_type=MESH)
    pl.semaphore_wait(barrier, len(partners))

    here = pl.ds(pl.multiple_of(core * rows, rows), rows)
    locals_, remotes = [], []
    for m, matrix in enumerate((query, key, value, output)):
        place = weights.at[dp, z, y, here, pl.ds(m * columns, columns)]
        mine = matrix.at[:, pl.ds(pl.multiple_of(core * columns, columns), columns)]
        theirs = matrix.at[:, pl.ds(pl.multiple_of((1 - core) * columns, columns), columns)]
        locals_.append(pltpu.make_async_copy(mine, place, core_local.at[m]))
        remotes.append(
            pltpu.make_async_remote_copy(
                theirs, place, core_send.at[m], core_recv.at[m], device_id=other, device_id_type=MESH
            )
        )
    segment_local = pltpu.make_async_copy(segments, segments_out.at[core], core_local.at[4])
    segment_remote = pltpu.make_async_remote_copy(
        segments, segments_out.at[core], core_send.at[4], core_recv.at[4], device_id=other, device_id_type=MESH
    )
    for copy in remotes + [segment_remote] + locals_ + [segment_local]:
        copy.start()
    for copy in remotes + locals_:
        copy.wait()

    def part(kind, dp_b, z_b, y_b, device):
        if kind in (Z_UP, Z_DOWN):
            ref = weights.at[dp_b, z_b, y_b]
        else:
            start = 0 if kind in (X_A, Y_A, Y_A2) else half
            ref = weights.at[dp_b, z_b, y_b, :, pl.ds(start, half)]
        return pltpu.make_async_remote_copy(
            ref, ref, send.at[kind, z_b], recv.at[kind, z_b], device_id=device, device_id_type=MESH
        )

    def own(kind, z_b):
        device = {Z_UP: z_next, Z_DOWN: z_last, X_A: x_next, X_B: x_next, Y_A: y_next, Y_B: y_next}[kind]
        return part(kind, dp, z_b, y, device)

    def from_x(kind, z_b):
        return part(kind, 1 - dp, z_b, y, x_next)

    def from_y(kind, z_b):
        return part(kind, dp, z_b, 1 - y, y_next)

    def on_y(z_b):
        return part(Y_A2, 1 - dp, z_b, y, y_next)

    def on_x(z_b):
        return part(X_B2, dp, z_b, 1 - y, x_next)

    def spread(z_b):
        for kind in (X_A, Y_B, X_B, Y_A):
            own(kind, z_b).start()

    def relay(z_b):
        from_x(X_A, z_b).wait_recv()
        on_y(z_b).start()
        from_y(Y_B, z_b).wait_recv()
        on_x(z_b).start()

    def at_step(step, act_up, act_down):
        @pl.when(z - step >= 0)
        def _():
            act_up(z - step)

        @pl.when(z + step < seq_n)
        def _():
            act_down(z + step)

    def come_up(z_b):
        own(Z_UP, z_b).wait_recv()

        @pl.when(z < seq_n - 1)
        def _():
            own(Z_UP, z_b).start()

        spread(z_b)

    def come_down(z_b):
        own(Z_DOWN, z_b).wait_recv()

        @pl.when(z > 0)
        def _():
            own(Z_DOWN, z_b).start()

        spread(z_b)

    def rows_of(n, source, target, act):
        for s in range(tokens.shape[0]):
            z_to = tokens.shape[0] * core + s
            for d in range(2):
                core_to = lax.rem(core + d, 2)
                ref = source.at[s, pl.ds(pl.multiple_of(core_to * piece, piece), piece), :]
                copy = pltpu.make_async_remote_copy(
                    ref,
                    target.at[z],
                    row_send.at[n, s, d],
                    row_recv.at[n, z],
                    device_id={"seq": z_to, "core": core_to},
                    device_id_type=MESH,
                )
                if d:
                    act(copy)
                else:
                    keep = pltpu.make_async_copy(ref, target.at[z], row_local.at[n])

                    @pl.when(z_to != z)
                    def _(copy=copy):
                        act(copy)

                    @pl.when(z_to == z)
                    def _(keep=keep):
                        if act is begin:
                            keep.start()
                        else:
                            keep.wait()

    def begin(copy):
        copy.start()

    def sent(copy):
        copy.wait_send()

    def rows_in(n, target):
        group = z // tokens.shape[0]
        for z_from in range(seq_n):
            copy = pltpu.make_async_remote_copy(
                target.at[z_from],
                target.at[z_from],
                row_send.at[n, 0, 0],
                row_recv.at[n, z_from],
                device_id=other,
                device_id_type=MESH,
            )

            @pl.when((z_from != z) | (group != core))
            def _(copy=copy):
                copy.wait_recv()

    @pl.when(z < seq_n - 1)
    def _():
        own(Z_UP, z).start()

    @pl.when(z > 0)
    def _():
        own(Z_DOWN, z).start()

    spread(z)
    for step in range(1, seq_n):
        at_step(step, come_up, come_down)
        if step == 1:
            relay(z)
        else:
            at_step(step - 1, relay, relay)
        if step == seq_n - 2:
            rows_of(0, tokens, tokens_out, begin)
    rows_of(1, grads, grads_out, begin)
    at_step(seq_n - 1, relay, relay)

    segment_remote.wait()
    segment_local.wait()
    for z_b in range(seq_n):
        from_y(Y_A, z_b).wait_recv()
        from_x(X_B, z_b).wait_recv()
        part(Y_A2, 1 - dp, z_b, 1 - y, y_next).wait_recv()
        part(X_B2, 1 - dp, z_b, 1 - y, x_next).wait_recv()
        for kind in (X_A, Y_B, X_B, Y_A):
            own(kind, z_b).wait_send()
        on_y(z_b).wait_send()
        on_x(z_b).wait_send()

        @pl.when((z < seq_n - 1) & (z_b <= z))
        def _(z_b=z_b):
            own(Z_UP, z_b).wait_send()

        @pl.when((z > 0) & (z_b >= z))
        def _(z_b=z_b):
            own(Z_DOWN, z_b).wait_send()

    rows_of(0, tokens, tokens_out, sent)
    rows_of(1, grads, grads_out, sent)
    rows_in(0, tokens_out)
    rows_in(1, grads_out)


def first_transfers(query, key, value, output, tokens, grads, segments, sizes):
    dp_n, seq_n, r_n, y_n, core_n = sizes
    rows, width = query.shape
    piece = tokens.shape[1] // core_n
    columns = width // core_n
    held = pl.BlockSpec(memory_space=pl.ANY)
    out = jax.ShapeDtypeStruct((seq_n, piece, width), bf16)
    dma = pltpu.SemaphoreType.DMA
    weights, tokens, grads, segments = pl.pallas_call(
        first_kernel,
        in_specs=[held] * 7,
        out_specs=[held] * 4,
        out_shape=[
            jax.ShapeDtypeStruct((dp_n, seq_n, y_n, core_n * rows, 4 * columns), bf16),
            out,
            out,
            jax.ShapeDtypeStruct((core_n,) + segments.shape, segments.dtype),
        ],
        scratch_shapes=[
            dma((8, seq_n)),
            dma((8, seq_n)),
            dma((5,)),
            dma((5,)),
            dma((5,)),
            dma((2, tokens.shape[0], 2)),
            dma((2, seq_n)),
            dma((2,)),
        ],
        compiler_params=pltpu.CompilerParams(collective_id=0, has_side_effects=True),
        cost_estimate=pl.CostEstimate(flops=0, bytes_accessed=2 * 4 * columns * width, transcendentals=0),
        name="first_transfers",
    )(query, key, value, output, tokens, grads, segments)
    return weights.reshape(width, 4 * columns), tokens, grads, segments


def visible_block(seg_row, seg_col, start, rows, cols):
    row_place = start + lax.broadcasted_iota(jnp.int32, (rows, cols), 0)
    col_place = lax.broadcasted_iota(jnp.int32, (rows, cols), 1)
    return (seg_col == seg_row) & (col_place <= row_place)


def turned(u, cosine, sine):
    return u * cosine + pltpu.roll(u, u.shape[1] // 2, 1) * sine


def attend_kernel(scale, block, qp, kp, vp, cosine, sine, seg_row, seg_col, q_out, k_out, v_out, mixed):
    length = qp.shape[0]
    q_out[...] = turned(qp[...], cosine[...], sine[...]).astype(bf16)
    k_out[...] = turned(kp[...], cosine[...], sine[...]).astype(bf16)
    v_out[...] = vp[...].astype(bf16)
    for start in range(0, length, block):
        stop = start + block
        scores = product_t(q_out[start:stop, :], k_out[:stop, :]) * scale
        seen = visible_block(seg_row[:, :stop], seg_col[start:stop, :], start, block, stop)
        scores = jnp.where(seen, scores, masked_score)
        top = jnp.max(scores, axis=1, keepdims=True)
        weights = jnp.exp(scores - top)
        total = jnp.sum(weights, axis=1, keepdims=True)
        summed = product(weights.astype(bf16), v_out[:stop, :])
        mixed[start:stop, :] = (summed / total).astype(bf16)


def attend(qkv, cosine, sine, seg_row, seg_col, heads):
    length, head = qkv.shape[0], cosine.shape[1]
    block = min(256, length)

    def column(offset):
        return pl.BlockSpec((length, head), lambda h: (0, offset + h))

    def whole(shape):
        return pl.BlockSpec(shape, lambda h: (0, 0))

    out = jax.ShapeDtypeStruct((length, heads * head), bf16)
    pairs = length * (length + block) // 2 * heads
    return pl.pallas_call(
        functools.partial(attend_kernel, head**-0.5, block),
        grid=(heads,),
        in_specs=[
            column(0),
            column(heads),
            column(2 * heads),
            whole((length, head)),
            whole((length, head)),
            whole((1, length)),
            whole((length, 1)),
        ],
        out_specs=[column(0)] * 4,
        out_shape=[out] * 4,
        compiler_params=pltpu.CompilerParams(vmem_limit_bytes=48 * 2**20),
        cost_estimate=pl.CostEstimate(
            flops=4 * pairs * head, bytes_accessed=20 * length * heads * head, transcendentals=pairs
        ),
        name="attend",
    )(qkv, qkv, qkv, cosine, sine, seg_row, seg_col)


def attend_back_kernel(
    scale, block, q, k, v, mixed, dmixed, cosine, sine, seg_row, seg_col, *rest
):
    dq_out, dk_out, dv_out, dk_sum, dv_sum = rest[-5:]
    length = q.shape[0]
    dk_sum[...] = jnp.zeros_like(dk_sum)
    dv_sum[...] = jnp.zeros_like(dv_sum)
    for start in range(0, length, block):
        stop = start + block
        scores = product_t(q[start:stop, :], k[:stop, :]) * scale
        seen = visible_block(seg_row[:, :stop], seg_col[start:stop, :], start, block, stop)
        scores = jnp.where(seen, scores, masked_score)
        top = jnp.max(scores, axis=1, keepdims=True)
        weights = jnp.exp(scores - top)
        inverse = 1.0 / jnp.sum(weights, axis=1, keepdims=True)
        grad = dmixed[start:stop, :].astype(f32)
        delta = jnp.sum(grad * mixed[start:stop, :].astype(f32), axis=1, keepdims=True) * inverse
        unit = (grad * inverse).astype(bf16)
        dweights = product_t(unit, v[:stop, :])
        dscores = (weights * (dweights - delta)).astype(bf16)
        dq = product(dscores, k[:stop, :]) * scale
        dq_out[start:stop, :] = turned(dq, cosine[start:stop, :], -sine[start:stop, :]).astype(bf16)
        dk_sum[:stop, :] += t_product(dscores, q[start:stop, :])
        dv_sum[:stop, :] += t_product(weights.astype(bf16), unit)
    dk_out[...] = turned(dk_sum[...] * scale, cosine[...], -sine[...]).astype(bf16)
    dv_out[...] = dv_sum[...].astype(bf16)


def attend_back(q, k, v, mixed, dmixed, cosine, sine, seg_row, seg_col, heads, *before):
    length, head = q.shape[0], cosine.shape[1]
    block = min(256, length)
    column = pl.BlockSpec((length, head), lambda h: (0, h))

    def whole(shape):
        return pl.BlockSpec(shape, lambda h: (0, 0))

    out = jax.ShapeDtypeStruct((length, heads * head), bf16)
    pairs = length * (length + block) // 2 * heads
    return pl.pallas_call(
        functools.partial(attend_back_kernel, head**-0.5, block),
        grid=(heads,),
        in_specs=[column] * 5
        + [whole((length, head)), whole((length, head)), whole((1, length)), whole((length, 1))]
        + [pl.BlockSpec(memory_space=pl.ANY)] * len(before),
        out_specs=[column] * 3,
        out_shape=[out] * 3,
        scratch_shapes=[pltpu.VMEM((length, head), f32)] * 2,
        compiler_params=pltpu.CompilerParams(vmem_limit_bytes=48 * 2**20),
        cost_estimate=pl.CostEstimate(
            flops=10 * pairs * head, bytes_accessed=16 * length * heads * head, transcendentals=pairs
        ),
        name="attend_back",
    )(q, k, v, mixed, dmixed, cosine, sine, seg_row, seg_col, *before)


def units_kernel(chunk, x, dy, gate, up, down, *rest):
    units, dgate, dup = rest[-3:]
    gate_w, up_w, down_w = gate[...], up[...], down[...]

    def step(i, carry):
        rows = pl.ds(pl.multiple_of(i * chunk, chunk), chunk)
        gpre = product(x[rows, :], gate_w)
        upre = product(x[rows, :], up_w)
        dunits = product_t(dy[rows, :], down_w)
        s = jax.nn.sigmoid(gpre)
        silu = gpre * s
        units[rows, :] = (silu * upre).astype(bf16)
        dgate[rows, :] = (dunits * upre * (s * (1.0 + gpre * (1.0 - s)))).astype(bf16)
        dup[rows, :] = (dunits * silu).astype(bf16)
        return carry

    lax.fori_loop(0, x.shape[0] // chunk, step, 0)


def expert_units(x, dy, gate, up, down, start, stop, *before):
    rows, width = x.shape
    units = stop - start
    chunk = tile_of(rows)
    tile = unit_tile(gate.shape[1])
    first = start // tile
    once = pl.BlockSpec((rows, width), lambda j: (0, 0), pipeline_mode=pl.Buffered(1))
    out = jax.ShapeDtypeStruct((rows, units), bf16)
    return pl.pallas_call(
        functools.partial(units_kernel, chunk),
        grid=(units // tile,),
        in_specs=[
            once,
            once,
            pl.BlockSpec((width, tile), lambda j: (0, first + j)),
            pl.BlockSpec((width, tile), lambda j: (0, first + j)),
            pl.BlockSpec((tile, width), lambda j: (first + j, 0)),
        ]
        + [pl.BlockSpec(memory_space=pl.ANY)] * len(before),
        out_specs=[pl.BlockSpec((rows, tile), lambda j: (0, j))] * 3,
        out_shape=[out] * 3,
        compiler_params=pltpu.CompilerParams(vmem_limit_bytes=56 * 2**20),
        cost_estimate=pl.CostEstimate(
            flops=6 * rows * width * units,
            bytes_accessed=4 * rows * width + 6 * width * units + 6 * rows * units,
            transcendentals=rows * units,
        ),
        name="expert_units",
    )(x, dy, gate, up, down, *before)


def unit_tile(units):
    return 256 if units % 256 == 0 else units


def unit_cut(units):
    tile = unit_tile(units)
    return units // tile * 3 // 4 * tile


def dispatch_kernel(me, hidden, dout, slot, routes, router, rows, dy_rows, gate):
    size = hidden.shape[1] * hidden.shape[3]
    width = hidden.shape[4]
    mine = me[3]
    tokens = hidden[...].reshape(size, width)
    logits = product(tokens, router[...])
    lanes = lax.broadcasted_iota(jnp.int32, logits.shape, 1)
    first, second = routes[0, :, 0:1], routes[0, :, 1:2]
    one = jnp.sum(jnp.where(lanes == first, logits, 0.0), axis=1, keepdims=True)
    two = jnp.sum(jnp.where(lanes == second, logits, 0.0), axis=1, keepdims=True)
    top = jnp.maximum(one, two)
    one, two = jnp.exp(one - top), jnp.exp(two - top)
    share = jnp.where(first == mine, one, jnp.where(second == mine, two, 0.0)) / (one + two)
    gate[0] = share
    chosen = (
        lax.broadcasted_iota(jnp.int32, (rows.shape[1], size), 0) == slot[0]
    ).astype(bf16)
    rows[0] = product(chosen, tokens).astype(bf16)
    dy = (share * dout[...].reshape(size, width).astype(f32)).astype(bf16)
    dy_rows[0] = product(chosen, dy).astype(bf16)


def plane_block(seq_n, piece, width):
    return pl.BlockSpec((1, 2, 1, piece, width), lambda b, me: (b // seq_n, 0, b % seq_n, 0, 0))


def relative_block(seq_n, piece, width):
    return pl.BlockSpec(
        (1, 1, 2, 1, piece, width),
        lambda b, me: (
            lax.rem(b // (2 * seq_n) + me[0], 2),
            lax.rem(b // seq_n + me[1], 2),
            0,
            b % seq_n,
            0,
            0,
        ),
    )


def dispatch(me, hidden, dout, slot, routes, router, seq_n, piece, cap):
    blocks, size = slot.shape[0], slot.shape[2]
    width = hidden.shape[1]
    seen = (4, 2, seq_n, piece, width)
    each = pl.BlockSpec((1, cap, width), lambda b, me: (b, 0, 0))
    out = jax.ShapeDtypeStruct((blocks, cap, width), bf16)
    spare = jnp.zeros((width, 128 - router.shape[1]), router.dtype)
    return pl.pallas_call(
        dispatch_kernel,
        grid_spec=pltpu.PrefetchScalarGridSpec(
            num_scalar_prefetch=1,
            grid=(blocks,),
            in_specs=[
                plane_block(seq_n, piece, width),
                plane_block(seq_n, piece, width),
                pl.BlockSpec((1, 1, size), lambda b, me: (b, 0, 0)),
                pl.BlockSpec((1, size, routes.shape[2]), lambda b, me: (b, 0, 0)),
                pl.BlockSpec((width, 128), lambda b, me: (0, 0)),
            ],
            out_specs=[each, each, pl.BlockSpec((1, size, 1), lambda b, me: (b, 0, 0))],
        ),
        out_shape=[out, out, jax.ShapeDtypeStruct((blocks, size, 1), f32)],
        compiler_params=pltpu.CompilerParams(vmem_limit_bytes=40 * 2**20),
        cost_estimate=pl.CostEstimate(
            flops=4 * blocks * size * width * (cap + 64),
            bytes_accessed=4 * blocks * (size + cap) * width,
            transcendentals=2 * blocks * size,
        ),
        name="dispatch",
    )(
        me,
        hidden.reshape(seen),
        dout.reshape(seen),
        slot,
        routes,
        jnp.concatenate([router, spare], axis=1),
    )


def spread_rows(slot, rows):
    size, cap = slot.shape[0], rows.shape[0]
    chosen = (lax.broadcasted_iota(jnp.int32, (size, cap), 1) == slot).astype(bf16)
    return product(chosen, rows)


def place_cores(me, out, dense):
    piece = out.shape[4]
    for core in range(2):
        out[0, 0, lax.rem(me[2] + core, 2), 0] = dense[core * piece : (core + 1) * piece, :].astype(bf16)


def combine_kernel(me, rows, slot, gate, dout, out, dgate):
    dense = spread_rows(slot[0], rows[0])
    grads = dout[...].reshape(dense.shape).astype(f32)
    dgate[0] = jnp.sum(grads * dense, axis=1, keepdims=True)
    place_cores(me, out, gate[0] * dense)


def collect_kernel(me, left, slot, right, *rest):
    dense = [spread_rows(slot[0], left[0]), spread_rows(slot[0], right[0])]
    place_cores(me, rest[-1], jnp.concatenate(dense, axis=1))


def combine(me, rows, slot, seq_n, piece, gate=None, dout=None, right=None):
    blocks, cap, part = rows.shape
    size = slot.shape[1]
    width = part if right is None else 2 * part
    column = pl.BlockSpec((1, size, 1), lambda b, me: (b, 0, 0))
    weigh = gate is not None
    operands = [rows, slot]
    in_specs = [pl.BlockSpec((1, cap, part), lambda b, me: (b, 0, 0)), column]
    out_specs = [relative_block(seq_n, piece, width)]
    out_shape = [jax.ShapeDtypeStruct((2, 2, 2, seq_n, piece, width), bf16)]
    if weigh:
        operands += [gate, dout.reshape(4, 2, seq_n, piece, width)]
        in_specs += [column, plane_block(seq_n, piece, width)]
        out_specs += [column]
        out_shape += [jax.ShapeDtypeStruct((blocks, size, 1), f32)]
    else:
        operands += [right]
        in_specs += in_specs[:1]
    return pl.pallas_call(
        combine_kernel if weigh else collect_kernel,
        grid_spec=pltpu.PrefetchScalarGridSpec(
            num_scalar_prefetch=1, grid=(blocks,), in_specs=in_specs, out_specs=out_specs
        ),
        out_shape=out_shape,
        compiler_params=pltpu.CompilerParams(vmem_limit_bytes=40 * 2**20),
        cost_estimate=pl.CostEstimate(
            flops=2 * blocks * size * width * cap,
            bytes_accessed=2 * blocks * (2 * size + cap) * width,
            transcendentals=0,
        ),
        name="combine" if weigh else "collect",
    )(me, *operands)


def down_kernel(cut, units_a, units_b, down, *rest):
    total = product(units_a[...], down[:cut, :]) + product(units_b[...], down[cut:, :])
    rest[-1][...] = total.astype(bf16)


def expert_down(units_a, units_b, down, *before):
    rows, cut = units_a.shape
    inner, width = down.shape
    m, n = tile_of(rows), tile_of(width)
    return pl.pallas_call(
        functools.partial(down_kernel, cut),
        grid=(width // n, rows // m),
        in_specs=[
            pl.BlockSpec((m, cut), lambda j, i: (i, 0)),
            pl.BlockSpec((m, inner - cut), lambda j, i: (i, 0)),
            pl.BlockSpec((inner, n), lambda j, i: (0, j)),
        ]
        + [pl.BlockSpec(memory_space=pl.ANY)] * len(before),
        out_specs=pl.BlockSpec((m, n), lambda j, i: (i, j)),
        out_shape=jax.ShapeDtypeStruct((rows, width), bf16),
        compiler_params=pltpu.CompilerParams(vmem_limit_bytes=48 * 2**20),
        cost_estimate=pl.CostEstimate(
            flops=2 * rows * inner * width,
            bytes_accessed=2 * (rows * inner + inner * width + rows * width),
            transcendentals=0,
        ),
        name="expert_down",
    )(units_a, units_b, down, *before)


def input_kernel(cut, dgate_a, dgate_b, dup_a, dup_b, gate, up, *rest):
    total = product_t(dgate_a[...], gate[:, :cut]) + product_t(dgate_b[...], gate[:, cut:])
    total += product_t(dup_a[...], up[:, :cut]) + product_t(dup_b[...], up[:, cut:])
    rest[-1][...] = total.astype(bf16)


def expert_input_grad(dgate_a, dgate_b, dup_a, dup_b, gate, up, start, stop, *before):
    rows, cut = dgate_a.shape
    inner = gate.shape[1]
    width = stop - start
    m, n = tile_of(rows), tile_of(width)
    first = start // n
    left_a = pl.BlockSpec((m, cut), lambda j, i: (i, 0))
    left_b = pl.BlockSpec((m, inner - cut), lambda j, i: (i, 0))
    right = pl.BlockSpec((n, inner), lambda j, i: (first + j, 0))
    return pl.pallas_call(
        functools.partial(input_kernel, cut),
        grid=(width // n, rows // m),
        in_specs=[left_a, left_b, left_a, left_b, right, right]
        + [pl.BlockSpec(memory_space=pl.ANY)] * len(before),
        out_specs=pl.BlockSpec((m, n), lambda j, i: (i, j)),
        out_shape=jax.ShapeDtypeStruct((rows, width), bf16),
        compiler_params=pltpu.CompilerParams(vmem_limit_bytes=52 * 2**20),
        cost_estimate=pl.CostEstimate(
            flops=4 * rows * inner * width,
            bytes_accessed=2 * (2 * rows * inner + 2 * inner * width + rows * width),
            transcendentals=0,
        ),
        name="expert_input_grad",
    )(dgate_a, dgate_b, dup_a, dup_b, gate, up, *before)


def tile_of(size):
    return max(c for c in range(16, 513, 16) if size % c == 0)


def anchor_kernel(*refs):
    pass


def after(a, *before):
    return pl.pallas_call(
        anchor_kernel,
        in_specs=[pl.BlockSpec(memory_space=pl.ANY)] * (1 + len(before)),
        out_specs=pl.BlockSpec(memory_space=pl.ANY),
        out_shape=jax.ShapeDtypeStruct(a.shape, a.dtype),
        input_output_aliases={0: 0},
        cost_estimate=pl.CostEstimate(flops=0, bytes_accessed=0, transcendentals=0),
        name="after",
    )(a, *before)


def norm_backward(grad_rows, normed, inverse, gain):
    weighted = grad_rows * gain
    mean_term = jnp.mean(weighted * normed, axis=-1, keepdims=True)
    return inverse * (weighted - normed * mean_term), jnp.sum(grad_rows * normed, axis=0)


def pick(a, index, axis):
    return lax.dynamic_index_in_dim(a, index, axis, keepdims=False)


def on_device(
    sizes,
    tokens,
    segments,
    routes,
    attn_norm,
    query_weight,
    key_weight,
    value_weight,
    output_weight,
    expert_norm,
    router,
    gate_weight,
    up_weight,
    down_weight,
    grad_out,
):
    dp_n, seq_n, r_n, y_n, core_n = sizes
    parts = r_n * core_n
    seq_count, seq_dev, width = tokens.shape
    piece = seq_dev // core_n
    length = segments.shape[1]
    home = seq_n * piece
    head = width // HEADS
    heads = HEADS // parts
    columns = width // parts
    experts = router.shape[1]
    topk = routes.shape[2]
    plane = 8 * home
    blocks = plane // seq_dev
    cap = 5 * seq_dev * topk // (4 * experts)
    dp_i, seq_i, r_i, y_i, core_i = (lax.axis_index(a) for a in EVERY)
    group, member = seq_i // seq_count, seq_i % seq_count

    rows_here = query_weight.shape[0]
    if r_n == 1 and parts == 2 and dp_n == 2 and y_n == 2 and seq_n == 2 * seq_count:
        weights, token_home, grad_home, chip_segments = first_transfers(
            query_weight, key_weight, value_weight, output_weight, tokens, grad_out, segments, sizes
        )
        segment = pick(pick(chip_segments, group, 0), member, 0)
    else:
        local = jnp.concatenate([query_weight, key_weight, value_weight, output_weight], axis=1)
        local = chip_exchange(local.reshape(rows_here, 4, parts, columns), 2, 0, parts)
        weights = lax.all_gather(
            local.reshape(parts * rows_here, 4 * columns), SPREAD, axis=0, tiled=True
        )
        weights = (
            weights.reshape(dp_n * seq_n, y_n, r_n, core_n * rows_here, -1)
            .transpose(0, 2, 1, 3, 4)
            .reshape(width, -1)
        )
        token_home, grad_home = to_sequences(tokens), to_sequences(grad_out)
        chip_segments = lax.all_gather(segments, "core")
        segment = pick(pick(chip_segments, group, 0), member, 0)
    weight_in, weight_out = weights[:, : 3 * columns], weights[:, 3 * columns :]

    token_float = token_home.astype(f32)
    inverse_one = lax.rsqrt(jnp.mean(token_float * token_float, axis=-1, keepdims=True) + epsilon)
    hidden_one = (token_float * inverse_one * attn_norm).astype(bf16)
    hidden_full = chip_gather(hidden_one, 1, parts).reshape(length, width)

    grad_plane = lax.all_gather(grad_home.reshape(home, width), PLANE, axis=0, tiled=True)

    half = head // 2
    frequency = theta_base ** (-jnp.arange(half, dtype=f32) / half)
    angles = jnp.arange(length, dtype=f32)[:, None] * frequency[None, :]
    cosine = jnp.concatenate([jnp.cos(angles)] * 2, axis=1)
    sine = jnp.concatenate([-jnp.sin(angles), jnp.sin(angles)], axis=1)
    seg_row, seg_col = segment[None, :], segment[:, None]

    qkv = product(hidden_full, weight_in)
    query, keys, values, mixed = attend(qkv, cosine, sine, seg_row, seg_col, heads)
    mixed_full = chip_gather(mixed, 1, parts)
    branch = product(mixed_full, weight_out).reshape(seq_n, parts, piece, columns)
    branch = chip_exchange(branch, 1, 3, parts).reshape(seq_n, piece, width)
    residual = token_float + branch
    inverse_two = lax.rsqrt(jnp.mean(residual * residual, axis=-1, keepdims=True) + epsilon)
    normed_two = residual * inverse_two
    hidden_two = (normed_two * expert_norm).astype(bf16).reshape(home, width)

    hidden_plane = lax.all_gather(hidden_two, PLANE, axis=0, tiled=True)
    small = after(jnp.transpose(routes, (2, 0, 1)).reshape(topk * seq_count, seq_dev), hidden_two)
    small = lax.all_gather(small, EVERY, axis=0, tiled=True).reshape(
        dp_n, seq_n, r_n, y_n, core_n, topk, seq_count, seq_dev
    )
    small = pick(pick(small, group, 4), member, 5)
    plane_routes = pick(small, r_i, 2).transpose(0, 2, 1, 3, 4)
    block_routes = plane_routes.reshape(blocks, topk, seq_dev)
    home_routes = (
        pick(pick(plane_routes, dp_i, 0), y_i, 0)
        .reshape(seq_n, topk, core_n, piece)
        .transpose(1, 2, 0, 3)
    )
    home_routes = pick(home_routes, core_i, 1).reshape(topk, home)
    mine = y_i * core_n + core_i
    chosen = jnp.any(block_routes == mine, axis=1)
    places = jnp.arange(seq_dev)
    rank = product(chosen.astype(bf16), (places[:, None] < places[None, :]).astype(bf16))
    slot = jnp.where(chosen, rank.astype(jnp.int32), -1)
    slot_row, slot_col = slot[:, None, :], slot[:, :, None]
    me = jnp.stack([dp_i, y_i, core_i, mine]).astype(jnp.int32)
    expert_rows, dy_rows, row_gate = dispatch(
        me,
        hidden_plane,
        grad_plane,
        slot_row,
        jnp.transpose(block_routes, (0, 2, 1)),
        router,
        seq_n,
        piece,
        cap,
    )
    expert_in = expert_rows.reshape(blocks * cap, width)
    dy_rows = dy_rows.reshape(blocks * cap, width)

    gate_one, up_one, down_one = gate_weight[0], up_weight[0], down_weight[0]
    inner = gate_one.shape[1]
    cut = unit_cut(inner)
    full = (gate_one, up_one, down_one)

    def over_ctx(part):
        return lax.psum_scatter(part, CTX, scatter_dimension=0, tiled=True)

    def rows_product(rows, part):
        return t_product(rows, part).astype(bf16)

    units_a, dgpre_a, dupre_a = expert_units(expert_in, dy_rows, *full, 0, cut)
    down_a = rows_product(dy_rows, units_a)
    units_b, dgpre_b, dupre_b = expert_units(expert_in, dy_rows, *full, cut, inner, down_a)
    down_b = rows_product(dy_rows, units_b)
    down_sum_a, down_sum_b = over_ctx(down_a), over_ctx(down_b)
    grads = (dgpre_a, dgpre_b, dupre_a, dupre_b, gate_one, up_one)
    left = expert_input_grad(*grads, 0, width // 2, down_b)
    right = expert_input_grad(*grads, width // 2, width, left)
    left, right = (part.reshape(blocks, cap, width // 2) for part in (left, right))
    [back] = combine(me, left, slot_col, seq_n, piece, right=right)
    gate_a = rows_product(expert_in, after(dgpre_a, back, down_sum_a))
    gate_b = rows_product(expert_in, after(dgpre_b, back))
    gate_sum_a, gate_sum_b = over_ctx(gate_a), over_ctx(gate_b)
    ypair = expert_down(units_a, units_b, down_one, gate_a)
    mixed_rows, dgate_plane = combine(
        me, ypair.reshape(blocks, cap, width), slot_col, seq_n, piece, row_gate, grad_plane
    )

    dgate_plane = dgate_plane.reshape(dp_n * y_n, seq_n, core_n, piece).transpose(0, 2, 1, 3)
    dgate_home = lax.all_to_all(
        dgate_plane.reshape(8, home), PLANE, split_axis=0, concat_axis=0, tiled=True
    ).reshape(dp_n, experts, home).sum(axis=0)

    logits = product(hidden_two, router)
    hot = home_routes[:, :, None] == jnp.arange(experts, dtype=jnp.int32)[None, None, :]
    gates = jax.nn.softmax(jnp.sum(jnp.where(hot, logits[None], 0.0), axis=2), axis=0)
    dgate = jnp.sum(jnp.where(hot, jnp.transpose(dgate_home)[None], 0.0), axis=2)
    dsel = gates * (dgate - jnp.sum(gates * dgate, axis=0, keepdims=True))
    dlogits = jnp.sum(jnp.where(hot, dsel[:, :, None], 0.0), axis=0).astype(bf16)
    router_grad = t_product(hidden_two, dlogits)
    dhidden_two = plane_scatter(back).reshape(home, width) + product_t(dlogits, router)

    flat_two = normed_two.reshape(home, width)
    dresid, expert_norm_grad = norm_backward(
        dhidden_two, flat_two, inverse_two.reshape(home, 1), expert_norm
    )
    dresid = dresid + grad_home.reshape(home, width).astype(f32)
    dbranch = chip_gather(dresid.astype(bf16).reshape(seq_n, piece, width), 1, parts).reshape(length, width)
    column_start = (r_i * core_n + core_i) * columns
    dbranch_here = lax.dynamic_slice_in_dim(dbranch, column_start, columns, 1)
    dmixed = chip_scatter(product_t(dbranch_here, weight_out).astype(bf16), 1, parts).astype(bf16)
    stages = {}

    def check(stage, *arrays):
        stages[stage] = arrays
        return arrays

    mixture = plane_scatter(after(mixed_rows, dbranch), check)
    dqpre, dkpre, dvpre = attend_back(
        query, keys, values, mixed, dmixed, cosine, sine, seg_row, seg_col, heads, down_sum_b, *stages[0]
    )
    dqkv = jnp.concatenate([dqpre, dkpre, dvpre], axis=1)
    dqkv = after(dqkv, gate_sum_a)
    dhidden_part = product_t(dqkv, weight_in).astype(bf16)
    in_grad = t_product(hidden_full, after(dqkv, dhidden_part, *stages[1])).astype(bf16)
    dhidden_one = chip_scatter(
        dhidden_part.reshape(seq_n, parts * piece, width), 1, parts
    )
    normed_one = token_float * inverse_one
    dtokens, attn_norm_grad = norm_backward(
        dhidden_one.reshape(home, width),
        normed_one.reshape(home, width),
        inverse_one.reshape(home, 1),
        attn_norm,
    )
    dtokens = (dtokens + dresid).astype(bf16).reshape(seq_n, piece, width)
    out_grad = t_product(mixed_full, after(dbranch_here, in_grad)).astype(bf16)
    up_b = rows_product(expert_in, after(dupre_b, out_grad, dtokens))
    output = (residual + mixture).astype(bf16)
    up_a = rows_product(expert_in, after(dupre_a, out_grad, output))

    grad_down = jnp.concatenate([down_sum_a, down_sum_b], axis=1).astype(f32).T[None]
    grad_gate = jnp.concatenate([gate_sum_a, gate_sum_b], axis=1).astype(f32)[None]
    grad_up = jnp.concatenate([over_ctx(up_a), over_ctx(up_b)], axis=1).astype(f32)[None]

    def seen(part):
        return part.reshape(dp_n, seq_n, r_n, y_n, core_n * rows_here, -1)

    def half(a, axis, index, name):
        keep, give = pick(a, index, axis), pick(a, 1 - index, axis)
        return total(keep, swap(give, name)).astype(bf16)

    first = [half(seen(a), 0, dp_i, "dp") for a in (out_grad, in_grad[:, :columns])]
    first.append(half(seen(in_grad[:, columns:]), 3, y_i, "y"))
    second = [half(a, 2, y_i, "y") for a in first[:2]] + [half(first[2], 0, dp_i, "dp")]
    grad_tokens = from_sequences(dtokens)
    output = from_sequences(output)
    part = total(*seq_pieces(jnp.concatenate(second, axis=-1))).astype(bf16)
    part = part.reshape(parts, rows_here, 4, 1, columns)
    part = chip_exchange(part, 0, 3, parts).reshape(rows_here, 4, width).astype(f32)
    grad_output, grad_query, grad_key, grad_value = (part[:, i] for i in range(4))
    grad_tokens = grad_tokens.astype(f32)

    gains = jnp.concatenate([attn_norm_grad[None], expert_norm_grad[None], router_grad.T], axis=0)
    gain_n = gains.shape[0]
    gains = gains.reshape(gain_n, -1, rows_here).transpose(1, 0, 2)
    gains = lax.all_to_all(gains, EVERY, split_axis=0, concat_axis=0, tiled=True)
    gains = jnp.sum(gains, axis=0).T

    return (
        output,
        grad_tokens,
        gains[:, 0],
        grad_query,
        grad_key,
        grad_value,
        grad_output,
        gains[:, 1],
        gains[:, 2:],
        grad_gate,
        grad_up,
        grad_down,
    )


def solution(mesh):
    dp_n, ctx_n, exp_n = mesh.shape["dp"], mesh.shape["ctx"], mesh.shape["exp"]

    def block(*arrays):
        tokens = arrays[0]
        seq_count = tokens.shape[0] // (dp_n * exp_n)
        seq_n = seq_count * CORES
        sizes = (dp_n, seq_n, ctx_n // seq_n, exp_n // CORES, CORES)
        fine = Mesh(mesh.devices.reshape(sizes), EVERY)
        group = ("dp", "y", "core")
        exp = ("y", "core")
        return jax.shard_map(
            functools.partial(on_device, sizes),
            mesh=fine,
            in_specs=(
                P(group, CTX, None),
                P(group, None),
                P(group, CTX, None),
                P(),
                P(EVERY, None),
                P(EVERY, None),
                P(EVERY, None),
                P(EVERY, None),
                P(),
                P(),
                P(exp, None, "dp"),
                P(exp, None, "dp"),
                P(exp, "dp", None),
                P(group, CTX, None),
            ),
            out_specs=(
                P(group, CTX, None),
                P(group, CTX, None),
                P(EVERY),
                P(EVERY, None),
                P(EVERY, None),
                P(EVERY, None),
                P(EVERY, None),
                P(EVERY),
                P(EVERY, None),
                P(exp, CTX, "dp"),
                P(exp, CTX, "dp"),
                P(exp, "dp", CTX),
            ),
            check_vma=False,
        )(*arrays)

    return block
```

```python
import functools

import jax
import jax.numpy as jnp
from jax import lax
from jax.experimental import pallas as pl
from jax.experimental.pallas import tpu as pltpu
from jax.sharding import Mesh, PartitionSpec as P

HEADS = 16
CORES = 2

epsilon = 1e-05
theta_base = 10000.0
masked_score = -1e30
bf16 = jnp.bfloat16
f32 = jnp.float32

PLANE = ("dp", "y", "core")
CHIP = ("r", "core")
SPREAD = ("dp", "seq", "y")
CTX = ("seq", "r")
EVERY = ("dp", "seq", "r", "y", "core")


def product(a, b):
    return jnp.dot(a, b, preferred_element_type=f32)


def product_t(a, b):
    return lax.dot_general(a, b, (((1,), (1,)), ((), ())), preferred_element_type=f32)


def t_product(a, b):
    return lax.dot_general(a, b, (((0,), (0,)), ((), ())), preferred_element_type=f32)


def swap(a, axis):
    return lax.ppermute(a, axis, [(0, 1), (1, 0)])


def halves(a, axis):
    size = a.shape[axis] // 2
    me = lax.axis_index("core")
    mine = lax.dynamic_slice_in_dim(a, me * size, size, axis)
    other = lax.dynamic_slice_in_dim(a, (1 - me) * size, size, axis)
    return mine, other


def by_core(mine, other, axis):
    first = lax.axis_index("core") == 0
    return jnp.concatenate([jnp.where(first, mine, other), jnp.where(first, other, mine)], axis=axis)


def chip_gather(a, axis, parts):
    if parts == 2:
        return by_core(a, swap(a, "core"), axis)
    return lax.all_gather(a, CHIP, axis=axis, tiled=True)


def chip_scatter(a, axis, parts):
    if parts == 2:
        mine, other = halves(a, axis)
        return mine.astype(f32) + swap(other, "core").astype(f32)
    return lax.psum_scatter(a, CHIP, scatter_dimension=axis, tiled=True).astype(f32)


def chip_exchange(a, split, concat, parts):
    if parts == 2:
        mine, other = halves(a, split)
        return by_core(mine, swap(other, "core"), concat)
    return lax.all_to_all(a, CHIP, split_axis=split, concat_axis=concat, tiled=True)


def core_exchange(a, split, concat):
    mine, other = halves(a, split)
    return by_core(mine, swap(other, "core"), concat)


def seq_pieces(a):
    count = a.shape[0]
    me = lax.axis_index("seq")
    pieces = [pick(a, me, 0)]
    for step in range(1, count):
        give = pick(a, lax.rem(me + step, count), 0)
        pieces.append(lax.ppermute(give, "seq", [(i, (i + step) % count) for i in range(count)]))
    return pieces


def seq_exchange(a):
    count = a.shape[0]
    me = lax.axis_index("seq")
    pieces = jnp.stack(seq_pieces(a))
    return jnp.stack([pick(pieces, lax.rem(me + count - s, count), 0) for s in range(count)])


def to_sequences(a):
    return seq_exchange(core_exchange(a, 1, 0))


def from_sequences(a):
    return core_exchange(seq_exchange(a), 0, 1)


def total(*parts):
    return sum(part.astype(f32) for part in parts)


def plane_scatter(blocks, check=lambda stage, *arrays: arrays):
    held = total(blocks[:, :, 0], swap(blocks[:, :, 1], "core")).astype(bf16)
    [held] = check(0, held)
    half = blocks.shape[3] // 2
    by_x = swap(held[1, 1, :half], "dp")
    by_y = swap(held[1, 1, half:], "y")
    to_x = jnp.concatenate([held[1, 0, :half], total(held[1, 0, half:], by_y).astype(bf16)], axis=0)
    to_y = jnp.concatenate([total(held[0, 1, :half], by_x).astype(bf16), held[0, 1, half:]], axis=0)
    to_x, to_y = check(1, to_x, to_y)
    return total(held[0, 0], swap(to_x, "dp"), swap(to_y, "y"))


MESH = pl.DeviceIdType.MESH
Z_UP, Z_DOWN, X_A, Y_A, Y_B, X_B, Y_A2, X_B2 = range(8)


def first_kernel(
    query,
    key,
    value,
    output,
    tokens,
    grads,
    segments,
    weights,
    tokens_out,
    grads_out,
    segments_out,
    send,
    recv,
    core_send,
    core_recv,
    core_local,
    row_send,
    row_recv,
    row_local,
):
    dp, z, y, core = (lax.axis_index(a) for a in ("dp", "seq", "y", "core"))
    seq_n = weights.shape[1]
    rows, columns = query.shape[0], weights.shape[4] // 4
    half = weights.shape[4] // 2
    piece = tokens_out.shape[1]
    x_next, y_next, z_next, z_last, other = (
        {"dp": 1 - dp},
        {"y": 1 - y},
        {"seq": lax.rem(z + 1, seq_n)},
        {"seq": lax.rem(z + seq_n - 1, seq_n)},
        {"core": 1 - core},
    )

    barrier = pltpu.get_barrier_semaphore()
    partners = [x_next, y_next] + [
        {"seq": lax.rem(z + dz, seq_n), "core": lax.rem(core + dc, 2)}
        for dz in range(seq_n)
        for dc in range(2)
        if dz or dc
    ]
    for partner in partners:
        pl.semaphore_signal(barrier, inc=1, device_id=partner, device_id_type=MESH)
    pl.semaphore_wait(barrier, len(partners))

    here = pl.ds(pl.multiple_of(core * rows, rows), rows)
    locals_, remotes = [], []
    for m, matrix in enumerate((query, key, value, output)):
        place = weights.at[dp, z, y, here, pl.ds(m * columns, columns)]
        mine = matrix.at[:, pl.ds(pl.multiple_of(core * columns, columns), columns)]
        theirs = matrix.at[:, pl.ds(pl.multiple_of((1 - core) * columns, columns), columns)]
        locals_.append(pltpu.make_async_copy(mine, place, core_local.at[m]))
        remotes.append(
            pltpu.make_async_remote_copy(
                theirs, place, core_send.at[m], core_recv.at[m], device_id=other, device_id_type=MESH
            )
        )
    segment_local = pltpu.make_async_copy(segments, segments_out.at[core], core_local.at[4])
    segment_remote = pltpu.make_async_remote_copy(
        segments, segments_out.at[core], core_send.at[4], core_recv.at[4], device_id=other, device_id_type=MESH
    )
    for copy in remotes + [segment_remote] + locals_ + [segment_local]:
        copy.start()
    for copy in remotes + locals_:
        copy.wait()

    def part(kind, dp_b, z_b, y_b, device):
        if kind in (Z_UP, Z_DOWN):
            ref = weights.at[dp_b, z_b, y_b]
        else:
            start = 0 if kind in (X_A, Y_A, Y_A2) else half
            ref = weights.at[dp_b, z_b, y_b, :, pl.ds(start, half)]
        return pltpu.make_async_remote_copy(
            ref, ref, send.at[kind, z_b], recv.at[kind, z_b], device_id=device, device_id_type=MESH
        )

    def own(kind, z_b):
        device = {Z_UP: z_next, Z_DOWN: z_last, X_A: x_next, X_B: x_next, Y_A: y_next, Y_B: y_next}[kind]
        return part(kind, dp, z_b, y, device)

    def from_x(kind, z_b):
        return part(kind, 1 - dp, z_b, y, x_next)

    def from_y(kind, z_b):
        return part(kind, dp, z_b, 1 - y, y_next)

    def on_y(z_b):
        return part(Y_A2, 1 - dp, z_b, y, y_next)

    def on_x(z_b):
        return part(X_B2, dp, z_b, 1 - y, x_next)

    def spread(z_b):
        for kind in (X_A, Y_B, X_B, Y_A):
            own(kind, z_b).start()

    def relay(z_b):
        from_x(X_A, z_b).wait_recv()
        on_y(z_b).start()
        from_y(Y_B, z_b).wait_recv()
        on_x(z_b).start()

    def at_step(step, act_up, act_down):
        @pl.when(z - step >= 0)
        def _():
            act_up(z - step)

        @pl.when(z + step < seq_n)
        def _():
            act_down(z + step)

    def come_up(z_b):
        own(Z_UP, z_b).wait_recv()

        @pl.when(z < seq_n - 1)
        def _():
            own(Z_UP, z_b).start()

        spread(z_b)

    def come_down(z_b):
        own(Z_DOWN, z_b).wait_recv()

        @pl.when(z > 0)
        def _():
            own(Z_DOWN, z_b).start()

        spread(z_b)

    def rows_of(n, source, target, act):
        for s in range(tokens.shape[0]):
            z_to = tokens.shape[0] * core + s
            for d in range(2):
                core_to = lax.rem(core + d, 2)
                ref = source.at[s, pl.ds(pl.multiple_of(core_to * piece, piece), piece), :]
                copy = pltpu.make_async_remote_copy(
                    ref,
                    target.at[z],
                    row_send.at[n, s, d],
                    row_recv.at[n, z],
                    device_id={"seq": z_to, "core": core_to},
                    device_id_type=MESH,
                )
                if d:
                    act(copy)
                else:
                    keep = pltpu.make_async_copy(ref, target.at[z], row_local.at[n])

                    @pl.when(z_to != z)
                    def _(copy=copy):
                        act(copy)

                    @pl.when(z_to == z)
                    def _(keep=keep):
                        if act is begin:
                            keep.start()
                        else:
                            keep.wait()

    def begin(copy):
        copy.start()

    def sent(copy):
        copy.wait_send()

    def rows_in(n, target):
        group = z // tokens.shape[0]
        for z_from in range(seq_n):
            copy = pltpu.make_async_remote_copy(
                target.at[z_from],
                target.at[z_from],
                row_send.at[n, 0, 0],
                row_recv.at[n, z_from],
                device_id=other,
                device_id_type=MESH,
            )

            @pl.when((z_from != z) | (group != core))
            def _(copy=copy):
                copy.wait_recv()

    @pl.when(z < seq_n - 1)
    def _():
        own(Z_UP, z).start()

    @pl.when(z > 0)
    def _():
        own(Z_DOWN, z).start()

    spread(z)
    for step in range(1, seq_n):
        at_step(step, come_up, come_down)
        if step == 1:
            relay(z)
        else:
            at_step(step - 1, relay, relay)
        if step == seq_n - 2:
            rows_of(0, tokens, tokens_out, begin)
    rows_of(1, grads, grads_out, begin)
    at_step(seq_n - 1, relay, relay)

    segment_remote.wait()
    segment_local.wait()
    for z_b in range(seq_n):
        from_y(Y_A, z_b).wait_recv()
        from_x(X_B, z_b).wait_recv()
        part(Y_A2, 1 - dp, z_b, 1 - y, y_next).wait_recv()
        part(X_B2, 1 - dp, z_b, 1 - y, x_next).wait_recv()
        for kind in (X_A, Y_B, X_B, Y_A):
            own(kind, z_b).wait_send()
        on_y(z_b).wait_send()
        on_x(z_b).wait_send()

        @pl.when((z < seq_n - 1) & (z_b <= z))
        def _(z_b=z_b):
            own(Z_UP, z_b).wait_send()

        @pl.when((z > 0) & (z_b >= z))
        def _(z_b=z_b):
            own(Z_DOWN, z_b).wait_send()

    rows_of(0, tokens, tokens_out, sent)
    rows_of(1, grads, grads_out, sent)
    rows_in(0, tokens_out)
    rows_in(1, grads_out)


def first_transfers(query, key, value, output, tokens, grads, segments, sizes):
    dp_n, seq_n, r_n, y_n, core_n = sizes
    rows, width = query.shape
    piece = tokens.shape[1] // core_n
    columns = width // core_n
    held = pl.BlockSpec(memory_space=pl.ANY)
    out = jax.ShapeDtypeStruct((seq_n, piece, width), bf16)
    dma = pltpu.SemaphoreType.DMA
    weights, tokens, grads, segments = pl.pallas_call(
        first_kernel,
        in_specs=[held] * 7,
        out_specs=[held] * 4,
        out_shape=[
            jax.ShapeDtypeStruct((dp_n, seq_n, y_n, core_n * rows, 4 * columns), bf16),
            out,
            out,
            jax.ShapeDtypeStruct((core_n,) + segments.shape, segments.dtype),
        ],
        scratch_shapes=[
            dma((8, seq_n)),
            dma((8, seq_n)),
            dma((5,)),
            dma((5,)),
            dma((5,)),
            dma((2, tokens.shape[0], 2)),
            dma((2, seq_n)),
            dma((2,)),
        ],
        compiler_params=pltpu.CompilerParams(collective_id=0, has_side_effects=True),
        cost_estimate=pl.CostEstimate(flops=0, bytes_accessed=2 * 4 * columns * width, transcendentals=0),
        name="first_transfers",
    )(query, key, value, output, tokens, grads, segments)
    return weights.reshape(width, 4 * columns), tokens, grads, segments


def visible_block(seg_row, seg_col, start, rows, cols):
    row_place = start + lax.broadcasted_iota(jnp.int32, (rows, cols), 0)
    col_place = lax.broadcasted_iota(jnp.int32, (rows, cols), 1)
    return (seg_col == seg_row) & (col_place <= row_place)


def turned(u, cosine, sine):
    return u * cosine + pltpu.roll(u, u.shape[1] // 2, 1) * sine


def attend_kernel(scale, block, qp, kp, vp, cosine, sine, seg_row, seg_col, q_out, k_out, v_out, mixed):
    length = qp.shape[0]
    q_out[...] = turned(qp[...], cosine[...], sine[...]).astype(bf16)
    k_out[...] = turned(kp[...], cosine[...], sine[...]).astype(bf16)
    v_out[...] = vp[...].astype(bf16)
    for start in range(0, length, block):
        stop = start + block
        scores = product_t(q_out[start:stop, :], k_out[:stop, :]) * scale
        seen = visible_block(seg_row[:, :stop], seg_col[start:stop, :], start, block, stop)
        scores = jnp.where(seen, scores, masked_score)
        top = jnp.max(scores, axis=1, keepdims=True)
        weights = jnp.exp(scores - top)
        total = jnp.sum(weights, axis=1, keepdims=True)
        summed = product(weights.astype(bf16), v_out[:stop, :])
        mixed[start:stop, :] = (summed / total).astype(bf16)


def attend(qkv, cosine, sine, seg_row, seg_col, heads):
    length, head = qkv.shape[0], cosine.shape[1]
    block = min(256, length)

    def column(offset):
        return pl.BlockSpec((length, head), lambda h: (0, offset + h))

    def whole(shape):
        return pl.BlockSpec(shape, lambda h: (0, 0))

    out = jax.ShapeDtypeStruct((length, heads * head), bf16)
    pairs = length * (length + block) // 2 * heads
    return pl.pallas_call(
        functools.partial(attend_kernel, head**-0.5, block),
        grid=(heads,),
        in_specs=[
            column(0),
            column(heads),
            column(2 * heads),
            whole((length, head)),
            whole((length, head)),
            whole((1, length)),
            whole((length, 1)),
        ],
        out_specs=[column(0)] * 4,
        out_shape=[out] * 4,
        compiler_params=pltpu.CompilerParams(vmem_limit_bytes=48 * 2**20),
        cost_estimate=pl.CostEstimate(
            flops=4 * pairs * head, bytes_accessed=20 * length * heads * head, transcendentals=pairs
        ),
        name="attend",
    )(qkv, qkv, qkv, cosine, sine, seg_row, seg_col)


def attend_back_kernel(
    scale, block, q, k, v, mixed, dmixed, cosine, sine, seg_row, seg_col, *rest
):
    dq_out, dk_out, dv_out, dk_sum, dv_sum = rest[-5:]
    length = q.shape[0]
    dk_sum[...] = jnp.zeros_like(dk_sum)
    dv_sum[...] = jnp.zeros_like(dv_sum)
    for start in range(0, length, block):
        stop = start + block
        scores = product_t(q[start:stop, :], k[:stop, :]) * scale
        seen = visible_block(seg_row[:, :stop], seg_col[start:stop, :], start, block, stop)
        scores = jnp.where(seen, scores, masked_score)
        top = jnp.max(scores, axis=1, keepdims=True)
        weights = jnp.exp(scores - top)
        inverse = 1.0 / jnp.sum(weights, axis=1, keepdims=True)
        grad = dmixed[start:stop, :].astype(f32)
        delta = jnp.sum(grad * mixed[start:stop, :].astype(f32), axis=1, keepdims=True) * inverse
        unit = (grad * inverse).astype(bf16)
        dweights = product_t(unit, v[:stop, :])
        dscores = (weights * (dweights - delta)).astype(bf16)
        dq = product(dscores, k[:stop, :]) * scale
        dq_out[start:stop, :] = turned(dq, cosine[start:stop, :], -sine[start:stop, :]).astype(bf16)
        dk_sum[:stop, :] += t_product(dscores, q[start:stop, :])
        dv_sum[:stop, :] += t_product(weights.astype(bf16), unit)
    dk_out[...] = turned(dk_sum[...] * scale, cosine[...], -sine[...]).astype(bf16)
    dv_out[...] = dv_sum[...].astype(bf16)


def attend_back(q, k, v, mixed, dmixed, cosine, sine, seg_row, seg_col, heads, *before):
    length, head = q.shape[0], cosine.shape[1]
    block = min(256, length)
    column = pl.BlockSpec((length, head), lambda h: (0, h))

    def whole(shape):
        return pl.BlockSpec(shape, lambda h: (0, 0))

    out = jax.ShapeDtypeStruct((length, heads * head), bf16)
    pairs = length * (length + block) // 2 * heads
    return pl.pallas_call(
        functools.partial(attend_back_kernel, head**-0.5, block),
        grid=(heads,),
        in_specs=[column] * 5
        + [whole((length, head)), whole((length, head)), whole((1, length)), whole((length, 1))]
        + [pl.BlockSpec(memory_space=pl.ANY)] * len(before),
        out_specs=[column] * 3,
        out_shape=[out] * 3,
        scratch_shapes=[pltpu.VMEM((length, head), f32)] * 2,
        compiler_params=pltpu.CompilerParams(vmem_limit_bytes=48 * 2**20),
        cost_estimate=pl.CostEstimate(
            flops=10 * pairs * head, bytes_accessed=16 * length * heads * head, transcendentals=pairs
        ),
        name="attend_back",
    )(q, k, v, mixed, dmixed, cosine, sine, seg_row, seg_col, *before)


def units_kernel(chunk, x, dy, gate, up, down, *rest):
    units, dgate, dup = rest[-3:]
    gate_w, up_w, down_w = gate[...], up[...], down[...]

    def step(i, carry):
        rows = pl.ds(pl.multiple_of(i * chunk, chunk), chunk)
        gpre = product(x[rows, :], gate_w)
        upre = product(x[rows, :], up_w)
        dunits = product_t(dy[rows, :], down_w)
        s = jax.nn.sigmoid(gpre)
        silu = gpre * s
        units[rows, :] = (silu * upre).astype(bf16)
        dgate[rows, :] = (dunits * upre * (s * (1.0 + gpre * (1.0 - s)))).astype(bf16)
        dup[rows, :] = (dunits * silu).astype(bf16)
        return carry

    lax.fori_loop(0, x.shape[0] // chunk, step, 0)


def expert_units(x, dy, gate, up, down, start, stop, *before):
    rows, width = x.shape
    units = stop - start
    chunk = tile_of(rows)
    tile = unit_tile(gate.shape[1])
    first = start // tile
    once = pl.BlockSpec((rows, width), lambda j: (0, 0), pipeline_mode=pl.Buffered(1))
    out = jax.ShapeDtypeStruct((rows, units), bf16)
    return pl.pallas_call(
        functools.partial(units_kernel, chunk),
        grid=(units // tile,),
        in_specs=[
            once,
            once,
            pl.BlockSpec((width, tile), lambda j: (0, first + j)),
            pl.BlockSpec((width, tile), lambda j: (0, first + j)),
            pl.BlockSpec((tile, width), lambda j: (first + j, 0)),
        ]
        + [pl.BlockSpec(memory_space=pl.ANY)] * len(before),
        out_specs=[pl.BlockSpec((rows, tile), lambda j: (0, j))] * 3,
        out_shape=[out] * 3,
        compiler_params=pltpu.CompilerParams(vmem_limit_bytes=56 * 2**20),
        cost_estimate=pl.CostEstimate(
            flops=6 * rows * width * units,
            bytes_accessed=4 * rows * width + 6 * width * units + 6 * rows * units,
            transcendentals=rows * units,
        ),
        name="expert_units",
    )(x, dy, gate, up, down, *before)


def unit_tile(units):
    return 256 if units % 256 == 0 else units


def unit_cut(units):
    tile = unit_tile(units)
    return units // tile * 3 // 4 * tile


def dispatch_kernel(me, hidden, dout, slot, routes, router, rows, dy_rows, gate):
    size = hidden.shape[1] * hidden.shape[3]
    width = hidden.shape[4]
    mine = me[3]
    tokens = hidden[...].reshape(size, width)
    logits = product(tokens, router[...])
    lanes = lax.broadcasted_iota(jnp.int32, logits.shape, 1)
    first, second = routes[0, :, 0:1], routes[0, :, 1:2]
    one = jnp.sum(jnp.where(lanes == first, logits, 0.0), axis=1, keepdims=True)
    two = jnp.sum(jnp.where(lanes == second, logits, 0.0), axis=1, keepdims=True)
    top = jnp.maximum(one, two)
    one, two = jnp.exp(one - top), jnp.exp(two - top)
    share = jnp.where(first == mine, one, jnp.where(second == mine, two, 0.0)) / (one + two)
    gate[0] = share
    chosen = (
        lax.broadcasted_iota(jnp.int32, (rows.shape[1], size), 0) == slot[0]
    ).astype(bf16)
    rows[0] = product(chosen, tokens).astype(bf16)
    dy = (share * dout[...].reshape(size, width).astype(f32)).astype(bf16)
    dy_rows[0] = product(chosen, dy).astype(bf16)


def plane_block(seq_n, piece, width):
    return pl.BlockSpec((1, 2, 1, piece, width), lambda b, me: (b // seq_n, 0, b % seq_n, 0, 0))


def relative_block(seq_n, piece, width):
    return pl.BlockSpec(
        (1, 1, 2, 1, piece, width),
        lambda b, me: (
            lax.rem(b // (2 * seq_n) + me[0], 2),
            lax.rem(b // seq_n + me[1], 2),
            0,
            b % seq_n,
            0,
            0,
        ),
    )


def dispatch(me, hidden, dout, slot, routes, router, seq_n, piece, cap):
    blocks, size = slot.shape[0], slot.shape[2]
    width = hidden.shape[1]
    seen = (4, 2, seq_n, piece, width)
    each = pl.BlockSpec((1, cap, width), lambda b, me: (b, 0, 0))
    out = jax.ShapeDtypeStruct((blocks, cap, width), bf16)
    spare = jnp.zeros((width, 128 - router.shape[1]), router.dtype)
    return pl.pallas_call(
        dispatch_kernel,
        grid_spec=pltpu.PrefetchScalarGridSpec(
            num_scalar_prefetch=1,
            grid=(blocks,),
            in_specs=[
                plane_block(seq_n, piece, width),
                plane_block(seq_n, piece, width),
                pl.BlockSpec((1, 1, size), lambda b, me: (b, 0, 0)),
                pl.BlockSpec((1, size, routes.shape[2]), lambda b, me: (b, 0, 0)),
                pl.BlockSpec((width, 128), lambda b, me: (0, 0)),
            ],
            out_specs=[each, each, pl.BlockSpec((1, size, 1), lambda b, me: (b, 0, 0))],
        ),
        out_shape=[out, out, jax.ShapeDtypeStruct((blocks, size, 1), f32)],
        compiler_params=pltpu.CompilerParams(vmem_limit_bytes=40 * 2**20),
        cost_estimate=pl.CostEstimate(
            flops=4 * blocks * size * width * (cap + 64),
            bytes_accessed=4 * blocks * (size + cap) * width,
            transcendentals=2 * blocks * size,
        ),
        name="dispatch",
    )(
        me,
        hidden.reshape(seen),
        dout.reshape(seen),
        slot,
        routes,
        jnp.concatenate([router, spare], axis=1),
    )


def spread_rows(slot, rows):
    size, cap = slot.shape[0], rows.shape[0]
    chosen = (lax.broadcasted_iota(jnp.int32, (size, cap), 1) == slot).astype(bf16)
    return product(chosen, rows)


def place_cores(me, out, dense):
    piece = out.shape[4]
    for core in range(2):
        out[0, 0, lax.rem(me[2] + core, 2), 0] = dense[core * piece : (core + 1) * piece, :].astype(bf16)


def combine_kernel(me, rows, slot, gate, dout, out, dgate):
    dense = spread_rows(slot[0], rows[0])
    grads = dout[...].reshape(dense.shape).astype(f32)
    dgate[0] = jnp.sum(grads * dense, axis=1, keepdims=True)
    place_cores(me, out, gate[0] * dense)


def collect_kernel(me, left, slot, right, *rest):
    dense = [spread_rows(slot[0], left[0]), spread_rows(slot[0], right[0])]
    place_cores(me, rest[-1], jnp.concatenate(dense, axis=1))


def combine(me, rows, slot, seq_n, piece, gate=None, dout=None, right=None):
    blocks, cap, part = rows.shape
    size = slot.shape[1]
    width = part if right is None else 2 * part
    column = pl.BlockSpec((1, size, 1), lambda b, me: (b, 0, 0))
    weigh = gate is not None
    operands = [rows, slot]
    in_specs = [pl.BlockSpec((1, cap, part), lambda b, me: (b, 0, 0)), column]
    out_specs = [relative_block(seq_n, piece, width)]
    out_shape = [jax.ShapeDtypeStruct((2, 2, 2, seq_n, piece, width), bf16)]
    if weigh:
        operands += [gate, dout.reshape(4, 2, seq_n, piece, width)]
        in_specs += [column, plane_block(seq_n, piece, width)]
        out_specs += [column]
        out_shape += [jax.ShapeDtypeStruct((blocks, size, 1), f32)]
    else:
        operands += [right]
        in_specs += in_specs[:1]
    return pl.pallas_call(
        combine_kernel if weigh else collect_kernel,
        grid_spec=pltpu.PrefetchScalarGridSpec(
            num_scalar_prefetch=1, grid=(blocks,), in_specs=in_specs, out_specs=out_specs
        ),
        out_shape=out_shape,
        compiler_params=pltpu.CompilerParams(vmem_limit_bytes=40 * 2**20),
        cost_estimate=pl.CostEstimate(
            flops=2 * blocks * size * width * cap,
            bytes_accessed=2 * blocks * (2 * size + cap) * width,
            transcendentals=0,
        ),
        name="combine" if weigh else "collect",
    )(me, *operands)


def down_kernel(cut, units_a, units_b, down, *rest):
    total = product(units_a[...], down[:cut, :]) + product(units_b[...], down[cut:, :])
    rest[-1][...] = total.astype(bf16)


def expert_down(units_a, units_b, down, *before):
    rows, cut = units_a.shape
    inner, width = down.shape
    m, n = tile_of(rows), tile_of(width)
    return pl.pallas_call(
        functools.partial(down_kernel, cut),
        grid=(width // n, rows // m),
        in_specs=[
            pl.BlockSpec((m, cut), lambda j, i: (i, 0)),
            pl.BlockSpec((m, inner - cut), lambda j, i: (i, 0)),
            pl.BlockSpec((inner, n), lambda j, i: (0, j)),
        ]
        + [pl.BlockSpec(memory_space=pl.ANY)] * len(before),
        out_specs=pl.BlockSpec((m, n), lambda j, i: (i, j)),
        out_shape=jax.ShapeDtypeStruct((rows, width), bf16),
        compiler_params=pltpu.CompilerParams(vmem_limit_bytes=48 * 2**20),
        cost_estimate=pl.CostEstimate(
            flops=2 * rows * inner * width,
            bytes_accessed=2 * (rows * inner + inner * width + rows * width),
            transcendentals=0,
        ),
        name="expert_down",
    )(units_a, units_b, down, *before)


def input_kernel(cut, dgate_a, dgate_b, dup_a, dup_b, gate, up, *rest):
    total = product_t(dgate_a[...], gate[:, :cut]) + product_t(dgate_b[...], gate[:, cut:])
    total += product_t(dup_a[...], up[:, :cut]) + product_t(dup_b[...], up[:, cut:])
    rest[-1][...] = total.astype(bf16)


def expert_input_grad(dgate_a, dgate_b, dup_a, dup_b, gate, up, start, stop, *before):
    rows, cut = dgate_a.shape
    inner = gate.shape[1]
    width = stop - start
    m, n = tile_of(rows), tile_of(width)
    first = start // n
    left_a = pl.BlockSpec((m, cut), lambda j, i: (i, 0))
    left_b = pl.BlockSpec((m, inner - cut), lambda j, i: (i, 0))
    right = pl.BlockSpec((n, inner), lambda j, i: (first + j, 0))
    return pl.pallas_call(
        functools.partial(input_kernel, cut),
        grid=(width // n, rows // m),
        in_specs=[left_a, left_b, left_a, left_b, right, right]
        + [pl.BlockSpec(memory_space=pl.ANY)] * len(before),
        out_specs=pl.BlockSpec((m, n), lambda j, i: (i, j)),
        out_shape=jax.ShapeDtypeStruct((rows, width), bf16),
        compiler_params=pltpu.CompilerParams(vmem_limit_bytes=52 * 2**20),
        cost_estimate=pl.CostEstimate(
            flops=4 * rows * inner * width,
            bytes_accessed=2 * (2 * rows * inner + 2 * inner * width + rows * width),
            transcendentals=0,
        ),
        name="expert_input_grad",
    )(dgate_a, dgate_b, dup_a, dup_b, gate, up, *before)


def tile_of(size):
    return max(c for c in range(16, 513, 16) if size % c == 0)


def anchor_kernel(*refs):
    pass


def after(a, *before):
    return pl.pallas_call(
        anchor_kernel,
        in_specs=[pl.BlockSpec(memory_space=pl.ANY)] * (1 + len(before)),
        out_specs=pl.BlockSpec(memory_space=pl.ANY),
        out_shape=jax.ShapeDtypeStruct(a.shape, a.dtype),
        input_output_aliases={0: 0},
        cost_estimate=pl.CostEstimate(flops=0, bytes_accessed=0, transcendentals=0),
        name="after",
    )(a, *before)


def norm_backward(grad_rows, normed, inverse, gain):
    weighted = grad_rows * gain
    mean_term = jnp.mean(weighted * normed, axis=-1, keepdims=True)
    return inverse * (weighted - normed * mean_term), jnp.sum(grad_rows * normed, axis=0)


def pick(a, index, axis):
    return lax.dynamic_index_in_dim(a, index, axis, keepdims=False)


def on_device(
    sizes,
    tokens,
    segments,
    routes,
    attn_norm,
    query_weight,
    key_weight,
    value_weight,
    output_weight,
    expert_norm,
    router,
    gate_weight,
    up_weight,
    down_weight,
    grad_out,
):
    dp_n, seq_n, r_n, y_n, core_n = sizes
    parts = r_n * core_n
    seq_count, seq_dev, width = tokens.shape
    piece = seq_dev // core_n
    length = segments.shape[1]
    home = seq_n * piece
    head = width // HEADS
    heads = HEADS // parts
    columns = width // parts
    experts = router.shape[1]
    topk = routes.shape[2]
    plane = 8 * home
    blocks = plane // seq_dev
    cap = 5 * seq_dev * topk // (4 * experts)
    dp_i, seq_i, r_i, y_i, core_i = (lax.axis_index(a) for a in EVERY)
    group, member = seq_i // seq_count, seq_i % seq_count

    rows_here = query_weight.shape[0]
    if r_n == 1 and parts == 2 and dp_n == 2 and y_n == 2 and seq_n == 2 * seq_count:
        weights, token_home, grad_home, chip_segments = first_transfers(
            query_weight, key_weight, value_weight, output_weight, tokens, grad_out, segments, sizes
        )
        segment = pick(pick(chip_segments, group, 0), member, 0)
    else:
        local = jnp.concatenate([query_weight, key_weight, value_weight, output_weight], axis=1)
        local = chip_exchange(local.reshape(rows_here, 4, parts, columns), 2, 0, parts)
        weights = lax.all_gather(
            local.reshape(parts * rows_here, 4 * columns), SPREAD, axis=0, tiled=True
        )
        weights = (
            weights.reshape(dp_n * seq_n, y_n, r_n, core_n * rows_here, -1)
            .transpose(0, 2, 1, 3, 4)
            .reshape(width, -1)
        )
        token_home, grad_home = to_sequences(tokens), to_sequences(grad_out)
        chip_segments = lax.all_gather(segments, "core")
        segment = pick(pick(chip_segments, group, 0), member, 0)
    weight_in, weight_out = weights[:, : 3 * columns], weights[:, 3 * columns :]

    token_float = token_home.astype(f32)
    inverse_one = lax.rsqrt(jnp.mean(token_float * token_float, axis=-1, keepdims=True) + epsilon)
    hidden_one = (token_float * inverse_one * attn_norm).astype(bf16)
    hidden_full = chip_gather(hidden_one, 1, parts).reshape(length, width)

    grad_plane = lax.all_gather(grad_home.reshape(home, width), PLANE, axis=0, tiled=True)

    half = head // 2
    frequency = theta_base ** (-jnp.arange(half, dtype=f32) / half)
    angles = jnp.arange(length, dtype=f32)[:, None] * frequency[None, :]
    cosine = jnp.concatenate([jnp.cos(angles)] * 2, axis=1)
    sine = jnp.concatenate([-jnp.sin(angles), jnp.sin(angles)], axis=1)
    seg_row, seg_col = segment[None, :], segment[:, None]

    qkv = product(hidden_full, weight_in)
    query, keys, values, mixed = attend(qkv, cosine, sine, seg_row, seg_col, heads)
    mixed_full = chip_gather(mixed, 1, parts)
    branch = product(mixed_full, weight_out).reshape(seq_n, parts, piece, columns)
    branch = chip_exchange(branch, 1, 3, parts).reshape(seq_n, piece, width)
    residual = token_float + branch
    inverse_two = lax.rsqrt(jnp.mean(residual * residual, axis=-1, keepdims=True) + epsilon)
    normed_two = residual * inverse_two
    hidden_two = (normed_two * expert_norm).astype(bf16).reshape(home, width)

    hidden_plane = lax.all_gather(hidden_two, PLANE, axis=0, tiled=True)
    small = after(jnp.transpose(routes, (2, 0, 1)).reshape(topk * seq_count, seq_dev), hidden_two)
    small = lax.all_gather(small, EVERY, axis=0, tiled=True).reshape(
        dp_n, seq_n, r_n, y_n, core_n, topk, seq_count, seq_dev
    )
    small = pick(pick(small, group, 4), member, 5)
    plane_routes = pick(small, r_i, 2).transpose(0, 2, 1, 3, 4)
    block_routes = plane_routes.reshape(blocks, topk, seq_dev)
    home_routes = (
        pick(pick(plane_routes, dp_i, 0), y_i, 0)
        .reshape(seq_n, topk, core_n, piece)
        .transpose(1, 2, 0, 3)
    )
    home_routes = pick(home_routes, core_i, 1).reshape(topk, home)
    mine = y_i * core_n + core_i
    chosen = jnp.any(block_routes == mine, axis=1)
    places = jnp.arange(seq_dev)
    rank = product(chosen.astype(bf16), (places[:, None] < places[None, :]).astype(bf16))
    slot = jnp.where(chosen, rank.astype(jnp.int32), -1)
    slot_row, slot_col = slot[:, None, :], slot[:, :, None]
    me = jnp.stack([dp_i, y_i, core_i, mine]).astype(jnp.int32)
    expert_rows, dy_rows, row_gate = dispatch(
        me,
        hidden_plane,
        grad_plane,
        slot_row,
        jnp.transpose(block_routes, (0, 2, 1)),
        router,
        seq_n,
        piece,
        cap,
    )
    expert_in = expert_rows.reshape(blocks * cap, width)
    dy_rows = dy_rows.reshape(blocks * cap, width)

    gate_one, up_one, down_one = gate_weight[0], up_weight[0], down_weight[0]
    inner = gate_one.shape[1]
    cut = unit_cut(inner)
    full = (gate_one, up_one, down_one)

    def over_ctx(part):
        return lax.psum_scatter(part, CTX, scatter_dimension=0, tiled=True)

    def rows_product(rows, part):
        return t_product(rows, part).astype(bf16)

    units_a, dgpre_a, dupre_a = expert_units(expert_in, dy_rows, *full, 0, cut)
    down_a = rows_product(dy_rows, units_a)
    units_b, dgpre_b, dupre_b = expert_units(expert_in, dy_rows, *full, cut, inner, down_a)
    down_b = rows_product(dy_rows, units_b)
    down_sum_a, down_sum_b = over_ctx(down_a), over_ctx(down_b)
    grads = (dgpre_a, dgpre_b, dupre_a, dupre_b, gate_one, up_one)
    left = expert_input_grad(*grads, 0, width // 2, down_b)
    right = expert_input_grad(*grads, width // 2, width, left)
    left, right = (part.reshape(blocks, cap, width // 2) for part in (left, right))
    [back] = combine(me, left, slot_col, seq_n, piece, right=right)
    gate_a = rows_product(expert_in, after(dgpre_a, back, down_sum_a))
    gate_b = rows_product(expert_in, after(dgpre_b, back))
    gate_sum_a, gate_sum_b = over_ctx(gate_a), over_ctx(gate_b)
    ypair = expert_down(units_a, units_b, down_one, gate_a)
    mixed_rows, dgate_plane = combine(
        me, ypair.reshape(blocks, cap, width), slot_col, seq_n, piece, row_gate, grad_plane
    )

    dgate_plane = dgate_plane.reshape(dp_n * y_n, seq_n, core_n, piece).transpose(0, 2, 1, 3)
    dgate_home = lax.all_to_all(
        dgate_plane.reshape(8, home), PLANE, split_axis=0, concat_axis=0, tiled=True
    ).reshape(dp_n, experts, home).sum(axis=0)

    logits = product(hidden_two, router)
    hot = home_routes[:, :, None] == jnp.arange(experts, dtype=jnp.int32)[None, None, :]
    gates = jax.nn.softmax(jnp.sum(jnp.where(hot, logits[None], 0.0), axis=2), axis=0)
    dgate = jnp.sum(jnp.where(hot, jnp.transpose(dgate_home)[None], 0.0), axis=2)
    dsel = gates * (dgate - jnp.sum(gates * dgate, axis=0, keepdims=True))
    dlogits = jnp.sum(jnp.where(hot, dsel[:, :, None], 0.0), axis=0).astype(bf16)
    router_grad = t_product(hidden_two, dlogits)
    def once_gate(stage, *arrays):
        return (after(arrays[0], gate_a),) + arrays[1:] if stage == 0 else arrays

    dhidden_two = plane_scatter(back, once_gate).reshape(home, width) + product_t(dlogits, router)

    flat_two = normed_two.reshape(home, width)
    dresid, expert_norm_grad = norm_backward(
        dhidden_two, flat_two, inverse_two.reshape(home, 1), expert_norm
    )
    dresid = dresid + grad_home.reshape(home, width).astype(f32)
    dbranch = chip_gather(dresid.astype(bf16).reshape(seq_n, piece, width), 1, parts).reshape(length, width)
    column_start = (r_i * core_n + core_i) * columns
    dbranch_here = lax.dynamic_slice_in_dim(dbranch, column_start, columns, 1)
    dmixed = chip_scatter(product_t(dbranch_here, weight_out).astype(bf16), 1, parts).astype(bf16)
    stages = {}

    def check(stage, *arrays):
        stages[stage] = arrays
        return arrays

    mixture = plane_scatter(after(mixed_rows, dbranch), check)
    up_b = rows_product(expert_in, after(dupre_b, dbranch))
    dqpre, dkpre, dvpre = attend_back(
        query, keys, values, mixed, dmixed, cosine, sine, seg_row, seg_col, heads, down_sum_b, up_b, *stages[0]
    )
    dqkv = jnp.concatenate([dqpre, dkpre, dvpre], axis=1)
    up_a = rows_product(expert_in, after(dupre_a, dqpre))
    dqkv = after(dqkv, up_a)
    dhidden_part = product_t(dqkv, weight_in).astype(bf16)
    in_grad = t_product(hidden_full, after(dqkv, dhidden_part, *stages[1])).astype(bf16)
    dhidden_one = chip_scatter(
        dhidden_part.reshape(seq_n, parts * piece, width), 1, parts
    )
    normed_one = token_float * inverse_one
    dtokens, attn_norm_grad = norm_backward(
        dhidden_one.reshape(home, width),
        normed_one.reshape(home, width),
        inverse_one.reshape(home, 1),
        attn_norm,
    )
    dtokens = (dtokens + dresid).astype(bf16).reshape(seq_n, piece, width)
    out_grad = t_product(mixed_full, after(dbranch_here, in_grad)).astype(bf16)
    output = (residual + mixture).astype(bf16)

    grad_down = jnp.concatenate([down_sum_a, down_sum_b], axis=1).astype(f32).T[None]
    grad_gate = jnp.concatenate([gate_sum_a, gate_sum_b], axis=1).astype(f32)[None]
    grad_up = jnp.concatenate([over_ctx(up_a), over_ctx(up_b)], axis=1).astype(f32)[None]

    def seen(part):
        return part.reshape(dp_n, seq_n, r_n, y_n, core_n * rows_here, -1)

    def half(a, axis, index, name):
        keep, give = pick(a, index, axis), pick(a, 1 - index, axis)
        return total(keep, swap(give, name)).astype(bf16)

    first = [half(seen(a), 0, dp_i, "dp") for a in (out_grad, in_grad[:, :columns])]
    first.append(half(seen(in_grad[:, columns:]), 3, y_i, "y"))
    second = [half(a, 2, y_i, "y") for a in first[:2]] + [half(first[2], 0, dp_i, "dp")]
    grad_tokens = from_sequences(dtokens)
    output = from_sequences(output)
    part = total(*seq_pieces(jnp.concatenate(second, axis=-1))).astype(bf16)
    part = part.reshape(parts, rows_here, 4, 1, columns)
    part = chip_exchange(part, 0, 3, parts).reshape(rows_here, 4, width).astype(f32)
    grad_output, grad_query, grad_key, grad_value = (part[:, i] for i in range(4))
    grad_tokens = grad_tokens.astype(f32)

    gains = jnp.concatenate([attn_norm_grad[None], expert_norm_grad[None], router_grad.T], axis=0)
    gain_n = gains.shape[0]
    gains = gains.reshape(gain_n, -1, rows_here).transpose(1, 0, 2)
    gains = lax.all_to_all(gains, EVERY, split_axis=0, concat_axis=0, tiled=True)
    gains = jnp.sum(gains, axis=0).T

    return (
        output,
        grad_tokens,
        gains[:, 0],
        grad_query,
        grad_key,
        grad_value,
        grad_output,
        gains[:, 1],
        gains[:, 2:],
        grad_gate,
        grad_up,
        grad_down,
    )


def solution(mesh):
    dp_n, ctx_n, exp_n = mesh.shape["dp"], mesh.shape["ctx"], mesh.shape["exp"]

    def block(*arrays):
        tokens = arrays[0]
        seq_count = tokens.shape[0] // (dp_n * exp_n)
        seq_n = seq_count * CORES
        sizes = (dp_n, seq_n, ctx_n // seq_n, exp_n // CORES, CORES)
        fine = Mesh(mesh.devices.reshape(sizes), EVERY)
        group = ("dp", "y", "core")
        exp = ("y", "core")
        return jax.shard_map(
            functools.partial(on_device, sizes),
            mesh=fine,
            in_specs=(
                P(group, CTX, None),
                P(group, None),
                P(group, CTX, None),
                P(),
                P(EVERY, None),
                P(EVERY, None),
                P(EVERY, None),
                P(EVERY, None),
                P(),
                P(),
                P(exp, None, "dp"),
                P(exp, None, "dp"),
                P(exp, "dp", None),
                P(group, CTX, None),
            ),
            out_specs=(
                P(group, CTX, None),
                P(group, CTX, None),
                P(EVERY),
                P(EVERY, None),
                P(EVERY, None),
                P(EVERY, None),
                P(EVERY, None),
                P(EVERY),
                P(EVERY, None),
                P(exp, CTX, "dp"),
                P(exp, CTX, "dp"),
                P(exp, "dp", CTX),
            ),
            check_vma=False,
        )(*arrays)

    return block
```

```python
import functools

import jax
import jax.numpy as jnp
from jax import lax
from jax.experimental import pallas as pl
from jax.experimental.pallas import tpu as pltpu
from jax.sharding import Mesh, PartitionSpec as P

HEADS = 16
CORES = 2

epsilon = 1e-05
theta_base = 10000.0
masked_score = -1e30
bf16 = jnp.bfloat16
f32 = jnp.float32

PLANE = ("dp", "y", "core")
CHIP = ("r", "core")
SPREAD = ("dp", "seq", "y")
CTX = ("seq", "r")
EVERY = ("dp", "seq", "r", "y", "core")


def product(a, b):
    return jnp.dot(a, b, preferred_element_type=f32)


def product_t(a, b):
    return lax.dot_general(a, b, (((1,), (1,)), ((), ())), preferred_element_type=f32)


def t_product(a, b):
    return lax.dot_general(a, b, (((0,), (0,)), ((), ())), preferred_element_type=f32)


def swap(a, axis):
    return lax.ppermute(a, axis, [(0, 1), (1, 0)])


def halves(a, axis):
    size = a.shape[axis] // 2
    me = lax.axis_index("core")
    mine = lax.dynamic_slice_in_dim(a, me * size, size, axis)
    other = lax.dynamic_slice_in_dim(a, (1 - me) * size, size, axis)
    return mine, other


def by_core(mine, other, axis):
    first = lax.axis_index("core") == 0
    return jnp.concatenate([jnp.where(first, mine, other), jnp.where(first, other, mine)], axis=axis)


def chip_gather(a, axis, parts):
    if parts == 2:
        return by_core(a, swap(a, "core"), axis)
    return lax.all_gather(a, CHIP, axis=axis, tiled=True)


def chip_scatter(a, axis, parts):
    if parts == 2:
        mine, other = halves(a, axis)
        return mine.astype(f32) + swap(other, "core").astype(f32)
    return lax.psum_scatter(a, CHIP, scatter_dimension=axis, tiled=True).astype(f32)


def chip_exchange(a, split, concat, parts):
    if parts == 2:
        mine, other = halves(a, split)
        return by_core(mine, swap(other, "core"), concat)
    return lax.all_to_all(a, CHIP, split_axis=split, concat_axis=concat, tiled=True)


def core_exchange(a, split, concat):
    mine, other = halves(a, split)
    return by_core(mine, swap(other, "core"), concat)


def seq_pieces(a):
    count = a.shape[0]
    me = lax.axis_index("seq")
    pieces = [pick(a, me, 0)]
    for step in range(1, count):
        give = pick(a, lax.rem(me + step, count), 0)
        pieces.append(lax.ppermute(give, "seq", [(i, (i + step) % count) for i in range(count)]))
    return pieces


def seq_exchange(a):
    count = a.shape[0]
    me = lax.axis_index("seq")
    pieces = jnp.stack(seq_pieces(a))
    return jnp.stack([pick(pieces, lax.rem(me + count - s, count), 0) for s in range(count)])


def to_sequences(a):
    return seq_exchange(core_exchange(a, 1, 0))


def from_sequences(a):
    return core_exchange(seq_exchange(a), 0, 1)


def total(*parts):
    return sum(part.astype(f32) for part in parts)


def plane_scatter(blocks, check=lambda stage, *arrays: arrays):
    held = total(blocks[:, :, 0], swap(blocks[:, :, 1], "core")).astype(bf16)
    [held] = check(0, held)
    half = blocks.shape[3] // 2
    by_x = swap(held[1, 1, :half], "dp")
    by_y = swap(held[1, 1, half:], "y")
    to_x = jnp.concatenate([held[1, 0, :half], total(held[1, 0, half:], by_y).astype(bf16)], axis=0)
    to_y = jnp.concatenate([total(held[0, 1, :half], by_x).astype(bf16), held[0, 1, half:]], axis=0)
    to_x, to_y = check(1, to_x, to_y)
    return total(held[0, 0], swap(to_x, "dp"), swap(to_y, "y"))


MESH = pl.DeviceIdType.MESH
Z_UP, Z_DOWN, X_A, Y_A, Y_B, X_B, Y_A2, X_B2 = range(8)


def first_kernel(
    query,
    key,
    value,
    output,
    tokens,
    grads,
    segments,
    weights,
    tokens_out,
    grads_out,
    segments_out,
    send,
    recv,
    core_send,
    core_recv,
    core_local,
    row_send,
    row_recv,
    row_local,
):
    dp, z, y, core = (lax.axis_index(a) for a in ("dp", "seq", "y", "core"))
    seq_n = weights.shape[1]
    rows, columns = query.shape[0], weights.shape[4] // 4
    half = weights.shape[4] // 2
    piece = tokens_out.shape[1]
    x_next, y_next, z_next, z_last, other = (
        {"dp": 1 - dp},
        {"y": 1 - y},
        {"seq": lax.rem(z + 1, seq_n)},
        {"seq": lax.rem(z + seq_n - 1, seq_n)},
        {"core": 1 - core},
    )

    barrier = pltpu.get_barrier_semaphore()
    partners = [x_next, y_next] + [
        {"seq": lax.rem(z + dz, seq_n), "core": lax.rem(core + dc, 2)}
        for dz in range(seq_n)
        for dc in range(2)
        if dz or dc
    ]
    for partner in partners:
        pl.semaphore_signal(barrier, inc=1, device_id=partner, device_id_type=MESH)
    pl.semaphore_wait(barrier, len(partners))

    here = pl.ds(pl.multiple_of(core * rows, rows), rows)
    locals_, remotes = [], []
    for m, matrix in enumerate((query, key, value, output)):
        place = weights.at[dp, z, y, here, pl.ds(m * columns, columns)]
        mine = matrix.at[:, pl.ds(pl.multiple_of(core * columns, columns), columns)]
        theirs = matrix.at[:, pl.ds(pl.multiple_of((1 - core) * columns, columns), columns)]
        locals_.append(pltpu.make_async_copy(mine, place, core_local.at[m]))
        remotes.append(
            pltpu.make_async_remote_copy(
                theirs, place, core_send.at[m], core_recv.at[m], device_id=other, device_id_type=MESH
            )
        )
    segment_local = pltpu.make_async_copy(segments, segments_out.at[core], core_local.at[4])
    segment_remote = pltpu.make_async_remote_copy(
        segments, segments_out.at[core], core_send.at[4], core_recv.at[4], device_id=other, device_id_type=MESH
    )
    for copy in remotes + [segment_remote] + locals_ + [segment_local]:
        copy.start()
    for copy in remotes + locals_:
        copy.wait()

    def part(kind, dp_b, z_b, y_b, device):
        if kind in (Z_UP, Z_DOWN):
            ref = weights.at[dp_b, z_b, y_b]
        else:
            start = 0 if kind in (X_A, Y_A, Y_A2) else half
            ref = weights.at[dp_b, z_b, y_b, :, pl.ds(start, half)]
        return pltpu.make_async_remote_copy(
            ref, ref, send.at[kind, z_b], recv.at[kind, z_b], device_id=device, device_id_type=MESH
        )

    def own(kind, z_b):
        device = {Z_UP: z_next, Z_DOWN: z_last, X_A: x_next, X_B: x_next, Y_A: y_next, Y_B: y_next}[kind]
        return part(kind, dp, z_b, y, device)

    def from_x(kind, z_b):
        return part(kind, 1 - dp, z_b, y, x_next)

    def from_y(kind, z_b):
        return part(kind, dp, z_b, 1 - y, y_next)

    def on_y(z_b):
        return part(Y_A2, 1 - dp, z_b, y, y_next)

    def on_x(z_b):
        return part(X_B2, dp, z_b, 1 - y, x_next)

    def spread(z_b):
        for kind in (X_A, Y_B, X_B, Y_A):
            own(kind, z_b).start()

    def relay(z_b):
        from_x(X_A, z_b).wait_recv()
        on_y(z_b).start()
        from_y(Y_B, z_b).wait_recv()
        on_x(z_b).start()

    def at_step(step, act_up, act_down):
        @pl.when(z - step >= 0)
        def _():
            act_up(z - step)

        @pl.when(z + step < seq_n)
        def _():
            act_down(z + step)

    def come_up(z_b):
        own(Z_UP, z_b).wait_recv()

        @pl.when(z < seq_n - 1)
        def _():
            own(Z_UP, z_b).start()

        spread(z_b)

    def come_down(z_b):
        own(Z_DOWN, z_b).wait_recv()

        @pl.when(z > 0)
        def _():
            own(Z_DOWN, z_b).start()

        spread(z_b)

    def rows_of(n, source, target, act):
        for s in range(tokens.shape[0]):
            z_to = tokens.shape[0] * core + s
            for d in range(2):
                core_to = lax.rem(core + d, 2)
                ref = source.at[s, pl.ds(pl.multiple_of(core_to * piece, piece), piece), :]
                copy = pltpu.make_async_remote_copy(
                    ref,
                    target.at[z],
                    row_send.at[n, s, d],
                    row_recv.at[n, z],
                    device_id={"seq": z_to, "core": core_to},
                    device_id_type=MESH,
                )
                if d:
                    act(copy)
                else:
                    keep = pltpu.make_async_copy(ref, target.at[z], row_local.at[n])

                    @pl.when(z_to != z)
                    def _(copy=copy):
                        act(copy)

                    @pl.when(z_to == z)
                    def _(keep=keep):
                        if act is begin:
                            keep.start()
                        else:
                            keep.wait()

    def begin(copy):
        copy.start()

    def sent(copy):
        copy.wait_send()

    def rows_in(n, target):
        group = z // tokens.shape[0]
        for z_from in range(seq_n):
            copy = pltpu.make_async_remote_copy(
                target.at[z_from],
                target.at[z_from],
                row_send.at[n, 0, 0],
                row_recv.at[n, z_from],
                device_id=other,
                device_id_type=MESH,
            )

            @pl.when((z_from != z) | (group != core))
            def _(copy=copy):
                copy.wait_recv()

    @pl.when(z < seq_n - 1)
    def _():
        own(Z_UP, z).start()

    @pl.when(z > 0)
    def _():
        own(Z_DOWN, z).start()

    spread(z)
    for step in range(1, seq_n):
        at_step(step, come_up, come_down)
        if step == 1:
            relay(z)
        else:
            at_step(step - 1, relay, relay)
        if step == seq_n - 2:
            rows_of(0, tokens, tokens_out, begin)
    rows_of(1, grads, grads_out, begin)
    at_step(seq_n - 1, relay, relay)

    segment_remote.wait()
    segment_local.wait()
    for z_b in range(seq_n):
        from_y(Y_A, z_b).wait_recv()
        from_x(X_B, z_b).wait_recv()
        part(Y_A2, 1 - dp, z_b, 1 - y, y_next).wait_recv()
        part(X_B2, 1 - dp, z_b, 1 - y, x_next).wait_recv()
        for kind in (X_A, Y_B, X_B, Y_A):
            own(kind, z_b).wait_send()
        on_y(z_b).wait_send()
        on_x(z_b).wait_send()

        @pl.when((z < seq_n - 1) & (z_b <= z))
        def _(z_b=z_b):
            own(Z_UP, z_b).wait_send()

        @pl.when((z > 0) & (z_b >= z))
        def _(z_b=z_b):
            own(Z_DOWN, z_b).wait_send()

    rows_of(0, tokens, tokens_out, sent)
    rows_of(1, grads, grads_out, sent)
    rows_in(0, tokens_out)
    rows_in(1, grads_out)


def first_transfers(query, key, value, output, tokens, grads, segments, sizes):
    dp_n, seq_n, r_n, y_n, core_n = sizes
    rows, width = query.shape
    piece = tokens.shape[1] // core_n
    columns = width // core_n
    held = pl.BlockSpec(memory_space=pl.ANY)
    out = jax.ShapeDtypeStruct((seq_n, piece, width), bf16)
    dma = pltpu.SemaphoreType.DMA
    weights, tokens, grads, segments = pl.pallas_call(
        first_kernel,
        in_specs=[held] * 7,
        out_specs=[held] * 4,
        out_shape=[
            jax.ShapeDtypeStruct((dp_n, seq_n, y_n, core_n * rows, 4 * columns), bf16),
            out,
            out,
            jax.ShapeDtypeStruct((core_n,) + segments.shape, segments.dtype),
        ],
        scratch_shapes=[
            dma((8, seq_n)),
            dma((8, seq_n)),
            dma((5,)),
            dma((5,)),
            dma((5,)),
            dma((2, tokens.shape[0], 2)),
            dma((2, seq_n)),
            dma((2,)),
        ],
        compiler_params=pltpu.CompilerParams(collective_id=0, has_side_effects=True),
        cost_estimate=pl.CostEstimate(flops=0, bytes_accessed=2 * 4 * columns * width, transcendentals=0),
        name="first_transfers",
    )(query, key, value, output, tokens, grads, segments)
    return weights.reshape(width, 4 * columns), tokens, grads, segments


def last_kernel(grads, tokens, output, grads_out, tokens_out, output_out, send, recv, row_send, row_recv, local):
    z, core = lax.axis_index("seq"), lax.axis_index("core")
    seq_n, piece = tokens.shape[:2]
    seq_count = tokens_out.shape[0]
    rows = grads.shape[1] // 2

    barrier = pltpu.get_barrier_semaphore()
    partners = [
        {"seq": lax.rem(z + dz, seq_n), "core": lax.rem(core + dc, 2)}
        for dz in range(seq_n)
        for dc in range(2)
        if dz or dc
    ]
    for partner in partners:
        pl.semaphore_signal(barrier, inc=1, device_id=partner, device_id_type=MESH)
    pl.semaphore_wait(barrier, len(partners))

    def grad_copy(dz, dc):
        z_to, core_to = lax.rem(z + dz, seq_n), lax.rem(core + dc, 2)
        source = grads.at[z_to, pl.ds(pl.multiple_of(core_to * rows, rows), rows), :]
        target = grads_out.at[core, z]
        if not (dz or dc):
            return pltpu.make_async_copy(source, target, local.at[2])
        return pltpu.make_async_remote_copy(
            source,
            target,
            send.at[dz, dc],
            recv.at[dz, dc],
            device_id={"seq": z_to, "core": core_to},
            device_id_type=MESH,
        )

    def grad_arrival(dz, dc):
        z_from, core_from = lax.rem(z + seq_n - dz, seq_n), lax.rem(core + dc, 2)
        ref = grads_out.at[core_from, z_from]
        return pltpu.make_async_remote_copy(
            ref, ref, send.at[dz, dc], recv.at[dz, dc], device_id=partners[0], device_id_type=MESH
        )

    group, member = z // seq_count, lax.rem(z, seq_count)

    def row_place(target, s, c):
        return target.at[s, pl.ds(pl.multiple_of(c * piece, piece), piece), :]

    def row_copy(n, source, target, dz):
        z_to = lax.rem(z + dz, seq_n)
        return pltpu.make_async_remote_copy(
            source.at[z_to],
            row_place(target, member, core),
            row_send.at[n, dz],
            row_recv.at[n, member, core],
            device_id={"seq": z_to, "core": group},
            device_id_type=MESH,
        )

    def each_row(remote, kept):
        for n, source, target in ((0, tokens, tokens_out), (1, output, output_out)):
            for dz in range(seq_n):
                if dz:
                    remote(row_copy(n, source, target, dz))
                else:

                    @pl.when(group != core)
                    def _(copy=row_copy(n, source, target, 0)):
                        remote(copy)

                    @pl.when(group == core)
                    def _(n=n, source=source, target=target):
                        kept(
                            pltpu.make_async_copy(
                                source.at[z], row_place(target, member, core), local.at[n]
                            )
                        )

    every = [(dz, dc) for dz in range(seq_n) for dc in range(2)]
    for dz, dc in reversed(every):
        grad_copy(dz, dc).start()
    each_row(lambda copy: copy.start(), lambda copy: copy.start())

    grad_copy(0, 0).wait()
    for dz, dc in every[1:]:
        grad_copy(dz, dc).wait_send()
        grad_arrival(dz, dc).wait_recv()
    each_row(lambda copy: copy.wait_send(), lambda copy: copy.wait())
    for n, target in ((0, tokens_out), (1, output_out)):
        for s in range(seq_count):
            for c in range(2):
                ref = row_place(target, s, c)
                copy = pltpu.make_async_remote_copy(
                    ref,
                    ref,
                    row_send.at[n, 0],
                    row_recv.at[n, s, c],
                    device_id=partners[0],
                    device_id_type=MESH,
                )

                @pl.when((z != seq_count * core + s) | (core != c))
                def _(copy=copy):
                    copy.wait_recv()


def last_transfers(grads, tokens, output, seq_count):
    seq_n, piece, width = tokens.shape
    rows = grads.shape[1] // 2
    held = pl.BlockSpec(memory_space=pl.ANY)
    out = jax.ShapeDtypeStruct((seq_count, 2 * piece, width), bf16)
    dma = pltpu.SemaphoreType.DMA
    return pl.pallas_call(
        last_kernel,
        in_specs=[held] * 3,
        out_specs=[held] * 3,
        out_shape=[jax.ShapeDtypeStruct((2, seq_n, rows, grads.shape[2]), bf16), out, out],
        scratch_shapes=[
            dma((seq_n, 2)),
            dma((seq_n, 2)),
            dma((2, seq_n)),
            dma((2, seq_count, 2)),
            dma((3,)),
        ],
        compiler_params=pltpu.CompilerParams(collective_id=1, has_side_effects=True),
        cost_estimate=pl.CostEstimate(flops=0, bytes_accessed=4 * grads.size, transcendentals=0),
        name="last_transfers",
    )(grads, tokens, output)


def visible_block(seg_row, seg_col, start, rows, cols):
    row_place = start + lax.broadcasted_iota(jnp.int32, (rows, cols), 0)
    col_place = lax.broadcasted_iota(jnp.int32, (rows, cols), 1)
    return (seg_col == seg_row) & (col_place <= row_place)


def turned(u, cosine, sine):
    return u * cosine + pltpu.roll(u, u.shape[1] // 2, 1) * sine


def attend_kernel(scale, block, qp, kp, vp, cosine, sine, seg_row, seg_col, q_out, k_out, v_out, mixed):
    length = qp.shape[0]
    q_out[...] = turned(qp[...], cosine[...], sine[...]).astype(bf16)
    k_out[...] = turned(kp[...], cosine[...], sine[...]).astype(bf16)
    v_out[...] = vp[...].astype(bf16)
    for start in range(0, length, block):
        stop = start + block
        scores = product_t(q_out[start:stop, :], k_out[:stop, :]) * scale
        seen = visible_block(seg_row[:, :stop], seg_col[start:stop, :], start, block, stop)
        scores = jnp.where(seen, scores, masked_score)
        top = jnp.max(scores, axis=1, keepdims=True)
        weights = jnp.exp(scores - top)
        total = jnp.sum(weights, axis=1, keepdims=True)
        summed = product(weights.astype(bf16), v_out[:stop, :])
        mixed[start:stop, :] = (summed / total).astype(bf16)


def attend(qkv, cosine, sine, seg_row, seg_col, heads):
    length, head = qkv.shape[0], cosine.shape[1]
    block = min(256, length)

    def column(offset):
        return pl.BlockSpec((length, head), lambda h: (0, offset + h))

    def whole(shape):
        return pl.BlockSpec(shape, lambda h: (0, 0))

    out = jax.ShapeDtypeStruct((length, heads * head), bf16)
    pairs = length * (length + block) // 2 * heads
    return pl.pallas_call(
        functools.partial(attend_kernel, head**-0.5, block),
        grid=(heads,),
        in_specs=[
            column(0),
            column(heads),
            column(2 * heads),
            whole((length, head)),
            whole((length, head)),
            whole((1, length)),
            whole((length, 1)),
        ],
        out_specs=[column(0)] * 4,
        out_shape=[out] * 4,
        compiler_params=pltpu.CompilerParams(vmem_limit_bytes=48 * 2**20),
        cost_estimate=pl.CostEstimate(
            flops=4 * pairs * head, bytes_accessed=20 * length * heads * head, transcendentals=pairs
        ),
        name="attend",
    )(qkv, qkv, qkv, cosine, sine, seg_row, seg_col)


def attend_back_kernel(
    scale, block, q, k, v, mixed, dmixed, cosine, sine, seg_row, seg_col, *rest
):
    dq_out, dk_out, dv_out, dk_sum, dv_sum = rest[-5:]
    length = q.shape[0]
    dk_sum[...] = jnp.zeros_like(dk_sum)
    dv_sum[...] = jnp.zeros_like(dv_sum)
    for start in range(0, length, block):
        stop = start + block
        scores = product_t(q[start:stop, :], k[:stop, :]) * scale
        seen = visible_block(seg_row[:, :stop], seg_col[start:stop, :], start, block, stop)
        scores = jnp.where(seen, scores, masked_score)
        top = jnp.max(scores, axis=1, keepdims=True)
        weights = jnp.exp(scores - top)
        inverse = 1.0 / jnp.sum(weights, axis=1, keepdims=True)
        grad = dmixed[start:stop, :].astype(f32)
        delta = jnp.sum(grad * mixed[start:stop, :].astype(f32), axis=1, keepdims=True) * inverse
        unit = (grad * inverse).astype(bf16)
        dweights = product_t(unit, v[:stop, :])
        dscores = (weights * (dweights - delta)).astype(bf16)
        dq = product(dscores, k[:stop, :]) * scale
        dq_out[start:stop, :] = turned(dq, cosine[start:stop, :], -sine[start:stop, :]).astype(bf16)
        dk_sum[:stop, :] += t_product(dscores, q[start:stop, :])
        dv_sum[:stop, :] += t_product(weights.astype(bf16), unit)
    dk_out[...] = turned(dk_sum[...] * scale, cosine[...], -sine[...]).astype(bf16)
    dv_out[...] = dv_sum[...].astype(bf16)


def attend_back(q, k, v, mixed, dmixed, cosine, sine, seg_row, seg_col, heads, *before):
    length, head = q.shape[0], cosine.shape[1]
    block = min(256, length)
    column = pl.BlockSpec((length, head), lambda h: (0, h))

    def whole(shape):
        return pl.BlockSpec(shape, lambda h: (0, 0))

    out = jax.ShapeDtypeStruct((length, heads * head), bf16)
    pairs = length * (length + block) // 2 * heads
    return pl.pallas_call(
        functools.partial(attend_back_kernel, head**-0.5, block),
        grid=(heads,),
        in_specs=[column] * 5
        + [whole((length, head)), whole((length, head)), whole((1, length)), whole((length, 1))]
        + [pl.BlockSpec(memory_space=pl.ANY)] * len(before),
        out_specs=[column] * 3,
        out_shape=[out] * 3,
        scratch_shapes=[pltpu.VMEM((length, head), f32)] * 2,
        compiler_params=pltpu.CompilerParams(vmem_limit_bytes=48 * 2**20),
        cost_estimate=pl.CostEstimate(
            flops=10 * pairs * head, bytes_accessed=16 * length * heads * head, transcendentals=pairs
        ),
        name="attend_back",
    )(q, k, v, mixed, dmixed, cosine, sine, seg_row, seg_col, *before)


def units_kernel(chunk, x, dy, gate, up, down, *rest):
    units, dgate, dup = rest[-3:]
    gate_w, up_w, down_w = gate[...], up[...], down[...]

    def step(i, carry):
        rows = pl.ds(pl.multiple_of(i * chunk, chunk), chunk)
        gpre = product(x[rows, :], gate_w)
        upre = product(x[rows, :], up_w)
        dunits = product_t(dy[rows, :], down_w)
        s = jax.nn.sigmoid(gpre)
        silu = gpre * s
        units[rows, :] = (silu * upre).astype(bf16)
        dgate[rows, :] = (dunits * upre * (s * (1.0 + gpre * (1.0 - s)))).astype(bf16)
        dup[rows, :] = (dunits * silu).astype(bf16)
        return carry

    lax.fori_loop(0, x.shape[0] // chunk, step, 0)


def expert_units(x, dy, gate, up, down, start, stop, half=None, made=(), before=()):
    rows, width = x.shape
    units = stop - start
    part, at = (rows, 0) if half is None else (rows // 2, half)
    chunk = tile_of(part)
    tile = unit_tile(gate.shape[1])
    first = start // tile
    once = pl.BlockSpec((part, width), lambda j: (at, 0), pipeline_mode=pl.Buffered(1))
    out = jax.ShapeDtypeStruct((rows, units), bf16)
    return pl.pallas_call(
        functools.partial(units_kernel, chunk),
        grid=(units // tile,),
        in_specs=[
            once,
            once,
            pl.BlockSpec((width, tile), lambda j: (0, first + j)),
            pl.BlockSpec((width, tile), lambda j: (0, first + j)),
            pl.BlockSpec((tile, width), lambda j: (first + j, 0)),
        ]
        + [pl.BlockSpec(memory_space=pl.ANY)] * (len(made) + len(before)),
        out_specs=[pl.BlockSpec((part, tile), lambda j: (at, j))] * 3,
        out_shape=[out] * 3,
        input_output_aliases={5 + i: i for i in range(len(made))},
        compiler_params=pltpu.CompilerParams(vmem_limit_bytes=56 * 2**20),
        cost_estimate=pl.CostEstimate(
            flops=6 * part * width * units,
            bytes_accessed=4 * part * width + 6 * width * units + 6 * part * units,
            transcendentals=part * units,
        ),
        name="expert_units",
    )(x, dy, gate, up, down, *made, *before)


def unit_tile(units):
    return 256 if units % 256 == 0 else units


def unit_cut(units):
    tile = unit_tile(units)
    return units // tile * 3 // 4 * tile


def dispatch_kernel(me, hidden, dout, slot, routes, router, *rest):
    rows, dy_rows, gate = rest[-3:]
    size = hidden.shape[1] * hidden.shape[3]
    width = hidden.shape[4]
    mine = me[3]
    tokens = hidden[...].reshape(size, width)
    logits = product(tokens, router[...])
    lanes = lax.broadcasted_iota(jnp.int32, logits.shape, 1)
    first, second = routes[0, :, 0:1], routes[0, :, 1:2]
    one = jnp.sum(jnp.where(lanes == first, logits, 0.0), axis=1, keepdims=True)
    two = jnp.sum(jnp.where(lanes == second, logits, 0.0), axis=1, keepdims=True)
    top = jnp.maximum(one, two)
    one, two = jnp.exp(one - top), jnp.exp(two - top)
    share = jnp.where(first == mine, one, jnp.where(second == mine, two, 0.0)) / (one + two)
    gate[0] = share
    chosen = (
        lax.broadcasted_iota(jnp.int32, (rows.shape[1], size), 0) == slot[0]
    ).astype(bf16)
    rows[0] = product(chosen, tokens).astype(bf16)
    dy = (share * dout[...].reshape(size, width).astype(f32)).astype(bf16)
    dy_rows[0] = product(chosen, dy).astype(bf16)


def block_place(b, span):
    return lax.rem(b, 4 * span) // span, (b // (4 * span)) * span + lax.rem(b, span)


def plane_block(seq_n, piece, width, first=0, seen=None):
    span = seq_n // 2

    def index(b, me):
        device, place = block_place(b + first, span)
        return (device, 0, place if seen is None else lax.rem(place, seen), 0, 0)

    return pl.BlockSpec((1, 2, 1, piece, width), index)


def relative_block(seq_n, piece, width):
    def index(b, me):
        device, place = block_place(b, seq_n // 2)
        return (lax.rem(device // 2 + me[0], 2), lax.rem(device + me[1], 2), 0, place, 0, 0)

    return pl.BlockSpec((1, 1, 2, 1, piece, width), index)


def dispatch(me, hidden, dout, slot, routes, router, seq_n, piece, cap, half, made=()):
    blocks, size = slot.shape[0], slot.shape[2]
    width = hidden.shape[1]
    span = seq_n // 2
    count = blocks // 2
    first = half * count

    def each(*shape):
        return pl.BlockSpec((1,) + shape, lambda b, me: (first + b, 0, 0))

    out = jax.ShapeDtypeStruct((blocks, cap, width), bf16)
    spare = jnp.zeros((width, 128 - router.shape[1]), router.dtype)
    return pl.pallas_call(
        dispatch_kernel,
        grid_spec=pltpu.PrefetchScalarGridSpec(
            num_scalar_prefetch=1,
            grid=(count,),
            in_specs=[
                plane_block(seq_n, piece, width, first, span),
                plane_block(seq_n, piece, width, first),
                each(1, size),
                each(size, routes.shape[2]),
                pl.BlockSpec((width, 128), lambda b, me: (0, 0)),
            ]
            + [pl.BlockSpec(memory_space=pl.ANY)] * len(made),
            out_specs=[each(cap, width), each(cap, width), each(size, 1)],
        ),
        out_shape=[out, out, jax.ShapeDtypeStruct((blocks, size, 1), f32)],
        input_output_aliases={6 + i: i for i in range(len(made))},
        compiler_params=pltpu.CompilerParams(vmem_limit_bytes=40 * 2**20),
        cost_estimate=pl.CostEstimate(
            flops=4 * count * size * width * (cap + 64),
            bytes_accessed=4 * count * (size + cap) * width,
            transcendentals=2 * count * size,
        ),
        name="dispatch",
    )(
        me,
        hidden.reshape(4, 2, span, piece, width),
        dout.reshape(4, 2, seq_n, piece, width),
        slot,
        routes,
        jnp.concatenate([router, spare], axis=1),
        *made,
    )


def spread_rows(slot, rows):
    size, cap = slot.shape[0], rows.shape[0]
    chosen = (lax.broadcasted_iota(jnp.int32, (size, cap), 1) == slot).astype(bf16)
    return product(chosen, rows)


def place_cores(me, out, dense):
    piece = out.shape[4]
    for core in range(2):
        out[0, 0, lax.rem(me[2] + core, 2), 0] = dense[core * piece : (core + 1) * piece, :].astype(bf16)


def combine_kernel(me, rows, slot, gate, dout, out, dgate):
    dense = spread_rows(slot[0], rows[0])
    grads = dout[...].reshape(dense.shape).astype(f32)
    dgate[0] = jnp.sum(grads * dense, axis=1, keepdims=True)
    place_cores(me, out, gate[0] * dense)


def collect_kernel(me, left, slot, right, *rest):
    dense = [spread_rows(slot[0], left[0]), spread_rows(slot[0], right[0])]
    place_cores(me, rest[-1], jnp.concatenate(dense, axis=1))


def combine(me, rows, slot, seq_n, piece, gate=None, dout=None, right=None):
    blocks, cap, part = rows.shape
    size = slot.shape[1]
    width = part if right is None else 2 * part
    column = pl.BlockSpec((1, size, 1), lambda b, me: (b, 0, 0))
    weigh = gate is not None
    operands = [rows, slot]
    in_specs = [pl.BlockSpec((1, cap, part), lambda b, me: (b, 0, 0)), column]
    out_specs = [relative_block(seq_n, piece, width)]
    out_shape = [jax.ShapeDtypeStruct((2, 2, 2, seq_n, piece, width), bf16)]
    if weigh:
        operands += [gate, dout.reshape(4, 2, seq_n, piece, width)]
        in_specs += [column, plane_block(seq_n, piece, width)]
        out_specs += [column]
        out_shape += [jax.ShapeDtypeStruct((blocks, size, 1), f32)]
    else:
        operands += [right]
        in_specs += in_specs[:1]
    return pl.pallas_call(
        combine_kernel if weigh else collect_kernel,
        grid_spec=pltpu.PrefetchScalarGridSpec(
            num_scalar_prefetch=1, grid=(blocks,), in_specs=in_specs, out_specs=out_specs
        ),
        out_shape=out_shape,
        compiler_params=pltpu.CompilerParams(vmem_limit_bytes=40 * 2**20),
        cost_estimate=pl.CostEstimate(
            flops=2 * blocks * size * width * cap,
            bytes_accessed=2 * blocks * (2 * size + cap) * width,
            transcendentals=0,
        ),
        name="combine" if weigh else "collect",
    )(me, *operands)


def down_kernel(cut, units_a, units_b, down, *rest):
    total = product(units_a[...], down[:cut, :]) + product(units_b[...], down[cut:, :])
    rest[-1][...] = total.astype(bf16)


def expert_down(units_a, units_b, down, *before):
    rows, cut = units_a.shape
    inner, width = down.shape
    m, n = tile_of(rows), tile_of(width)
    return pl.pallas_call(
        functools.partial(down_kernel, cut),
        grid=(width // n, rows // m),
        in_specs=[
            pl.BlockSpec((m, cut), lambda j, i: (i, 0)),
            pl.BlockSpec((m, inner - cut), lambda j, i: (i, 0)),
            pl.BlockSpec((inner, n), lambda j, i: (0, j)),
        ]
        + [pl.BlockSpec(memory_space=pl.ANY)] * len(before),
        out_specs=pl.BlockSpec((m, n), lambda j, i: (i, j)),
        out_shape=jax.ShapeDtypeStruct((rows, width), bf16),
        compiler_params=pltpu.CompilerParams(vmem_limit_bytes=48 * 2**20),
        cost_estimate=pl.CostEstimate(
            flops=2 * rows * inner * width,
            bytes_accessed=2 * (rows * inner + inner * width + rows * width),
            transcendentals=0,
        ),
        name="expert_down",
    )(units_a, units_b, down, *before)


def input_kernel(cut, dgate_a, dgate_b, dup_a, dup_b, gate, up, *rest):
    total = product_t(dgate_a[...], gate[:, :cut]) + product_t(dgate_b[...], gate[:, cut:])
    total += product_t(dup_a[...], up[:, :cut]) + product_t(dup_b[...], up[:, cut:])
    rest[-1][...] = total.astype(bf16)


def expert_input_grad(dgate_a, dgate_b, dup_a, dup_b, gate, up, start, stop, *before):
    rows, cut = dgate_a.shape
    inner = gate.shape[1]
    width = stop - start
    m, n = tile_of(rows), tile_of(width)
    first = start // n
    left_a = pl.BlockSpec((m, cut), lambda j, i: (i, 0))
    left_b = pl.BlockSpec((m, inner - cut), lambda j, i: (i, 0))
    right = pl.BlockSpec((n, inner), lambda j, i: (first + j, 0))
    return pl.pallas_call(
        functools.partial(input_kernel, cut),
        grid=(width // n, rows // m),
        in_specs=[left_a, left_b, left_a, left_b, right, right]
        + [pl.BlockSpec(memory_space=pl.ANY)] * len(before),
        out_specs=pl.BlockSpec((m, n), lambda j, i: (i, j)),
        out_shape=jax.ShapeDtypeStruct((rows, width), bf16),
        compiler_params=pltpu.CompilerParams(vmem_limit_bytes=52 * 2**20),
        cost_estimate=pl.CostEstimate(
            flops=4 * rows * inner * width,
            bytes_accessed=2 * (2 * rows * inner + 2 * inner * width + rows * width),
            transcendentals=0,
        ),
        name="expert_input_grad",
    )(dgate_a, dgate_b, dup_a, dup_b, gate, up, *before)


def tile_of(size):
    return max(c for c in range(16, 513, 16) if size % c == 0)


def anchor_kernel(*refs):
    pass


def after(a, *before):
    return pl.pallas_call(
        anchor_kernel,
        in_specs=[pl.BlockSpec(memory_space=pl.ANY)] * (1 + len(before)),
        out_specs=pl.BlockSpec(memory_space=pl.ANY),
        out_shape=jax.ShapeDtypeStruct(a.shape, a.dtype),
        input_output_aliases={0: 0},
        cost_estimate=pl.CostEstimate(flops=0, bytes_accessed=0, transcendentals=0),
        name="after",
    )(a, *before)


def norm_backward(grad_rows, normed, inverse, gain):
    weighted = grad_rows * gain
    mean_term = jnp.mean(weighted * normed, axis=-1, keepdims=True)
    return inverse * (weighted - normed * mean_term), jnp.sum(grad_rows * normed, axis=0)


def pick(a, index, axis):
    return lax.dynamic_index_in_dim(a, index, axis, keepdims=False)


def on_device(
    sizes,
    tokens,
    segments,
    routes,
    attn_norm,
    query_weight,
    key_weight,
    value_weight,
    output_weight,
    expert_norm,
    router,
    gate_weight,
    up_weight,
    down_weight,
    grad_out,
):
    dp_n, seq_n, r_n, y_n, core_n = sizes
    parts = r_n * core_n
    seq_count, seq_dev, width = tokens.shape
    piece = seq_dev // core_n
    length = segments.shape[1]
    home = seq_n * piece
    head = width // HEADS
    heads = HEADS // parts
    columns = width // parts
    experts = router.shape[1]
    topk = routes.shape[2]
    plane = 8 * home
    blocks = plane // seq_dev
    cap = 5 * seq_dev * topk // (4 * experts)
    dp_i, seq_i, r_i, y_i, core_i = (lax.axis_index(a) for a in EVERY)
    group, member = seq_i // seq_count, seq_i % seq_count

    rows_here = query_weight.shape[0]
    if r_n == 1 and parts == 2 and dp_n == 2 and y_n == 2 and seq_n == 2 * seq_count:
        weights, token_home, grad_home, chip_segments = first_transfers(
            query_weight, key_weight, value_weight, output_weight, tokens, grad_out, segments, sizes
        )
        segment = pick(pick(chip_segments, group, 0), member, 0)
    else:
        local = jnp.concatenate([query_weight, key_weight, value_weight, output_weight], axis=1)
        local = chip_exchange(local.reshape(rows_here, 4, parts, columns), 2, 0, parts)
        weights = lax.all_gather(
            local.reshape(parts * rows_here, 4 * columns), SPREAD, axis=0, tiled=True
        )
        weights = (
            weights.reshape(dp_n * seq_n, y_n, r_n, core_n * rows_here, -1)
            .transpose(0, 2, 1, 3, 4)
            .reshape(width, -1)
        )
        token_home, grad_home = to_sequences(tokens), to_sequences(grad_out)
        chip_segments = lax.all_gather(segments, "core")
        segment = pick(pick(chip_segments, group, 0), member, 0)
    weight_in, weight_out = weights[:, : 3 * columns], weights[:, 3 * columns :]

    token_float = token_home.astype(f32)
    inverse_one = lax.rsqrt(jnp.mean(token_float * token_float, axis=-1, keepdims=True) + epsilon)
    hidden_one = (token_float * inverse_one * attn_norm).astype(bf16)
    hidden_full = chip_gather(hidden_one, 1, parts).reshape(length, width)

    grad_plane = lax.all_gather(grad_home.reshape(home, width), PLANE, axis=0, tiled=True)

    half = head // 2
    frequency = theta_base ** (-jnp.arange(half, dtype=f32) / half)
    angles = jnp.arange(length, dtype=f32)[:, None] * frequency[None, :]
    cosine = jnp.concatenate([jnp.cos(angles)] * 2, axis=1)
    sine = jnp.concatenate([-jnp.sin(angles), jnp.sin(angles)], axis=1)
    seg_row, seg_col = segment[None, :], segment[:, None]

    qkv = product(hidden_full, weight_in)
    query, keys, values, mixed = attend(qkv, cosine, sine, seg_row, seg_col, heads)
    mixed_full = chip_gather(mixed, 1, parts)
    branch = product(mixed_full, weight_out).reshape(seq_n, parts, piece, columns)
    branch = chip_exchange(branch, 1, 3, parts).reshape(seq_n, piece, width)
    residual = token_float + branch
    inverse_two = lax.rsqrt(jnp.mean(residual * residual, axis=-1, keepdims=True) + epsilon)
    normed_two = residual * inverse_two
    hidden_two = (normed_two * expert_norm).astype(bf16).reshape(home, width)
    hidden_two = after(hidden_two, grad_plane)

    hidden_parts = [
        lax.all_gather(part, PLANE, axis=0, tiled=True) for part in jnp.split(hidden_two, 2)
    ]
    small = after(jnp.transpose(routes, (2, 0, 1)).reshape(topk * seq_count, seq_dev), hidden_two)
    small = lax.all_gather(small, EVERY, axis=0, tiled=True).reshape(
        dp_n, seq_n, r_n, y_n, core_n, topk, seq_count, seq_dev
    )
    small = pick(pick(small, group, 4), member, 5)
    plane_routes = pick(small, r_i, 2).transpose(0, 2, 1, 3, 4)
    block_routes = plane_routes.reshape(4, 2, seq_n // 2, topk, seq_dev)
    block_routes = block_routes.transpose(1, 0, 2, 3, 4).reshape(blocks, topk, seq_dev)
    home_routes = (
        pick(pick(plane_routes, dp_i, 0), y_i, 0)
        .reshape(seq_n, topk, core_n, piece)
        .transpose(1, 2, 0, 3)
    )
    home_routes = pick(home_routes, core_i, 1).reshape(topk, home)
    mine = y_i * core_n + core_i
    chosen = jnp.any(block_routes == mine, axis=1)
    places = jnp.arange(seq_dev)
    rank = product(chosen.astype(bf16), (places[:, None] < places[None, :]).astype(bf16))
    slot = jnp.where(chosen, rank.astype(jnp.int32), -1)
    slot_row, slot_col = slot[:, None, :], slot[:, :, None]
    me = jnp.stack([dp_i, y_i, core_i, mine]).astype(jnp.int32)
    gate_one, up_one, down_one = gate_weight[0], up_weight[0], down_weight[0]
    inner = gate_one.shape[1]
    cut = unit_cut(inner)
    full = (gate_one, up_one, down_one)
    route_col = jnp.transpose(block_routes, (0, 2, 1))
    picked, unit_parts = (), ()
    for part, hidden_part in enumerate(hidden_parts):
        picked = dispatch(
            me, hidden_part, grad_plane, slot_row, route_col, router, seq_n, piece, cap, part, picked
        )
        expert_in, dy_rows = (rows.reshape(blocks * cap, width) for rows in picked[:2])
        unit_parts = expert_units(expert_in, dy_rows, *full, 0, cut, part, unit_parts)
    row_gate = picked[2]
    units_a, dgpre_a, dupre_a = unit_parts

    def over_ctx(part):
        return lax.psum_scatter(part, CTX, scatter_dimension=0, tiled=True)

    def rows_product(rows, part):
        return t_product(rows, part).astype(bf16)

    down_a = rows_product(dy_rows, units_a)
    units_b, dgpre_b, dupre_b = expert_units(expert_in, dy_rows, *full, cut, inner, before=(down_a,))
    down_b = rows_product(dy_rows, units_b)
    down_sum_a, down_sum_b = over_ctx(down_a), over_ctx(down_b)
    grads = (dgpre_a, dgpre_b, dupre_a, dupre_b, gate_one, up_one)
    left = expert_input_grad(*grads, 0, width // 2, down_b)
    right = expert_input_grad(*grads, width // 2, width, left)
    left, right = (part.reshape(blocks, cap, width // 2) for part in (left, right))
    [back] = combine(me, left, slot_col, seq_n, piece, right=right)
    gate_a = rows_product(expert_in, after(dgpre_a, back, down_sum_a))
    gate_b = rows_product(expert_in, after(dgpre_b, back))
    gate_sum_a, gate_sum_b = over_ctx(gate_a), over_ctx(gate_b)
    ypair = expert_down(units_a, units_b, down_one, gate_a)
    mixed_rows, dgate_plane = combine(
        me, ypair.reshape(blocks, cap, width), slot_col, seq_n, piece, row_gate, grad_plane
    )

    dgate_plane = dgate_plane.reshape(2, 4, seq_n // 2, core_n, piece).transpose(1, 3, 0, 2, 4)
    dgate_home = lax.all_to_all(
        dgate_plane.reshape(8, home), PLANE, split_axis=0, concat_axis=0, tiled=True
    ).reshape(dp_n, experts, home).sum(axis=0)

    logits = product(hidden_two, router)
    hot = home_routes[:, :, None] == jnp.arange(experts, dtype=jnp.int32)[None, None, :]
    gates = jax.nn.softmax(jnp.sum(jnp.where(hot, logits[None], 0.0), axis=2), axis=0)
    dgate = jnp.sum(jnp.where(hot, jnp.transpose(dgate_home)[None], 0.0), axis=2)
    dsel = gates * (dgate - jnp.sum(gates * dgate, axis=0, keepdims=True))
    dlogits = jnp.sum(jnp.where(hot, dsel[:, :, None], 0.0), axis=0).astype(bf16)
    router_grad = t_product(hidden_two, dlogits)
    def once_gate(stage, *arrays):
        return (after(arrays[0], gate_a),) + arrays[1:] if stage == 0 else arrays

    dhidden_two = plane_scatter(back, once_gate).reshape(home, width) + product_t(dlogits, router)

    flat_two = normed_two.reshape(home, width)
    dresid, expert_norm_grad = norm_backward(
        dhidden_two, flat_two, inverse_two.reshape(home, 1), expert_norm
    )
    dresid = dresid + grad_home.reshape(home, width).astype(f32)
    dbranch = chip_gather(dresid.astype(bf16).reshape(seq_n, piece, width), 1, parts).reshape(length, width)
    column_start = (r_i * core_n + core_i) * columns
    dbranch_here = lax.dynamic_slice_in_dim(dbranch, column_start, columns, 1)
    dmixed = chip_scatter(product_t(dbranch_here, weight_out).astype(bf16), 1, parts).astype(bf16)
    stages = {}

    def check(stage, *arrays):
        stages[stage] = arrays
        return arrays

    mixture = plane_scatter(after(mixed_rows, dbranch), check)
    up_b = rows_product(expert_in, after(dupre_b, dbranch))
    dqpre, dkpre, dvpre = attend_back(
        query, keys, values, mixed, dmixed, cosine, sine, seg_row, seg_col, heads, down_sum_b, up_b, *stages[0]
    )
    dqkv = jnp.concatenate([dqpre, dkpre, dvpre], axis=1)
    out_grad = t_product(mixed_full, after(dbranch_here, dqpre)).astype(bf16)
    in_grad = t_product(hidden_full, after(dqkv, out_grad)).astype(bf16)
    up_a = rows_product(expert_in, after(dupre_a, in_grad))
    dhidden_part = product_t(after(dqkv, up_a, *stages[1]), weight_in).astype(bf16)
    dhidden_one = chip_scatter(
        dhidden_part.reshape(seq_n, parts * piece, width), 1, parts
    )
    normed_one = token_float * inverse_one
    dtokens, attn_norm_grad = norm_backward(
        dhidden_one.reshape(home, width),
        normed_one.reshape(home, width),
        inverse_one.reshape(home, 1),
        attn_norm,
    )
    dtokens = (dtokens + dresid).astype(bf16).reshape(seq_n, piece, width)
    output = (residual + mixture).astype(bf16)

    grad_down = jnp.concatenate([down_sum_a, down_sum_b], axis=1).astype(f32).T[None]
    grad_gate = jnp.concatenate([gate_sum_a, gate_sum_b], axis=1).astype(f32)[None]
    grad_up = jnp.concatenate([over_ctx(up_a), over_ctx(up_b)], axis=1).astype(f32)[None]

    def seen(part):
        return part.reshape(dp_n, seq_n, r_n, y_n, core_n * rows_here, -1)

    def half(a, axis, index, name):
        keep, give = pick(a, index, axis), pick(a, 1 - index, axis)
        return total(keep, swap(give, name)).astype(bf16)

    first = [half(seen(a), 0, dp_i, "dp") for a in (out_grad, in_grad[:, :columns])]
    first.append(half(seen(in_grad[:, columns:]), 3, y_i, "y"))
    second = [half(a, 2, y_i, "y") for a in first[:2]] + [half(first[2], 0, dp_i, "dp")]
    second = jnp.concatenate(second, axis=-1)
    if r_n == 1 and parts == 2 and seq_n == 2 * seq_count:
        part, grad_tokens, output = last_transfers(
            second.reshape(seq_n, core_n * rows_here, 4 * columns), dtokens, output, seq_count
        )
        part = total(*(part[:, i] for i in range(seq_n))).reshape(core_n, rows_here, 4, columns)
        part = part.transpose(1, 2, 0, 3).reshape(rows_here, 4, width)
    else:
        grad_tokens = from_sequences(dtokens)
        output = from_sequences(output)
        part = total(*seq_pieces(second)).astype(bf16)
        part = part.reshape(parts, rows_here, 4, 1, columns)
        part = chip_exchange(part, 0, 3, parts).reshape(rows_here, 4, width).astype(f32)
    grad_output, grad_query, grad_key, grad_value = (part[:, i] for i in range(4))
    grad_tokens = grad_tokens.astype(f32)

    gains = jnp.concatenate([attn_norm_grad[None], expert_norm_grad[None], router_grad.T], axis=0)
    gain_n = gains.shape[0]
    gains = gains.reshape(gain_n, -1, rows_here).transpose(1, 0, 2)
    gains = lax.all_to_all(gains, EVERY, split_axis=0, concat_axis=0, tiled=True)
    gains = jnp.sum(gains, axis=0).T

    return (
        output,
        grad_tokens,
        gains[:, 0],
        grad_query,
        grad_key,
        grad_value,
        grad_output,
        gains[:, 1],
        gains[:, 2:],
        grad_gate,
        grad_up,
        grad_down,
    )


def solution(mesh):
    dp_n, ctx_n, exp_n = mesh.shape["dp"], mesh.shape["ctx"], mesh.shape["exp"]

    def block(*arrays):
        tokens = arrays[0]
        seq_count = tokens.shape[0] // (dp_n * exp_n)
        seq_n = seq_count * CORES
        sizes = (dp_n, seq_n, ctx_n // seq_n, exp_n // CORES, CORES)
        fine = Mesh(mesh.devices.reshape(sizes), EVERY)
        group = ("dp", "y", "core")
        exp = ("y", "core")
        return jax.shard_map(
            functools.partial(on_device, sizes),
            mesh=fine,
            in_specs=(
                P(group, CTX, None),
                P(group, None),
                P(group, CTX, None),
                P(),
                P(EVERY, None),
                P(EVERY, None),
                P(EVERY, None),
                P(EVERY, None),
                P(),
                P(),
                P(exp, None, "dp"),
                P(exp, None, "dp"),
                P(exp, "dp", None),
                P(group, CTX, None),
            ),
            out_specs=(
                P(group, CTX, None),
                P(group, CTX, None),
                P(EVERY),
                P(EVERY, None),
                P(EVERY, None),
                P(EVERY, None),
                P(EVERY, None),
                P(EVERY),
                P(EVERY, None),
                P(exp, CTX, "dp"),
                P(exp, CTX, "dp"),
                P(exp, "dp", CTX),
            ),
            check_vma=False,
        )(*arrays)

    return block
```

```python
import functools

import jax
import jax.numpy as jnp
from jax import lax
from jax.experimental import pallas as pl
from jax.experimental.pallas import tpu as pltpu
from jax.sharding import Mesh, PartitionSpec as P

HEADS = 16
CORES = 2

epsilon = 1e-05
theta_base = 10000.0
masked_score = -1e30
bf16 = jnp.bfloat16
f32 = jnp.float32

PLANE = ("dp", "y", "core")
CHIP = ("r", "core")
SPREAD = ("dp", "seq", "y")
CTX = ("seq", "r")
EVERY = ("dp", "seq", "r", "y", "core")


def product(a, b):
    return jnp.dot(a, b, preferred_element_type=f32)


def product_t(a, b):
    return lax.dot_general(a, b, (((1,), (1,)), ((), ())), preferred_element_type=f32)


def t_product(a, b):
    return lax.dot_general(a, b, (((0,), (0,)), ((), ())), preferred_element_type=f32)


def swap(a, axis):
    return lax.ppermute(a, axis, [(0, 1), (1, 0)])


def halves(a, axis):
    size = a.shape[axis] // 2
    me = lax.axis_index("core")
    mine = lax.dynamic_slice_in_dim(a, me * size, size, axis)
    other = lax.dynamic_slice_in_dim(a, (1 - me) * size, size, axis)
    return mine, other


def by_core(mine, other, axis):
    first = lax.axis_index("core") == 0
    return jnp.concatenate([jnp.where(first, mine, other), jnp.where(first, other, mine)], axis=axis)


def chip_gather(a, axis, parts):
    if parts == 2:
        return by_core(a, swap(a, "core"), axis)
    return lax.all_gather(a, CHIP, axis=axis, tiled=True)


def chip_scatter(a, axis, parts):
    if parts == 2:
        mine, other = halves(a, axis)
        return mine.astype(f32) + swap(other, "core").astype(f32)
    return lax.psum_scatter(a, CHIP, scatter_dimension=axis, tiled=True).astype(f32)


def chip_exchange(a, split, concat, parts):
    if parts == 2:
        mine, other = halves(a, split)
        return by_core(mine, swap(other, "core"), concat)
    return lax.all_to_all(a, CHIP, split_axis=split, concat_axis=concat, tiled=True)


def core_exchange(a, split, concat):
    mine, other = halves(a, split)
    return by_core(mine, swap(other, "core"), concat)


def seq_pieces(a):
    count = a.shape[0]
    me = lax.axis_index("seq")
    pieces = [pick(a, me, 0)]
    for step in range(1, count):
        give = pick(a, lax.rem(me + step, count), 0)
        pieces.append(lax.ppermute(give, "seq", [(i, (i + step) % count) for i in range(count)]))
    return pieces


def seq_exchange(a):
    count = a.shape[0]
    me = lax.axis_index("seq")
    pieces = jnp.stack(seq_pieces(a))
    return jnp.stack([pick(pieces, lax.rem(me + count - s, count), 0) for s in range(count)])


def to_sequences(a):
    return seq_exchange(core_exchange(a, 1, 0))


def from_sequences(a):
    return core_exchange(seq_exchange(a), 0, 1)


def total(*parts):
    return sum(part.astype(f32) for part in parts)


def plane_scatter(blocks, check=lambda stage, *arrays: arrays):
    held = total(blocks[:, :, 0], swap(blocks[:, :, 1], "core")).astype(bf16)
    [held] = check(0, held)
    half = blocks.shape[3] // 2
    by_x = swap(held[1, 1, :half], "dp")
    by_y = swap(held[1, 1, half:], "y")
    to_x = jnp.concatenate([held[1, 0, :half], total(held[1, 0, half:], by_y).astype(bf16)], axis=0)
    to_y = jnp.concatenate([total(held[0, 1, :half], by_x).astype(bf16), held[0, 1, half:]], axis=0)
    to_x, to_y = check(1, to_x, to_y)
    return total(held[0, 0], swap(to_x, "dp"), swap(to_y, "y"))


MESH = pl.DeviceIdType.MESH
Z_UP, Z_DOWN, X_A, Y_A, Y_B, X_B, Y_A2, X_B2 = range(8)


def first_kernel(
    query,
    key,
    value,
    output,
    tokens,
    grads,
    segments,
    weights,
    tokens_out,
    grads_out,
    segments_out,
    send,
    recv,
    core_send,
    core_recv,
    core_local,
    row_send,
    row_recv,
    row_local,
):
    dp, z, y, core = (lax.axis_index(a) for a in ("dp", "seq", "y", "core"))
    seq_n = weights.shape[1]
    rows, columns = query.shape[0], weights.shape[4] // 4
    half = weights.shape[4] // 2
    piece = tokens_out.shape[1]
    x_next, y_next, z_next, z_last, other = (
        {"dp": 1 - dp},
        {"y": 1 - y},
        {"seq": lax.rem(z + 1, seq_n)},
        {"seq": lax.rem(z + seq_n - 1, seq_n)},
        {"core": 1 - core},
    )

    barrier = pltpu.get_barrier_semaphore()
    partners = [x_next, y_next] + [
        {"seq": lax.rem(z + dz, seq_n), "core": lax.rem(core + dc, 2)}
        for dz in range(seq_n)
        for dc in range(2)
        if dz or dc
    ]
    for partner in partners:
        pl.semaphore_signal(barrier, inc=1, device_id=partner, device_id_type=MESH)
    pl.semaphore_wait(barrier, len(partners))

    here = pl.ds(pl.multiple_of(core * rows, rows), rows)
    locals_, remotes = [], []
    for m, matrix in enumerate((query, key, value, output)):
        place = weights.at[dp, z, y, here, pl.ds(m * columns, columns)]
        mine = matrix.at[:, pl.ds(pl.multiple_of(core * columns, columns), columns)]
        theirs = matrix.at[:, pl.ds(pl.multiple_of((1 - core) * columns, columns), columns)]
        locals_.append(pltpu.make_async_copy(mine, place, core_local.at[m]))
        remotes.append(
            pltpu.make_async_remote_copy(
                theirs, place, core_send.at[m], core_recv.at[m], device_id=other, device_id_type=MESH
            )
        )
    segment_local = pltpu.make_async_copy(segments, segments_out.at[core], core_local.at[4])
    segment_remote = pltpu.make_async_remote_copy(
        segments, segments_out.at[core], core_send.at[4], core_recv.at[4], device_id=other, device_id_type=MESH
    )
    for copy in remotes + [segment_remote] + locals_ + [segment_local]:
        copy.start()
    for copy in remotes + locals_:
        copy.wait()

    def part(kind, dp_b, z_b, y_b, device):
        if kind in (Z_UP, Z_DOWN):
            ref = weights.at[dp_b, z_b, y_b]
        else:
            start = 0 if kind in (X_A, Y_A, Y_A2) else half
            ref = weights.at[dp_b, z_b, y_b, :, pl.ds(start, half)]
        return pltpu.make_async_remote_copy(
            ref, ref, send.at[kind, z_b], recv.at[kind, z_b], device_id=device, device_id_type=MESH
        )

    def own(kind, z_b):
        device = {Z_UP: z_next, Z_DOWN: z_last, X_A: x_next, X_B: x_next, Y_A: y_next, Y_B: y_next}[kind]
        return part(kind, dp, z_b, y, device)

    def from_x(kind, z_b):
        return part(kind, 1 - dp, z_b, y, x_next)

    def from_y(kind, z_b):
        return part(kind, dp, z_b, 1 - y, y_next)

    def on_y(z_b):
        return part(Y_A2, 1 - dp, z_b, y, y_next)

    def on_x(z_b):
        return part(X_B2, dp, z_b, 1 - y, x_next)

    def spread(z_b):
        for kind in (X_A, Y_B, X_B, Y_A):
            own(kind, z_b).start()

    def relay(z_b):
        from_x(X_A, z_b).wait_recv()
        on_y(z_b).start()
        from_y(Y_B, z_b).wait_recv()
        on_x(z_b).start()

    def at_step(step, act_up, act_down):
        @pl.when(z - step >= 0)
        def _():
            act_up(z - step)

        @pl.when(z + step < seq_n)
        def _():
            act_down(z + step)

    def come_up(z_b):
        own(Z_UP, z_b).wait_recv()

        @pl.when(z < seq_n - 1)
        def _():
            own(Z_UP, z_b).start()

        spread(z_b)

    def come_down(z_b):
        own(Z_DOWN, z_b).wait_recv()

        @pl.when(z > 0)
        def _():
            own(Z_DOWN, z_b).start()

        spread(z_b)

    def rows_of(n, source, target, act):
        for s in range(tokens.shape[0]):
            z_to = tokens.shape[0] * core + s
            for d in range(2):
                core_to = lax.rem(core + d, 2)
                ref = source.at[s, pl.ds(pl.multiple_of(core_to * piece, piece), piece), :]
                copy = pltpu.make_async_remote_copy(
                    ref,
                    target.at[z],
                    row_send.at[n, s, d],
                    row_recv.at[n, z],
                    device_id={"seq": z_to, "core": core_to},
                    device_id_type=MESH,
                )
                if d:
                    act(copy)
                else:
                    keep = pltpu.make_async_copy(ref, target.at[z], row_local.at[n])

                    @pl.when(z_to != z)
                    def _(copy=copy):
                        act(copy)

                    @pl.when(z_to == z)
                    def _(keep=keep):
                        if act is begin:
                            keep.start()
                        else:
                            keep.wait()

    def begin(copy):
        copy.start()

    def sent(copy):
        copy.wait_send()

    def rows_in(n, target):
        group = z // tokens.shape[0]
        for z_from in range(seq_n):
            copy = pltpu.make_async_remote_copy(
                target.at[z_from],
                target.at[z_from],
                row_send.at[n, 0, 0],
                row_recv.at[n, z_from],
                device_id=other,
                device_id_type=MESH,
            )

            @pl.when((z_from != z) | (group != core))
            def _(copy=copy):
                copy.wait_recv()

    @pl.when(z < seq_n - 1)
    def _():
        own(Z_UP, z).start()

    @pl.when(z > 0)
    def _():
        own(Z_DOWN, z).start()

    spread(z)
    for step in range(1, seq_n):
        at_step(step, come_up, come_down)
        if step == 1:
            relay(z)
        else:
            at_step(step - 1, relay, relay)
        if step == seq_n - 2:
            rows_of(0, tokens, tokens_out, begin)
    rows_of(1, grads, grads_out, begin)
    at_step(seq_n - 1, relay, relay)

    segment_remote.wait()
    segment_local.wait()
    for z_b in range(seq_n):
        from_y(Y_A, z_b).wait_recv()
        from_x(X_B, z_b).wait_recv()
        part(Y_A2, 1 - dp, z_b, 1 - y, y_next).wait_recv()
        part(X_B2, 1 - dp, z_b, 1 - y, x_next).wait_recv()
        for kind in (X_A, Y_B, X_B, Y_A):
            own(kind, z_b).wait_send()
        on_y(z_b).wait_send()
        on_x(z_b).wait_send()

        @pl.when((z < seq_n - 1) & (z_b <= z))
        def _(z_b=z_b):
            own(Z_UP, z_b).wait_send()

        @pl.when((z > 0) & (z_b >= z))
        def _(z_b=z_b):
            own(Z_DOWN, z_b).wait_send()

    rows_of(0, tokens, tokens_out, sent)
    rows_of(1, grads, grads_out, sent)
    rows_in(0, tokens_out)
    rows_in(1, grads_out)


def first_transfers(query, key, value, output, tokens, grads, segments, sizes):
    dp_n, seq_n, r_n, y_n, core_n = sizes
    rows, width = query.shape
    piece = tokens.shape[1] // core_n
    columns = width // core_n
    held = pl.BlockSpec(memory_space=pl.ANY)
    out = jax.ShapeDtypeStruct((seq_n, piece, width), bf16)
    dma = pltpu.SemaphoreType.DMA
    weights, tokens, grads, segments = pl.pallas_call(
        first_kernel,
        in_specs=[held] * 7,
        out_specs=[held] * 4,
        out_shape=[
            jax.ShapeDtypeStruct((dp_n, seq_n, y_n, core_n * rows, 4 * columns), bf16),
            out,
            out,
            jax.ShapeDtypeStruct((core_n,) + segments.shape, segments.dtype),
        ],
        scratch_shapes=[
            dma((8, seq_n)),
            dma((8, seq_n)),
            dma((5,)),
            dma((5,)),
            dma((5,)),
            dma((2, tokens.shape[0], 2)),
            dma((2, seq_n)),
            dma((2,)),
        ],
        compiler_params=pltpu.CompilerParams(collective_id=0, has_side_effects=True),
        cost_estimate=pl.CostEstimate(flops=0, bytes_accessed=2 * 4 * columns * width, transcendentals=0),
        name="first_transfers",
    )(query, key, value, output, tokens, grads, segments)
    return weights.reshape(width, 4 * columns), tokens, grads, segments


def last_kernel(
    grads,
    tokens,
    output,
    grads_out,
    tokens_out,
    output_out,
    mine,
    theirs,
    pair_send,
    pair_recv,
    send,
    recv,
    row_send,
    row_recv,
    local,
):
    z, core = lax.axis_index("seq"), lax.axis_index("core")
    seq_n, piece = tokens.shape[:2]
    seq_count = tokens_out.shape[0]
    rows = grads.shape[1] // 2
    odd = lax.rem(z, 2)
    neighbour = z + 1 - 2 * odd
    far = lax.rem(z + 2, seq_n)

    barrier = pltpu.get_barrier_semaphore()
    partners = [
        {"seq": lax.rem(z + dz, seq_n), "core": lax.rem(core + dc, 2)}
        for dz in range(seq_n)
        for dc in range(2)
        if dz or dc
    ]
    for partner in partners:
        pl.semaphore_signal(barrier, inc=1, device_id=partner, device_id_type=MESH)
    pl.semaphore_wait(barrier, len(partners))

    pair = [
        pltpu.make_async_remote_copy(
            grads.at[2 * i + 1 - odd],
            theirs.at[i],
            pair_send.at[i],
            pair_recv.at[i],
            device_id={"seq": neighbour},
            device_id_type=MESH,
        )
        for i in range(2)
    ]
    kept = [pltpu.make_async_copy(grads.at[2 * i + odd], mine.at[i], local.at[3 + i]) for i in range(2)]

    def rows_to(core_to):
        return pl.ds(pl.multiple_of(core_to * rows, rows), rows)

    def far_copy(dc):
        core_to = lax.rem(core + dc, 2)
        return pltpu.make_async_remote_copy(
            mine.at[far // 2, rows_to(core_to), :],
            grads_out.at[core, 1],
            send.at[1, dc],
            recv.at[1, dc],
            device_id={"seq": far, "core": core_to},
            device_id_type=MESH,
        )

    def near_copy():
        return pltpu.make_async_remote_copy(
            mine.at[z // 2, rows_to(1 - core), :],
            grads_out.at[core, 0],
            send.at[0, 1],
            recv.at[0, 1],
            device_id={"core": 1 - core},
            device_id_type=MESH,
        )

    def own_copy():
        return pltpu.make_async_copy(
            mine.at[z // 2, rows_to(core), :], grads_out.at[core, 0], local.at[2]
        )

    def arrival(place, dc):
        ref = grads_out.at[lax.rem(core + dc, 2), place]
        return pltpu.make_async_remote_copy(
            ref,
            ref,
            send.at[place, dc],
            recv.at[place, dc],
            device_id={"core": 1 - core},
            device_id_type=MESH,
        )

    group, member = z // seq_count, lax.rem(z, seq_count)

    def row_place(target, s, c):
        return target.at[s, pl.ds(pl.multiple_of(c * piece, piece), piece), :]

    def row_copy(n, source, target, dz):
        z_to = lax.rem(z + dz, seq_n)
        return pltpu.make_async_remote_copy(
            source.at[z_to],
            row_place(target, member, core),
            row_send.at[n, dz],
            row_recv.at[n, member, core],
            device_id={"seq": z_to, "core": group},
            device_id_type=MESH,
        )

    def each_row(remote, kept):
        for n, source, target in ((0, tokens, tokens_out), (1, output, output_out)):
            for dz in range(seq_n):
                if dz:
                    remote(row_copy(n, source, target, dz))
                else:

                    @pl.when(group != core)
                    def _(copy=row_copy(n, source, target, 0)):
                        remote(copy)

                    @pl.when(group == core)
                    def _(n=n, source=source, target=target):
                        kept(
                            pltpu.make_async_copy(
                                source.at[z], row_place(target, member, core), local.at[n]
                            )
                        )

    for copy in pair + kept:
        copy.start()
    each_row(lambda copy: copy.start(), lambda copy: copy.start())

    for copy in kept:
        copy.wait()
    for copy in pair:
        copy.wait_recv()
    step = mine.shape[1] // 8

    def add(i, carry):
        span = pl.ds(pl.multiple_of(i * step, step), step)
        for part in range(2):
            mine[part, span, :] = total(mine[part, span, :], theirs[part, span, :]).astype(bf16)
        return carry

    lax.fori_loop(0, 8, add, 0)
    for copy in (far_copy(0), far_copy(1), near_copy(), own_copy()):
        copy.start()
    for copy in pair:
        copy.wait_send()
    own_copy().wait()
    for copy in (far_copy(0), far_copy(1), near_copy()):
        copy.wait_send()
    for place, dc in ((1, 0), (1, 1), (0, 1)):
        arrival(place, dc).wait_recv()
    each_row(lambda copy: copy.wait_send(), lambda copy: copy.wait())
    for n, target in ((0, tokens_out), (1, output_out)):
        for s in range(seq_count):
            for c in range(2):
                ref = row_place(target, s, c)
                copy = pltpu.make_async_remote_copy(
                    ref,
                    ref,
                    row_send.at[n, 0],
                    row_recv.at[n, s, c],
                    device_id=partners[0],
                    device_id_type=MESH,
                )

                @pl.when((z != seq_count * core + s) | (core != c))
                def _(copy=copy):
                    copy.wait_recv()


def last_transfers(grads, tokens, output, seq_count):
    seq_n, piece, width = tokens.shape
    rows = grads.shape[1] // 2
    held = pl.BlockSpec(memory_space=pl.ANY)
    out = jax.ShapeDtypeStruct((seq_count, 2 * piece, width), bf16)
    dma = pltpu.SemaphoreType.DMA
    return pl.pallas_call(
        last_kernel,
        in_specs=[held] * 3,
        out_specs=[held] * 3,
        out_shape=[jax.ShapeDtypeStruct((2, 2, rows, grads.shape[2]), bf16), out, out],
        scratch_shapes=[
            pltpu.VMEM((2,) + grads.shape[1:], bf16),
            pltpu.VMEM((2,) + grads.shape[1:], bf16),
            dma((2,)),
            dma((2,)),
            dma((2, 2)),
            dma((2, 2)),
            dma((2, seq_n)),
            dma((2, seq_count, 2)),
            dma((5,)),
        ],
        compiler_params=pltpu.CompilerParams(
            collective_id=1, has_side_effects=True, vmem_limit_bytes=24 * 2**20
        ),
        cost_estimate=pl.CostEstimate(flops=0, bytes_accessed=4 * grads.size, transcendentals=0),
        name="last_transfers",
    )(grads, tokens, output)


def visible_block(seg_row, seg_col, start, rows, cols):
    row_place = start + lax.broadcasted_iota(jnp.int32, (rows, cols), 0)
    col_place = lax.broadcasted_iota(jnp.int32, (rows, cols), 1)
    return (seg_col == seg_row) & (col_place <= row_place)


def turned(u, cosine, sine):
    return u * cosine + pltpu.roll(u, u.shape[1] // 2, 1) * sine


def attend_kernel(scale, block, qp, kp, vp, cosine, sine, seg_row, seg_col, q_out, k_out, v_out, mixed):
    length = qp.shape[0]
    q_out[...] = turned(qp[...], cosine[...], sine[...]).astype(bf16)
    k_out[...] = turned(kp[...], cosine[...], sine[...]).astype(bf16)
    v_out[...] = vp[...].astype(bf16)
    for start in range(0, length, block):
        stop = start + block
        scores = product_t(q_out[start:stop, :], k_out[:stop, :]) * scale
        seen = visible_block(seg_row[:, :stop], seg_col[start:stop, :], start, block, stop)
        scores = jnp.where(seen, scores, masked_score)
        top = jnp.max(scores, axis=1, keepdims=True)
        weights = jnp.exp(scores - top)
        total = jnp.sum(weights, axis=1, keepdims=True)
        summed = product(weights.astype(bf16), v_out[:stop, :])
        mixed[start:stop, :] = (summed / total).astype(bf16)


def attend(qkv, cosine, sine, seg_row, seg_col, heads):
    length, head = qkv.shape[0], cosine.shape[1]
    block = min(256, length)

    def column(offset):
        return pl.BlockSpec((length, head), lambda h: (0, offset + h))

    def whole(shape):
        return pl.BlockSpec(shape, lambda h: (0, 0))

    out = jax.ShapeDtypeStruct((length, heads * head), bf16)
    pairs = length * (length + block) // 2 * heads
    return pl.pallas_call(
        functools.partial(attend_kernel, head**-0.5, block),
        grid=(heads,),
        in_specs=[
            column(0),
            column(heads),
            column(2 * heads),
            whole((length, head)),
            whole((length, head)),
            whole((1, length)),
            whole((length, 1)),
        ],
        out_specs=[column(0)] * 4,
        out_shape=[out] * 4,
        compiler_params=pltpu.CompilerParams(vmem_limit_bytes=48 * 2**20),
        cost_estimate=pl.CostEstimate(
            flops=4 * pairs * head, bytes_accessed=20 * length * heads * head, transcendentals=pairs
        ),
        name="attend",
    )(qkv, qkv, qkv, cosine, sine, seg_row, seg_col)


def attend_back_kernel(
    scale, block, q, k, v, mixed, dmixed, cosine, sine, seg_row, seg_col, *rest
):
    dq_out, dk_out, dv_out, dk_sum, dv_sum = rest[-5:]
    length = q.shape[0]
    dk_sum[...] = jnp.zeros_like(dk_sum)
    dv_sum[...] = jnp.zeros_like(dv_sum)
    for start in range(0, length, block):
        stop = start + block
        scores = product_t(q[start:stop, :], k[:stop, :]) * scale
        seen = visible_block(seg_row[:, :stop], seg_col[start:stop, :], start, block, stop)
        scores = jnp.where(seen, scores, masked_score)
        top = jnp.max(scores, axis=1, keepdims=True)
        weights = jnp.exp(scores - top)
        inverse = 1.0 / jnp.sum(weights, axis=1, keepdims=True)
        grad = dmixed[start:stop, :].astype(f32)
        delta = jnp.sum(grad * mixed[start:stop, :].astype(f32), axis=1, keepdims=True) * inverse
        unit = (grad * inverse).astype(bf16)
        dweights = product_t(unit, v[:stop, :])
        dscores = (weights * (dweights - delta)).astype(bf16)
        dq = product(dscores, k[:stop, :]) * scale
        dq_out[start:stop, :] = turned(dq, cosine[start:stop, :], -sine[start:stop, :]).astype(bf16)
        dk_sum[:stop, :] += t_product(dscores, q[start:stop, :])
        dv_sum[:stop, :] += t_product(weights.astype(bf16), unit)
    dk_out[...] = turned(dk_sum[...] * scale, cosine[...], -sine[...]).astype(bf16)
    dv_out[...] = dv_sum[...].astype(bf16)


def attend_back(q, k, v, mixed, dmixed, cosine, sine, seg_row, seg_col, heads, *before):
    length, head = q.shape[0], cosine.shape[1]
    block = min(256, length)
    column = pl.BlockSpec((length, head), lambda h: (0, h))

    def whole(shape):
        return pl.BlockSpec(shape, lambda h: (0, 0))

    out = jax.ShapeDtypeStruct((length, heads * head), bf16)
    pairs = length * (length + block) // 2 * heads
    return pl.pallas_call(
        functools.partial(attend_back_kernel, head**-0.5, block),
        grid=(heads,),
        in_specs=[column] * 5
        + [whole((length, head)), whole((length, head)), whole((1, length)), whole((length, 1))]
        + [pl.BlockSpec(memory_space=pl.ANY)] * len(before),
        out_specs=[column] * 3,
        out_shape=[out] * 3,
        scratch_shapes=[pltpu.VMEM((length, head), f32)] * 2,
        compiler_params=pltpu.CompilerParams(vmem_limit_bytes=48 * 2**20),
        cost_estimate=pl.CostEstimate(
            flops=10 * pairs * head, bytes_accessed=16 * length * heads * head, transcendentals=pairs
        ),
        name="attend_back",
    )(q, k, v, mixed, dmixed, cosine, sine, seg_row, seg_col, *before)


def units_kernel(chunk, x, dy, gate, up, down, *rest):
    units, dgate, dup = rest[-3:]
    gate_w, up_w, down_w = gate[...], up[...], down[...]

    def step(i, carry):
        rows = pl.ds(pl.multiple_of(i * chunk, chunk), chunk)
        gpre = product(x[rows, :], gate_w)
        upre = product(x[rows, :], up_w)
        dunits = product_t(dy[rows, :], down_w)
        s = jax.nn.sigmoid(gpre)
        silu = gpre * s
        units[rows, :] = (silu * upre).astype(bf16)
        dgate[rows, :] = (dunits * upre * (s * (1.0 + gpre * (1.0 - s)))).astype(bf16)
        dup[rows, :] = (dunits * silu).astype(bf16)
        return carry

    lax.fori_loop(0, x.shape[0] // chunk, step, 0)


def expert_units(x, dy, gate, up, down, start, stop, half=None, made=(), before=()):
    rows, width = x.shape
    units = stop - start
    part, at = (rows, 0) if half is None else (rows // 2, half)
    chunk = tile_of(part)
    tile = unit_tile(gate.shape[1])
    first = start // tile
    once = pl.BlockSpec((part, width), lambda j: (at, 0), pipeline_mode=pl.Buffered(1))
    out = jax.ShapeDtypeStruct((rows, units), bf16)
    return pl.pallas_call(
        functools.partial(units_kernel, chunk),
        grid=(units // tile,),
        in_specs=[
            once,
            once,
            pl.BlockSpec((width, tile), lambda j: (0, first + j)),
            pl.BlockSpec((width, tile), lambda j: (0, first + j)),
            pl.BlockSpec((tile, width), lambda j: (first + j, 0)),
        ]
        + [pl.BlockSpec(memory_space=pl.ANY)] * (len(made) + len(before)),
        out_specs=[pl.BlockSpec((part, tile), lambda j: (at, j))] * 3,
        out_shape=[out] * 3,
        input_output_aliases={5 + i: i for i in range(len(made))},
        compiler_params=pltpu.CompilerParams(vmem_limit_bytes=56 * 2**20),
        cost_estimate=pl.CostEstimate(
            flops=6 * part * width * units,
            bytes_accessed=4 * part * width + 6 * width * units + 6 * part * units,
            transcendentals=part * units,
        ),
        name="expert_units",
    )(x, dy, gate, up, down, *made, *before)


def unit_tile(units):
    return 256 if units % 256 == 0 else units


def unit_cut(units):
    tile = unit_tile(units)
    return units // tile * 3 // 4 * tile


def dispatch_kernel(me, hidden, dout, slot, routes, router, *rest):
    rows, dy_rows, gate = rest[-3:]
    size = hidden.shape[1] * hidden.shape[3]
    width = hidden.shape[4]
    mine = me[3]
    tokens = hidden[...].reshape(size, width)
    logits = product(tokens, router[...])
    lanes = lax.broadcasted_iota(jnp.int32, logits.shape, 1)
    first, second = routes[0, :, 0:1], routes[0, :, 1:2]
    one = jnp.sum(jnp.where(lanes == first, logits, 0.0), axis=1, keepdims=True)
    two = jnp.sum(jnp.where(lanes == second, logits, 0.0), axis=1, keepdims=True)
    top = jnp.maximum(one, two)
    one, two = jnp.exp(one - top), jnp.exp(two - top)
    share = jnp.where(first == mine, one, jnp.where(second == mine, two, 0.0)) / (one + two)
    gate[0] = share
    chosen = (
        lax.broadcasted_iota(jnp.int32, (rows.shape[1], size), 0) == slot[0]
    ).astype(bf16)
    rows[0] = product(chosen, tokens).astype(bf16)
    dy = (share * dout[...].reshape(size, width).astype(f32)).astype(bf16)
    dy_rows[0] = product(chosen, dy).astype(bf16)


def block_place(b, span):
    return lax.rem(b, 4 * span) // span, (b // (4 * span)) * span + lax.rem(b, span)


def plane_block(seq_n, piece, width, first=0, seen=None):
    span = seq_n // 2

    def index(b, me):
        device, place = block_place(b + first, span)
        return (device, 0, place if seen is None else lax.rem(place, seen), 0, 0)

    return pl.BlockSpec((1, 2, 1, piece, width), index)


def relative_block(seq_n, piece, width):
    def index(b, me):
        device, place = block_place(b, seq_n // 2)
        return (lax.rem(device // 2 + me[0], 2), lax.rem(device + me[1], 2), 0, place, 0, 0)

    return pl.BlockSpec((1, 1, 2, 1, piece, width), index)


def dispatch(me, hidden, dout, slot, routes, router, seq_n, piece, cap, half, made=()):
    blocks, size = slot.shape[0], slot.shape[2]
    width = hidden.shape[1]
    span = seq_n // 2
    count = blocks // 2
    first = half * count

    def each(*shape):
        return pl.BlockSpec((1,) + shape, lambda b, me: (first + b, 0, 0))

    out = jax.ShapeDtypeStruct((blocks, cap, width), bf16)
    spare = jnp.zeros((width, 128 - router.shape[1]), router.dtype)
    return pl.pallas_call(
        dispatch_kernel,
        grid_spec=pltpu.PrefetchScalarGridSpec(
            num_scalar_prefetch=1,
            grid=(count,),
            in_specs=[
                plane_block(seq_n, piece, width, first, span),
                plane_block(seq_n, piece, width, first),
                each(1, size),
                each(size, routes.shape[2]),
                pl.BlockSpec((width, 128), lambda b, me: (0, 0)),
            ]
            + [pl.BlockSpec(memory_space=pl.ANY)] * len(made),
            out_specs=[each(cap, width), each(cap, width), each(size, 1)],
        ),
        out_shape=[out, out, jax.ShapeDtypeStruct((blocks, size, 1), f32)],
        input_output_aliases={6 + i: i for i in range(len(made))},
        compiler_params=pltpu.CompilerParams(vmem_limit_bytes=40 * 2**20),
        cost_estimate=pl.CostEstimate(
            flops=4 * count * size * width * (cap + 64),
            bytes_accessed=4 * count * (size + cap) * width,
            transcendentals=2 * count * size,
        ),
        name="dispatch",
    )(
        me,
        hidden.reshape(4, 2, span, piece, width),
        dout.reshape(4, 2, seq_n, piece, width),
        slot,
        routes,
        jnp.concatenate([router, spare], axis=1),
        *made,
    )


def spread_rows(slot, rows):
    size, cap = slot.shape[0], rows.shape[0]
    chosen = (lax.broadcasted_iota(jnp.int32, (size, cap), 1) == slot).astype(bf16)
    return product(chosen, rows)


def place_cores(me, out, dense):
    piece = out.shape[4]
    for core in range(2):
        out[0, 0, lax.rem(me[2] + core, 2), 0] = dense[core * piece : (core + 1) * piece, :].astype(bf16)


def combine_kernel(me, rows, slot, gate, dout, out, dgate):
    dense = spread_rows(slot[0], rows[0])
    grads = dout[...].reshape(dense.shape).astype(f32)
    dgate[0] = jnp.sum(grads * dense, axis=1, keepdims=True)
    place_cores(me, out, gate[0] * dense)


def collect_kernel(me, left, slot, right, *rest):
    dense = [spread_rows(slot[0], left[0]), spread_rows(slot[0], right[0])]
    place_cores(me, rest[-1], jnp.concatenate(dense, axis=1))


def combine(me, rows, slot, seq_n, piece, gate=None, dout=None, right=None):
    blocks, cap, part = rows.shape
    size = slot.shape[1]
    width = part if right is None else 2 * part
    column = pl.BlockSpec((1, size, 1), lambda b, me: (b, 0, 0))
    weigh = gate is not None
    operands = [rows, slot]
    in_specs = [pl.BlockSpec((1, cap, part), lambda b, me: (b, 0, 0)), column]
    out_specs = [relative_block(seq_n, piece, width)]
    out_shape = [jax.ShapeDtypeStruct((2, 2, 2, seq_n, piece, width), bf16)]
    if weigh:
        operands += [gate, dout.reshape(4, 2, seq_n, piece, width)]
        in_specs += [column, plane_block(seq_n, piece, width)]
        out_specs += [column]
        out_shape += [jax.ShapeDtypeStruct((blocks, size, 1), f32)]
    else:
        operands += [right]
        in_specs += in_specs[:1]
    return pl.pallas_call(
        combine_kernel if weigh else collect_kernel,
        grid_spec=pltpu.PrefetchScalarGridSpec(
            num_scalar_prefetch=1, grid=(blocks,), in_specs=in_specs, out_specs=out_specs
        ),
        out_shape=out_shape,
        compiler_params=pltpu.CompilerParams(vmem_limit_bytes=40 * 2**20),
        cost_estimate=pl.CostEstimate(
            flops=2 * blocks * size * width * cap,
            bytes_accessed=2 * blocks * (2 * size + cap) * width,
            transcendentals=0,
        ),
        name="combine" if weigh else "collect",
    )(me, *operands)


def down_kernel(cut, units_a, units_b, down, *rest):
    total = product(units_a[...], down[:cut, :]) + product(units_b[...], down[cut:, :])
    rest[-1][...] = total.astype(bf16)


def expert_down(units_a, units_b, down, *before):
    rows, cut = units_a.shape
    inner, width = down.shape
    m, n = tile_of(rows), tile_of(width)
    return pl.pallas_call(
        functools.partial(down_kernel, cut),
        grid=(width // n, rows // m),
        in_specs=[
            pl.BlockSpec((m, cut), lambda j, i: (i, 0)),
            pl.BlockSpec((m, inner - cut), lambda j, i: (i, 0)),
            pl.BlockSpec((inner, n), lambda j, i: (0, j)),
        ]
        + [pl.BlockSpec(memory_space=pl.ANY)] * len(before),
        out_specs=pl.BlockSpec((m, n), lambda j, i: (i, j)),
        out_shape=jax.ShapeDtypeStruct((rows, width), bf16),
        compiler_params=pltpu.CompilerParams(vmem_limit_bytes=48 * 2**20),
        cost_estimate=pl.CostEstimate(
            flops=2 * rows * inner * width,
            bytes_accessed=2 * (rows * inner + inner * width + rows * width),
            transcendentals=0,
        ),
        name="expert_down",
    )(units_a, units_b, down, *before)


def input_kernel(cut, dgate_a, dgate_b, dup_a, dup_b, gate, up, *rest):
    total = product_t(dgate_a[...], gate[:, :cut]) + product_t(dgate_b[...], gate[:, cut:])
    total += product_t(dup_a[...], up[:, :cut]) + product_t(dup_b[...], up[:, cut:])
    rest[-1][...] = total.astype(bf16)


def expert_input_grad(dgate_a, dgate_b, dup_a, dup_b, gate, up, start, stop, *before):
    rows, cut = dgate_a.shape
    inner = gate.shape[1]
    width = stop - start
    m, n = tile_of(rows), tile_of(width)
    first = start // n
    left_a = pl.BlockSpec((m, cut), lambda j, i: (i, 0))
    left_b = pl.BlockSpec((m, inner - cut), lambda j, i: (i, 0))
    right = pl.BlockSpec((n, inner), lambda j, i: (first + j, 0))
    return pl.pallas_call(
        functools.partial(input_kernel, cut),
        grid=(width // n, rows // m),
        in_specs=[left_a, left_b, left_a, left_b, right, right]
        + [pl.BlockSpec(memory_space=pl.ANY)] * len(before),
        out_specs=pl.BlockSpec((m, n), lambda j, i: (i, j)),
        out_shape=jax.ShapeDtypeStruct((rows, width), bf16),
        compiler_params=pltpu.CompilerParams(vmem_limit_bytes=52 * 2**20),
        cost_estimate=pl.CostEstimate(
            flops=4 * rows * inner * width,
            bytes_accessed=2 * (2 * rows * inner + 2 * inner * width + rows * width),
            transcendentals=0,
        ),
        name="expert_input_grad",
    )(dgate_a, dgate_b, dup_a, dup_b, gate, up, *before)


def tile_of(size):
    return max(c for c in range(16, 513, 16) if size % c == 0)


def anchor_kernel(*refs):
    pass


def after(a, *before):
    return pl.pallas_call(
        anchor_kernel,
        in_specs=[pl.BlockSpec(memory_space=pl.ANY)] * (1 + len(before)),
        out_specs=pl.BlockSpec(memory_space=pl.ANY),
        out_shape=jax.ShapeDtypeStruct(a.shape, a.dtype),
        input_output_aliases={0: 0},
        cost_estimate=pl.CostEstimate(flops=0, bytes_accessed=0, transcendentals=0),
        name="after",
    )(a, *before)


def norm_backward(grad_rows, normed, inverse, gain):
    weighted = grad_rows * gain
    mean_term = jnp.mean(weighted * normed, axis=-1, keepdims=True)
    return inverse * (weighted - normed * mean_term), jnp.sum(grad_rows * normed, axis=0)


def pick(a, index, axis):
    return lax.dynamic_index_in_dim(a, index, axis, keepdims=False)


def on_device(
    sizes,
    tokens,
    segments,
    routes,
    attn_norm,
    query_weight,
    key_weight,
    value_weight,
    output_weight,
    expert_norm,
    router,
    gate_weight,
    up_weight,
    down_weight,
    grad_out,
):
    dp_n, seq_n, r_n, y_n, core_n = sizes
    parts = r_n * core_n
    seq_count, seq_dev, width = tokens.shape
    piece = seq_dev // core_n
    length = segments.shape[1]
    home = seq_n * piece
    head = width // HEADS
    heads = HEADS // parts
    columns = width // parts
    experts = router.shape[1]
    topk = routes.shape[2]
    plane = 8 * home
    blocks = plane // seq_dev
    cap = 5 * seq_dev * topk // (4 * experts)
    dp_i, seq_i, r_i, y_i, core_i = (lax.axis_index(a) for a in EVERY)
    group, member = seq_i // seq_count, seq_i % seq_count

    rows_here = query_weight.shape[0]
    if r_n == 1 and parts == 2 and dp_n == 2 and y_n == 2 and seq_n == 2 * seq_count:
        weights, token_home, grad_home, chip_segments = first_transfers(
            query_weight, key_weight, value_weight, output_weight, tokens, grad_out, segments, sizes
        )
        segment = pick(pick(chip_segments, group, 0), member, 0)
    else:
        local = jnp.concatenate([query_weight, key_weight, value_weight, output_weight], axis=1)
        local = chip_exchange(local.reshape(rows_here, 4, parts, columns), 2, 0, parts)
        weights = lax.all_gather(
            local.reshape(parts * rows_here, 4 * columns), SPREAD, axis=0, tiled=True
        )
        weights = (
            weights.reshape(dp_n * seq_n, y_n, r_n, core_n * rows_here, -1)
            .transpose(0, 2, 1, 3, 4)
            .reshape(width, -1)
        )
        token_home, grad_home = to_sequences(tokens), to_sequences(grad_out)
        chip_segments = lax.all_gather(segments, "core")
        segment = pick(pick(chip_segments, group, 0), member, 0)
    weight_in, weight_out = weights[:, : 3 * columns], weights[:, 3 * columns :]

    token_float = token_home.astype(f32)
    inverse_one = lax.rsqrt(jnp.mean(token_float * token_float, axis=-1, keepdims=True) + epsilon)
    hidden_one = (token_float * inverse_one * attn_norm).astype(bf16)
    hidden_full = chip_gather(hidden_one, 1, parts).reshape(length, width)

    grad_plane = lax.all_gather(grad_home.reshape(home, width), PLANE, axis=0, tiled=True)

    half = head // 2
    frequency = theta_base ** (-jnp.arange(half, dtype=f32) / half)
    angles = jnp.arange(length, dtype=f32)[:, None] * frequency[None, :]
    cosine = jnp.concatenate([jnp.cos(angles)] * 2, axis=1)
    sine = jnp.concatenate([-jnp.sin(angles), jnp.sin(angles)], axis=1)
    seg_row, seg_col = segment[None, :], segment[:, None]

    qkv = product(hidden_full, weight_in)
    query, keys, values, mixed = attend(qkv, cosine, sine, seg_row, seg_col, heads)
    mixed_full = chip_gather(mixed, 1, parts)
    branch = product(mixed_full, weight_out).reshape(seq_n, parts, piece, columns)
    branch = chip_exchange(branch, 1, 3, parts).reshape(seq_n, piece, width)
    residual = token_float + branch
    inverse_two = lax.rsqrt(jnp.mean(residual * residual, axis=-1, keepdims=True) + epsilon)
    normed_two = residual * inverse_two
    hidden_two = (normed_two * expert_norm).astype(bf16).reshape(home, width)
    hidden_two = after(hidden_two, grad_plane)

    hidden_parts = [
        lax.all_gather(part, PLANE, axis=0, tiled=True) for part in jnp.split(hidden_two, 2)
    ]
    small = after(jnp.transpose(routes, (2, 0, 1)).reshape(topk * seq_count, seq_dev), hidden_two)
    small = lax.all_gather(small, EVERY, axis=0, tiled=True).reshape(
        dp_n, seq_n, r_n, y_n, core_n, topk, seq_count, seq_dev
    )
    small = pick(pick(small, group, 4), member, 5)
    plane_routes = pick(small, r_i, 2).transpose(0, 2, 1, 3, 4)
    block_routes = plane_routes.reshape(4, 2, seq_n // 2, topk, seq_dev)
    block_routes = block_routes.transpose(1, 0, 2, 3, 4).reshape(blocks, topk, seq_dev)
    home_routes = (
        pick(pick(plane_routes, dp_i, 0), y_i, 0)
        .reshape(seq_n, topk, core_n, piece)
        .transpose(1, 2, 0, 3)
    )
    home_routes = pick(home_routes, core_i, 1).reshape(topk, home)
    mine = y_i * core_n + core_i
    chosen = jnp.any(block_routes == mine, axis=1)
    places = jnp.arange(seq_dev)
    rank = product(chosen.astype(bf16), (places[:, None] < places[None, :]).astype(bf16))
    slot = jnp.where(chosen, rank.astype(jnp.int32), -1)
    slot_row, slot_col = slot[:, None, :], slot[:, :, None]
    me = jnp.stack([dp_i, y_i, core_i, mine]).astype(jnp.int32)
    gate_one, up_one, down_one = gate_weight[0], up_weight[0], down_weight[0]
    inner = gate_one.shape[1]
    cut = unit_cut(inner)
    full = (gate_one, up_one, down_one)
    route_col = jnp.transpose(block_routes, (0, 2, 1))
    picked, unit_parts = (), ()
    for part, hidden_part in enumerate(hidden_parts):
        picked = dispatch(
            me, hidden_part, grad_plane, slot_row, route_col, router, seq_n, piece, cap, part, picked
        )
        expert_in, dy_rows = (rows.reshape(blocks * cap, width) for rows in picked[:2])
        unit_parts = expert_units(expert_in, dy_rows, *full, 0, cut, part, unit_parts)
    row_gate = picked[2]
    units_a, dgpre_a, dupre_a = unit_parts

    def over_ctx(part):
        return lax.psum_scatter(part, CTX, scatter_dimension=0, tiled=True)

    def rows_product(rows, part):
        return t_product(rows, part).astype(bf16)

    down_a = rows_product(dy_rows, units_a)
    units_b, dgpre_b, dupre_b = expert_units(expert_in, dy_rows, *full, cut, inner, before=(down_a,))
    down_b = rows_product(dy_rows, units_b)
    down_sum_a, down_sum_b = over_ctx(down_a), over_ctx(down_b)
    grads = (dgpre_a, dgpre_b, dupre_a, dupre_b, gate_one, up_one)
    left = expert_input_grad(*grads, 0, width // 2, down_b)
    right = expert_input_grad(*grads, width // 2, width, left)
    left, right = (part.reshape(blocks, cap, width // 2) for part in (left, right))
    [back] = combine(me, left, slot_col, seq_n, piece, right=right)
    gate_a = rows_product(expert_in, after(dgpre_a, back, down_sum_a))
    gate_b = rows_product(expert_in, after(dgpre_b, back))
    gate_sum_a, gate_sum_b = over_ctx(gate_a), over_ctx(gate_b)
    ypair = expert_down(units_a, units_b, down_one, gate_a)
    mixed_rows, dgate_plane = combine(
        me, ypair.reshape(blocks, cap, width), slot_col, seq_n, piece, row_gate, grad_plane
    )

    dgate_plane = dgate_plane.reshape(2, 4, seq_n // 2, core_n, piece).transpose(1, 3, 0, 2, 4)
    dgate_home = lax.all_to_all(
        dgate_plane.reshape(8, home), PLANE, split_axis=0, concat_axis=0, tiled=True
    ).reshape(dp_n, experts, home).sum(axis=0)

    logits = product(hidden_two, router)
    hot = home_routes[:, :, None] == jnp.arange(experts, dtype=jnp.int32)[None, None, :]
    gates = jax.nn.softmax(jnp.sum(jnp.where(hot, logits[None], 0.0), axis=2), axis=0)
    dgate = jnp.sum(jnp.where(hot, jnp.transpose(dgate_home)[None], 0.0), axis=2)
    dsel = gates * (dgate - jnp.sum(gates * dgate, axis=0, keepdims=True))
    dlogits = jnp.sum(jnp.where(hot, dsel[:, :, None], 0.0), axis=0).astype(bf16)
    router_grad = t_product(hidden_two, dlogits)
    up_b = rows_product(expert_in, after(dupre_b, gate_a))

    def once_gate(stage, *arrays):
        return (after(arrays[0], up_b if stage else gate_a),) + arrays[1:]

    dhidden_two = plane_scatter(back, once_gate).reshape(home, width) + product_t(dlogits, router)

    flat_two = normed_two.reshape(home, width)
    dresid, expert_norm_grad = norm_backward(
        dhidden_two, flat_two, inverse_two.reshape(home, 1), expert_norm
    )
    dresid = dresid + grad_home.reshape(home, width).astype(f32)
    dbranch = chip_gather(dresid.astype(bf16).reshape(seq_n, piece, width), 1, parts).reshape(length, width)
    column_start = (r_i * core_n + core_i) * columns
    dbranch_here = lax.dynamic_slice_in_dim(dbranch, column_start, columns, 1)
    dmixed = chip_scatter(product_t(dbranch_here, weight_out).astype(bf16), 1, parts).astype(bf16)
    stages = {}

    def check(stage, *arrays):
        stages[stage] = arrays
        return arrays

    mixture = plane_scatter(after(mixed_rows, dbranch), check)
    dqpre, dkpre, dvpre = attend_back(
        query, keys, values, mixed, dmixed, cosine, sine, seg_row, seg_col, heads, down_sum_b, up_b, *stages[0]
    )
    dqkv = jnp.concatenate([dqpre, dkpre, dvpre], axis=1)
    out_grad = t_product(mixed_full, after(dbranch_here, dqpre, *stages[1])).astype(bf16)
    in_grad = t_product(hidden_full, after(dqkv, out_grad)).astype(bf16)
    up_a = rows_product(expert_in, after(dupre_a, in_grad))
    output = (residual + mixture).astype(bf16)
    dhidden_part = product_t(after(dqkv, up_a, output), weight_in).astype(bf16)
    dhidden_one = chip_scatter(
        dhidden_part.reshape(seq_n, parts * piece, width), 1, parts
    )
    normed_one = token_float * inverse_one
    dtokens, attn_norm_grad = norm_backward(
        dhidden_one.reshape(home, width),
        normed_one.reshape(home, width),
        inverse_one.reshape(home, 1),
        attn_norm,
    )
    dtokens = (dtokens + dresid).astype(bf16).reshape(seq_n, piece, width)

    grad_down = jnp.concatenate([down_sum_a, down_sum_b], axis=1).astype(f32).T[None]
    grad_gate = jnp.concatenate([gate_sum_a, gate_sum_b], axis=1).astype(f32)[None]
    grad_up = jnp.concatenate([over_ctx(up_a), over_ctx(up_b)], axis=1).astype(f32)[None]

    def seen(part):
        return part.reshape(dp_n, seq_n, r_n, y_n, core_n * rows_here, -1)

    def half(a, axis, index, name):
        keep, give = pick(a, index, axis), pick(a, 1 - index, axis)
        return total(keep, swap(give, name)).astype(bf16)

    first = [half(seen(a), 0, dp_i, "dp") for a in (out_grad, in_grad[:, :columns])]
    first.append(half(seen(in_grad[:, columns:]), 3, y_i, "y"))
    second = [half(a, 2, y_i, "y") for a in first[:2]] + [half(first[2], 0, dp_i, "dp")]
    second = jnp.concatenate(second, axis=-1)
    if r_n == 1 and parts == 2 and seq_n == 2 * seq_count == 4:
        part, grad_tokens, output = last_transfers(
            second.reshape(seq_n, core_n * rows_here, 4 * columns), dtokens, output, seq_count
        )
        part = total(part[:, 0], part[:, 1]).reshape(core_n, rows_here, 4, columns)
        part = part.transpose(1, 2, 0, 3).reshape(rows_here, 4, width)
    else:
        grad_tokens = from_sequences(dtokens)
        output = from_sequences(output)
        part = total(*seq_pieces(second)).astype(bf16)
        part = part.reshape(parts, rows_here, 4, 1, columns)
        part = chip_exchange(part, 0, 3, parts).reshape(rows_here, 4, width).astype(f32)
    grad_output, grad_query, grad_key, grad_value = (part[:, i] for i in range(4))
    grad_tokens = grad_tokens.astype(f32)

    gains = jnp.concatenate([attn_norm_grad[None], expert_norm_grad[None], router_grad.T], axis=0)
    gain_n = gains.shape[0]
    gains = gains.reshape(gain_n, -1, rows_here).transpose(1, 0, 2)
    gains = lax.all_to_all(gains, EVERY, split_axis=0, concat_axis=0, tiled=True)
    gains = jnp.sum(gains, axis=0).T

    return (
        output,
        grad_tokens,
        gains[:, 0],
        grad_query,
        grad_key,
        grad_value,
        grad_output,
        gains[:, 1],
        gains[:, 2:],
        grad_gate,
        grad_up,
        grad_down,
    )


def solution(mesh):
    dp_n, ctx_n, exp_n = mesh.shape["dp"], mesh.shape["ctx"], mesh.shape["exp"]

    def block(*arrays):
        tokens = arrays[0]
        seq_count = tokens.shape[0] // (dp_n * exp_n)
        seq_n = seq_count * CORES
        sizes = (dp_n, seq_n, ctx_n // seq_n, exp_n // CORES, CORES)
        fine = Mesh(mesh.devices.reshape(sizes), EVERY)
        group = ("dp", "y", "core")
        exp = ("y", "core")
        return jax.shard_map(
            functools.partial(on_device, sizes),
            mesh=fine,
            in_specs=(
                P(group, CTX, None),
                P(group, None),
                P(group, CTX, None),
                P(),
                P(EVERY, None),
                P(EVERY, None),
                P(EVERY, None),
                P(EVERY, None),
                P(),
                P(),
                P(exp, None, "dp"),
                P(exp, None, "dp"),
                P(exp, "dp", None),
                P(group, CTX, None),
            ),
            out_specs=(
                P(group, CTX, None),
                P(group, CTX, None),
                P(EVERY),
                P(EVERY, None),
                P(EVERY, None),
                P(EVERY, None),
                P(EVERY, None),
                P(EVERY),
                P(EVERY, None),
                P(exp, CTX, "dp"),
                P(exp, CTX, "dp"),
                P(exp, "dp", CTX),
            ),
            check_vma=False,
        )(*arrays)

    return block
```

```python
import functools

import jax
import jax.numpy as jnp
from jax import lax
from jax.experimental import pallas as pl
from jax.experimental.pallas import tpu as pltpu
from jax.sharding import Mesh, PartitionSpec as P

HEADS = 16
CORES = 2

epsilon = 1e-05
theta_base = 10000.0
masked_score = -1e30
bf16 = jnp.bfloat16
f32 = jnp.float32

PLANE = ("dp", "y", "core")
CHIP = ("r", "core")
SPREAD = ("dp", "seq", "y")
CTX = ("seq", "r")
EVERY = ("dp", "seq", "r", "y", "core")


def product(a, b):
    return jnp.dot(a, b, preferred_element_type=f32)


def product_t(a, b):
    return lax.dot_general(a, b, (((1,), (1,)), ((), ())), preferred_element_type=f32)


def t_product(a, b):
    return lax.dot_general(a, b, (((0,), (0,)), ((), ())), preferred_element_type=f32)


def swap(a, axis):
    return lax.ppermute(a, axis, [(0, 1), (1, 0)])


def halves(a, axis):
    size = a.shape[axis] // 2
    me = lax.axis_index("core")
    mine = lax.dynamic_slice_in_dim(a, me * size, size, axis)
    other = lax.dynamic_slice_in_dim(a, (1 - me) * size, size, axis)
    return mine, other


def by_core(mine, other, axis):
    first = lax.axis_index("core") == 0
    return jnp.concatenate([jnp.where(first, mine, other), jnp.where(first, other, mine)], axis=axis)


def chip_gather(a, axis, parts):
    if parts == 2:
        return by_core(a, swap(a, "core"), axis)
    return lax.all_gather(a, CHIP, axis=axis, tiled=True)


def chip_scatter(a, axis, parts):
    if parts == 2:
        mine, other = halves(a, axis)
        return mine.astype(f32) + swap(other, "core").astype(f32)
    return lax.psum_scatter(a, CHIP, scatter_dimension=axis, tiled=True).astype(f32)


def chip_exchange(a, split, concat, parts):
    if parts == 2:
        mine, other = halves(a, split)
        return by_core(mine, swap(other, "core"), concat)
    return lax.all_to_all(a, CHIP, split_axis=split, concat_axis=concat, tiled=True)


def core_exchange(a, split, concat):
    mine, other = halves(a, split)
    return by_core(mine, swap(other, "core"), concat)


def seq_pieces(a):
    count = a.shape[0]
    me = lax.axis_index("seq")
    pieces = [pick(a, me, 0)]
    for step in range(1, count):
        give = pick(a, lax.rem(me + step, count), 0)
        pieces.append(lax.ppermute(give, "seq", [(i, (i + step) % count) for i in range(count)]))
    return pieces


def seq_exchange(a):
    count = a.shape[0]
    me = lax.axis_index("seq")
    pieces = jnp.stack(seq_pieces(a))
    return jnp.stack([pick(pieces, lax.rem(me + count - s, count), 0) for s in range(count)])


def to_sequences(a):
    return seq_exchange(core_exchange(a, 1, 0))


def from_sequences(a):
    return core_exchange(seq_exchange(a), 0, 1)


def total(*parts):
    return sum(part.astype(f32) for part in parts)


def plane_scatter(blocks, check=lambda stage, *arrays: arrays):
    held = total(blocks[:, :, 0], swap(blocks[:, :, 1], "core")).astype(bf16)
    [held] = check(0, held)
    half = blocks.shape[3] // 2
    by_x = swap(held[1, 1, :half], "dp")
    by_y = swap(held[1, 1, half:], "y")
    to_x = jnp.concatenate([held[1, 0, :half], total(held[1, 0, half:], by_y).astype(bf16)], axis=0)
    to_y = jnp.concatenate([total(held[0, 1, :half], by_x).astype(bf16), held[0, 1, half:]], axis=0)
    to_x, to_y = check(1, to_x, to_y)
    return total(held[0, 0], swap(to_x, "dp"), swap(to_y, "y"))


MESH = pl.DeviceIdType.MESH
Z_UP, Z_DOWN, X_A, Y_A, Y_B, X_B, Y_A2, X_B2 = range(8)


def first_kernel(
    query,
    key,
    value,
    output,
    tokens,
    grads,
    segments,
    weights,
    tokens_out,
    grads_out,
    segments_out,
    send,
    recv,
    core_send,
    core_recv,
    core_local,
    row_send,
    row_recv,
    row_local,
):
    dp, z, y, core = (lax.axis_index(a) for a in ("dp", "seq", "y", "core"))
    seq_n = weights.shape[1]
    rows, columns = query.shape[0], weights.shape[4] // 4
    half = weights.shape[4] // 2
    piece = tokens_out.shape[1]
    x_next, y_next, z_next, z_last, other = (
        {"dp": 1 - dp},
        {"y": 1 - y},
        {"seq": lax.rem(z + 1, seq_n)},
        {"seq": lax.rem(z + seq_n - 1, seq_n)},
        {"core": 1 - core},
    )

    barrier = pltpu.get_barrier_semaphore()
    partners = [x_next, y_next] + [
        {"seq": lax.rem(z + dz, seq_n), "core": lax.rem(core + dc, 2)}
        for dz in range(seq_n)
        for dc in range(2)
        if dz or dc
    ]
    for partner in partners:
        pl.semaphore_signal(barrier, inc=1, device_id=partner, device_id_type=MESH)
    pl.semaphore_wait(barrier, len(partners))

    here = pl.ds(pl.multiple_of(core * rows, rows), rows)
    locals_, remotes = [], []
    for m, matrix in enumerate((query, key, value, output)):
        place = weights.at[dp, z, y, here, pl.ds(m * columns, columns)]
        mine = matrix.at[:, pl.ds(pl.multiple_of(core * columns, columns), columns)]
        theirs = matrix.at[:, pl.ds(pl.multiple_of((1 - core) * columns, columns), columns)]
        locals_.append(pltpu.make_async_copy(mine, place, core_local.at[m]))
        remotes.append(
            pltpu.make_async_remote_copy(
                theirs, place, core_send.at[m], core_recv.at[m], device_id=other, device_id_type=MESH
            )
        )
    segment_local = pltpu.make_async_copy(segments, segments_out.at[core], core_local.at[4])
    segment_remote = pltpu.make_async_remote_copy(
        segments, segments_out.at[core], core_send.at[4], core_recv.at[4], device_id=other, device_id_type=MESH
    )
    for copy in remotes + [segment_remote] + locals_ + [segment_local]:
        copy.start()
    for copy in remotes + locals_:
        copy.wait()

    def part(kind, dp_b, z_b, y_b, device):
        if kind in (Z_UP, Z_DOWN):
            ref = weights.at[dp_b, z_b, y_b]
        else:
            start = 0 if kind in (X_A, Y_A, Y_A2) else half
            ref = weights.at[dp_b, z_b, y_b, :, pl.ds(start, half)]
        return pltpu.make_async_remote_copy(
            ref, ref, send.at[kind, z_b], recv.at[kind, z_b], device_id=device, device_id_type=MESH
        )

    def own(kind, z_b):
        device = {Z_UP: z_next, Z_DOWN: z_last, X_A: x_next, X_B: x_next, Y_A: y_next, Y_B: y_next}[kind]
        return part(kind, dp, z_b, y, device)

    def from_x(kind, z_b):
        return part(kind, 1 - dp, z_b, y, x_next)

    def from_y(kind, z_b):
        return part(kind, dp, z_b, 1 - y, y_next)

    def on_y(z_b):
        return part(Y_A2, 1 - dp, z_b, y, y_next)

    def on_x(z_b):
        return part(X_B2, dp, z_b, 1 - y, x_next)

    def spread(z_b):
        for kind in (X_A, Y_B, X_B, Y_A):
            own(kind, z_b).start()

    def relay(z_b):
        from_x(X_A, z_b).wait_recv()
        on_y(z_b).start()
        from_y(Y_B, z_b).wait_recv()
        on_x(z_b).start()

    def at_step(step, act_up, act_down):
        @pl.when(z - step >= 0)
        def _():
            act_up(z - step)

        @pl.when(z + step < seq_n)
        def _():
            act_down(z + step)

    def come_up(z_b):
        own(Z_UP, z_b).wait_recv()

        @pl.when(z < seq_n - 1)
        def _():
            own(Z_UP, z_b).start()

        spread(z_b)

    def come_down(z_b):
        own(Z_DOWN, z_b).wait_recv()

        @pl.when(z > 0)
        def _():
            own(Z_DOWN, z_b).start()

        spread(z_b)

    def rows_of(n, source, target, act):
        for s in range(tokens.shape[0]):
            z_to = tokens.shape[0] * core + s
            for d in range(2):
                core_to = lax.rem(core + d, 2)
                ref = source.at[s, pl.ds(pl.multiple_of(core_to * piece, piece), piece), :]
                copy = pltpu.make_async_remote_copy(
                    ref,
                    target.at[z],
                    row_send.at[n, s, d],
                    row_recv.at[n, z],
                    device_id={"seq": z_to, "core": core_to},
                    device_id_type=MESH,
                )
                if d:
                    act(copy)
                else:
                    keep = pltpu.make_async_copy(ref, target.at[z], row_local.at[n])

                    @pl.when(z_to != z)
                    def _(copy=copy):
                        act(copy)

                    @pl.when(z_to == z)
                    def _(keep=keep):
                        if act is begin:
                            keep.start()
                        else:
                            keep.wait()

    def begin(copy):
        copy.start()

    def sent(copy):
        copy.wait_send()

    def rows_in(n, target):
        group = z // tokens.shape[0]
        for z_from in range(seq_n):
            copy = pltpu.make_async_remote_copy(
                target.at[z_from],
                target.at[z_from],
                row_send.at[n, 0, 0],
                row_recv.at[n, z_from],
                device_id=other,
                device_id_type=MESH,
            )

            @pl.when((z_from != z) | (group != core))
            def _(copy=copy):
                copy.wait_recv()

    @pl.when(z < seq_n - 1)
    def _():
        own(Z_UP, z).start()

    @pl.when(z > 0)
    def _():
        own(Z_DOWN, z).start()

    spread(z)
    for step in range(1, seq_n):
        at_step(step, come_up, come_down)
        if step == 1:
            relay(z)
        else:
            at_step(step - 1, relay, relay)
        if step == seq_n - 2:
            rows_of(0, tokens, tokens_out, begin)
    rows_of(1, grads, grads_out, begin)
    at_step(seq_n - 1, relay, relay)

    segment_remote.wait()
    segment_local.wait()
    for z_b in range(seq_n):
        from_y(Y_A, z_b).wait_recv()
        from_x(X_B, z_b).wait_recv()
        part(Y_A2, 1 - dp, z_b, 1 - y, y_next).wait_recv()
        part(X_B2, 1 - dp, z_b, 1 - y, x_next).wait_recv()
        for kind in (X_A, Y_B, X_B, Y_A):
            own(kind, z_b).wait_send()
        on_y(z_b).wait_send()
        on_x(z_b).wait_send()

        @pl.when((z < seq_n - 1) & (z_b <= z))
        def _(z_b=z_b):
            own(Z_UP, z_b).wait_send()

        @pl.when((z > 0) & (z_b >= z))
        def _(z_b=z_b):
            own(Z_DOWN, z_b).wait_send()

    rows_of(0, tokens, tokens_out, sent)
    rows_of(1, grads, grads_out, sent)
    rows_in(0, tokens_out)
    rows_in(1, grads_out)


def first_transfers(query, key, value, output, tokens, grads, segments, sizes):
    dp_n, seq_n, r_n, y_n, core_n = sizes
    rows, width = query.shape
    piece = tokens.shape[1] // core_n
    columns = width // core_n
    held = pl.BlockSpec(memory_space=pl.ANY)
    out = jax.ShapeDtypeStruct((seq_n, piece, width), bf16)
    dma = pltpu.SemaphoreType.DMA
    weights, tokens, grads, segments = pl.pallas_call(
        first_kernel,
        in_specs=[held] * 7,
        out_specs=[held] * 4,
        out_shape=[
            jax.ShapeDtypeStruct((dp_n, seq_n, y_n, core_n * rows, 4 * columns), bf16),
            out,
            out,
            jax.ShapeDtypeStruct((core_n,) + segments.shape, segments.dtype),
        ],
        scratch_shapes=[
            dma((8, seq_n)),
            dma((8, seq_n)),
            dma((5,)),
            dma((5,)),
            dma((5,)),
            dma((2, tokens.shape[0], 2)),
            dma((2, seq_n)),
            dma((2,)),
        ],
        compiler_params=pltpu.CompilerParams(collective_id=0, has_side_effects=True),
        cost_estimate=pl.CostEstimate(flops=0, bytes_accessed=2 * 4 * columns * width, transcendentals=0),
        name="first_transfers",
    )(query, key, value, output, tokens, grads, segments)
    return weights.reshape(width, 4 * columns), tokens, grads, segments


def last_kernel(
    grads,
    tokens,
    output,
    grads_out,
    tokens_out,
    output_out,
    mine,
    theirs,
    pair_send,
    pair_recv,
    send,
    recv,
    row_send,
    row_recv,
    local,
):
    z, core = lax.axis_index("seq"), lax.axis_index("core")
    seq_n, piece = tokens.shape[:2]
    seq_count = tokens_out.shape[0]
    rows = grads.shape[1] // 2
    odd = lax.rem(z, 2)
    neighbour = z + 1 - 2 * odd
    far = lax.rem(z + 2, seq_n)

    barrier = pltpu.get_barrier_semaphore()
    partners = [
        {"seq": lax.rem(z + dz, seq_n), "core": lax.rem(core + dc, 2)}
        for dz in range(seq_n)
        for dc in range(2)
        if dz or dc
    ]
    for partner in partners:
        pl.semaphore_signal(barrier, inc=1, device_id=partner, device_id_type=MESH)
    pl.semaphore_wait(barrier, len(partners))

    pair = [
        pltpu.make_async_remote_copy(
            grads.at[2 * i + 1 - odd],
            theirs.at[i],
            pair_send.at[i],
            pair_recv.at[i],
            device_id={"seq": neighbour},
            device_id_type=MESH,
        )
        for i in range(2)
    ]
    kept = [pltpu.make_async_copy(grads.at[2 * i + odd], mine.at[i], local.at[3 + i]) for i in range(2)]

    def rows_to(core_to):
        return pl.ds(pl.multiple_of(core_to * rows, rows), rows)

    def far_copy(dc):
        core_to = lax.rem(core + dc, 2)
        return pltpu.make_async_remote_copy(
            mine.at[far // 2, rows_to(core_to), :],
            grads_out.at[core, 1],
            send.at[1, dc],
            recv.at[1, dc],
            device_id={"seq": far, "core": core_to},
            device_id_type=MESH,
        )

    def near_copy():
        return pltpu.make_async_remote_copy(
            mine.at[z // 2, rows_to(1 - core), :],
            grads_out.at[core, 0],
            send.at[0, 1],
            recv.at[0, 1],
            device_id={"core": 1 - core},
            device_id_type=MESH,
        )

    def own_copy():
        return pltpu.make_async_copy(
            mine.at[z // 2, rows_to(core), :], grads_out.at[core, 0], local.at[2]
        )

    def arrival(place, dc):
        ref = grads_out.at[lax.rem(core + dc, 2), place]
        return pltpu.make_async_remote_copy(
            ref,
            ref,
            send.at[place, dc],
            recv.at[place, dc],
            device_id={"core": 1 - core},
            device_id_type=MESH,
        )

    group, member = z // seq_count, lax.rem(z, seq_count)

    def row_place(target, s, c):
        return target.at[s, pl.ds(pl.multiple_of(c * piece, piece), piece), :]

    def row_copy(n, source, target, dz):
        z_to = lax.rem(z + dz, seq_n)
        return pltpu.make_async_remote_copy(
            source.at[z_to],
            row_place(target, member, core),
            row_send.at[n, dz],
            row_recv.at[n, member, core],
            device_id={"seq": z_to, "core": group},
            device_id_type=MESH,
        )

    def each_row(remote, kept):
        for n, source, target in ((0, tokens, tokens_out), (1, output, output_out)):
            for dz in range(seq_n):
                if dz:
                    remote(row_copy(n, source, target, dz))
                else:

                    @pl.when(group != core)
                    def _(copy=row_copy(n, source, target, 0)):
                        remote(copy)

                    @pl.when(group == core)
                    def _(n=n, source=source, target=target):
                        kept(
                            pltpu.make_async_copy(
                                source.at[z], row_place(target, member, core), local.at[n]
                            )
                        )

    for copy in pair + kept:
        copy.start()
    each_row(lambda copy: copy.start(), lambda copy: copy.start())

    for copy in kept:
        copy.wait()
    for copy in pair:
        copy.wait_recv()
    step = mine.shape[1] // 8

    def add(i, carry):
        span = pl.ds(pl.multiple_of(i * step, step), step)
        for part in range(2):
            mine[part, span, :] = total(mine[part, span, :], theirs[part, span, :]).astype(bf16)
        return carry

    lax.fori_loop(0, 8, add, 0)
    for copy in (far_copy(0), far_copy(1), near_copy(), own_copy()):
        copy.start()
    for copy in pair:
        copy.wait_send()
    own_copy().wait()
    for copy in (far_copy(0), far_copy(1), near_copy()):
        copy.wait_send()
    for place, dc in ((1, 0), (1, 1), (0, 1)):
        arrival(place, dc).wait_recv()
    each_row(lambda copy: copy.wait_send(), lambda copy: copy.wait())
    for n, target in ((0, tokens_out), (1, output_out)):
        for s in range(seq_count):
            for c in range(2):
                ref = row_place(target, s, c)
                copy = pltpu.make_async_remote_copy(
                    ref,
                    ref,
                    row_send.at[n, 0],
                    row_recv.at[n, s, c],
                    device_id=partners[0],
                    device_id_type=MESH,
                )

                @pl.when((z != seq_count * core + s) | (core != c))
                def _(copy=copy):
                    copy.wait_recv()


def last_transfers(grads, tokens, output, seq_count):
    seq_n, piece, width = tokens.shape
    rows = grads.shape[1] // 2
    held = pl.BlockSpec(memory_space=pl.ANY)
    out = jax.ShapeDtypeStruct((seq_count, 2 * piece, width), bf16)
    dma = pltpu.SemaphoreType.DMA
    return pl.pallas_call(
        last_kernel,
        in_specs=[held] * 3,
        out_specs=[held] * 3,
        out_shape=[jax.ShapeDtypeStruct((2, 2, rows, grads.shape[2]), bf16), out, out],
        scratch_shapes=[
            pltpu.VMEM((2,) + grads.shape[1:], bf16),
            pltpu.VMEM((2,) + grads.shape[1:], bf16),
            dma((2,)),
            dma((2,)),
            dma((2, 2)),
            dma((2, 2)),
            dma((2, seq_n)),
            dma((2, seq_count, 2)),
            dma((5,)),
        ],
        compiler_params=pltpu.CompilerParams(
            collective_id=1, has_side_effects=True, vmem_limit_bytes=24 * 2**20
        ),
        cost_estimate=pl.CostEstimate(flops=0, bytes_accessed=4 * grads.size, transcendentals=0),
        name="last_transfers",
    )(grads, tokens, output)


def visible_block(seg_row, seg_col, start, rows, cols):
    row_place = start + lax.broadcasted_iota(jnp.int32, (rows, cols), 0)
    col_place = lax.broadcasted_iota(jnp.int32, (rows, cols), 1)
    return (seg_col == seg_row) & (col_place <= row_place)


def turned(u, cosine, sine):
    return u * cosine + pltpu.roll(u, u.shape[1] // 2, 1) * sine


def attend_kernel(scale, block, qp, kp, vp, cosine, sine, seg_row, seg_col, q_out, k_out, v_out, mixed):
    length = qp.shape[0]
    q_out[...] = turned(qp[...], cosine[...], sine[...]).astype(bf16)
    k_out[...] = turned(kp[...], cosine[...], sine[...]).astype(bf16)
    v_out[...] = vp[...].astype(bf16)
    for start in range(0, length, block):
        stop = start + block
        scores = product_t(q_out[start:stop, :], k_out[:stop, :]) * scale
        seen = visible_block(seg_row[:, :stop], seg_col[start:stop, :], start, block, stop)
        scores = jnp.where(seen, scores, masked_score)
        top = jnp.max(scores, axis=1, keepdims=True)
        weights = jnp.exp(scores - top)
        total = jnp.sum(weights, axis=1, keepdims=True)
        summed = product(weights.astype(bf16), v_out[:stop, :])
        mixed[start:stop, :] = (summed / total).astype(bf16)


def attend(qkv, cosine, sine, seg_row, seg_col, heads):
    length, head = qkv.shape[0], cosine.shape[1]
    block = min(256, length)

    def column(offset):
        return pl.BlockSpec((length, head), lambda h: (0, offset + h))

    def whole(shape):
        return pl.BlockSpec(shape, lambda h: (0, 0))

    out = jax.ShapeDtypeStruct((length, heads * head), bf16)
    pairs = length * (length + block) // 2 * heads
    return pl.pallas_call(
        functools.partial(attend_kernel, head**-0.5, block),
        grid=(heads,),
        in_specs=[
            column(0),
            column(heads),
            column(2 * heads),
            whole((length, head)),
            whole((length, head)),
            whole((1, length)),
            whole((length, 1)),
        ],
        out_specs=[column(0)] * 4,
        out_shape=[out] * 4,
        compiler_params=pltpu.CompilerParams(vmem_limit_bytes=48 * 2**20),
        cost_estimate=pl.CostEstimate(
            flops=4 * pairs * head, bytes_accessed=20 * length * heads * head, transcendentals=pairs
        ),
        name="attend",
    )(qkv, qkv, qkv, cosine, sine, seg_row, seg_col)


def attend_back_kernel(
    scale, block, q, k, v, mixed, dmixed, cosine, sine, seg_row, seg_col, *rest
):
    dq_out, dk_out, dv_out, dk_sum, dv_sum = rest[-5:]
    length = q.shape[0]
    dk_sum[...] = jnp.zeros_like(dk_sum)
    dv_sum[...] = jnp.zeros_like(dv_sum)
    for start in range(0, length, block):
        stop = start + block
        scores = product_t(q[start:stop, :], k[:stop, :]) * scale
        seen = visible_block(seg_row[:, :stop], seg_col[start:stop, :], start, block, stop)
        scores = jnp.where(seen, scores, masked_score)
        top = jnp.max(scores, axis=1, keepdims=True)
        weights = jnp.exp(scores - top)
        inverse = 1.0 / jnp.sum(weights, axis=1, keepdims=True)
        grad = dmixed[start:stop, :].astype(f32)
        delta = jnp.sum(grad * mixed[start:stop, :].astype(f32), axis=1, keepdims=True) * inverse
        unit = (grad * inverse).astype(bf16)
        dweights = product_t(unit, v[:stop, :])
        dscores = (weights * (dweights - delta)).astype(bf16)
        dq = product(dscores, k[:stop, :]) * scale
        dq_out[start:stop, :] = turned(dq, cosine[start:stop, :], -sine[start:stop, :]).astype(bf16)
        dk_sum[:stop, :] += t_product(dscores, q[start:stop, :])
        dv_sum[:stop, :] += t_product(weights.astype(bf16), unit)
    dk_out[...] = turned(dk_sum[...] * scale, cosine[...], -sine[...]).astype(bf16)
    dv_out[...] = dv_sum[...].astype(bf16)


def attend_back(q, k, v, mixed, dmixed, cosine, sine, seg_row, seg_col, heads, *before):
    length, head = q.shape[0], cosine.shape[1]
    block = min(256, length)
    column = pl.BlockSpec((length, head), lambda h: (0, h))

    def whole(shape):
        return pl.BlockSpec(shape, lambda h: (0, 0))

    out = jax.ShapeDtypeStruct((length, heads * head), bf16)
    pairs = length * (length + block) // 2 * heads
    return pl.pallas_call(
        functools.partial(attend_back_kernel, head**-0.5, block),
        grid=(heads,),
        in_specs=[column] * 5
        + [whole((length, head)), whole((length, head)), whole((1, length)), whole((length, 1))]
        + [pl.BlockSpec(memory_space=pl.ANY)] * len(before),
        out_specs=[column] * 3,
        out_shape=[out] * 3,
        scratch_shapes=[pltpu.VMEM((length, head), f32)] * 2,
        compiler_params=pltpu.CompilerParams(vmem_limit_bytes=48 * 2**20),
        cost_estimate=pl.CostEstimate(
            flops=10 * pairs * head, bytes_accessed=16 * length * heads * head, transcendentals=pairs
        ),
        name="attend_back",
    )(q, k, v, mixed, dmixed, cosine, sine, seg_row, seg_col, *before)


def units_kernel(chunk, x, dy, gate, up, down, *rest):
    units, dgate, dup = rest[-3:]
    gate_w, up_w, down_w = gate[...], up[...], down[...]

    def step(i, carry):
        rows = pl.ds(pl.multiple_of(i * chunk, chunk), chunk)
        gpre = product(x[rows, :], gate_w)
        upre = product(x[rows, :], up_w)
        dunits = product_t(dy[rows, :], down_w)
        s = jax.nn.sigmoid(gpre)
        silu = gpre * s
        units[rows, :] = (silu * upre).astype(bf16)
        dgate[rows, :] = (dunits * upre * (s * (1.0 + gpre * (1.0 - s)))).astype(bf16)
        dup[rows, :] = (dunits * silu).astype(bf16)
        return carry

    lax.fori_loop(0, x.shape[0] // chunk, step, 0)


def expert_units(x, dy, gate, up, down, start, stop, half=None, made=(), before=()):
    rows, width = x.shape
    units = stop - start
    part, at = (rows, 0) if half is None else (rows // 2, half)
    chunk = tile_of(part)
    tile = unit_tile(gate.shape[1])
    first = start // tile
    once = pl.BlockSpec((part, width), lambda j: (at, 0), pipeline_mode=pl.Buffered(1))
    out = jax.ShapeDtypeStruct((rows, units), bf16)
    return pl.pallas_call(
        functools.partial(units_kernel, chunk),
        grid=(units // tile,),
        in_specs=[
            once,
            once,
            pl.BlockSpec((width, tile), lambda j: (0, first + j)),
            pl.BlockSpec((width, tile), lambda j: (0, first + j)),
            pl.BlockSpec((tile, width), lambda j: (first + j, 0)),
        ]
        + [pl.BlockSpec(memory_space=pl.ANY)] * (len(made) + len(before)),
        out_specs=[pl.BlockSpec((part, tile), lambda j: (at, j))] * 3,
        out_shape=[out] * 3,
        input_output_aliases={5 + i: i for i in range(len(made))},
        compiler_params=pltpu.CompilerParams(vmem_limit_bytes=56 * 2**20),
        cost_estimate=pl.CostEstimate(
            flops=6 * part * width * units,
            bytes_accessed=4 * part * width + 6 * width * units + 6 * part * units,
            transcendentals=part * units,
        ),
        name="expert_units",
    )(x, dy, gate, up, down, *made, *before)


def unit_tile(units):
    return 256 if units % 256 == 0 else units


def unit_cut(units):
    tile = unit_tile(units)
    return units // tile * 3 // 4 * tile


def dispatch_kernel(me, hidden, dout, slot, routes, router, *rest):
    rows, dy_rows, gate = rest[-3:]
    size = hidden.shape[1] * hidden.shape[3]
    width = hidden.shape[4]
    mine = me[3]
    tokens = hidden[...].reshape(size, width)
    logits = product(tokens, router[...])
    lanes = lax.broadcasted_iota(jnp.int32, logits.shape, 1)
    first, second = routes[0, :, 0:1], routes[0, :, 1:2]
    one = jnp.sum(jnp.where(lanes == first, logits, 0.0), axis=1, keepdims=True)
    two = jnp.sum(jnp.where(lanes == second, logits, 0.0), axis=1, keepdims=True)
    top = jnp.maximum(one, two)
    one, two = jnp.exp(one - top), jnp.exp(two - top)
    share = jnp.where(first == mine, one, jnp.where(second == mine, two, 0.0)) / (one + two)
    gate[0] = share
    chosen = (
        lax.broadcasted_iota(jnp.int32, (rows.shape[1], size), 0) == slot[0]
    ).astype(bf16)
    rows[0] = product(chosen, tokens).astype(bf16)
    dy = (share * dout[...].reshape(size, width).astype(f32)).astype(bf16)
    dy_rows[0] = product(chosen, dy).astype(bf16)


def block_place(b, span):
    return lax.rem(b, 4 * span) // span, (b // (4 * span)) * span + lax.rem(b, span)


def plane_block(seq_n, piece, width, first=0, seen=None):
    span = seq_n // 2

    def index(b, me):
        device, place = block_place(b + first, span)
        return (device, 0, place if seen is None else lax.rem(place, seen), 0, 0)

    return pl.BlockSpec((1, 2, 1, piece, width), index)


def relative_block(seq_n, piece, width):
    def index(b, me):
        device, place = block_place(b, seq_n // 2)
        return (lax.rem(device // 2 + me[0], 2), lax.rem(device + me[1], 2), 0, place, 0, 0)

    return pl.BlockSpec((1, 1, 2, 1, piece, width), index)


def dispatch(me, hidden, dout, slot, routes, router, seq_n, piece, cap, half, made=()):
    blocks, size = slot.shape[0], slot.shape[2]
    width = hidden.shape[1]
    span = seq_n // 2
    count = blocks // 2
    first = half * count

    def each(*shape):
        return pl.BlockSpec((1,) + shape, lambda b, me: (first + b, 0, 0))

    out = jax.ShapeDtypeStruct((blocks, cap, width), bf16)
    spare = jnp.zeros((width, 128 - router.shape[1]), router.dtype)
    return pl.pallas_call(
        dispatch_kernel,
        grid_spec=pltpu.PrefetchScalarGridSpec(
            num_scalar_prefetch=1,
            grid=(count,),
            in_specs=[
                plane_block(seq_n, piece, width, first, span),
                plane_block(seq_n, piece, width, first),
                each(1, size),
                each(size, routes.shape[2]),
                pl.BlockSpec((width, 128), lambda b, me: (0, 0)),
            ]
            + [pl.BlockSpec(memory_space=pl.ANY)] * len(made),
            out_specs=[each(cap, width), each(cap, width), each(size, 1)],
        ),
        out_shape=[out, out, jax.ShapeDtypeStruct((blocks, size, 1), f32)],
        input_output_aliases={6 + i: i for i in range(len(made))},
        compiler_params=pltpu.CompilerParams(vmem_limit_bytes=40 * 2**20),
        cost_estimate=pl.CostEstimate(
            flops=4 * count * size * width * (cap + 64),
            bytes_accessed=4 * count * (size + cap) * width,
            transcendentals=2 * count * size,
        ),
        name="dispatch",
    )(
        me,
        hidden.reshape(4, 2, span, piece, width),
        dout.reshape(4, 2, seq_n, piece, width),
        slot,
        routes,
        jnp.concatenate([router, spare], axis=1),
        *made,
    )


def spread_rows(slot, rows):
    size, cap = slot.shape[0], rows.shape[0]
    chosen = (lax.broadcasted_iota(jnp.int32, (size, cap), 1) == slot).astype(bf16)
    return product(chosen, rows)


def place_cores(me, out, dense):
    piece = out.shape[4]
    for core in range(2):
        out[0, 0, lax.rem(me[2] + core, 2), 0] = dense[core * piece : (core + 1) * piece, :].astype(bf16)


def combine_kernel(me, rows, slot, gate, dout, out, dgate):
    dense = spread_rows(slot[0], rows[0])
    grads = dout[...].reshape(dense.shape).astype(f32)
    dgate[0] = jnp.sum(grads * dense, axis=1, keepdims=True)
    place_cores(me, out, gate[0] * dense)


def collect_kernel(me, left, slot, right, *rest):
    dense = [spread_rows(slot[0], left[0]), spread_rows(slot[0], right[0])]
    place_cores(me, rest[-1], jnp.concatenate(dense, axis=1))


def combine(me, rows, slot, seq_n, piece, gate=None, dout=None, right=None):
    blocks, cap, part = rows.shape
    size = slot.shape[1]
    width = part if right is None else 2 * part
    column = pl.BlockSpec((1, size, 1), lambda b, me: (b, 0, 0))
    weigh = gate is not None
    operands = [rows, slot]
    in_specs = [pl.BlockSpec((1, cap, part), lambda b, me: (b, 0, 0)), column]
    out_specs = [relative_block(seq_n, piece, width)]
    out_shape = [jax.ShapeDtypeStruct((2, 2, 2, seq_n, piece, width), bf16)]
    if weigh:
        operands += [gate, dout.reshape(4, 2, seq_n, piece, width)]
        in_specs += [column, plane_block(seq_n, piece, width)]
        out_specs += [column]
        out_shape += [jax.ShapeDtypeStruct((blocks, size, 1), f32)]
    else:
        operands += [right]
        in_specs += in_specs[:1]
    return pl.pallas_call(
        combine_kernel if weigh else collect_kernel,
        grid_spec=pltpu.PrefetchScalarGridSpec(
            num_scalar_prefetch=1, grid=(blocks,), in_specs=in_specs, out_specs=out_specs
        ),
        out_shape=out_shape,
        compiler_params=pltpu.CompilerParams(vmem_limit_bytes=40 * 2**20),
        cost_estimate=pl.CostEstimate(
            flops=2 * blocks * size * width * cap,
            bytes_accessed=2 * blocks * (2 * size + cap) * width,
            transcendentals=0,
        ),
        name="combine" if weigh else "collect",
    )(me, *operands)


def down_kernel(cut, units_a, units_b, down, *rest):
    total = product(units_a[...], down[:cut, :]) + product(units_b[...], down[cut:, :])
    rest[-1][...] = total.astype(bf16)


def expert_down(units_a, units_b, down, *before):
    rows, cut = units_a.shape
    inner, width = down.shape
    m, n = tile_of(rows), tile_of(width)
    return pl.pallas_call(
        functools.partial(down_kernel, cut),
        grid=(width // n, rows // m),
        in_specs=[
            pl.BlockSpec((m, cut), lambda j, i: (i, 0)),
            pl.BlockSpec((m, inner - cut), lambda j, i: (i, 0)),
            pl.BlockSpec((inner, n), lambda j, i: (0, j)),
        ]
        + [pl.BlockSpec(memory_space=pl.ANY)] * len(before),
        out_specs=pl.BlockSpec((m, n), lambda j, i: (i, j)),
        out_shape=jax.ShapeDtypeStruct((rows, width), bf16),
        compiler_params=pltpu.CompilerParams(vmem_limit_bytes=48 * 2**20),
        cost_estimate=pl.CostEstimate(
            flops=2 * rows * inner * width,
            bytes_accessed=2 * (rows * inner + inner * width + rows * width),
            transcendentals=0,
        ),
        name="expert_down",
    )(units_a, units_b, down, *before)


def input_kernel(cut, dgate_a, dgate_b, dup_a, dup_b, gate, up, *rest):
    total = product_t(dgate_a[...], gate[:, :cut]) + product_t(dgate_b[...], gate[:, cut:])
    total += product_t(dup_a[...], up[:, :cut]) + product_t(dup_b[...], up[:, cut:])
    rest[-1][...] = total.astype(bf16)


def expert_input_grad(dgate_a, dgate_b, dup_a, dup_b, gate, up, start, stop, *before):
    rows, cut = dgate_a.shape
    inner = gate.shape[1]
    width = stop - start
    m, n = tile_of(rows), tile_of(width)
    first = start // n
    left_a = pl.BlockSpec((m, cut), lambda j, i: (i, 0))
    left_b = pl.BlockSpec((m, inner - cut), lambda j, i: (i, 0))
    right = pl.BlockSpec((n, inner), lambda j, i: (first + j, 0))
    return pl.pallas_call(
        functools.partial(input_kernel, cut),
        grid=(width // n, rows // m),
        in_specs=[left_a, left_b, left_a, left_b, right, right]
        + [pl.BlockSpec(memory_space=pl.ANY)] * len(before),
        out_specs=pl.BlockSpec((m, n), lambda j, i: (i, j)),
        out_shape=jax.ShapeDtypeStruct((rows, width), bf16),
        compiler_params=pltpu.CompilerParams(vmem_limit_bytes=52 * 2**20),
        cost_estimate=pl.CostEstimate(
            flops=4 * rows * inner * width,
            bytes_accessed=2 * (2 * rows * inner + 2 * inner * width + rows * width),
            transcendentals=0,
        ),
        name="expert_input_grad",
    )(dgate_a, dgate_b, dup_a, dup_b, gate, up, *before)


def tile_of(size):
    return max(c for c in range(16, 513, 16) if size % c == 0)


def anchor_kernel(*refs):
    pass


def after(a, *before):
    return pl.pallas_call(
        anchor_kernel,
        in_specs=[pl.BlockSpec(memory_space=pl.ANY)] * (1 + len(before)),
        out_specs=pl.BlockSpec(memory_space=pl.ANY),
        out_shape=jax.ShapeDtypeStruct(a.shape, a.dtype),
        input_output_aliases={0: 0},
        cost_estimate=pl.CostEstimate(flops=0, bytes_accessed=0, transcendentals=0),
        name="after",
    )(a, *before)


def norm_backward(grad_rows, normed, inverse, gain):
    weighted = grad_rows * gain
    mean_term = jnp.mean(weighted * normed, axis=-1, keepdims=True)
    return inverse * (weighted - normed * mean_term), jnp.sum(grad_rows * normed, axis=0)


def pick(a, index, axis):
    return lax.dynamic_index_in_dim(a, index, axis, keepdims=False)


def on_device(
    sizes,
    tokens,
    segments,
    routes,
    attn_norm,
    query_weight,
    key_weight,
    value_weight,
    output_weight,
    expert_norm,
    router,
    gate_weight,
    up_weight,
    down_weight,
    grad_out,
):
    dp_n, seq_n, r_n, y_n, core_n = sizes
    parts = r_n * core_n
    seq_count, seq_dev, width = tokens.shape
    piece = seq_dev // core_n
    length = segments.shape[1]
    home = seq_n * piece
    head = width // HEADS
    heads = HEADS // parts
    columns = width // parts
    experts = router.shape[1]
    topk = routes.shape[2]
    plane = 8 * home
    blocks = plane // seq_dev
    cap = 5 * seq_dev * topk // (4 * experts)
    dp_i, seq_i, r_i, y_i, core_i = (lax.axis_index(a) for a in EVERY)
    group, member = seq_i // seq_count, seq_i % seq_count

    rows_here = query_weight.shape[0]
    if r_n == 1 and parts == 2 and dp_n == 2 and y_n == 2 and seq_n == 2 * seq_count:
        weights, token_home, grad_home, chip_segments = first_transfers(
            query_weight, key_weight, value_weight, output_weight, tokens, grad_out, segments, sizes
        )
        segment = pick(pick(chip_segments, group, 0), member, 0)
    else:
        local = jnp.concatenate([query_weight, key_weight, value_weight, output_weight], axis=1)
        local = chip_exchange(local.reshape(rows_here, 4, parts, columns), 2, 0, parts)
        weights = lax.all_gather(
            local.reshape(parts * rows_here, 4 * columns), SPREAD, axis=0, tiled=True
        )
        weights = (
            weights.reshape(dp_n * seq_n, y_n, r_n, core_n * rows_here, -1)
            .transpose(0, 2, 1, 3, 4)
            .reshape(width, -1)
        )
        token_home, grad_home = to_sequences(tokens), to_sequences(grad_out)
        chip_segments = lax.all_gather(segments, "core")
        segment = pick(pick(chip_segments, group, 0), member, 0)
    weight_in, weight_out = weights[:, : 3 * columns], weights[:, 3 * columns :]

    token_float = token_home.astype(f32)
    inverse_one = lax.rsqrt(jnp.mean(token_float * token_float, axis=-1, keepdims=True) + epsilon)
    hidden_one = (token_float * inverse_one * attn_norm).astype(bf16)
    hidden_full = chip_gather(hidden_one, 1, parts).reshape(length, width)

    grad_plane = lax.all_gather(grad_home.reshape(home, width), PLANE, axis=0, tiled=True)

    half = head // 2
    frequency = theta_base ** (-jnp.arange(half, dtype=f32) / half)
    angles = jnp.arange(length, dtype=f32)[:, None] * frequency[None, :]
    cosine = jnp.concatenate([jnp.cos(angles)] * 2, axis=1)
    sine = jnp.concatenate([-jnp.sin(angles), jnp.sin(angles)], axis=1)
    seg_row, seg_col = segment[None, :], segment[:, None]

    qkv = product(hidden_full, weight_in)
    query, keys, values, mixed = attend(qkv, cosine, sine, seg_row, seg_col, heads)
    mixed_full = chip_gather(mixed, 1, parts)
    branch = product(mixed_full, weight_out).reshape(seq_n, parts, piece, columns)
    branch = chip_exchange(branch, 1, 3, parts).reshape(seq_n, piece, width)
    residual = token_float + branch
    inverse_two = lax.rsqrt(jnp.mean(residual * residual, axis=-1, keepdims=True) + epsilon)
    normed_two = residual * inverse_two
    hidden_two = (normed_two * expert_norm).astype(bf16).reshape(home, width)
    hidden_two = after(hidden_two, grad_plane)

    hidden_parts = [
        lax.all_gather(part, PLANE, axis=0, tiled=True) for part in jnp.split(hidden_two, 2)
    ]
    small = after(jnp.transpose(routes, (2, 0, 1)).reshape(topk * seq_count, seq_dev), hidden_two)
    small = lax.all_gather(small, EVERY, axis=0, tiled=True).reshape(
        dp_n, seq_n, r_n, y_n, core_n, topk, seq_count, seq_dev
    )
    small = pick(pick(small, group, 4), member, 5)
    plane_routes = pick(small, r_i, 2).transpose(0, 2, 1, 3, 4)
    block_routes = plane_routes.reshape(4, 2, seq_n // 2, topk, seq_dev)
    block_routes = block_routes.transpose(1, 0, 2, 3, 4).reshape(blocks, topk, seq_dev)
    home_routes = (
        pick(pick(plane_routes, dp_i, 0), y_i, 0)
        .reshape(seq_n, topk, core_n, piece)
        .transpose(1, 2, 0, 3)
    )
    home_routes = pick(home_routes, core_i, 1).reshape(topk, home)
    mine = y_i * core_n + core_i
    chosen = jnp.any(block_routes == mine, axis=1)
    places = jnp.arange(seq_dev)
    rank = product(chosen.astype(bf16), (places[:, None] < places[None, :]).astype(bf16))
    slot = jnp.where(chosen, rank.astype(jnp.int32), -1)
    slot_row, slot_col = slot[:, None, :], slot[:, :, None]
    me = jnp.stack([dp_i, y_i, core_i, mine]).astype(jnp.int32)
    gate_one, up_one, down_one = gate_weight[0], up_weight[0], down_weight[0]
    inner = gate_one.shape[1]
    cut = unit_cut(inner)
    full = (gate_one, up_one, down_one)
    route_col = jnp.transpose(block_routes, (0, 2, 1))
    picked, unit_parts = (), ()
    for part, hidden_part in enumerate(hidden_parts):
        picked = dispatch(
            me, hidden_part, grad_plane, slot_row, route_col, router, seq_n, piece, cap, part, picked
        )
        expert_in, dy_rows = (rows.reshape(blocks * cap, width) for rows in picked[:2])
        unit_parts = expert_units(expert_in, dy_rows, *full, 0, cut, part, unit_parts)
    row_gate = picked[2]
    units_a, dgpre_a, dupre_a = unit_parts

    def over_ctx(part):
        return lax.psum_scatter(part, CTX, scatter_dimension=0, tiled=True)

    def rows_product(rows, part):
        return t_product(rows, part).astype(bf16)

    down_a = rows_product(dy_rows, units_a)
    units_b, dgpre_b, dupre_b = expert_units(expert_in, dy_rows, *full, cut, inner, before=(down_a,))
    down_b = rows_product(dy_rows, units_b)
    down_sum_a, down_sum_b = over_ctx(down_a), over_ctx(down_b)
    grads = (dgpre_a, dgpre_b, dupre_a, dupre_b, gate_one, up_one)
    left = expert_input_grad(*grads, 0, width // 2, down_b)
    right = expert_input_grad(*grads, width // 2, width, left)
    left, right = (part.reshape(blocks, cap, width // 2) for part in (left, right))
    [back] = combine(me, left, slot_col, seq_n, piece, right=right)
    gate_a = rows_product(expert_in, after(dgpre_a, back, down_sum_a))
    gate_b = rows_product(expert_in, after(dgpre_b, back))
    gate_sum_a, gate_sum_b = over_ctx(gate_a), over_ctx(gate_b)
    ypair = expert_down(units_a, units_b, down_one, gate_a)
    mixed_rows, dgate_plane = combine(
        me, ypair.reshape(blocks, cap, width), slot_col, seq_n, piece, row_gate, grad_plane
    )

    dgate_plane = dgate_plane.reshape(2, 4, seq_n // 2, core_n, piece).transpose(1, 3, 0, 2, 4)
    dgate_home = lax.all_to_all(
        dgate_plane.reshape(8, home), PLANE, split_axis=0, concat_axis=0, tiled=True
    ).reshape(dp_n, experts, home).sum(axis=0)

    logits = product(hidden_two, router)
    hot = home_routes[:, :, None] == jnp.arange(experts, dtype=jnp.int32)[None, None, :]
    gates = jax.nn.softmax(jnp.sum(jnp.where(hot, logits[None], 0.0), axis=2), axis=0)
    dgate = jnp.sum(jnp.where(hot, jnp.transpose(dgate_home)[None], 0.0), axis=2)
    dsel = gates * (dgate - jnp.sum(gates * dgate, axis=0, keepdims=True))
    dlogits = jnp.sum(jnp.where(hot, dsel[:, :, None], 0.0), axis=0).astype(bf16)
    router_grad = t_product(hidden_two, dlogits)
    up_b = rows_product(expert_in, after(dupre_b, gate_a))

    def once_gate(stage, *arrays):
        return (after(arrays[0], up_b if stage else gate_a),) + arrays[1:]

    dhidden_two = plane_scatter(back, once_gate).reshape(home, width) + product_t(dlogits, router)

    flat_two = normed_two.reshape(home, width)
    dresid, expert_norm_grad = norm_backward(
        dhidden_two, flat_two, inverse_two.reshape(home, 1), expert_norm
    )
    dresid = dresid + grad_home.reshape(home, width).astype(f32)
    dbranch = chip_gather(dresid.astype(bf16).reshape(seq_n, piece, width), 1, parts).reshape(length, width)
    column_start = (r_i * core_n + core_i) * columns
    dbranch_here = lax.dynamic_slice_in_dim(dbranch, column_start, columns, 1)
    dmixed = chip_scatter(product_t(dbranch_here, weight_out).astype(bf16), 1, parts).astype(bf16)
    stages = {}

    def check(stage, *arrays):
        stages[stage] = arrays
        return arrays

    mixture = plane_scatter(after(mixed_rows, dbranch), check)
    dqpre, dkpre, dvpre = attend_back(
        query, keys, values, mixed, dmixed, cosine, sine, seg_row, seg_col, heads, down_sum_b, up_b, *stages[0]
    )
    up_a = rows_product(expert_in, after(dupre_a, dqpre, *stages[1]))
    output = (residual + mixture).astype(bf16)
    out_grad = t_product(mixed_full, after(dbranch_here, up_a, output)).astype(bf16)
    dkv = jnp.concatenate([dkpre, dvpre], axis=1)
    kv_grad = t_product(hidden_full, after(dkv, out_grad)).astype(bf16)
    query_grad = t_product(hidden_full, after(dqpre, out_grad)).astype(bf16)
    dqkv = after(jnp.concatenate([dqpre, dkpre, dvpre], axis=1), kv_grad, query_grad)
    dhidden_part = product_t(dqkv, weight_in).astype(bf16)
    dhidden_one = chip_scatter(
        dhidden_part.reshape(seq_n, parts * piece, width), 1, parts
    )
    normed_one = token_float * inverse_one
    dtokens, attn_norm_grad = norm_backward(
        dhidden_one.reshape(home, width),
        normed_one.reshape(home, width),
        inverse_one.reshape(home, 1),
        attn_norm,
    )
    dtokens = (dtokens + dresid).astype(bf16).reshape(seq_n, piece, width)

    grad_down = jnp.concatenate([down_sum_a, down_sum_b], axis=1).astype(f32).T[None]
    grad_gate = jnp.concatenate([gate_sum_a, gate_sum_b], axis=1).astype(f32)[None]
    grad_up = jnp.concatenate([over_ctx(up_a), over_ctx(up_b)], axis=1).astype(f32)[None]

    def seen(part):
        return part.reshape(dp_n, seq_n, r_n, y_n, core_n * rows_here, -1)

    def half(a, axis, index, name):
        keep, give = pick(a, index, axis), pick(a, 1 - index, axis)
        return total(keep, swap(give, name)).astype(bf16)

    first = [half(seen(a), 0, dp_i, "dp") for a in (out_grad, query_grad)]
    first.append(half(seen(kv_grad), 3, y_i, "y"))
    second = [half(a, 2, y_i, "y") for a in first[:2]] + [half(first[2], 0, dp_i, "dp")]
    second = jnp.concatenate(second, axis=-1)
    if r_n == 1 and parts == 2 and seq_n == 2 * seq_count == 4:
        part, grad_tokens, output = last_transfers(
            second.reshape(seq_n, core_n * rows_here, 4 * columns), dtokens, output, seq_count
        )
        part = total(part[:, 0], part[:, 1]).reshape(core_n, rows_here, 4, columns)
        part = part.transpose(1, 2, 0, 3).reshape(rows_here, 4, width)
    else:
        grad_tokens = from_sequences(dtokens)
        output = from_sequences(output)
        part = total(*seq_pieces(second)).astype(bf16)
        part = part.reshape(parts, rows_here, 4, 1, columns)
        part = chip_exchange(part, 0, 3, parts).reshape(rows_here, 4, width).astype(f32)
    grad_output, grad_query, grad_key, grad_value = (part[:, i] for i in range(4))
    grad_tokens = grad_tokens.astype(f32)

    gains = jnp.concatenate([attn_norm_grad[None], expert_norm_grad[None], router_grad.T], axis=0)
    gain_n = gains.shape[0]
    gains = gains.reshape(gain_n, -1, rows_here).transpose(1, 0, 2)
    gains = lax.all_to_all(gains, EVERY, split_axis=0, concat_axis=0, tiled=True)
    gains = jnp.sum(gains, axis=0).T

    return (
        output,
        grad_tokens,
        gains[:, 0],
        grad_query,
        grad_key,
        grad_value,
        grad_output,
        gains[:, 1],
        gains[:, 2:],
        grad_gate,
        grad_up,
        grad_down,
    )


def solution(mesh):
    dp_n, ctx_n, exp_n = mesh.shape["dp"], mesh.shape["ctx"], mesh.shape["exp"]

    def block(*arrays):
        tokens = arrays[0]
        seq_count = tokens.shape[0] // (dp_n * exp_n)
        seq_n = seq_count * CORES
        sizes = (dp_n, seq_n, ctx_n // seq_n, exp_n // CORES, CORES)
        fine = Mesh(mesh.devices.reshape(sizes), EVERY)
        group = ("dp", "y", "core")
        exp = ("y", "core")
        return jax.shard_map(
            functools.partial(on_device, sizes),
            mesh=fine,
            in_specs=(
                P(group, CTX, None),
                P(group, None),
                P(group, CTX, None),
                P(),
                P(EVERY, None),
                P(EVERY, None),
                P(EVERY, None),
                P(EVERY, None),
                P(),
                P(),
                P(exp, None, "dp"),
                P(exp, None, "dp"),
                P(exp, "dp", None),
                P(group, CTX, None),
            ),
            out_specs=(
                P(group, CTX, None),
                P(group, CTX, None),
                P(EVERY),
                P(EVERY, None),
                P(EVERY, None),
                P(EVERY, None),
                P(EVERY, None),
                P(EVERY),
                P(EVERY, None),
                P(exp, CTX, "dp"),
                P(exp, CTX, "dp"),
                P(exp, "dp", CTX),
            ),
            check_vma=False,
        )(*arrays)

    return block
```

```python
import functools

import jax
import jax.numpy as jnp
from jax import lax
from jax.experimental import pallas as pl
from jax.experimental.pallas import tpu as pltpu
from jax.sharding import Mesh, PartitionSpec as P

HEADS = 16
CORES = 2

epsilon = 1e-05
theta_base = 10000.0
masked_score = -1e30
bf16 = jnp.bfloat16
f32 = jnp.float32

PLANE = ("dp", "y", "core")
CHIP = ("r", "core")
SPREAD = ("dp", "seq", "y")
CTX = ("seq", "r")
EVERY = ("dp", "seq", "r", "y", "core")


def product(a, b):
    return jnp.dot(a, b, preferred_element_type=f32)


def product_t(a, b):
    return lax.dot_general(a, b, (((1,), (1,)), ((), ())), preferred_element_type=f32)


def t_product(a, b):
    return lax.dot_general(a, b, (((0,), (0,)), ((), ())), preferred_element_type=f32)


def swap(a, axis):
    return lax.ppermute(a, axis, [(0, 1), (1, 0)])


def halves(a, axis):
    size = a.shape[axis] // 2
    me = lax.axis_index("core")
    mine = lax.dynamic_slice_in_dim(a, me * size, size, axis)
    other = lax.dynamic_slice_in_dim(a, (1 - me) * size, size, axis)
    return mine, other


def by_core(mine, other, axis):
    first = lax.axis_index("core") == 0
    return jnp.concatenate([jnp.where(first, mine, other), jnp.where(first, other, mine)], axis=axis)


def chip_gather(a, axis, parts):
    if parts == 2:
        return by_core(a, swap(a, "core"), axis)
    return lax.all_gather(a, CHIP, axis=axis, tiled=True)


def chip_scatter(a, axis, parts):
    if parts == 2:
        mine, other = halves(a, axis)
        return mine.astype(f32) + swap(other, "core").astype(f32)
    return lax.psum_scatter(a, CHIP, scatter_dimension=axis, tiled=True).astype(f32)


def chip_exchange(a, split, concat, parts):
    if parts == 2:
        mine, other = halves(a, split)
        return by_core(mine, swap(other, "core"), concat)
    return lax.all_to_all(a, CHIP, split_axis=split, concat_axis=concat, tiled=True)


def core_exchange(a, split, concat):
    mine, other = halves(a, split)
    return by_core(mine, swap(other, "core"), concat)


def seq_pieces(a):
    count = a.shape[0]
    me = lax.axis_index("seq")
    pieces = [pick(a, me, 0)]
    for step in range(1, count):
        give = pick(a, lax.rem(me + step, count), 0)
        pieces.append(lax.ppermute(give, "seq", [(i, (i + step) % count) for i in range(count)]))
    return pieces


def seq_order(pieces):
    count = len(pieces)
    me = lax.axis_index("seq")
    pieces = jnp.stack(pieces)
    return jnp.stack([pick(pieces, lax.rem(me + count - s, count), 0) for s in range(count)])


def seq_exchange(a):
    return seq_order(seq_pieces(a))


def to_sequences(a):
    return seq_exchange(core_exchange(a, 1, 0))


def from_sequences(a):
    return core_exchange(seq_exchange(a), 0, 1)


def total(*parts):
    return sum(part.astype(f32) for part in parts)


def plane_scatter(blocks, check=lambda stage, *arrays: arrays):
    held = total(blocks[:, :, 0], swap(blocks[:, :, 1], "core")).astype(bf16)
    [held] = check(0, held)
    half = blocks.shape[3] // 2
    by_x = swap(held[1, 1, :half], "dp")
    by_y = swap(held[1, 1, half:], "y")
    to_x = jnp.concatenate([held[1, 0, :half], total(held[1, 0, half:], by_y).astype(bf16)], axis=0)
    to_y = jnp.concatenate([total(held[0, 1, :half], by_x).astype(bf16), held[0, 1, half:]], axis=0)
    to_x, to_y = check(1, to_x, to_y)
    return total(held[0, 0], swap(to_x, "dp"), swap(to_y, "y"))


MESH = pl.DeviceIdType.MESH
Z_UP, Z_DOWN, X_A, Y_A, Y_B, X_B, Y_A2, X_B2 = range(8)


def first_kernel(
    query,
    key,
    value,
    output,
    tokens,
    grads,
    segments,
    weights,
    tokens_out,
    grads_out,
    segments_out,
    send,
    recv,
    core_send,
    core_recv,
    core_local,
    row_send,
    row_recv,
    row_local,
):
    dp, z, y, core = (lax.axis_index(a) for a in ("dp", "seq", "y", "core"))
    seq_n = weights.shape[1]
    rows, columns = query.shape[0], weights.shape[4] // 4
    half = weights.shape[4] // 2
    piece = tokens_out.shape[1]
    x_next, y_next, z_next, z_last, other = (
        {"dp": 1 - dp},
        {"y": 1 - y},
        {"seq": lax.rem(z + 1, seq_n)},
        {"seq": lax.rem(z + seq_n - 1, seq_n)},
        {"core": 1 - core},
    )

    barrier = pltpu.get_barrier_semaphore()
    partners = [x_next, y_next] + [
        {"seq": lax.rem(z + dz, seq_n), "core": lax.rem(core + dc, 2)}
        for dz in range(seq_n)
        for dc in range(2)
        if dz or dc
    ]
    for partner in partners:
        pl.semaphore_signal(barrier, inc=1, device_id=partner, device_id_type=MESH)
    pl.semaphore_wait(barrier, len(partners))

    here = pl.ds(pl.multiple_of(core * rows, rows), rows)
    locals_, remotes = [], []
    for m, matrix in enumerate((query, key, value, output)):
        place = weights.at[dp, z, y, here, pl.ds(m * columns, columns)]
        mine = matrix.at[:, pl.ds(pl.multiple_of(core * columns, columns), columns)]
        theirs = matrix.at[:, pl.ds(pl.multiple_of((1 - core) * columns, columns), columns)]
        locals_.append(pltpu.make_async_copy(mine, place, core_local.at[m]))
        remotes.append(
            pltpu.make_async_remote_copy(
                theirs, place, core_send.at[m], core_recv.at[m], device_id=other, device_id_type=MESH
            )
        )
    segment_local = pltpu.make_async_copy(segments, segments_out.at[core], core_local.at[4])
    segment_remote = pltpu.make_async_remote_copy(
        segments, segments_out.at[core], core_send.at[4], core_recv.at[4], device_id=other, device_id_type=MESH
    )
    for copy in remotes + [segment_remote] + locals_ + [segment_local]:
        copy.start()
    for copy in remotes + locals_:
        copy.wait()

    def part(kind, dp_b, z_b, y_b, device):
        if kind in (Z_UP, Z_DOWN):
            ref = weights.at[dp_b, z_b, y_b]
        else:
            start = 0 if kind in (X_A, Y_A, Y_A2) else half
            ref = weights.at[dp_b, z_b, y_b, :, pl.ds(start, half)]
        return pltpu.make_async_remote_copy(
            ref, ref, send.at[kind, z_b], recv.at[kind, z_b], device_id=device, device_id_type=MESH
        )

    def own(kind, z_b):
        device = {Z_UP: z_next, Z_DOWN: z_last, X_A: x_next, X_B: x_next, Y_A: y_next, Y_B: y_next}[kind]
        return part(kind, dp, z_b, y, device)

    def from_x(kind, z_b):
        return part(kind, 1 - dp, z_b, y, x_next)

    def from_y(kind, z_b):
        return part(kind, dp, z_b, 1 - y, y_next)

    def on_y(z_b):
        return part(Y_A2, 1 - dp, z_b, y, y_next)

    def on_x(z_b):
        return part(X_B2, dp, z_b, 1 - y, x_next)

    def spread(z_b):
        for kind in (X_A, Y_B, X_B, Y_A):
            own(kind, z_b).start()

    def relay(z_b):
        from_x(X_A, z_b).wait_recv()
        on_y(z_b).start()
        from_y(Y_B, z_b).wait_recv()
        on_x(z_b).start()

    def at_step(step, act_up, act_down):
        @pl.when(z - step >= 0)
        def _():
            act_up(z - step)

        @pl.when(z + step < seq_n)
        def _():
            act_down(z + step)

    def come_up(z_b):
        own(Z_UP, z_b).wait_recv()

        @pl.when(z < seq_n - 1)
        def _():
            own(Z_UP, z_b).start()

        spread(z_b)

    def come_down(z_b):
        own(Z_DOWN, z_b).wait_recv()

        @pl.when(z > 0)
        def _():
            own(Z_DOWN, z_b).start()

        spread(z_b)

    def rows_of(n, source, target, act):
        for s in range(tokens.shape[0]):
            z_to = tokens.shape[0] * core + s
            for d in range(2):
                core_to = lax.rem(core + d, 2)
                ref = source.at[s, pl.ds(pl.multiple_of(core_to * piece, piece), piece), :]
                copy = pltpu.make_async_remote_copy(
                    ref,
                    target.at[z],
                    row_send.at[n, s, d],
                    row_recv.at[n, z],
                    device_id={"seq": z_to, "core": core_to},
                    device_id_type=MESH,
                )
                if d:
                    act(copy)
                else:
                    keep = pltpu.make_async_copy(ref, target.at[z], row_local.at[n])

                    @pl.when(z_to != z)
                    def _(copy=copy):
                        act(copy)

                    @pl.when(z_to == z)
                    def _(keep=keep):
                        if act is begin:
                            keep.start()
                        else:
                            keep.wait()

    def begin(copy):
        copy.start()

    def sent(copy):
        copy.wait_send()

    def rows_in(n, target):
        group = z // tokens.shape[0]
        for z_from in range(seq_n):
            copy = pltpu.make_async_remote_copy(
                target.at[z_from],
                target.at[z_from],
                row_send.at[n, 0, 0],
                row_recv.at[n, z_from],
                device_id=other,
                device_id_type=MESH,
            )

            @pl.when((z_from != z) | (group != core))
            def _(copy=copy):
                copy.wait_recv()

    @pl.when(z < seq_n - 1)
    def _():
        own(Z_UP, z).start()

    @pl.when(z > 0)
    def _():
        own(Z_DOWN, z).start()

    spread(z)
    for step in range(1, seq_n):
        at_step(step, come_up, come_down)
        if step == 1:
            relay(z)
        else:
            at_step(step - 1, relay, relay)
        if step == seq_n - 2:
            rows_of(0, tokens, tokens_out, begin)
    rows_of(1, grads, grads_out, begin)
    at_step(seq_n - 1, relay, relay)

    segment_remote.wait()
    segment_local.wait()
    for z_b in range(seq_n):
        from_y(Y_A, z_b).wait_recv()
        from_x(X_B, z_b).wait_recv()
        part(Y_A2, 1 - dp, z_b, 1 - y, y_next).wait_recv()
        part(X_B2, 1 - dp, z_b, 1 - y, x_next).wait_recv()
        for kind in (X_A, Y_B, X_B, Y_A):
            own(kind, z_b).wait_send()
        on_y(z_b).wait_send()
        on_x(z_b).wait_send()

        @pl.when((z < seq_n - 1) & (z_b <= z))
        def _(z_b=z_b):
            own(Z_UP, z_b).wait_send()

        @pl.when((z > 0) & (z_b >= z))
        def _(z_b=z_b):
            own(Z_DOWN, z_b).wait_send()

    rows_of(0, tokens, tokens_out, sent)
    rows_of(1, grads, grads_out, sent)
    rows_in(0, tokens_out)
    rows_in(1, grads_out)


def first_transfers(query, key, value, output, tokens, grads, segments, sizes):
    dp_n, seq_n, r_n, y_n, core_n = sizes
    rows, width = query.shape
    piece = tokens.shape[1] // core_n
    columns = width // core_n
    held = pl.BlockSpec(memory_space=pl.ANY)
    out = jax.ShapeDtypeStruct((seq_n, piece, width), bf16)
    dma = pltpu.SemaphoreType.DMA
    weights, tokens, grads, segments = pl.pallas_call(
        first_kernel,
        in_specs=[held] * 7,
        out_specs=[held] * 4,
        out_shape=[
            jax.ShapeDtypeStruct((dp_n, seq_n, y_n, core_n * rows, 4 * columns), bf16),
            out,
            out,
            jax.ShapeDtypeStruct((core_n,) + segments.shape, segments.dtype),
        ],
        scratch_shapes=[
            dma((8, seq_n)),
            dma((8, seq_n)),
            dma((5,)),
            dma((5,)),
            dma((5,)),
            dma((2, tokens.shape[0], 2)),
            dma((2, seq_n)),
            dma((2,)),
        ],
        compiler_params=pltpu.CompilerParams(collective_id=0, has_side_effects=True),
        cost_estimate=pl.CostEstimate(flops=0, bytes_accessed=2 * 4 * columns * width, transcendentals=0),
        name="first_transfers",
    )(query, key, value, output, tokens, grads, segments)
    return weights.reshape(width, 4 * columns), tokens, grads, segments


def last_kernel(
    grads,
    tokens,
    before,
    grads_out,
    tokens_out,
    mine,
    theirs,
    pair_send,
    pair_recv,
    send,
    recv,
    row_send,
    row_recv,
    local,
):
    z, core = lax.axis_index("seq"), lax.axis_index("core")
    seq_n, piece = tokens.shape[:2]
    seq_count = tokens_out.shape[0]
    rows = grads.shape[1] // 2
    odd = lax.rem(z, 2)
    neighbour = z + 1 - 2 * odd
    far = lax.rem(z + 2, seq_n)

    barrier = pltpu.get_barrier_semaphore()
    partners = [
        {"seq": lax.rem(z + dz, seq_n), "core": lax.rem(core + dc, 2)}
        for dz in range(seq_n)
        for dc in range(2)
        if dz or dc
    ]
    for partner in partners:
        pl.semaphore_signal(barrier, inc=1, device_id=partner, device_id_type=MESH)
    pl.semaphore_wait(barrier, len(partners))

    pair = [
        pltpu.make_async_remote_copy(
            grads.at[2 * i + 1 - odd],
            theirs.at[i],
            pair_send.at[i],
            pair_recv.at[i],
            device_id={"seq": neighbour},
            device_id_type=MESH,
        )
        for i in range(2)
    ]
    kept = [pltpu.make_async_copy(grads.at[2 * i + odd], mine.at[i], local.at[3 + i]) for i in range(2)]

    def rows_to(core_to):
        return pl.ds(pl.multiple_of(core_to * rows, rows), rows)

    def far_copy(dc):
        core_to = lax.rem(core + dc, 2)
        return pltpu.make_async_remote_copy(
            mine.at[far // 2, rows_to(core_to), :],
            grads_out.at[core, 1],
            send.at[1, dc],
            recv.at[1, dc],
            device_id={"seq": far, "core": core_to},
            device_id_type=MESH,
        )

    def near_copy():
        return pltpu.make_async_remote_copy(
            mine.at[z // 2, rows_to(1 - core), :],
            grads_out.at[core, 0],
            send.at[0, 1],
            recv.at[0, 1],
            device_id={"core": 1 - core},
            device_id_type=MESH,
        )

    def own_copy():
        return pltpu.make_async_copy(
            mine.at[z // 2, rows_to(core), :], grads_out.at[core, 0], local.at[2]
        )

    def arrival(place, dc):
        ref = grads_out.at[lax.rem(core + dc, 2), place]
        return pltpu.make_async_remote_copy(
            ref,
            ref,
            send.at[place, dc],
            recv.at[place, dc],
            device_id={"core": 1 - core},
            device_id_type=MESH,
        )

    group, member = z // seq_count, lax.rem(z, seq_count)

    def row_place(target, s, c):
        return target.at[s, pl.ds(pl.multiple_of(c * piece, piece), piece), :]

    def row_copy(n, source, target, dz):
        z_to = lax.rem(z + dz, seq_n)
        return pltpu.make_async_remote_copy(
            source.at[z_to],
            row_place(target, member, core),
            row_send.at[n, dz],
            row_recv.at[n, member, core],
            device_id={"seq": z_to, "core": group},
            device_id_type=MESH,
        )

    def each_row(remote, kept):
        for n, source, target in ((0, tokens, tokens_out),):
            for dz in range(seq_n):
                if dz:
                    remote(row_copy(n, source, target, dz))
                else:

                    @pl.when(group != core)
                    def _(copy=row_copy(n, source, target, 0)):
                        remote(copy)

                    @pl.when(group == core)
                    def _(n=n, source=source, target=target):
                        kept(
                            pltpu.make_async_copy(
                                source.at[z], row_place(target, member, core), local.at[n]
                            )
                        )

    for copy in pair + kept:
        copy.start()
    each_row(lambda copy: copy.start(), lambda copy: copy.start())

    for copy in kept:
        copy.wait()
    for copy in pair:
        copy.wait_recv()
    step = mine.shape[1] // 8

    def add(i, carry):
        span = pl.ds(pl.multiple_of(i * step, step), step)
        for part in range(2):
            mine[part, span, :] = total(mine[part, span, :], theirs[part, span, :]).astype(bf16)
        return carry

    lax.fori_loop(0, 8, add, 0)
    for copy in (far_copy(0), far_copy(1), near_copy(), own_copy()):
        copy.start()
    for copy in pair:
        copy.wait_send()
    own_copy().wait()
    for copy in (far_copy(0), far_copy(1), near_copy()):
        copy.wait_send()
    for place, dc in ((1, 0), (1, 1), (0, 1)):
        arrival(place, dc).wait_recv()
    each_row(lambda copy: copy.wait_send(), lambda copy: copy.wait())
    for n, target in ((0, tokens_out),):
        for s in range(seq_count):
            for c in range(2):
                ref = row_place(target, s, c)
                copy = pltpu.make_async_remote_copy(
                    ref,
                    ref,
                    row_send.at[n, 0],
                    row_recv.at[n, s, c],
                    device_id=partners[0],
                    device_id_type=MESH,
                )

                @pl.when((z != seq_count * core + s) | (core != c))
                def _(copy=copy):
                    copy.wait_recv()


def last_transfers(grads, tokens, before, seq_count):
    seq_n, piece, width = tokens.shape
    rows = grads.shape[1] // 2
    held = pl.BlockSpec(memory_space=pl.ANY)
    out = jax.ShapeDtypeStruct((seq_count, 2 * piece, width), bf16)
    dma = pltpu.SemaphoreType.DMA
    return pl.pallas_call(
        last_kernel,
        in_specs=[held] * 3,
        out_specs=[held] * 2,
        out_shape=[jax.ShapeDtypeStruct((2, 2, rows, grads.shape[2]), bf16), out],
        scratch_shapes=[
            pltpu.VMEM((2,) + grads.shape[1:], bf16),
            pltpu.VMEM((2,) + grads.shape[1:], bf16),
            dma((2,)),
            dma((2,)),
            dma((2, 2)),
            dma((2, 2)),
            dma((1, seq_n)),
            dma((1, seq_count, 2)),
            dma((5,)),
        ],
        compiler_params=pltpu.CompilerParams(
            collective_id=1, has_side_effects=True, vmem_limit_bytes=24 * 2**20
        ),
        cost_estimate=pl.CostEstimate(flops=0, bytes_accessed=4 * grads.size, transcendentals=0),
        name="last_transfers",
    )(grads, tokens, before)


def visible_block(seg_row, seg_col, start, rows, cols):
    row_place = start + lax.broadcasted_iota(jnp.int32, (rows, cols), 0)
    col_place = lax.broadcasted_iota(jnp.int32, (rows, cols), 1)
    return (seg_col == seg_row) & (col_place <= row_place)


def turned(u, cosine, sine):
    return u * cosine + pltpu.roll(u, u.shape[1] // 2, 1) * sine


def attend_kernel(scale, block, qp, kp, vp, cosine, sine, seg_row, seg_col, q_out, k_out, v_out, mixed):
    length = qp.shape[0]
    q_out[...] = turned(qp[...], cosine[...], sine[...]).astype(bf16)
    k_out[...] = turned(kp[...], cosine[...], sine[...]).astype(bf16)
    v_out[...] = vp[...].astype(bf16)
    for start in range(0, length, block):
        stop = start + block
        scores = product_t(q_out[start:stop, :], k_out[:stop, :]) * scale
        seen = visible_block(seg_row[:, :stop], seg_col[start:stop, :], start, block, stop)
        scores = jnp.where(seen, scores, masked_score)
        top = jnp.max(scores, axis=1, keepdims=True)
        weights = jnp.exp(scores - top)
        total = jnp.sum(weights, axis=1, keepdims=True)
        summed = product(weights.astype(bf16), v_out[:stop, :])
        mixed[start:stop, :] = (summed / total).astype(bf16)


def attend(qkv, cosine, sine, seg_row, seg_col, heads):
    length, head = qkv.shape[0], cosine.shape[1]
    block = min(256, length)

    def column(offset):
        return pl.BlockSpec((length, head), lambda h: (0, offset + h))

    def whole(shape):
        return pl.BlockSpec(shape, lambda h: (0, 0))

    out = jax.ShapeDtypeStruct((length, heads * head), bf16)
    pairs = length * (length + block) // 2 * heads
    return pl.pallas_call(
        functools.partial(attend_kernel, head**-0.5, block),
        grid=(heads,),
        in_specs=[
            column(0),
            column(heads),
            column(2 * heads),
            whole((length, head)),
            whole((length, head)),
            whole((1, length)),
            whole((length, 1)),
        ],
        out_specs=[column(0)] * 4,
        out_shape=[out] * 4,
        compiler_params=pltpu.CompilerParams(vmem_limit_bytes=48 * 2**20),
        cost_estimate=pl.CostEstimate(
            flops=4 * pairs * head, bytes_accessed=20 * length * heads * head, transcendentals=pairs
        ),
        name="attend",
    )(qkv, qkv, qkv, cosine, sine, seg_row, seg_col)


def attend_back_kernel(
    scale, block, q, k, v, mixed, dmixed, cosine, sine, seg_row, seg_col, *rest
):
    dq_out, dk_out, dv_out, dk_sum, dv_sum = rest[-5:]
    length = q.shape[0]
    dk_sum[...] = jnp.zeros_like(dk_sum)
    dv_sum[...] = jnp.zeros_like(dv_sum)
    for start in range(0, length, block):
        stop = start + block
        scores = product_t(q[start:stop, :], k[:stop, :]) * scale
        seen = visible_block(seg_row[:, :stop], seg_col[start:stop, :], start, block, stop)
        scores = jnp.where(seen, scores, masked_score)
        top = jnp.max(scores, axis=1, keepdims=True)
        weights = jnp.exp(scores - top)
        inverse = 1.0 / jnp.sum(weights, axis=1, keepdims=True)
        grad = dmixed[start:stop, :].astype(f32)
        delta = jnp.sum(grad * mixed[start:stop, :].astype(f32), axis=1, keepdims=True) * inverse
        unit = (grad * inverse).astype(bf16)
        dweights = product_t(unit, v[:stop, :])
        dscores = (weights * (dweights - delta)).astype(bf16)
        dq = product(dscores, k[:stop, :]) * scale
        dq_out[start:stop, :] = turned(dq, cosine[start:stop, :], -sine[start:stop, :]).astype(bf16)
        dk_sum[:stop, :] += t_product(dscores, q[start:stop, :])
        dv_sum[:stop, :] += t_product(weights.astype(bf16), unit)
    dk_out[...] = turned(dk_sum[...] * scale, cosine[...], -sine[...]).astype(bf16)
    dv_out[...] = dv_sum[...].astype(bf16)


def attend_back(q, k, v, mixed, dmixed, cosine, sine, seg_row, seg_col, heads, *before):
    length, head = q.shape[0], cosine.shape[1]
    block = min(256, length)
    column = pl.BlockSpec((length, head), lambda h: (0, h))

    def whole(shape):
        return pl.BlockSpec(shape, lambda h: (0, 0))

    out = jax.ShapeDtypeStruct((length, heads * head), bf16)
    pairs = length * (length + block) // 2 * heads
    return pl.pallas_call(
        functools.partial(attend_back_kernel, head**-0.5, block),
        grid=(heads,),
        in_specs=[column] * 5
        + [whole((length, head)), whole((length, head)), whole((1, length)), whole((length, 1))]
        + [pl.BlockSpec(memory_space=pl.ANY)] * len(before),
        out_specs=[column] * 3,
        out_shape=[out] * 3,
        scratch_shapes=[pltpu.VMEM((length, head), f32)] * 2,
        compiler_params=pltpu.CompilerParams(vmem_limit_bytes=48 * 2**20),
        cost_estimate=pl.CostEstimate(
            flops=10 * pairs * head, bytes_accessed=16 * length * heads * head, transcendentals=pairs
        ),
        name="attend_back",
    )(q, k, v, mixed, dmixed, cosine, sine, seg_row, seg_col, *before)


def units_kernel(chunk, x, dy, gate, up, down, *rest):
    units, dgate, dup = rest[-3:]
    gate_w, up_w, down_w = gate[...], up[...], down[...]

    def step(i, carry):
        rows = pl.ds(pl.multiple_of(i * chunk, chunk), chunk)
        gpre = product(x[rows, :], gate_w)
        upre = product(x[rows, :], up_w)
        dunits = product_t(dy[rows, :], down_w)
        s = jax.nn.sigmoid(gpre)
        silu = gpre * s
        units[rows, :] = (silu * upre).astype(bf16)
        dgate[rows, :] = (dunits * upre * (s * (1.0 + gpre * (1.0 - s)))).astype(bf16)
        dup[rows, :] = (dunits * silu).astype(bf16)
        return carry

    lax.fori_loop(0, x.shape[0] // chunk, step, 0)


def expert_units(x, dy, gate, up, down, start, stop, half=None, made=(), before=()):
    rows, width = x.shape
    units = stop - start
    part, at = (rows, 0) if half is None else (rows // 2, half)
    chunk = tile_of(part)
    tile = unit_tile(gate.shape[1])
    first = start // tile
    once = pl.BlockSpec((part, width), lambda j: (at, 0), pipeline_mode=pl.Buffered(1))
    out = jax.ShapeDtypeStruct((rows, units), bf16)
    return pl.pallas_call(
        functools.partial(units_kernel, chunk),
        grid=(units // tile,),
        in_specs=[
            once,
            once,
            pl.BlockSpec((width, tile), lambda j: (0, first + j)),
            pl.BlockSpec((width, tile), lambda j: (0, first + j)),
            pl.BlockSpec((tile, width), lambda j: (first + j, 0)),
        ]
        + [pl.BlockSpec(memory_space=pl.ANY)] * (len(made) + len(before)),
        out_specs=[pl.BlockSpec((part, tile), lambda j: (at, j))] * 3,
        out_shape=[out] * 3,
        input_output_aliases={5 + i: i for i in range(len(made))},
        compiler_params=pltpu.CompilerParams(vmem_limit_bytes=56 * 2**20),
        cost_estimate=pl.CostEstimate(
            flops=6 * part * width * units,
            bytes_accessed=4 * part * width + 6 * width * units + 6 * part * units,
            transcendentals=part * units,
        ),
        name="expert_units",
    )(x, dy, gate, up, down, *made, *before)


def unit_tile(units):
    return 256 if units % 256 == 0 else units


def unit_cut(units):
    tile = unit_tile(units)
    return units // tile * 3 // 4 * tile


def dispatch_kernel(me, hidden, dout, slot, routes, router, *rest):
    rows, dy_rows, gate = rest[-3:]
    size = hidden.shape[1] * hidden.shape[3]
    width = hidden.shape[4]
    mine = me[3]
    tokens = hidden[...].reshape(size, width)
    logits = product(tokens, router[...])
    lanes = lax.broadcasted_iota(jnp.int32, logits.shape, 1)
    first, second = routes[0, :, 0:1], routes[0, :, 1:2]
    one = jnp.sum(jnp.where(lanes == first, logits, 0.0), axis=1, keepdims=True)
    two = jnp.sum(jnp.where(lanes == second, logits, 0.0), axis=1, keepdims=True)
    top = jnp.maximum(one, two)
    one, two = jnp.exp(one - top), jnp.exp(two - top)
    share = jnp.where(first == mine, one, jnp.where(second == mine, two, 0.0)) / (one + two)
    gate[0] = share
    chosen = (
        lax.broadcasted_iota(jnp.int32, (rows.shape[1], size), 0) == slot[0]
    ).astype(bf16)
    rows[0] = product(chosen, tokens).astype(bf16)
    dy = (share * dout[...].reshape(size, width).astype(f32)).astype(bf16)
    dy_rows[0] = product(chosen, dy).astype(bf16)


def block_place(b, span):
    return lax.rem(b, 4 * span) // span, (b // (4 * span)) * span + lax.rem(b, span)


def plane_block(seq_n, piece, width, first=0, seen=None):
    span = seq_n // 2

    def index(b, me):
        device, place = block_place(b + first, span)
        return (device, 0, place if seen is None else lax.rem(place, seen), 0, 0)

    return pl.BlockSpec((1, 2, 1, piece, width), index)


def relative_block(seq_n, piece, width):
    def index(b, me):
        device, place = block_place(b, seq_n // 2)
        return (lax.rem(device // 2 + me[0], 2), lax.rem(device + me[1], 2), 0, place, 0, 0)

    return pl.BlockSpec((1, 1, 2, 1, piece, width), index)


def dispatch(me, hidden, dout, slot, routes, router, seq_n, piece, cap, half, made=()):
    blocks, size = slot.shape[0], slot.shape[2]
    width = hidden.shape[1]
    span = seq_n // 2
    count = blocks // 2
    first = half * count

    def each(*shape):
        return pl.BlockSpec((1,) + shape, lambda b, me: (first + b, 0, 0))

    out = jax.ShapeDtypeStruct((blocks, cap, width), bf16)
    spare = jnp.zeros((width, 128 - router.shape[1]), router.dtype)
    return pl.pallas_call(
        dispatch_kernel,
        grid_spec=pltpu.PrefetchScalarGridSpec(
            num_scalar_prefetch=1,
            grid=(count,),
            in_specs=[
                plane_block(seq_n, piece, width, first, span),
                plane_block(seq_n, piece, width, first),
                each(1, size),
                each(size, routes.shape[2]),
                pl.BlockSpec((width, 128), lambda b, me: (0, 0)),
            ]
            + [pl.BlockSpec(memory_space=pl.ANY)] * len(made),
            out_specs=[each(cap, width), each(cap, width), each(size, 1)],
        ),
        out_shape=[out, out, jax.ShapeDtypeStruct((blocks, size, 1), f32)],
        input_output_aliases={6 + i: i for i in range(len(made))},
        compiler_params=pltpu.CompilerParams(vmem_limit_bytes=40 * 2**20),
        cost_estimate=pl.CostEstimate(
            flops=4 * count * size * width * (cap + 64),
            bytes_accessed=4 * count * (size + cap) * width,
            transcendentals=2 * count * size,
        ),
        name="dispatch",
    )(
        me,
        hidden.reshape(4, 2, span, piece, width),
        dout.reshape(4, 2, seq_n, piece, width),
        slot,
        routes,
        jnp.concatenate([router, spare], axis=1),
        *made,
    )


def spread_rows(slot, rows):
    size, cap = slot.shape[0], rows.shape[0]
    chosen = (lax.broadcasted_iota(jnp.int32, (size, cap), 1) == slot).astype(bf16)
    return product(chosen, rows)


def place_cores(me, out, dense):
    piece = out.shape[4]
    for core in range(2):
        out[0, 0, lax.rem(me[2] + core, 2), 0] = dense[core * piece : (core + 1) * piece, :].astype(bf16)


def combine_kernel(me, rows, slot, gate, dout, out, dgate):
    dense = spread_rows(slot[0], rows[0])
    grads = dout[...].reshape(dense.shape).astype(f32)
    dgate[0] = jnp.sum(grads * dense, axis=1, keepdims=True)
    place_cores(me, out, gate[0] * dense)


def collect_kernel(me, left, slot, right, *rest):
    dense = [spread_rows(slot[0], left[0]), spread_rows(slot[0], right[0])]
    place_cores(me, rest[-1], jnp.concatenate(dense, axis=1))


def combine(me, rows, slot, seq_n, piece, gate=None, dout=None, right=None):
    blocks, cap, part = rows.shape
    size = slot.shape[1]
    width = part if right is None else 2 * part
    column = pl.BlockSpec((1, size, 1), lambda b, me: (b, 0, 0))
    weigh = gate is not None
    operands = [rows, slot]
    in_specs = [pl.BlockSpec((1, cap, part), lambda b, me: (b, 0, 0)), column]
    out_specs = [relative_block(seq_n, piece, width)]
    out_shape = [jax.ShapeDtypeStruct((2, 2, 2, seq_n, piece, width), bf16)]
    if weigh:
        operands += [gate, dout.reshape(4, 2, seq_n, piece, width)]
        in_specs += [column, plane_block(seq_n, piece, width)]
        out_specs += [column]
        out_shape += [jax.ShapeDtypeStruct((blocks, size, 1), f32)]
    else:
        operands += [right]
        in_specs += in_specs[:1]
    return pl.pallas_call(
        combine_kernel if weigh else collect_kernel,
        grid_spec=pltpu.PrefetchScalarGridSpec(
            num_scalar_prefetch=1, grid=(blocks,), in_specs=in_specs, out_specs=out_specs
        ),
        out_shape=out_shape,
        compiler_params=pltpu.CompilerParams(vmem_limit_bytes=40 * 2**20),
        cost_estimate=pl.CostEstimate(
            flops=2 * blocks * size * width * cap,
            bytes_accessed=2 * blocks * (2 * size + cap) * width,
            transcendentals=0,
        ),
        name="combine" if weigh else "collect",
    )(me, *operands)


def down_kernel(cut, units_a, units_b, down, *rest):
    total = product(units_a[...], down[:cut, :]) + product(units_b[...], down[cut:, :])
    rest[-1][...] = total.astype(bf16)


def expert_down(units_a, units_b, down, *before):
    rows, cut = units_a.shape
    inner, width = down.shape
    m, n = tile_of(rows), tile_of(width)
    return pl.pallas_call(
        functools.partial(down_kernel, cut),
        grid=(width // n, rows // m),
        in_specs=[
            pl.BlockSpec((m, cut), lambda j, i: (i, 0)),
            pl.BlockSpec((m, inner - cut), lambda j, i: (i, 0)),
            pl.BlockSpec((inner, n), lambda j, i: (0, j)),
        ]
        + [pl.BlockSpec(memory_space=pl.ANY)] * len(before),
        out_specs=pl.BlockSpec((m, n), lambda j, i: (i, j)),
        out_shape=jax.ShapeDtypeStruct((rows, width), bf16),
        compiler_params=pltpu.CompilerParams(vmem_limit_bytes=48 * 2**20),
        cost_estimate=pl.CostEstimate(
            flops=2 * rows * inner * width,
            bytes_accessed=2 * (rows * inner + inner * width + rows * width),
            transcendentals=0,
        ),
        name="expert_down",
    )(units_a, units_b, down, *before)


def input_kernel(cut, dgate_a, dgate_b, dup_a, dup_b, gate, up, *rest):
    total = product_t(dgate_a[...], gate[:, :cut]) + product_t(dgate_b[...], gate[:, cut:])
    total += product_t(dup_a[...], up[:, :cut]) + product_t(dup_b[...], up[:, cut:])
    rest[-1][...] = total.astype(bf16)


def expert_input_grad(dgate_a, dgate_b, dup_a, dup_b, gate, up, start, stop, *before):
    rows, cut = dgate_a.shape
    inner = gate.shape[1]
    width = stop - start
    m, n = tile_of(rows), tile_of(width)
    first = start // n
    left_a = pl.BlockSpec((m, cut), lambda j, i: (i, 0))
    left_b = pl.BlockSpec((m, inner - cut), lambda j, i: (i, 0))
    right = pl.BlockSpec((n, inner), lambda j, i: (first + j, 0))
    return pl.pallas_call(
        functools.partial(input_kernel, cut),
        grid=(width // n, rows // m),
        in_specs=[left_a, left_b, left_a, left_b, right, right]
        + [pl.BlockSpec(memory_space=pl.ANY)] * len(before),
        out_specs=pl.BlockSpec((m, n), lambda j, i: (i, j)),
        out_shape=jax.ShapeDtypeStruct((rows, width), bf16),
        compiler_params=pltpu.CompilerParams(vmem_limit_bytes=52 * 2**20),
        cost_estimate=pl.CostEstimate(
            flops=4 * rows * inner * width,
            bytes_accessed=2 * (2 * rows * inner + 2 * inner * width + rows * width),
            transcendentals=0,
        ),
        name="expert_input_grad",
    )(dgate_a, dgate_b, dup_a, dup_b, gate, up, *before)


def tile_of(size):
    return max(c for c in range(16, 513, 16) if size % c == 0)


def anchor_kernel(*refs):
    pass


def after(a, *before):
    return pl.pallas_call(
        anchor_kernel,
        in_specs=[pl.BlockSpec(memory_space=pl.ANY)] * (1 + len(before)),
        out_specs=pl.BlockSpec(memory_space=pl.ANY),
        out_shape=jax.ShapeDtypeStruct(a.shape, a.dtype),
        input_output_aliases={0: 0},
        cost_estimate=pl.CostEstimate(flops=0, bytes_accessed=0, transcendentals=0),
        name="after",
    )(a, *before)


def norm_backward(grad_rows, normed, inverse, gain):
    weighted = grad_rows * gain
    mean_term = jnp.mean(weighted * normed, axis=-1, keepdims=True)
    return inverse * (weighted - normed * mean_term), jnp.sum(grad_rows * normed, axis=0)


def pick(a, index, axis):
    return lax.dynamic_index_in_dim(a, index, axis, keepdims=False)


def on_device(
    sizes,
    tokens,
    segments,
    routes,
    attn_norm,
    query_weight,
    key_weight,
    value_weight,
    output_weight,
    expert_norm,
    router,
    gate_weight,
    up_weight,
    down_weight,
    grad_out,
):
    dp_n, seq_n, r_n, y_n, core_n = sizes
    parts = r_n * core_n
    seq_count, seq_dev, width = tokens.shape
    piece = seq_dev // core_n
    length = segments.shape[1]
    home = seq_n * piece
    head = width // HEADS
    heads = HEADS // parts
    columns = width // parts
    experts = router.shape[1]
    topk = routes.shape[2]
    plane = 8 * home
    blocks = plane // seq_dev
    cap = 5 * seq_dev * topk // (4 * experts)
    dp_i, seq_i, r_i, y_i, core_i = (lax.axis_index(a) for a in EVERY)
    group, member = seq_i // seq_count, seq_i % seq_count

    rows_here = query_weight.shape[0]
    if r_n == 1 and parts == 2 and dp_n == 2 and y_n == 2 and seq_n == 2 * seq_count:
        weights, token_home, grad_home, chip_segments = first_transfers(
            query_weight, key_weight, value_weight, output_weight, tokens, grad_out, segments, sizes
        )
        segment = pick(pick(chip_segments, group, 0), member, 0)
    else:
        local = jnp.concatenate([query_weight, key_weight, value_weight, output_weight], axis=1)
        local = chip_exchange(local.reshape(rows_here, 4, parts, columns), 2, 0, parts)
        weights = lax.all_gather(
            local.reshape(parts * rows_here, 4 * columns), SPREAD, axis=0, tiled=True
        )
        weights = (
            weights.reshape(dp_n * seq_n, y_n, r_n, core_n * rows_here, -1)
            .transpose(0, 2, 1, 3, 4)
            .reshape(width, -1)
        )
        token_home, grad_home = to_sequences(tokens), to_sequences(grad_out)
        chip_segments = lax.all_gather(segments, "core")
        segment = pick(pick(chip_segments, group, 0), member, 0)
    weight_in, weight_out = weights[:, : 3 * columns], weights[:, 3 * columns :]

    token_float = token_home.astype(f32)
    inverse_one = lax.rsqrt(jnp.mean(token_float * token_float, axis=-1, keepdims=True) + epsilon)
    hidden_one = (token_float * inverse_one * attn_norm).astype(bf16)
    hidden_full = chip_gather(hidden_one, 1, parts).reshape(length, width)

    grad_plane = lax.all_gather(grad_home.reshape(home, width), PLANE, axis=0, tiled=True)

    half = head // 2
    frequency = theta_base ** (-jnp.arange(half, dtype=f32) / half)
    angles = jnp.arange(length, dtype=f32)[:, None] * frequency[None, :]
    cosine = jnp.concatenate([jnp.cos(angles)] * 2, axis=1)
    sine = jnp.concatenate([-jnp.sin(angles), jnp.sin(angles)], axis=1)
    seg_row, seg_col = segment[None, :], segment[:, None]

    qkv = product(hidden_full, weight_in)
    query, keys, values, mixed = attend(qkv, cosine, sine, seg_row, seg_col, heads)
    mixed_full = chip_gather(mixed, 1, parts)
    branch = product(mixed_full, weight_out).reshape(seq_n, parts, piece, columns)
    branch = chip_exchange(branch, 1, 3, parts).reshape(seq_n, piece, width)
    residual = token_float + branch
    inverse_two = lax.rsqrt(jnp.mean(residual * residual, axis=-1, keepdims=True) + epsilon)
    normed_two = residual * inverse_two
    hidden_two = (normed_two * expert_norm).astype(bf16).reshape(home, width)
    hidden_two = after(hidden_two, grad_plane)

    hidden_parts = [
        lax.all_gather(part, PLANE, axis=0, tiled=True) for part in jnp.split(hidden_two, 2)
    ]
    small = after(jnp.transpose(routes, (2, 0, 1)).reshape(topk * seq_count, seq_dev), hidden_two)
    small = lax.all_gather(small, EVERY, axis=0, tiled=True).reshape(
        dp_n, seq_n, r_n, y_n, core_n, topk, seq_count, seq_dev
    )
    small = pick(pick(small, group, 4), member, 5)
    plane_routes = pick(small, r_i, 2).transpose(0, 2, 1, 3, 4)
    block_routes = plane_routes.reshape(4, 2, seq_n // 2, topk, seq_dev)
    block_routes = block_routes.transpose(1, 0, 2, 3, 4).reshape(blocks, topk, seq_dev)
    home_routes = (
        pick(pick(plane_routes, dp_i, 0), y_i, 0)
        .reshape(seq_n, topk, core_n, piece)
        .transpose(1, 2, 0, 3)
    )
    home_routes = pick(home_routes, core_i, 1).reshape(topk, home)
    mine = y_i * core_n + core_i
    chosen = jnp.any(block_routes == mine, axis=1)
    places = jnp.arange(seq_dev)
    rank = product(chosen.astype(bf16), (places[:, None] < places[None, :]).astype(bf16))
    slot = jnp.where(chosen, rank.astype(jnp.int32), -1)
    slot_row, slot_col = slot[:, None, :], slot[:, :, None]
    me = jnp.stack([dp_i, y_i, core_i, mine]).astype(jnp.int32)
    gate_one, up_one, down_one = gate_weight[0], up_weight[0], down_weight[0]
    inner = gate_one.shape[1]
    cut = unit_cut(inner)
    full = (gate_one, up_one, down_one)
    route_col = jnp.transpose(block_routes, (0, 2, 1))
    picked, unit_parts = (), ()
    for part, hidden_part in enumerate(hidden_parts):
        picked = dispatch(
            me, hidden_part, grad_plane, slot_row, route_col, router, seq_n, piece, cap, part, picked
        )
        expert_in, dy_rows = (rows.reshape(blocks * cap, width) for rows in picked[:2])
        unit_parts = expert_units(expert_in, dy_rows, *full, 0, cut, part, unit_parts)
    row_gate = picked[2]
    units_a, dgpre_a, dupre_a = unit_parts

    def over_ctx(part):
        return lax.psum_scatter(part, CTX, scatter_dimension=0, tiled=True)

    def rows_product(rows, part):
        return t_product(rows, part).astype(bf16)

    down_a = rows_product(dy_rows, units_a)
    units_b, dgpre_b, dupre_b = expert_units(expert_in, dy_rows, *full, cut, inner, before=(down_a,))
    down_b = rows_product(dy_rows, units_b)
    down_sum_a, down_sum_b = over_ctx(down_a), over_ctx(down_b)
    grads = (dgpre_a, dgpre_b, dupre_a, dupre_b, gate_one, up_one)
    left = expert_input_grad(*grads, 0, width // 2, down_b)
    right = expert_input_grad(*grads, width // 2, width, left)
    left, right = (part.reshape(blocks, cap, width // 2) for part in (left, right))
    [back] = combine(me, left, slot_col, seq_n, piece, right=right)
    gate_a = rows_product(expert_in, after(dgpre_a, back, down_sum_a))
    gate_b = rows_product(expert_in, after(dgpre_b, back))
    gate_sum_a, gate_sum_b = over_ctx(gate_a), over_ctx(gate_b)
    ypair = expert_down(units_a, units_b, down_one, gate_a)
    mixed_rows, dgate_plane = combine(
        me, ypair.reshape(blocks, cap, width), slot_col, seq_n, piece, row_gate, grad_plane
    )

    dgate_plane = dgate_plane.reshape(2, 4, seq_n // 2, core_n, piece).transpose(1, 3, 0, 2, 4)
    dgate_home = lax.all_to_all(
        dgate_plane.reshape(8, home), PLANE, split_axis=0, concat_axis=0, tiled=True
    ).reshape(dp_n, experts, home).sum(axis=0)

    logits = product(hidden_two, router)
    hot = home_routes[:, :, None] == jnp.arange(experts, dtype=jnp.int32)[None, None, :]
    gates = jax.nn.softmax(jnp.sum(jnp.where(hot, logits[None], 0.0), axis=2), axis=0)
    dgate = jnp.sum(jnp.where(hot, jnp.transpose(dgate_home)[None], 0.0), axis=2)
    dsel = gates * (dgate - jnp.sum(gates * dgate, axis=0, keepdims=True))
    dlogits = jnp.sum(jnp.where(hot, dsel[:, :, None], 0.0), axis=0).astype(bf16)
    router_grad = t_product(hidden_two, dlogits)
    up_b = rows_product(expert_in, after(dupre_b, gate_a))

    def once_gate(stage, *arrays):
        return (after(arrays[0], up_b if stage else gate_a),) + arrays[1:]

    dhidden_two = plane_scatter(back, once_gate).reshape(home, width) + product_t(dlogits, router)

    flat_two = normed_two.reshape(home, width)
    dresid, expert_norm_grad = norm_backward(
        dhidden_two, flat_two, inverse_two.reshape(home, 1), expert_norm
    )
    dresid = dresid + grad_home.reshape(home, width).astype(f32)
    dbranch = chip_gather(dresid.astype(bf16).reshape(seq_n, piece, width), 1, parts).reshape(length, width)
    column_start = (r_i * core_n + core_i) * columns
    dbranch_here = lax.dynamic_slice_in_dim(dbranch, column_start, columns, 1)
    dmixed = chip_scatter(product_t(dbranch_here, weight_out).astype(bf16), 1, parts).astype(bf16)
    stages = {}

    def check(stage, *arrays):
        stages[stage] = arrays
        return arrays

    mixture = plane_scatter(after(mixed_rows, dbranch), check)
    dqpre, dkpre, dvpre = attend_back(
        query, keys, values, mixed, dmixed, cosine, sine, seg_row, seg_col, heads, down_sum_b, up_b, *stages[0]
    )
    up_a = rows_product(expert_in, after(dupre_a, dqpre, *stages[1]))
    output = (residual + mixture).astype(bf16)
    out_grad = t_product(mixed_full, after(dbranch_here, up_a, output)).astype(bf16)
    dkv = jnp.concatenate([dkpre, dvpre], axis=1)
    kv_grad = t_product(hidden_full, after(dkv, out_grad)).astype(bf16)
    query_grad = t_product(hidden_full, after(dqpre, out_grad)).astype(bf16)
    dqkv = after(jnp.concatenate([dqpre, dkpre, dvpre], axis=1), kv_grad, query_grad)
    dhidden_part = product_t(dqkv, weight_in).astype(bf16)
    dhidden_one = chip_scatter(
        dhidden_part.reshape(seq_n, parts * piece, width), 1, parts
    )
    normed_one = token_float * inverse_one
    dtokens, attn_norm_grad = norm_backward(
        dhidden_one.reshape(home, width),
        normed_one.reshape(home, width),
        inverse_one.reshape(home, 1),
        attn_norm,
    )
    dtokens = (dtokens + dresid).astype(bf16).reshape(seq_n, piece, width)

    grad_down = jnp.concatenate([down_sum_a, down_sum_b], axis=1).astype(f32).T[None]
    grad_gate = jnp.concatenate([gate_sum_a, gate_sum_b], axis=1).astype(f32)[None]
    grad_up = jnp.concatenate([over_ctx(up_a), over_ctx(up_b)], axis=1).astype(f32)[None]

    def seen(part):
        return part.reshape(dp_n, seq_n, r_n, y_n, core_n * rows_here, -1)

    def half(a, axis, index, name):
        keep, give = pick(a, index, axis), pick(a, 1 - index, axis)
        return total(keep, swap(give, name)).astype(bf16)

    first = [half(seen(a), 0, dp_i, "dp") for a in (out_grad, query_grad)]
    first.append(half(seen(kv_grad), 3, y_i, "y"))
    output = [after(piece, first[2]) for piece in seq_pieces(output)]
    output = core_exchange(seq_order(output), 0, 1)
    second = [half(a, 2, y_i, "y") for a in first[:2]] + [half(first[2], 0, dp_i, "dp")]
    second = jnp.concatenate(second, axis=-1)
    if r_n == 1 and parts == 2 and seq_n == 2 * seq_count == 4:
        part, grad_tokens = last_transfers(
            second.reshape(seq_n, core_n * rows_here, 4 * columns), dtokens, output, seq_count
        )
        part = total(part[:, 0], part[:, 1]).reshape(core_n, rows_here, 4, columns)
        part = part.transpose(1, 2, 0, 3).reshape(rows_here, 4, width)
    else:
        grad_tokens = from_sequences(dtokens)
        part = total(*seq_pieces(second)).astype(bf16)
        part = part.reshape(parts, rows_here, 4, 1, columns)
        part = chip_exchange(part, 0, 3, parts).reshape(rows_here, 4, width).astype(f32)
    grad_output, grad_query, grad_key, grad_value = (part[:, i] for i in range(4))
    grad_tokens = grad_tokens.astype(f32)

    gains = jnp.concatenate([attn_norm_grad[None], expert_norm_grad[None], router_grad.T], axis=0)
    gain_n = gains.shape[0]
    gains = gains.reshape(gain_n, -1, rows_here).transpose(1, 0, 2)
    gains = lax.all_to_all(gains, EVERY, split_axis=0, concat_axis=0, tiled=True)
    gains = jnp.sum(gains, axis=0).T

    return (
        output,
        grad_tokens,
        gains[:, 0],
        grad_query,
        grad_key,
        grad_value,
        grad_output,
        gains[:, 1],
        gains[:, 2:],
        grad_gate,
        grad_up,
        grad_down,
    )


def solution(mesh):
    dp_n, ctx_n, exp_n = mesh.shape["dp"], mesh.shape["ctx"], mesh.shape["exp"]

    def block(*arrays):
        tokens = arrays[0]
        seq_count = tokens.shape[0] // (dp_n * exp_n)
        seq_n = seq_count * CORES
        sizes = (dp_n, seq_n, ctx_n // seq_n, exp_n // CORES, CORES)
        fine = Mesh(mesh.devices.reshape(sizes), EVERY)
        group = ("dp", "y", "core")
        exp = ("y", "core")
        return jax.shard_map(
            functools.partial(on_device, sizes),
            mesh=fine,
            in_specs=(
                P(group, CTX, None),
                P(group, None),
                P(group, CTX, None),
                P(),
                P(EVERY, None),
                P(EVERY, None),
                P(EVERY, None),
                P(EVERY, None),
                P(),
                P(),
                P(exp, None, "dp"),
                P(exp, None, "dp"),
                P(exp, "dp", None),
                P(group, CTX, None),
            ),
            out_specs=(
                P(group, CTX, None),
                P(group, CTX, None),
                P(EVERY),
                P(EVERY, None),
                P(EVERY, None),
                P(EVERY, None),
                P(EVERY, None),
                P(EVERY),
                P(EVERY, None),
                P(exp, CTX, "dp"),
                P(exp, CTX, "dp"),
                P(exp, "dp", CTX),
            ),
            check_vma=False,
        )(*arrays)

    return block
```

```python
import functools

import jax
import jax.numpy as jnp
from jax import lax
from jax.experimental import pallas as pl
from jax.experimental.pallas import tpu as pltpu
from jax.sharding import Mesh, PartitionSpec as P

HEADS = 16
CORES = 2

epsilon = 1e-05
theta_base = 10000.0
masked_score = -1e30
bf16 = jnp.bfloat16
f32 = jnp.float32

PLANE = ("dp", "y", "core")
CHIP = ("r", "core")
SPREAD = ("dp", "seq", "y")
CTX = ("seq", "r")
EVERY = ("dp", "seq", "r", "y", "core")


def product(a, b):
    return jnp.dot(a, b, preferred_element_type=f32)


def product_t(a, b):
    return lax.dot_general(a, b, (((1,), (1,)), ((), ())), preferred_element_type=f32)


def t_product(a, b):
    return lax.dot_general(a, b, (((0,), (0,)), ((), ())), preferred_element_type=f32)


def swap(a, axis):
    return lax.ppermute(a, axis, [(0, 1), (1, 0)])


def halves(a, axis):
    size = a.shape[axis] // 2
    me = lax.axis_index("core")
    mine = lax.dynamic_slice_in_dim(a, me * size, size, axis)
    other = lax.dynamic_slice_in_dim(a, (1 - me) * size, size, axis)
    return mine, other


def by_core(mine, other, axis):
    first = lax.axis_index("core") == 0
    return jnp.concatenate([jnp.where(first, mine, other), jnp.where(first, other, mine)], axis=axis)


def chip_gather(a, axis, parts):
    if parts == 2:
        return by_core(a, swap(a, "core"), axis)
    return lax.all_gather(a, CHIP, axis=axis, tiled=True)


def chip_scatter(a, axis, parts):
    if parts == 2:
        mine, other = halves(a, axis)
        return mine.astype(f32) + swap(other, "core").astype(f32)
    return lax.psum_scatter(a, CHIP, scatter_dimension=axis, tiled=True).astype(f32)


def chip_exchange(a, split, concat, parts):
    if parts == 2:
        mine, other = halves(a, split)
        return by_core(mine, swap(other, "core"), concat)
    return lax.all_to_all(a, CHIP, split_axis=split, concat_axis=concat, tiled=True)


def core_exchange(a, split, concat):
    mine, other = halves(a, split)
    return by_core(mine, swap(other, "core"), concat)


def seq_pieces(a):
    count = a.shape[0]
    me = lax.axis_index("seq")
    pieces = [pick(a, me, 0)]
    for step in range(1, count):
        give = pick(a, lax.rem(me + step, count), 0)
        pieces.append(lax.ppermute(give, "seq", [(i, (i + step) % count) for i in range(count)]))
    return pieces


def seq_order(pieces):
    count = len(pieces)
    me = lax.axis_index("seq")
    pieces = jnp.stack(pieces)
    return jnp.stack([pick(pieces, lax.rem(me + count - s, count), 0) for s in range(count)])


def seq_exchange(a):
    return seq_order(seq_pieces(a))


def to_sequences(a):
    return seq_exchange(core_exchange(a, 1, 0))


def from_sequences(a):
    return core_exchange(seq_exchange(a), 0, 1)


def total(*parts):
    return sum(part.astype(f32) for part in parts)


def plane_scatter(blocks, check=lambda stage, *arrays: arrays):
    held = total(blocks[:, :, 0], swap(blocks[:, :, 1], "core")).astype(bf16)
    [held] = check(0, held)
    half = blocks.shape[3] // 2
    by_x = swap(held[1, 1, :half], "dp")
    by_y = swap(held[1, 1, half:], "y")
    to_x = jnp.concatenate([held[1, 0, :half], total(held[1, 0, half:], by_y).astype(bf16)], axis=0)
    to_y = jnp.concatenate([total(held[0, 1, :half], by_x).astype(bf16), held[0, 1, half:]], axis=0)
    to_x, to_y = check(1, to_x, to_y)
    return total(held[0, 0], swap(to_x, "dp"), swap(to_y, "y"))


MESH = pl.DeviceIdType.MESH
Z_UP, Z_DOWN, X_A, Y_A, Y_B, X_B, Y_A2, X_B2 = range(8)


def first_kernel(
    query,
    key,
    value,
    output,
    tokens,
    grads,
    segments,
    weights,
    tokens_out,
    grads_out,
    segments_out,
    send,
    recv,
    core_send,
    core_recv,
    core_local,
    row_send,
    row_recv,
    row_local,
):
    dp, z, y, core = (lax.axis_index(a) for a in ("dp", "seq", "y", "core"))
    seq_n = weights.shape[1]
    rows, columns = query.shape[0], weights.shape[4] // 4
    half = weights.shape[4] // 2
    piece = tokens_out.shape[1]
    x_next, y_next, z_next, z_last, other = (
        {"dp": 1 - dp},
        {"y": 1 - y},
        {"seq": lax.rem(z + 1, seq_n)},
        {"seq": lax.rem(z + seq_n - 1, seq_n)},
        {"core": 1 - core},
    )

    barrier = pltpu.get_barrier_semaphore()
    partners = [x_next, y_next] + [
        {"seq": lax.rem(z + dz, seq_n), "core": lax.rem(core + dc, 2)}
        for dz in range(seq_n)
        for dc in range(2)
        if dz or dc
    ]
    for partner in partners:
        pl.semaphore_signal(barrier, inc=1, device_id=partner, device_id_type=MESH)
    pl.semaphore_wait(barrier, len(partners))

    here = pl.ds(pl.multiple_of(core * rows, rows), rows)
    locals_, remotes = [], []
    for m, matrix in enumerate((query, key, value, output)):
        place = weights.at[dp, z, y, here, pl.ds(m * columns, columns)]
        mine = matrix.at[:, pl.ds(pl.multiple_of(core * columns, columns), columns)]
        theirs = matrix.at[:, pl.ds(pl.multiple_of((1 - core) * columns, columns), columns)]
        locals_.append(pltpu.make_async_copy(mine, place, core_local.at[m]))
        remotes.append(
            pltpu.make_async_remote_copy(
                theirs, place, core_send.at[m], core_recv.at[m], device_id=other, device_id_type=MESH
            )
        )
    segment_local = pltpu.make_async_copy(segments, segments_out.at[core], core_local.at[4])
    segment_remote = pltpu.make_async_remote_copy(
        segments, segments_out.at[core], core_send.at[4], core_recv.at[4], device_id=other, device_id_type=MESH
    )
    for copy in remotes + [segment_remote] + locals_ + [segment_local]:
        copy.start()
    for copy in remotes + locals_:
        copy.wait()

    def part(kind, dp_b, z_b, y_b, device):
        if kind in (Z_UP, Z_DOWN):
            ref = weights.at[dp_b, z_b, y_b]
        else:
            start = 0 if kind in (X_A, Y_A, Y_A2) else half
            ref = weights.at[dp_b, z_b, y_b, :, pl.ds(start, half)]
        return pltpu.make_async_remote_copy(
            ref, ref, send.at[kind, z_b], recv.at[kind, z_b], device_id=device, device_id_type=MESH
        )

    def own(kind, z_b):
        device = {Z_UP: z_next, Z_DOWN: z_last, X_A: x_next, X_B: x_next, Y_A: y_next, Y_B: y_next}[kind]
        return part(kind, dp, z_b, y, device)

    def from_x(kind, z_b):
        return part(kind, 1 - dp, z_b, y, x_next)

    def from_y(kind, z_b):
        return part(kind, dp, z_b, 1 - y, y_next)

    def on_y(z_b):
        return part(Y_A2, 1 - dp, z_b, y, y_next)

    def on_x(z_b):
        return part(X_B2, dp, z_b, 1 - y, x_next)

    def spread(z_b):
        for kind in (X_A, Y_B, X_B, Y_A):
            own(kind, z_b).start()

    def relay(z_b):
        from_x(X_A, z_b).wait_recv()
        on_y(z_b).start()
        from_y(Y_B, z_b).wait_recv()
        on_x(z_b).start()

    def at_step(step, act_up, act_down):
        @pl.when(z - step >= 0)
        def _():
            act_up(z - step)

        @pl.when(z + step < seq_n)
        def _():
            act_down(z + step)

    def come_up(z_b):
        own(Z_UP, z_b).wait_recv()

        @pl.when(z < seq_n - 1)
        def _():
            own(Z_UP, z_b).start()

        spread(z_b)

    def come_down(z_b):
        own(Z_DOWN, z_b).wait_recv()

        @pl.when(z > 0)
        def _():
            own(Z_DOWN, z_b).start()

        spread(z_b)

    def rows_of(n, source, target, act):
        for s in range(tokens.shape[0]):
            z_to = tokens.shape[0] * core + s
            for d in range(2):
                core_to = lax.rem(core + d, 2)
                ref = source.at[s, pl.ds(pl.multiple_of(core_to * piece, piece), piece), :]
                copy = pltpu.make_async_remote_copy(
                    ref,
                    target.at[z],
                    row_send.at[n, s, d],
                    row_recv.at[n, z],
                    device_id={"seq": z_to, "core": core_to},
                    device_id_type=MESH,
                )
                if d:
                    act(copy)
                else:
                    keep = pltpu.make_async_copy(ref, target.at[z], row_local.at[n])

                    @pl.when(z_to != z)
                    def _(copy=copy):
                        act(copy)

                    @pl.when(z_to == z)
                    def _(keep=keep):
                        if act is begin:
                            keep.start()
                        else:
                            keep.wait()

    def begin(copy):
        copy.start()

    def sent(copy):
        copy.wait_send()

    def rows_in(n, target):
        group = z // tokens.shape[0]
        for z_from in range(seq_n):
            copy = pltpu.make_async_remote_copy(
                target.at[z_from],
                target.at[z_from],
                row_send.at[n, 0, 0],
                row_recv.at[n, z_from],
                device_id=other,
                device_id_type=MESH,
            )

            @pl.when((z_from != z) | (group != core))
            def _(copy=copy):
                copy.wait_recv()

    @pl.when(z < seq_n - 1)
    def _():
        own(Z_UP, z).start()

    @pl.when(z > 0)
    def _():
        own(Z_DOWN, z).start()

    spread(z)
    for step in range(1, seq_n):
        at_step(step, come_up, come_down)
        if step == 1:
            relay(z)
        else:
            at_step(step - 1, relay, relay)
        if step == seq_n - 2:
            rows_of(0, tokens, tokens_out, begin)
    rows_of(1, grads, grads_out, begin)
    at_step(seq_n - 1, relay, relay)

    segment_remote.wait()
    segment_local.wait()
    for z_b in range(seq_n):
        from_y(Y_A, z_b).wait_recv()
        from_x(X_B, z_b).wait_recv()
        part(Y_A2, 1 - dp, z_b, 1 - y, y_next).wait_recv()
        part(X_B2, 1 - dp, z_b, 1 - y, x_next).wait_recv()
        for kind in (X_A, Y_B, X_B, Y_A):
            own(kind, z_b).wait_send()
        on_y(z_b).wait_send()
        on_x(z_b).wait_send()

        @pl.when((z < seq_n - 1) & (z_b <= z))
        def _(z_b=z_b):
            own(Z_UP, z_b).wait_send()

        @pl.when((z > 0) & (z_b >= z))
        def _(z_b=z_b):
            own(Z_DOWN, z_b).wait_send()

    rows_of(0, tokens, tokens_out, sent)
    rows_of(1, grads, grads_out, sent)
    rows_in(0, tokens_out)
    rows_in(1, grads_out)


def first_transfers(query, key, value, output, tokens, grads, segments, sizes):
    dp_n, seq_n, r_n, y_n, core_n = sizes
    rows, width = query.shape
    piece = tokens.shape[1] // core_n
    columns = width // core_n
    held = pl.BlockSpec(memory_space=pl.ANY)
    out = jax.ShapeDtypeStruct((seq_n, piece, width), bf16)
    dma = pltpu.SemaphoreType.DMA
    weights, tokens, grads, segments = pl.pallas_call(
        first_kernel,
        in_specs=[held] * 7,
        out_specs=[held] * 4,
        out_shape=[
            jax.ShapeDtypeStruct((dp_n, seq_n, y_n, core_n * rows, 4 * columns), bf16),
            out,
            out,
            jax.ShapeDtypeStruct((core_n,) + segments.shape, segments.dtype),
        ],
        scratch_shapes=[
            dma((8, seq_n)),
            dma((8, seq_n)),
            dma((5,)),
            dma((5,)),
            dma((5,)),
            dma((2, tokens.shape[0], 2)),
            dma((2, seq_n)),
            dma((2,)),
        ],
        compiler_params=pltpu.CompilerParams(collective_id=0, has_side_effects=True),
        cost_estimate=pl.CostEstimate(flops=0, bytes_accessed=2 * 4 * columns * width, transcendentals=0),
        name="first_transfers",
    )(query, key, value, output, tokens, grads, segments)
    return weights.reshape(width, 4 * columns), tokens, grads, segments


def last_kernel(
    grads,
    tokens,
    before,
    grads_out,
    tokens_out,
    mine,
    theirs,
    pair_send,
    pair_recv,
    send,
    recv,
    row_send,
    row_recv,
    local,
):
    z, core = lax.axis_index("seq"), lax.axis_index("core")
    seq_n, piece = tokens.shape[:2]
    seq_count = tokens_out.shape[0]
    rows = grads.shape[1] // 2
    odd = lax.rem(z, 2)
    neighbour = z + 1 - 2 * odd
    far = lax.rem(z + 2, seq_n)

    barrier = pltpu.get_barrier_semaphore()
    partners = [
        {"seq": lax.rem(z + dz, seq_n), "core": lax.rem(core + dc, 2)}
        for dz in range(seq_n)
        for dc in range(2)
        if dz or dc
    ]
    for partner in partners:
        pl.semaphore_signal(barrier, inc=1, device_id=partner, device_id_type=MESH)
    pl.semaphore_wait(barrier, len(partners))

    pair = [
        pltpu.make_async_remote_copy(
            grads.at[2 * i + 1 - odd],
            theirs.at[i],
            pair_send.at[i],
            pair_recv.at[i],
            device_id={"seq": neighbour},
            device_id_type=MESH,
        )
        for i in range(2)
    ]
    kept = [pltpu.make_async_copy(grads.at[2 * i + odd], mine.at[i], local.at[3 + i]) for i in range(2)]

    def rows_to(core_to):
        return pl.ds(pl.multiple_of(core_to * rows, rows), rows)

    def far_copy(dc):
        core_to = lax.rem(core + dc, 2)
        return pltpu.make_async_remote_copy(
            mine.at[far // 2, rows_to(core_to), :],
            grads_out.at[core, 1],
            send.at[1, dc],
            recv.at[1, dc],
            device_id={"seq": far, "core": core_to},
            device_id_type=MESH,
        )

    def near_copy():
        return pltpu.make_async_remote_copy(
            mine.at[z // 2, rows_to(1 - core), :],
            grads_out.at[core, 0],
            send.at[0, 1],
            recv.at[0, 1],
            device_id={"core": 1 - core},
            device_id_type=MESH,
        )

    def own_copy():
        return pltpu.make_async_copy(
            mine.at[z // 2, rows_to(core), :], grads_out.at[core, 0], local.at[2]
        )

    def arrival(place, dc):
        ref = grads_out.at[lax.rem(core + dc, 2), place]
        return pltpu.make_async_remote_copy(
            ref,
            ref,
            send.at[place, dc],
            recv.at[place, dc],
            device_id={"core": 1 - core},
            device_id_type=MESH,
        )

    group, member = z // seq_count, lax.rem(z, seq_count)

    def row_place(target, s, c):
        return target.at[s, pl.ds(pl.multiple_of(c * piece, piece), piece), :]

    def row_copy(n, source, target, dz):
        z_to = lax.rem(z + dz, seq_n)
        return pltpu.make_async_remote_copy(
            source.at[z_to],
            row_place(target, member, core),
            row_send.at[n, dz],
            row_recv.at[n, member, core],
            device_id={"seq": z_to, "core": group},
            device_id_type=MESH,
        )

    def each_row(remote, kept):
        for n, source, target in ((0, tokens, tokens_out),):
            for dz in range(seq_n):
                if dz:
                    remote(row_copy(n, source, target, dz))
                else:

                    @pl.when(group != core)
                    def _(copy=row_copy(n, source, target, 0)):
                        remote(copy)

                    @pl.when(group == core)
                    def _(n=n, source=source, target=target):
                        kept(
                            pltpu.make_async_copy(
                                source.at[z], row_place(target, member, core), local.at[n]
                            )
                        )

    for copy in pair + kept:
        copy.start()
    each_row(lambda copy: copy.start(), lambda copy: copy.start())

    for copy in kept:
        copy.wait()
    for copy in pair:
        copy.wait_recv()
    step = mine.shape[1] // 8

    def add(i, carry):
        span = pl.ds(pl.multiple_of(i * step, step), step)
        for part in range(2):
            mine[part, span, :] = total(mine[part, span, :], theirs[part, span, :]).astype(bf16)
        return carry

    lax.fori_loop(0, 8, add, 0)
    for copy in (far_copy(0), far_copy(1), near_copy(), own_copy()):
        copy.start()
    for copy in pair:
        copy.wait_send()
    own_copy().wait()
    for copy in (far_copy(0), far_copy(1), near_copy()):
        copy.wait_send()
    for place, dc in ((1, 0), (1, 1), (0, 1)):
        arrival(place, dc).wait_recv()
    each_row(lambda copy: copy.wait_send(), lambda copy: copy.wait())
    for n, target in ((0, tokens_out),):
        for s in range(seq_count):
            for c in range(2):
                ref = row_place(target, s, c)
                copy = pltpu.make_async_remote_copy(
                    ref,
                    ref,
                    row_send.at[n, 0],
                    row_recv.at[n, s, c],
                    device_id=partners[0],
                    device_id_type=MESH,
                )

                @pl.when((z != seq_count * core + s) | (core != c))
                def _(copy=copy):
                    copy.wait_recv()


def last_transfers(grads, tokens, before, seq_count):
    seq_n, piece, width = tokens.shape
    rows = grads.shape[1] // 2
    held = pl.BlockSpec(memory_space=pl.ANY)
    out = jax.ShapeDtypeStruct((seq_count, 2 * piece, width), bf16)
    dma = pltpu.SemaphoreType.DMA
    return pl.pallas_call(
        last_kernel,
        in_specs=[held] * 3,
        out_specs=[held] * 2,
        out_shape=[jax.ShapeDtypeStruct((2, 2, rows, grads.shape[2]), bf16), out],
        scratch_shapes=[
            pltpu.VMEM((2,) + grads.shape[1:], bf16),
            pltpu.VMEM((2,) + grads.shape[1:], bf16),
            dma((2,)),
            dma((2,)),
            dma((2, 2)),
            dma((2, 2)),
            dma((1, seq_n)),
            dma((1, seq_count, 2)),
            dma((5,)),
        ],
        compiler_params=pltpu.CompilerParams(
            collective_id=1, has_side_effects=True, vmem_limit_bytes=24 * 2**20
        ),
        cost_estimate=pl.CostEstimate(flops=0, bytes_accessed=4 * grads.size, transcendentals=0),
        name="last_transfers",
    )(grads, tokens, before)


def visible_block(seg_row, seg_col, start, rows, cols):
    row_place = start + lax.broadcasted_iota(jnp.int32, (rows, cols), 0)
    col_place = lax.broadcasted_iota(jnp.int32, (rows, cols), 1)
    return (seg_col == seg_row) & (col_place <= row_place)


def turned(u, cosine, sine):
    return u * cosine + pltpu.roll(u, u.shape[1] // 2, 1) * sine


def attend_kernel(scale, block, qp, kp, vp, cosine, sine, seg_row, seg_col, q_out, k_out, v_out, mixed):
    length = qp.shape[0]
    q_out[...] = turned(qp[...], cosine[...], sine[...]).astype(bf16)
    k_out[...] = turned(kp[...], cosine[...], sine[...]).astype(bf16)
    v_out[...] = vp[...].astype(bf16)
    for start in range(0, length, block):
        stop = start + block
        scores = product_t(q_out[start:stop, :], k_out[:stop, :]) * scale
        seen = visible_block(seg_row[:, :stop], seg_col[start:stop, :], start, block, stop)
        scores = jnp.where(seen, scores, masked_score)
        top = jnp.max(scores, axis=1, keepdims=True)
        weights = jnp.exp(scores - top)
        total = jnp.sum(weights, axis=1, keepdims=True)
        summed = product(weights.astype(bf16), v_out[:stop, :])
        mixed[start:stop, :] = (summed / total).astype(bf16)


def attend(qkv, cosine, sine, seg_row, seg_col, heads):
    length, head = qkv.shape[0], cosine.shape[1]
    block = min(256, length)

    def column(offset):
        return pl.BlockSpec((length, head), lambda h: (0, offset + h))

    def whole(shape):
        return pl.BlockSpec(shape, lambda h: (0, 0))

    out = jax.ShapeDtypeStruct((length, heads * head), bf16)
    pairs = length * (length + block) // 2 * heads
    return pl.pallas_call(
        functools.partial(attend_kernel, head**-0.5, block),
        grid=(heads,),
        in_specs=[
            column(0),
            column(heads),
            column(2 * heads),
            whole((length, head)),
            whole((length, head)),
            whole((1, length)),
            whole((length, 1)),
        ],
        out_specs=[column(0)] * 4,
        out_shape=[out] * 4,
        compiler_params=pltpu.CompilerParams(vmem_limit_bytes=48 * 2**20),
        cost_estimate=pl.CostEstimate(
            flops=4 * pairs * head, bytes_accessed=20 * length * heads * head, transcendentals=pairs
        ),
        name="attend",
    )(qkv, qkv, qkv, cosine, sine, seg_row, seg_col)


def attend_back_kernel(
    scale, block, q, k, v, mixed, dmixed, cosine, sine, seg_row, seg_col, *rest
):
    dq_out, dk_out, dv_out, dk_sum, dv_sum = rest[-5:]
    length = q.shape[0]
    dk_sum[...] = jnp.zeros_like(dk_sum)
    dv_sum[...] = jnp.zeros_like(dv_sum)
    for start in range(0, length, block):
        stop = start + block
        scores = product_t(q[start:stop, :], k[:stop, :]) * scale
        seen = visible_block(seg_row[:, :stop], seg_col[start:stop, :], start, block, stop)
        scores = jnp.where(seen, scores, masked_score)
        top = jnp.max(scores, axis=1, keepdims=True)
        weights = jnp.exp(scores - top)
        inverse = 1.0 / jnp.sum(weights, axis=1, keepdims=True)
        grad = dmixed[start:stop, :].astype(f32)
        delta = jnp.sum(grad * mixed[start:stop, :].astype(f32), axis=1, keepdims=True) * inverse
        unit = (grad * inverse).astype(bf16)
        dweights = product_t(unit, v[:stop, :])
        dscores = (weights * (dweights - delta)).astype(bf16)
        dq = product(dscores, k[:stop, :]) * scale
        dq_out[start:stop, :] = turned(dq, cosine[start:stop, :], -sine[start:stop, :]).astype(bf16)
        dk_sum[:stop, :] += t_product(dscores, q[start:stop, :])
        dv_sum[:stop, :] += t_product(weights.astype(bf16), unit)
    dk_out[...] = turned(dk_sum[...] * scale, cosine[...], -sine[...]).astype(bf16)
    dv_out[...] = dv_sum[...].astype(bf16)


def attend_back(q, k, v, mixed, dmixed, cosine, sine, seg_row, seg_col, heads, *before):
    length, head = q.shape[0], cosine.shape[1]
    block = min(256, length)
    column = pl.BlockSpec((length, head), lambda h: (0, h))

    def whole(shape):
        return pl.BlockSpec(shape, lambda h: (0, 0))

    out = jax.ShapeDtypeStruct((length, heads * head), bf16)
    pairs = length * (length + block) // 2 * heads
    return pl.pallas_call(
        functools.partial(attend_back_kernel, head**-0.5, block),
        grid=(heads,),
        in_specs=[column] * 5
        + [whole((length, head)), whole((length, head)), whole((1, length)), whole((length, 1))]
        + [pl.BlockSpec(memory_space=pl.ANY)] * len(before),
        out_specs=[column] * 3,
        out_shape=[out] * 3,
        scratch_shapes=[pltpu.VMEM((length, head), f32)] * 2,
        compiler_params=pltpu.CompilerParams(vmem_limit_bytes=48 * 2**20),
        cost_estimate=pl.CostEstimate(
            flops=10 * pairs * head, bytes_accessed=16 * length * heads * head, transcendentals=pairs
        ),
        name="attend_back",
    )(q, k, v, mixed, dmixed, cosine, sine, seg_row, seg_col, *before)


def units_kernel(chunk, x, dy, gate, up, down, *rest):
    units, dgate, dup = rest[-3:]
    gate_w, up_w, down_w = gate[...], up[...], down[...]

    def step(i, carry):
        rows = pl.ds(pl.multiple_of(i * chunk, chunk), chunk)
        gpre = product(x[rows, :], gate_w)
        upre = product(x[rows, :], up_w)
        dunits = product_t(dy[rows, :], down_w)
        s = jax.nn.sigmoid(gpre)
        silu = gpre * s
        units[rows, :] = (silu * upre).astype(bf16)
        dgate[rows, :] = (dunits * upre * (s * (1.0 + gpre * (1.0 - s)))).astype(bf16)
        dup[rows, :] = (dunits * silu).astype(bf16)
        return carry

    lax.fori_loop(0, x.shape[0] // chunk, step, 0)


def expert_units(x, dy, gate, up, down, start, stop, half=None, made=(), before=()):
    rows, width = x.shape
    units = stop - start
    part, at = (rows, 0) if half is None else (rows // 2, half)
    chunk = tile_of(part)
    tile = unit_tile(gate.shape[1])
    first = start // tile
    once = pl.BlockSpec((part, width), lambda j: (at, 0), pipeline_mode=pl.Buffered(1))
    out = jax.ShapeDtypeStruct((rows, units), bf16)
    return pl.pallas_call(
        functools.partial(units_kernel, chunk),
        grid=(units // tile,),
        in_specs=[
            once,
            once,
            pl.BlockSpec((width, tile), lambda j: (0, first + j)),
            pl.BlockSpec((width, tile), lambda j: (0, first + j)),
            pl.BlockSpec((tile, width), lambda j: (first + j, 0)),
        ]
        + [pl.BlockSpec(memory_space=pl.ANY)] * (len(made) + len(before)),
        out_specs=[pl.BlockSpec((part, tile), lambda j: (at, j))] * 3,
        out_shape=[out] * 3,
        input_output_aliases={5 + i: i for i in range(len(made))},
        compiler_params=pltpu.CompilerParams(vmem_limit_bytes=56 * 2**20),
        cost_estimate=pl.CostEstimate(
            flops=6 * part * width * units,
            bytes_accessed=4 * part * width + 6 * width * units + 6 * part * units,
            transcendentals=part * units,
        ),
        name="expert_units",
    )(x, dy, gate, up, down, *made, *before)


def unit_tile(units):
    return 256 if units % 256 == 0 else units


def unit_cut(units):
    tile = unit_tile(units)
    return units // tile * 3 // 4 * tile


def dispatch_kernel(me, hidden, dout, slot, routes, router, *rest):
    rows, dy_rows, gate = rest[-3:]
    size = hidden.shape[1] * hidden.shape[3]
    width = hidden.shape[4]
    mine = me[3]
    tokens = hidden[...].reshape(size, width)
    logits = product(tokens, router[...])
    lanes = lax.broadcasted_iota(jnp.int32, logits.shape, 1)
    first, second = routes[0, :, 0:1], routes[0, :, 1:2]
    one = jnp.sum(jnp.where(lanes == first, logits, 0.0), axis=1, keepdims=True)
    two = jnp.sum(jnp.where(lanes == second, logits, 0.0), axis=1, keepdims=True)
    top = jnp.maximum(one, two)
    one, two = jnp.exp(one - top), jnp.exp(two - top)
    share = jnp.where(first == mine, one, jnp.where(second == mine, two, 0.0)) / (one + two)
    gate[0] = share
    chosen = (
        lax.broadcasted_iota(jnp.int32, (rows.shape[1], size), 0) == slot[0]
    ).astype(bf16)
    rows[0] = product(chosen, tokens).astype(bf16)
    dy = (share * dout[...].reshape(size, width).astype(f32)).astype(bf16)
    dy_rows[0] = product(chosen, dy).astype(bf16)


def block_place(b, span):
    return lax.rem(b, 4 * span) // span, (b // (4 * span)) * span + lax.rem(b, span)


def plane_block(seq_n, piece, width, first=0, seen=None):
    span = seq_n // 2

    def index(b, me):
        device, place = block_place(b + first, span)
        return (device, 0, place if seen is None else lax.rem(place, seen), 0, 0)

    return pl.BlockSpec((1, 2, 1, piece, width), index)


def relative_block(seq_n, piece, width):
    def index(b, me):
        device, place = block_place(b, seq_n // 2)
        return (lax.rem(device // 2 + me[0], 2), lax.rem(device + me[1], 2), 0, place, 0, 0)

    return pl.BlockSpec((1, 1, 2, 1, piece, width), index)


def dispatch(me, hidden, dout, slot, routes, router, seq_n, piece, cap, half, made=()):
    blocks, size = slot.shape[0], slot.shape[2]
    width = hidden.shape[1]
    span = seq_n // 2
    count = blocks // 2
    first = half * count

    def each(*shape):
        return pl.BlockSpec((1,) + shape, lambda b, me: (first + b, 0, 0))

    out = jax.ShapeDtypeStruct((blocks, cap, width), bf16)
    spare = jnp.zeros((width, 128 - router.shape[1]), router.dtype)
    return pl.pallas_call(
        dispatch_kernel,
        grid_spec=pltpu.PrefetchScalarGridSpec(
            num_scalar_prefetch=1,
            grid=(count,),
            in_specs=[
                plane_block(seq_n, piece, width, first, span),
                plane_block(seq_n, piece, width, first),
                each(1, size),
                each(size, routes.shape[2]),
                pl.BlockSpec((width, 128), lambda b, me: (0, 0)),
            ]
            + [pl.BlockSpec(memory_space=pl.ANY)] * len(made),
            out_specs=[each(cap, width), each(cap, width), each(size, 1)],
        ),
        out_shape=[out, out, jax.ShapeDtypeStruct((blocks, size, 1), f32)],
        input_output_aliases={6 + i: i for i in range(len(made))},
        compiler_params=pltpu.CompilerParams(vmem_limit_bytes=40 * 2**20),
        cost_estimate=pl.CostEstimate(
            flops=4 * count * size * width * (cap + 64),
            bytes_accessed=4 * count * (size + cap) * width,
            transcendentals=2 * count * size,
        ),
        name="dispatch",
    )(
        me,
        hidden.reshape(4, 2, span, piece, width),
        dout.reshape(4, 2, seq_n, piece, width),
        slot,
        routes,
        jnp.concatenate([router, spare], axis=1),
        *made,
    )


def spread_rows(slot, rows):
    size, cap = slot.shape[0], rows.shape[0]
    chosen = (lax.broadcasted_iota(jnp.int32, (size, cap), 1) == slot).astype(bf16)
    return product(chosen, rows)


def place_cores(me, out, dense):
    piece = out.shape[4]
    for core in range(2):
        out[0, 0, lax.rem(me[2] + core, 2), 0] = dense[core * piece : (core + 1) * piece, :].astype(bf16)


def combine_kernel(me, rows, slot, gate, dout, out, dgate):
    dense = spread_rows(slot[0], rows[0])
    grads = dout[...].reshape(dense.shape).astype(f32)
    dgate[0] = jnp.sum(grads * dense, axis=1, keepdims=True)
    place_cores(me, out, gate[0] * dense)


def collect_kernel(me, left, slot, right, *rest):
    dense = [spread_rows(slot[0], left[0]), spread_rows(slot[0], right[0])]
    place_cores(me, rest[-1], jnp.concatenate(dense, axis=1))


def combine(me, rows, slot, seq_n, piece, gate=None, dout=None, right=None):
    blocks, cap, part = rows.shape
    size = slot.shape[1]
    width = part if right is None else 2 * part
    column = pl.BlockSpec((1, size, 1), lambda b, me: (b, 0, 0))
    weigh = gate is not None
    operands = [rows, slot]
    in_specs = [pl.BlockSpec((1, cap, part), lambda b, me: (b, 0, 0)), column]
    out_specs = [relative_block(seq_n, piece, width)]
    out_shape = [jax.ShapeDtypeStruct((2, 2, 2, seq_n, piece, width), bf16)]
    if weigh:
        operands += [gate, dout.reshape(4, 2, seq_n, piece, width)]
        in_specs += [column, plane_block(seq_n, piece, width)]
        out_specs += [column]
        out_shape += [jax.ShapeDtypeStruct((blocks, size, 1), f32)]
    else:
        operands += [right]
        in_specs += in_specs[:1]
    return pl.pallas_call(
        combine_kernel if weigh else collect_kernel,
        grid_spec=pltpu.PrefetchScalarGridSpec(
            num_scalar_prefetch=1, grid=(blocks,), in_specs=in_specs, out_specs=out_specs
        ),
        out_shape=out_shape,
        compiler_params=pltpu.CompilerParams(vmem_limit_bytes=40 * 2**20),
        cost_estimate=pl.CostEstimate(
            flops=2 * blocks * size * width * cap,
            bytes_accessed=2 * blocks * (2 * size + cap) * width,
            transcendentals=0,
        ),
        name="combine" if weigh else "collect",
    )(me, *operands)


def down_kernel(cut, units_a, units_b, down, *rest):
    total = product(units_a[...], down[:cut, :]) + product(units_b[...], down[cut:, :])
    rest[-1][...] = total.astype(bf16)


def expert_down(units_a, units_b, down, *before):
    rows, cut = units_a.shape
    inner, width = down.shape
    m, n = tile_of(rows), tile_of(width)
    return pl.pallas_call(
        functools.partial(down_kernel, cut),
        grid=(width // n, rows // m),
        in_specs=[
            pl.BlockSpec((m, cut), lambda j, i: (i, 0)),
            pl.BlockSpec((m, inner - cut), lambda j, i: (i, 0)),
            pl.BlockSpec((inner, n), lambda j, i: (0, j)),
        ]
        + [pl.BlockSpec(memory_space=pl.ANY)] * len(before),
        out_specs=pl.BlockSpec((m, n), lambda j, i: (i, j)),
        out_shape=jax.ShapeDtypeStruct((rows, width), bf16),
        compiler_params=pltpu.CompilerParams(vmem_limit_bytes=48 * 2**20),
        cost_estimate=pl.CostEstimate(
            flops=2 * rows * inner * width,
            bytes_accessed=2 * (rows * inner + inner * width + rows * width),
            transcendentals=0,
        ),
        name="expert_down",
    )(units_a, units_b, down, *before)


def input_kernel(cut, dgate_a, dgate_b, dup_a, dup_b, gate, up, *rest):
    total = product_t(dgate_a[...], gate[:, :cut]) + product_t(dgate_b[...], gate[:, cut:])
    total += product_t(dup_a[...], up[:, :cut]) + product_t(dup_b[...], up[:, cut:])
    rest[-1][...] = total.astype(bf16)


def expert_input_grad(dgate_a, dgate_b, dup_a, dup_b, gate, up, start, stop, *before):
    rows, cut = dgate_a.shape
    inner = gate.shape[1]
    width = stop - start
    m, n = tile_of(rows), tile_of(width)
    first = start // n
    left_a = pl.BlockSpec((m, cut), lambda j, i: (i, 0))
    left_b = pl.BlockSpec((m, inner - cut), lambda j, i: (i, 0))
    right = pl.BlockSpec((n, inner), lambda j, i: (first + j, 0))
    return pl.pallas_call(
        functools.partial(input_kernel, cut),
        grid=(width // n, rows // m),
        in_specs=[left_a, left_b, left_a, left_b, right, right]
        + [pl.BlockSpec(memory_space=pl.ANY)] * len(before),
        out_specs=pl.BlockSpec((m, n), lambda j, i: (i, j)),
        out_shape=jax.ShapeDtypeStruct((rows, width), bf16),
        compiler_params=pltpu.CompilerParams(vmem_limit_bytes=52 * 2**20),
        cost_estimate=pl.CostEstimate(
            flops=4 * rows * inner * width,
            bytes_accessed=2 * (2 * rows * inner + 2 * inner * width + rows * width),
            transcendentals=0,
        ),
        name="expert_input_grad",
    )(dgate_a, dgate_b, dup_a, dup_b, gate, up, *before)


def tile_of(size):
    return max(c for c in range(16, 513, 16) if size % c == 0)


def anchor_kernel(*refs):
    pass


def after(a, *before):
    return pl.pallas_call(
        anchor_kernel,
        in_specs=[pl.BlockSpec(memory_space=pl.ANY)] * (1 + len(before)),
        out_specs=pl.BlockSpec(memory_space=pl.ANY),
        out_shape=jax.ShapeDtypeStruct(a.shape, a.dtype),
        input_output_aliases={0: 0},
        cost_estimate=pl.CostEstimate(flops=0, bytes_accessed=0, transcendentals=0),
        name="after",
    )(a, *before)


def norm_backward(grad_rows, normed, inverse, gain):
    weighted = grad_rows * gain
    mean_term = jnp.mean(weighted * normed, axis=-1, keepdims=True)
    return inverse * (weighted - normed * mean_term), jnp.sum(grad_rows * normed, axis=0)


def pick(a, index, axis):
    return lax.dynamic_index_in_dim(a, index, axis, keepdims=False)


def on_device(
    sizes,
    tokens,
    segments,
    routes,
    attn_norm,
    query_weight,
    key_weight,
    value_weight,
    output_weight,
    expert_norm,
    router,
    gate_weight,
    up_weight,
    down_weight,
    grad_out,
):
    dp_n, seq_n, r_n, y_n, core_n = sizes
    parts = r_n * core_n
    seq_count, seq_dev, width = tokens.shape
    piece = seq_dev // core_n
    length = segments.shape[1]
    home = seq_n * piece
    head = width // HEADS
    heads = HEADS // parts
    columns = width // parts
    experts = router.shape[1]
    topk = routes.shape[2]
    plane = 8 * home
    blocks = plane // seq_dev
    cap = 5 * seq_dev * topk // (4 * experts)
    dp_i, seq_i, r_i, y_i, core_i = (lax.axis_index(a) for a in EVERY)
    group, member = seq_i // seq_count, seq_i % seq_count

    rows_here = query_weight.shape[0]
    if r_n == 1 and parts == 2 and dp_n == 2 and y_n == 2 and seq_n == 2 * seq_count:
        weights, token_home, grad_home, chip_segments = first_transfers(
            query_weight, key_weight, value_weight, output_weight, tokens, grad_out, segments, sizes
        )
        segment = pick(pick(chip_segments, group, 0), member, 0)
    else:
        local = jnp.concatenate([query_weight, key_weight, value_weight, output_weight], axis=1)
        local = chip_exchange(local.reshape(rows_here, 4, parts, columns), 2, 0, parts)
        weights = lax.all_gather(
            local.reshape(parts * rows_here, 4 * columns), SPREAD, axis=0, tiled=True
        )
        weights = (
            weights.reshape(dp_n * seq_n, y_n, r_n, core_n * rows_here, -1)
            .transpose(0, 2, 1, 3, 4)
            .reshape(width, -1)
        )
        token_home, grad_home = to_sequences(tokens), to_sequences(grad_out)
        chip_segments = lax.all_gather(segments, "core")
        segment = pick(pick(chip_segments, group, 0), member, 0)
    weight_in, weight_out = weights[:, : 3 * columns], weights[:, 3 * columns :]

    token_float = token_home.astype(f32)
    inverse_one = lax.rsqrt(jnp.mean(token_float * token_float, axis=-1, keepdims=True) + epsilon)
    hidden_one = (token_float * inverse_one * attn_norm).astype(bf16)
    hidden_full = chip_gather(hidden_one, 1, parts).reshape(length, width)

    grad_plane = lax.all_gather(grad_home.reshape(home, width), PLANE, axis=0, tiled=True)

    half = head // 2
    frequency = theta_base ** (-jnp.arange(half, dtype=f32) / half)
    angles = jnp.arange(length, dtype=f32)[:, None] * frequency[None, :]
    cosine = jnp.concatenate([jnp.cos(angles)] * 2, axis=1)
    sine = jnp.concatenate([-jnp.sin(angles), jnp.sin(angles)], axis=1)
    seg_row, seg_col = segment[None, :], segment[:, None]

    qkv = product(hidden_full, weight_in)
    query, keys, values, mixed = attend(qkv, cosine, sine, seg_row, seg_col, heads)
    mixed_full = chip_gather(mixed, 1, parts)
    branch = product(mixed_full, weight_out).reshape(seq_n, parts, piece, columns)
    branch = chip_exchange(branch, 1, 3, parts).reshape(seq_n, piece, width)
    residual = token_float + branch
    inverse_two = lax.rsqrt(jnp.mean(residual * residual, axis=-1, keepdims=True) + epsilon)
    normed_two = residual * inverse_two
    hidden_two = (normed_two * expert_norm).astype(bf16).reshape(home, width)
    hidden_two = after(hidden_two, grad_plane)

    hidden_parts = [
        lax.all_gather(part, PLANE, axis=0, tiled=True) for part in jnp.split(hidden_two, 2)
    ]
    small = after(jnp.transpose(routes, (2, 0, 1)).reshape(topk * seq_count, seq_dev), hidden_two)
    small = lax.all_gather(small, EVERY, axis=0, tiled=True).reshape(
        dp_n, seq_n, r_n, y_n, core_n, topk, seq_count, seq_dev
    )
    small = pick(pick(small, group, 4), member, 5)
    plane_routes = pick(small, r_i, 2).transpose(0, 2, 1, 3, 4)
    block_routes = plane_routes.reshape(4, 2, seq_n // 2, topk, seq_dev)
    block_routes = block_routes.transpose(1, 0, 2, 3, 4).reshape(blocks, topk, seq_dev)
    home_routes = (
        pick(pick(plane_routes, dp_i, 0), y_i, 0)
        .reshape(seq_n, topk, core_n, piece)
        .transpose(1, 2, 0, 3)
    )
    home_routes = pick(home_routes, core_i, 1).reshape(topk, home)
    mine = y_i * core_n + core_i
    chosen = jnp.any(block_routes == mine, axis=1)
    places = jnp.arange(seq_dev)
    rank = product(chosen.astype(bf16), (places[:, None] < places[None, :]).astype(bf16))
    slot = jnp.where(chosen, rank.astype(jnp.int32), -1)
    slot_row, slot_col = slot[:, None, :], slot[:, :, None]
    me = jnp.stack([dp_i, y_i, core_i, mine]).astype(jnp.int32)
    gate_one, up_one, down_one = gate_weight[0], up_weight[0], down_weight[0]
    inner = gate_one.shape[1]
    cut = unit_cut(inner)
    full = (gate_one, up_one, down_one)
    route_col = jnp.transpose(block_routes, (0, 2, 1))
    picked, unit_parts = (), ()
    for part, hidden_part in enumerate(hidden_parts):
        picked = dispatch(
            me, hidden_part, grad_plane, slot_row, route_col, router, seq_n, piece, cap, part, picked
        )
        expert_in, dy_rows = (rows.reshape(blocks * cap, width) for rows in picked[:2])
        unit_parts = expert_units(expert_in, dy_rows, *full, 0, cut, part, unit_parts)
    row_gate = picked[2]
    units_a, dgpre_a, dupre_a = unit_parts

    def over_ctx(part):
        return lax.psum_scatter(part, CTX, scatter_dimension=0, tiled=True)

    def rows_product(rows, part):
        return t_product(rows, part).astype(bf16)

    down_a = rows_product(dy_rows, units_a)
    units_b, dgpre_b, dupre_b = expert_units(expert_in, dy_rows, *full, cut, inner, before=(down_a,))
    down_b = rows_product(dy_rows, units_b)
    down_sum_a, down_sum_b = over_ctx(down_a), over_ctx(down_b)
    grads = (dgpre_a, dgpre_b, dupre_a, dupre_b, gate_one, up_one)
    left = expert_input_grad(*grads, 0, width // 2, down_b)
    right = expert_input_grad(*grads, width // 2, width, left)
    left, right = (part.reshape(blocks, cap, width // 2) for part in (left, right))
    [back] = combine(me, left, slot_col, seq_n, piece, right=right)
    gate_a = rows_product(expert_in, after(dgpre_a, back, down_sum_a))
    gate_b = rows_product(expert_in, after(dgpre_b, back))
    gate_sum_a, gate_sum_b = over_ctx(gate_a), over_ctx(gate_b)
    ypair = expert_down(units_a, units_b, down_one, gate_a)
    mixed_rows, dgate_plane = combine(
        me, ypair.reshape(blocks, cap, width), slot_col, seq_n, piece, row_gate, grad_plane
    )

    dgate_plane = dgate_plane.reshape(2, 4, seq_n // 2, core_n, piece).transpose(1, 3, 0, 2, 4)
    dgate_home = lax.all_to_all(
        dgate_plane.reshape(8, home), PLANE, split_axis=0, concat_axis=0, tiled=True
    ).reshape(dp_n, experts, home).sum(axis=0)

    logits = product(hidden_two, router)
    hot = home_routes[:, :, None] == jnp.arange(experts, dtype=jnp.int32)[None, None, :]
    gates = jax.nn.softmax(jnp.sum(jnp.where(hot, logits[None], 0.0), axis=2), axis=0)
    dgate = jnp.sum(jnp.where(hot, jnp.transpose(dgate_home)[None], 0.0), axis=2)
    dsel = gates * (dgate - jnp.sum(gates * dgate, axis=0, keepdims=True))
    dlogits = jnp.sum(jnp.where(hot, dsel[:, :, None], 0.0), axis=0).astype(bf16)
    router_grad = t_product(hidden_two, dlogits)
    up_b = rows_product(expert_in, after(dupre_b, gate_a))

    def once_gate(stage, *arrays):
        return (after(arrays[0], up_b if stage else gate_a),) + arrays[1:]

    dhidden_two = plane_scatter(back, once_gate).reshape(home, width) + product_t(dlogits, router)

    flat_two = normed_two.reshape(home, width)
    dresid, expert_norm_grad = norm_backward(
        dhidden_two, flat_two, inverse_two.reshape(home, 1), expert_norm
    )
    dresid = dresid + grad_home.reshape(home, width).astype(f32)
    dbranch = chip_gather(dresid.astype(bf16).reshape(seq_n, piece, width), 1, parts).reshape(length, width)
    column_start = (r_i * core_n + core_i) * columns
    dbranch_here = lax.dynamic_slice_in_dim(dbranch, column_start, columns, 1)
    dmixed = chip_scatter(product_t(dbranch_here, weight_out).astype(bf16), 1, parts).astype(bf16)
    stages = {}

    def check(stage, *arrays):
        stages[stage] = arrays
        return arrays

    mixture = plane_scatter(after(mixed_rows, dbranch), check)
    dqpre, dkpre, dvpre = attend_back(
        query, keys, values, mixed, dmixed, cosine, sine, seg_row, seg_col, heads, down_sum_b, up_b, *stages[0]
    )
    dqkv = jnp.concatenate([dqpre, dkpre, dvpre], axis=1)
    dhidden_part = product_t(dqkv, weight_in).astype(bf16)
    up_a = rows_product(expert_in, after(dupre_a, dhidden_part, *stages[1]))
    output = (residual + mixture).astype(bf16)
    out_grad = t_product(mixed_full, after(dbranch_here, up_a, output)).astype(bf16)
    dkv = jnp.concatenate([dkpre, dvpre], axis=1)
    kv_grad = t_product(hidden_full, after(dkv, out_grad)).astype(bf16)
    query_grad = t_product(hidden_full, after(dqpre, out_grad)).astype(bf16)
    dhidden_one = chip_scatter(
        dhidden_part.reshape(seq_n, parts * piece, width), 1, parts
    )
    normed_one = token_float * inverse_one
    dtokens, attn_norm_grad = norm_backward(
        dhidden_one.reshape(home, width),
        normed_one.reshape(home, width),
        inverse_one.reshape(home, 1),
        attn_norm,
    )
    dtokens = (dtokens + dresid).astype(bf16).reshape(seq_n, piece, width)

    grad_down = jnp.concatenate([down_sum_a, down_sum_b], axis=1).astype(f32).T[None]
    grad_gate = jnp.concatenate([gate_sum_a, gate_sum_b], axis=1).astype(f32)[None]
    grad_up = jnp.concatenate([over_ctx(up_a), over_ctx(up_b)], axis=1).astype(f32)[None]

    def seen(part):
        return part.reshape(dp_n, seq_n, r_n, y_n, core_n * rows_here, -1)

    def half(a, axis, index, name):
        keep, give = pick(a, index, axis), pick(a, 1 - index, axis)
        return total(keep, swap(give, name)).astype(bf16)

    first = [half(seen(a), 0, dp_i, "dp") for a in (out_grad, query_grad)]
    first.append(half(seen(kv_grad), 3, y_i, "y"))
    output = [after(piece, first[2]) for piece in seq_pieces(output)]
    output = core_exchange(seq_order(output), 0, 1)
    second = [half(a, 2, y_i, "y") for a in first[:2]] + [half(first[2], 0, dp_i, "dp")]
    second = jnp.concatenate(second, axis=-1)
    if r_n == 1 and parts == 2 and seq_n == 2 * seq_count == 4:
        part, grad_tokens = last_transfers(
            second.reshape(seq_n, core_n * rows_here, 4 * columns), dtokens, output, seq_count
        )
        part = total(part[:, 0], part[:, 1]).reshape(core_n, rows_here, 4, columns)
        part = part.transpose(1, 2, 0, 3).reshape(rows_here, 4, width)
    else:
        grad_tokens = from_sequences(dtokens)
        part = total(*seq_pieces(second)).astype(bf16)
        part = part.reshape(parts, rows_here, 4, 1, columns)
        part = chip_exchange(part, 0, 3, parts).reshape(rows_here, 4, width).astype(f32)
    grad_output, grad_query, grad_key, grad_value = (part[:, i] for i in range(4))
    grad_tokens = grad_tokens.astype(f32)

    gains = jnp.concatenate([attn_norm_grad[None], expert_norm_grad[None], router_grad.T], axis=0)
    gain_n = gains.shape[0]
    gains = gains.reshape(gain_n, -1, rows_here).transpose(1, 0, 2)
    gains = lax.all_to_all(gains, EVERY, split_axis=0, concat_axis=0, tiled=True)
    gains = jnp.sum(gains, axis=0).T

    return (
        output,
        grad_tokens,
        gains[:, 0],
        grad_query,
        grad_key,
        grad_value,
        grad_output,
        gains[:, 1],
        gains[:, 2:],
        grad_gate,
        grad_up,
        grad_down,
    )


def solution(mesh):
    dp_n, ctx_n, exp_n = mesh.shape["dp"], mesh.shape["ctx"], mesh.shape["exp"]

    def block(*arrays):
        tokens = arrays[0]
        seq_count = tokens.shape[0] // (dp_n * exp_n)
        seq_n = seq_count * CORES
        sizes = (dp_n, seq_n, ctx_n // seq_n, exp_n // CORES, CORES)
        fine = Mesh(mesh.devices.reshape(sizes), EVERY)
        group = ("dp", "y", "core")
        exp = ("y", "core")
        return jax.shard_map(
            functools.partial(on_device, sizes),
            mesh=fine,
            in_specs=(
                P(group, CTX, None),
                P(group, None),
                P(group, CTX, None),
                P(),
                P(EVERY, None),
                P(EVERY, None),
                P(EVERY, None),
                P(EVERY, None),
                P(),
                P(),
                P(exp, None, "dp"),
                P(exp, None, "dp"),
                P(exp, "dp", None),
                P(group, CTX, None),
            ),
            out_specs=(
                P(group, CTX, None),
                P(group, CTX, None),
                P(EVERY),
                P(EVERY, None),
                P(EVERY, None),
                P(EVERY, None),
                P(EVERY, None),
                P(EVERY),
                P(EVERY, None),
                P(exp, CTX, "dp"),
                P(exp, CTX, "dp"),
                P(exp, "dp", CTX),
            ),
            check_vma=False,
        )(*arrays)

    return block
```
